32 devices in a mesh: ctx: 16 (over z, x, core), wsh: 2 (over y).
Axes of the slice: x: 2, y: 2, z: 4, core: 2. Of those that a mesh axis runs over, the one named last changes fastest.
Arguments:
- patches: bfloat16 [2, 4096, 768], P('wsh', 'ctx'), may hold values from -6 to 6
- doc_lengths: int32 [2, 8], P('wsh'), may hold values from 1 to 2048, 4096 in all within a row
- norm1_gain: bfloat16 [768], P('wsh'), may hold values from 0.5 to 1.5
- norm1_bias: bfloat16 [768], P('wsh'), may hold values from -3 to 3
- w_qkv: bfloat16 [768, 2304], P('wsh'), may hold values from -0.21875 to 0.21875
- b_qv: bfloat16 [1536], P('wsh'), may hold values from -3 to 3
- w_out: bfloat16 [768, 768], P('wsh'), may hold values from -6 to 6
- b_out: bfloat16 [768], P('wsh'), may hold values from -2 to 2
- norm2_gain: bfloat16 [768], P('wsh'), may hold values from 0.5 to 1.5
- norm2_bias: bfloat16 [768], P('wsh'), may hold values from -3 to 3
- w_up: bfloat16 [768, 3072], P('wsh'), may hold values from -0.21875 to 0.21875
- b_up: bfloat16 [3072], P('wsh'), may hold values from -3 to 3
- w_down: bfloat16 [3072, 768], P('wsh'), may hold values from -0.109375 to 0.109375
- b_down: bfloat16 [768], P('wsh'), may hold values from -3 to 3
- cotangent: bfloat16 [2, 4096, 768], P('wsh', 'ctx'), may hold values from -6 to 6
Outputs:
- mixed: bfloat16 [2, 4096, 768], P('wsh', 'ctx')
- patches_grad: float32 [2, 4096, 768], P('wsh', 'ctx')
- norm1_gain_grad: float32 [768], P('wsh')
- norm1_bias_grad: float32 [768], P('wsh')
- w_qkv_grad: float32 [768, 2304], P('wsh')
- b_qv_grad: float32 [1536], P('wsh')
- w_out_grad: float32 [768, 768], P('wsh')
- b_out_grad: float32 [768], P('wsh')
- norm2_gain_grad: float32 [768], P('wsh')
- norm2_bias_grad: float32 [768], P('wsh')
- w_up_grad: float32 [768, 3072], P('wsh')
- b_up_grad: float32 [3072], P('wsh')
- w_down_grad: float32 [3072, 768], P('wsh')
- b_down_grad: float32 [768], P('wsh')
The draws below stay inside these ranges and needn't reach their ends.
Inputs may be any that keep to these rules, and one draw needn't show every extreme that they name: Each row of doc_lengths sums to 4096, and its largest entry is exactly 2048.
All inputs are finite; a program needn't handle non-finite values.
Results may differ from the reference program's by a relative error of at most 0.02.
Values may be sent and summed in bfloat16 or wider, within the bound.
A program may use at most 128 MiB of HBM per device.

```python
import math
import jax
import jax.numpy as jnp
import numpy as np
from jax import lax

D = 768
H = 12
HD = 64
FF = 3072
DOCS = 8
SEQ = 4096
DOC_MOST = 2048
N_WSH = 2


def block_levels(rng, shape, pieces, least, high):
    loudness = 1.0
    for dim, blocks in pieces:
        draws = jax.random.uniform(jax.random.fold_in(jax.random.fold_in(rng, 6), dim), (blocks,), jnp.float32, least / len(pieces), high / len(pieces))
        loudness = loudness * jnp.repeat(jnp.exp(draws), shape[dim] // blocks).reshape((-1,) + (1,) * (len(shape) - 1 - dim))
    return loudness


def length_profile(number_of, total, reach, lean):
    loads = [(1 << 20) // math.isqrt(grade ** lean) + 1 for grade in range(2, number_of + 1)]
    surplus, holding = total - reach - (number_of - 1), [1] * (number_of - 1)
    while surplus > 0:
        candidates = [i for i in range(number_of - 1) if holding[i] < reach]
        pool, budget = sum([loads[i] for i in candidates]), surplus
        for i in candidates:
            addition = min(reach - holding[i], max(1, budget * loads[i] // pool), surplus)
            holding[i] = holding[i] + addition
            surplus = surplus - addition
    return np.array([reach] + holding)


def uneven_parts(own_key, number_of, total, most, slope):
    if number_of == 2:
        one = jax.random.randint(own_key, (), max(1, total - most), min(most, total - 1) + 1)
        return jnp.stack([one, total - one])
    sizes = jnp.asarray(length_profile(number_of, total, most, slope), jnp.int32)
    twos = (number_of - 1) // 2
    donor, receiver = sizes[1:1 + 2 * twos:2], sizes[2:2 + 2 * twos:2]
    margin = jnp.minimum(donor - 1, most - receiver)
    passed = jax.random.randint(jax.random.fold_in(own_key, 1), (twos,), 0, 1 << 20) % (margin + 1)
    sizes = sizes.at[1:1 + 2 * twos:2].set(donor - passed).at[2:2 + 2 * twos:2].set(receiver + passed)
    return sizes[jax.random.permutation(jax.random.fold_in(own_key, 2), number_of)]


def centred(own_key, shape, scale, reach, cuts=(), kind=jnp.bfloat16):
    result = jax.random.normal(own_key, shape, jnp.float32) * scale
    if len(cuts) > 0:
        result = block_levels(own_key, shape, cuts, -0.22, 0.18) * result
    return jnp.clip(result, min=-reach, max=reach).astype(kind)


def setup_inputs(seed: int = 0) -> dict:
    arg_keys = jax.random.split(jax.random.key(seed), 16)
    patches = centred(arg_keys[0], (N_WSH, SEQ, D), 1.0, 6.0, ((0, 2), (1, 16)))
    doc_lengths = jax.vmap(lambda own: uneven_parts(own, DOCS, SEQ, DOC_MOST, 2))(jax.random.split(arg_keys[1], N_WSH)).reshape((N_WSH, DOCS)).astype(jnp.int32)
    norm1_gain = jnp.clip(1.0 + 0.1 * jax.random.normal(arg_keys[2], (D,), jnp.float32), 0.5, 1.5).astype(jnp.bfloat16)
    norm1_bias = centred(arg_keys[3], (D,), 0.5, 3.0, ((0, 2),))
    w_qkv = centred(arg_keys[4], (D, 3 * D), D ** -0.5, 0.21875, ((0, 2),))
    b_qv = centred(arg_keys[5], (2 * D,), 0.5, 3.0, ((0, 2),))
    w_out = centred(arg_keys[6], (D, D), 1 ** -0.5, 6.0, ((0, 2),))
    b_out = centred(arg_keys[7], (D,), 0.3, 2.0, ((0, 2),))
    norm2_gain = jnp.clip(1.0 + 0.1 * jax.random.normal(arg_keys[8], (D,), jnp.float32), 0.5, 1.5).astype(jnp.bfloat16)
    norm2_bias = centred(arg_keys[9], (D,), 0.5, 3.0, ((0, 2),))
    w_up = centred(arg_keys[10], (D, FF), D ** -0.5, 0.21875, ((0, 2),))
    b_up = centred(arg_keys[11], (FF,), 0.5, 3.0, ((0, 2),))
    w_down = centred(arg_keys[12], (FF, D), FF ** -0.5, 0.109375, ((0, 2),))
    b_down = centred(arg_keys[13], (D,), 0.6, 3.0, ((0, 2),))
    cotangent = centred(arg_keys[14], (N_WSH, SEQ, D), 1.0, 6.0, ((0, 2), (1, 16)))
    return dict(patches=patches, doc_lengths=doc_lengths, norm1_gain=norm1_gain, norm1_bias=norm1_bias, w_qkv=w_qkv, b_qv=b_qv, w_out=w_out, b_out=b_out, norm2_gain=norm2_gain, norm2_bias=norm2_bias, w_up=w_up, b_up=b_up, w_down=w_down, b_down=b_down, cotangent=cotangent)


epsilon = 1e-05
masked_score = -1e+30

@jax.custom_vjp
def low(v):
    return lax.optimization_barrier(v.astype(jnp.bfloat16)).astype(jnp.float32)

@jax.custom_vjp
def low_back(v):
    return v

def low_keep(v):
    return (low(v), None)

def low_pass(kept, grad):
    return (grad,)

def back_keep(v):
    return (v, None)

def back_low(kept, grad):
    return (low(grad),)
low.defvjp(low_keep, low_pass)
low_back.defvjp(back_keep, back_low)

def layer_norm(values, gain, offset):
    centre = lax.optimization_barrier(jnp.mean(values, axis=-1, keepdims=True))
    shifted = values - centre
    spread = lax.optimization_barrier(jnp.mean(shifted * shifted, axis=-1, keepdims=True))
    return shifted * lax.rsqrt(spread + epsilon) * gain + offset

def doc_index(positions, doc_starts):
    hits = (doc_starts[None, :] <= positions[:, None]).astype(jnp.int32)
    return (lax.optimization_barrier(jnp.sum(hits, axis=1)) - 1).astype(jnp.int32)

def highest_dot(left, right):
    return jnp.dot(left, right, precision=lax.Precision.HIGHEST)

def attend_rows(item, key_heads, value_heads, key_docs):
    query_block, query_docs = item
    scores = low_back(jnp.einsum('qhd,khd->hqk', query_block, key_heads, precision=lax.Precision.HIGHEST) * 0.125)
    same_doc = (query_docs[:, None] == key_docs[None, :])[None]
    probs = jax.nn.softmax(jnp.where(same_doc, scores, masked_score), axis=-1)
    return jnp.einsum('hqk,khd->qhd', low(probs), value_heads, precision=lax.Precision.HIGHEST)

def forward_one(inputs, params, lengths):
    gain1, bias1, wqkv, bqv, wout, bout, gain2, bias2, wup, bup, wdown, bdown = params
    doc_starts = (jnp.cumsum(lengths) - lengths).astype(jnp.int32)
    docs = doc_index(jnp.arange(SEQ, dtype=jnp.int32), doc_starts)
    normed1 = low(layer_norm(inputs, gain1, bias1))
    projected = highest_dot(normed1, wqkv)
    query = low_back(low(projected[:, :D] + bqv[:D]))
    key = low_back(low(projected[:, D:2 * D]))
    value = low_back(low(projected[:, 2 * D:] + bqv[D:]))
    block = math.gcd(SEQ, 512)
    blocks = SEQ // block
    key_heads = key.reshape(SEQ, H, HD)
    value_heads = value.reshape(SEQ, H, HD)
    step = jax.checkpoint(lambda item: attend_rows(item, key_heads, value_heads, docs))
    attended = lax.map(step, (query.reshape(blocks, block, H, HD), docs.reshape(blocks, block)))
    attended = low_back(low(attended.reshape(SEQ, D)))
    branch = low_back(highest_dot(attended, wout) + bout)
    hidden_sum = inputs + branch
    normed2 = low(layer_norm(hidden_sum, gain2, bias2))
    pre_act = low_back(highest_dot(normed2, wup) + bup)
    activated = low(jax.nn.gelu(pre_act, approximate=False))
    return hidden_sum + highest_dot(activated, wdown) + bdown

def forward_all(inputs, params, doc_lengths):
    outputs = [forward_one(inputs[index], params, doc_lengths[index]) for index in range(N_WSH)]
    return jnp.stack(outputs)

def reference(patches, doc_lengths, norm1_gain, norm1_bias, w_qkv, b_qv, w_out, b_out, norm2_gain, norm2_bias, w_up, b_up, w_down, b_down, cotangent):
    params = tuple((item.astype(jnp.float32) for item in (norm1_gain, norm1_bias, w_qkv, b_qv, w_out, b_out, norm2_gain, norm2_bias, w_up, b_up, w_down, b_down)))
    inputs = patches.astype(jnp.float32)
    mixed, backward = jax.vjp(lambda values, weights: forward_all(values, weights, doc_lengths), inputs, params)
    inputs_grad, grads = backward(cotangent.astype(jnp.float32))
    return (mixed.astype(jnp.bfloat16), inputs_grad, grads[0], grads[1], grads[2], grads[3], grads[4], grads[5], grads[6], grads[7], grads[8], grads[9], grads[10], grads[11])
```

```python
import functools

import jax
import jax.numpy as jnp
from jax import lax
from jax.experimental import pallas as pl
from jax.experimental.pallas import tpu as pltpu
from jax.sharding import PartitionSpec as P

H = 12
HD = 64
GROUPS = 4
PER_GROUP = H // GROUPS
PEERS = 4
MESH = pl.DeviceIdType.MESH
MIB = 2**20

epsilon = 1e-05
masked_score = -1e30


def params(vmem_mib, collective_id=None):
    if collective_id is None:
        return pltpu.CompilerParams(vmem_limit_bytes=vmem_mib * MIB)
    return pltpu.CompilerParams(
        vmem_limit_bytes=vmem_mib * MIB, collective_id=collective_id, has_side_effects=True
    )


def here():
    ctx = lax.axis_index("ctx")
    return ctx // PEERS, (ctx // 2) % 2, ctx % 2, lax.axis_index("wsh")


def at(z, x, core, y):
    return (z * PEERS + x * 2 + core, y)


def remote(src, dst, send, recv, device):
    return pltpu.make_async_remote_copy(
        src_ref=src,
        dst_ref=dst,
        send_sem=send,
        recv_sem=recv,
        device_id=device,
        device_id_type=MESH,
    )


def greet(devices):
    barrier = pltpu.get_barrier_semaphore()
    for device in devices:
        pl.semaphore_signal(barrier, inc=1, device_id=device, device_id_type=MESH)
    pl.semaphore_wait(barrier, len(devices))


def weight_pieces(shapes, most):
    pieces = []
    for index, (rows, columns) in enumerate(shapes):
        quarter = rows // PEERS
        step = quarter
        while step * columns * 2 > most and step % 32 == 0:
            step //= 2
        pieces += [(index, first, step) for first in range(0, quarter, step)]
    return pieces


def weights_kernel(count, pieces, *refs):
    halves, fulls = refs[: count + 1], refs[count + 1 : 2 * count + 2]
    local, ysend, yrecv, xsend, xrecv, csend, crecv, fsend, frecv, small_sem = refs[2 * count + 2 :]
    z, x, core, y = here()
    over_y, over_x, over_core = at(z, x, core, 1 - y), at(z, 1 - x, core, y), at(z, x, 1 - core, y)
    greet([over_y, over_x, over_core])
    small = remote(halves[count], fulls[count].at[y], small_sem.at[0], small_sem.at[1], over_y)
    small.start()
    own = [
        pltpu.make_async_copy(halves[i], fulls[i].at[y], local.at[i]) for i in range(count + 1)
    ]

    def spot(piece, px, pcore):
        index, first, rows = piece
        quarter = fulls[index].shape[1] // PEERS
        return pl.ds((px * 2 + pcore) * quarter + first, rows)

    sends = []
    for k, piece in enumerate(pieces):
        index = piece[0]
        rows = spot(piece, x, core)
        copy = remote(
            halves[index].at[rows], fulls[index].at[y, rows], ysend.at[k], yrecv.at[k], over_y
        )
        copy.start()
        sends.append(copy)
    for copy in own:
        copy.start()

    def landing(k, px, pcore, sem):
        index = pieces[k][0]
        view = fulls[index].at[1 - y, spot(pieces[k], px, pcore)]
        return remote(view, view, sem, sem, over_core)

    def forward(k, px, pcore, send, recv, device):
        index = pieces[k][0]
        view = fulls[index].at[1 - y, spot(pieces[k], px, pcore)]
        copy = remote(view, view, send.at[k], recv.at[k], device)
        copy.start()
        sends.append(copy)

    total = len(pieces)
    for k in range(total + 1):
        if k < total:
            landing(k, x, core, yrecv.at[k]).wait_recv()
            forward(k, x, core, xsend, xrecv, over_x)
            forward(k, x, core, csend, crecv, over_core)
        if k >= 1:
            landing(k - 1, 1 - x, core, xrecv.at[k - 1]).wait_recv()
            forward(k - 1, 1 - x, core, fsend, frecv, over_core)
    for k in range(total):
        landing(k, x, 1 - core, crecv.at[k]).wait_recv()
        landing(k, 1 - x, 1 - core, frecv.at[k]).wait_recv()
    small.wait()
    for copy in own:
        copy.wait()
    for copy in sends:
        copy.wait_send()


def gather_weights(halves, small):
    pieces = weight_pieces([half.shape for half in halves], 320 * 1024)
    count, total = len(halves), len(pieces)
    everything = list(halves) + [small]
    anywhere = pl.BlockSpec(memory_space=pltpu.HBM)
    sems = [pltpu.SemaphoreType.DMA((count + 1,))]
    sems += [pltpu.SemaphoreType.DMA((total,))] * 8 + [pltpu.SemaphoreType.DMA((2,))]
    return pl.pallas_call(
        functools.partial(weights_kernel, count, pieces),
        out_shape=[jax.ShapeDtypeStruct((2,) + a.shape, a.dtype) for a in everything],
        in_specs=[anywhere] * (count + 1),
        out_specs=[anywhere] * (count + 1),
        scratch_shapes=sems,
        compiler_params=params(16, 1),
        name="gather_weights",
    )(*everything)


def spread_kernel(mine, query, keys, local, zsend, zrecv, xsend, xrecv, csend, crecv, fsend, frecv):
    z, x, core, y = here()
    width = query.shape[1]
    over_x, over_core = at(z, 1 - x, core, y), at(z, x, 1 - core, y)
    around = [at((z + d) % GROUPS, x, core, y) for d in range(1, GROUPS)]
    greet(around + [over_x, over_core])
    sends = []

    def go(src, dst, send, recv, device):
        copy = remote(src, dst, send, recv, device)
        copy.start()
        sends.append(copy)

    def block(pz, px, pcore):
        return keys.at[pz * PEERS + px * 2 + pcore]

    own_query = pltpu.make_async_copy(mine.at[z, pl.ds(0, width)], query.at[z], local.at[0])
    own_keys = pltpu.make_async_copy(
        mine.at[z, pl.ds(width, 2 * width)], block(z, x, core), local.at[1]
    )
    own_keys.start()
    own_query.start()
    for d in (2, 1, 3):
        target = (z + d) % GROUPS
        src = mine.at[target, pl.ds(width, 2 * width)]
        go(src, block(z, x, core), zsend.at[d], zrecv.at[d], around[d - 1])
    for d in (2, 1, 3):
        target = (z + d) % GROUPS
        src = mine.at[target, pl.ds(0, width)]
        go(src, query.at[z], zsend.at[GROUPS + d], zrecv.at[GROUPS + d], around[d - 1])
    order = (0, 3, 1, 2)
    for step in range(GROUPS + 1):
        if step < GROUPS:
            d = order[step]
            pz = (z + GROUPS - d) % GROUPS
            view = block(pz, x, core)
            if d == 0:
                own_keys.wait()
            else:
                remote(view, view, zsend.at[d], zrecv.at[d], over_x).wait_recv()
            go(view, view, xsend.at[d], xrecv.at[d], over_x)
            go(view, view, csend.at[d], crecv.at[d], over_core)
        if step >= 1:
            d = order[step - 1]
            view = block((z + GROUPS - d) % GROUPS, 1 - x, core)
            remote(view, view, xsend.at[d], xrecv.at[d], over_x).wait_recv()
            go(view, view, fsend.at[d], frecv.at[d], over_core)
    for d in range(GROUPS):
        pz = (z + GROUPS - d) % GROUPS
        near, far = block(pz, x, 1 - core), block(pz, 1 - x, 1 - core)
        remote(near, near, csend.at[d], crecv.at[d], over_core).wait_recv()
        remote(far, far, fsend.at[d], frecv.at[d], over_core).wait_recv()
        if d > 0:
            part = query.at[pz]
            sem = GROUPS + d
            remote(part, part, zsend.at[sem], zrecv.at[sem], over_x).wait_recv()
    own_query.wait()
    for copy in sends:
        copy.wait_send()


def spread_heads(projected):
    groups, width, rows = projected.shape
    width //= 3
    anywhere = pl.BlockSpec(memory_space=pltpu.HBM)
    sems = [pltpu.SemaphoreType.DMA((2,))] + [pltpu.SemaphoreType.DMA((2 * groups,))] * 2
    sems += [pltpu.SemaphoreType.DMA((groups,))] * 6
    return pl.pallas_call(
        spread_kernel,
        out_shape=[
            jax.ShapeDtypeStruct((groups, width, rows), projected.dtype),
            jax.ShapeDtypeStruct((groups * PEERS, 2 * width, rows), projected.dtype),
        ],
        in_specs=[anywhere],
        out_specs=[anywhere] * 2,
        scratch_shapes=sems,
        compiler_params=params(16, 2),
        name="spread_heads",
    )(projected)


def swap_kernel(mine, theirs, local, send, recv):
    z, x, core, y = here()
    around = [at((z + d) % GROUPS, x, core, y) for d in range(1, GROUPS)]
    greet(around)
    copies = []
    for d in (2, 1, 3):
        target = (z + d) % GROUPS
        copy = remote(mine.at[target], theirs.at[z], send.at[d], recv.at[d], around[d - 1])
        copy.start()
        copies.append(copy)
    own = pltpu.make_async_copy(mine.at[z], theirs.at[z], local)
    own.start()
    for d in range(1, GROUPS):
        view = theirs.at[(z + GROUPS - d) % GROUPS]
        remote(view, view, send.at[d], recv.at[d], around[d - 1]).wait_recv()
    for copy in copies:
        copy.wait_send()
    own.wait()


def swap_groups(mine):
    anywhere = pl.BlockSpec(memory_space=pltpu.HBM)
    return pl.pallas_call(
        swap_kernel,
        out_shape=jax.ShapeDtypeStruct(mine.shape, mine.dtype),
        in_specs=[anywhere],
        out_specs=anywhere,
        scratch_shapes=[pltpu.SemaphoreType.DMA] + [pltpu.SemaphoreType.DMA((GROUPS,))] * 2,
        compiler_params=params(16, 3),
        name="swap_groups",
    )(mine)


def collect_kernel(
    query_grad, key_grad, out, near, half, far, own, local, csend, crecv, xsend, xrecv, zsend, zrecv
):
    z, x, core, y = here()
    width = query_grad.shape[1]
    over_x, over_core = at(z, 1 - x, core, y), at(z, x, 1 - core, y)
    around = [at((z + d) % GROUPS, x, core, y) for d in range(1, GROUPS)]
    greet(around + [over_x, over_core])
    sends = []

    def go(src, dst, send, recv, device):
        copy = remote(src, dst, send, recv, device)
        copy.start()
        sends.append(copy)

    order = (2, 1, 3, 0)
    for d in order:
        pz = (z + d) % GROUPS
        for k in range(2):
            px = (x + 1 + k) % 2
            src = key_grad.at[pz * PEERS + px * 2 + 1 - core]
            slot = 2 * d + k
            go(src, near.at[slot], csend.at[slot], crecv.at[slot], over_core)
    for d in (2, 1, 3):
        pz = (z + d) % GROUPS
        go(query_grad.at[pz], out.at[z, pl.ds(0, width)], zsend.at[d], zrecv.at[d], around[d - 1])
    own_query = pltpu.make_async_copy(query_grad.at[z], out.at[z, pl.ds(0, width)], local.at[0])
    own_query.start()
    for step in range(GROUPS + 1):
        if step < GROUPS:
            d = order[step]
            pz = (z + d) % GROUPS
            for k in range(2):
                px = (x + 1 + k) % 2
                slot = 2 * d + k
                landed = near.at[slot]
                remote(landed, landed, csend.at[slot], crecv.at[slot], over_core).wait_recv()
                mine = key_grad[pz * PEERS + px * 2 + core].astype(jnp.float32)
                both = (mine + near[slot].astype(jnp.float32)).astype(out.dtype)
                half[slot] = both
                if k == 0:
                    go(half.at[slot], far.at[d], xsend.at[d], xrecv.at[d], over_x)
        if step >= 1:
            d = order[step - 1]
            landed = far.at[d]
            remote(landed, landed, xsend.at[d], xrecv.at[d], over_x).wait_recv()
            total = half[2 * d + 1].astype(jnp.float32) + far[d].astype(jnp.float32)
            own[d] = total.astype(out.dtype)
            place = out.at[z, pl.ds(width, 2 * width)]
            if d == 0:
                own_keys = pltpu.make_async_copy(own.at[0], place, local.at[1])
                own_keys.start()
            else:
                sem = GROUPS + d
                go(own.at[d], place, zsend.at[sem], zrecv.at[sem], around[d - 1])
    for d in range(1, GROUPS):
        pz = (z + GROUPS - d) % GROUPS
        part = out.at[pz, pl.ds(0, width)]
        remote(part, part, zsend.at[d], zrecv.at[d], over_x).wait_recv()
        part = out.at[pz, pl.ds(width, 2 * width)]
        sem = GROUPS + d
        remote(part, part, zsend.at[sem], zrecv.at[sem], over_x).wait_recv()
    own_query.wait()
    own_keys.wait()
    for copy in sends:
        copy.wait_send()


def collect_heads(query_grad, key_grad):
    groups, width, rows = query_grad.shape
    vmem = pl.BlockSpec(memory_space=pltpu.VMEM)
    anywhere = pl.BlockSpec(memory_space=pltpu.HBM)
    piece = (2 * width, rows)
    kind = query_grad.dtype
    sems = [pltpu.SemaphoreType.DMA((2,))] + [pltpu.SemaphoreType.DMA((2 * groups,))] * 2
    sems += [pltpu.SemaphoreType.DMA((groups,))] * 2 + [pltpu.SemaphoreType.DMA((2 * groups,))] * 2
    return pl.pallas_call(
        collect_kernel,
        out_shape=jax.ShapeDtypeStruct((groups, 3 * width, rows), kind),
        in_specs=[anywhere, vmem],
        out_specs=anywhere,
        scratch_shapes=[
            pltpu.VMEM((2 * groups,) + piece, kind),
            pltpu.VMEM((2 * groups,) + piece, kind),
            pltpu.VMEM((groups,) + piece, kind),
            pltpu.VMEM((groups,) + piece, kind),
        ]
        + sems,
        compiler_params=params(32, 4),
        name="collect_heads",
    )(query_grad, key_grad)


def reduce_kernel(
    chunks,
    grads,
    vector,
    out,
    vector_out,
    c_land,
    y_from,
    y_land,
    x_from,
    x_land,
    z_from,
    z_land,
    vectors,
    v_land,
    csend,
    crecv,
    ysend,
    yrecv,
    xsend,
    xrecv,
    zsend,
    zrecv,
    gsend,
    grecv,
    hsend,
    hrecv,
    isend,
    irecv,
    vsend,
    vrecv,
):
    z, x, core, y = here()
    over_x, over_core, over_y = (
        at(z, 1 - x, core, y),
        at(z, x, 1 - core, y),
        at(z, x, core, 1 - y),
    )
    around = [at((z + d) % GROUPS, x, core, y) for d in range(1, GROUPS)]
    greet(around + [over_x, over_core, over_y])
    sends = []
    f32 = jnp.float32

    def go(src, dst, send, recv, device):
        copy = remote(src, dst, send, recv, device)
        copy.start()
        sends.append(copy)

    def landed(view, sem):
        remote(view, view, sem, sem, over_core).wait_recv()

    half = c_land.shape[2]
    rows_y, rows_x, rows_z = y_land.shape[1], x_land.shape[1], z_land.shape[2]

    def columns(c):
        return pl.ds(pl.multiple_of(c * half, half), half)

    for k in range(chunks):
        go(grads.at[k, :, columns(1 - core)], c_land.at[k], csend.at[k], crecv.at[k], over_core)

    vectors[0] = vector[...]
    go(vectors.at[0], v_land.at[0], vsend.at[0], vrecv.at[0], over_core)

    def stage_core(k):
        landed(c_land.at[k], crecv.at[k])
        other = pl.ds((1 - y) * rows_y, rows_y)
        mine = pl.ds(y * rows_y, rows_y)
        y_from[k] = (
            grads[k, other, columns(core)].astype(f32) + c_land[k, other].astype(f32)
        ).astype(out.dtype)
        go(y_from.at[k], y_land.at[k], ysend.at[k], yrecv.at[k], over_y)
        x_from[k] = (
            grads[k, mine, columns(core)].astype(f32) + c_land[k, mine].astype(f32)
        ).astype(out.dtype)

    def stage_y(k):
        landed(y_land.at[k], yrecv.at[k])
        other = pl.ds((1 - x) * rows_x, rows_x)
        mine = pl.ds(x * rows_x, rows_x)
        total = x_from[k, other].astype(f32) + y_land[k, other].astype(f32)
        x_from[k, other] = total.astype(out.dtype)
        go(x_from.at[k, other], x_land.at[k], xsend.at[k], xrecv.at[k], over_x)
        total = x_from[k, mine].astype(f32) + y_land[k, mine].astype(f32)
        z_from[k] = total.astype(out.dtype)

    def stage_x(k):
        landed(x_land.at[k], xrecv.at[k])
        total = z_from[k].astype(f32) + x_land[k].astype(f32)
        z_from[k] = total.astype(out.dtype)
        for d in (2, 1, 3):
            part = pl.ds(((z + d) % GROUPS) * rows_z, rows_z)
            go(
                z_from.at[k, part],
                z_land.at[k, d],
                zsend.at[GROUPS * k + d],
                zrecv.at[GROUPS * k + d],
                around[d - 1],
            )

    def shard(k, pz, px, pcore):
        return out.at[k, pl.ds(px * rows_x + pz * rows_z, rows_z), columns(pcore)]

    def quarter(k, px, pcore):
        return out.at[k, pl.ds(px * rows_x, rows_x), columns(pcore)]

    def stage_z(k):
        total = z_from[k, pl.ds(z * rows_z, rows_z)].astype(f32)
        for d in range(1, GROUPS):
            landed(z_land.at[k, d], zrecv.at[GROUPS * k + d])
            total += z_land[k, d].astype(f32)
        rows = pl.ds(x * rows_x + z * rows_z, rows_z)
        out[k, rows, columns(core)] = total.astype(out.dtype)
        for d in (2, 1, 3):
            view = shard(k, z, x, core)
            sem = GROUPS * k + d
            go(view, view, gsend.at[sem], grecv.at[sem], around[d - 1])

    def stage_spread(k):
        for d in range(1, GROUPS):
            landed(shard(k, (z + GROUPS - d) % GROUPS, x, core), grecv.at[GROUPS * k + d])
        view = quarter(k, x, core)
        go(view, view, hsend.at[k], hrecv.at[k], over_x)
        go(view, view, isend.at[2 * k], irecv.at[2 * k], over_core)

    def stage_last(k):
        view = quarter(k, 1 - x, core)
        landed(view, hrecv.at[k])
        go(view, view, isend.at[2 * k + 1], irecv.at[2 * k + 1], over_core)

    def vector_step(n):
        if n == 0:
            landed(v_land.at[0], vrecv.at[0])
            vectors[1] = vectors[0] + v_land[0]
            go(vectors.at[1], v_land.at[1], vsend.at[1], vrecv.at[1], over_x)
        elif n == 1:
            landed(v_land.at[1], vrecv.at[1])
            vectors[2] = vectors[1] + v_land[1]
            go(vectors.at[2], v_land.at[2], vsend.at[2], vrecv.at[2], over_y)
        elif n == 2:
            landed(v_land.at[2], vrecv.at[2])
            vectors[3] = vectors[2] + v_land[2]
            for d in range(1, GROUPS):
                go(vectors.at[3], v_land.at[2 + d], vsend.at[2 + d], vrecv.at[2 + d], around[d - 1])
        elif n == 3:
            total = vectors[3]
            for d in range(1, GROUPS):
                landed(v_land.at[2 + d], vrecv.at[2 + d])
                total += v_land[2 + d]
            size = vector_out.shape[0]
            v_land[0] = total
            vector_out[...] = v_land[0, pl.ds(y * size, size)]

    stages = (stage_core, stage_y, stage_x, stage_z, stage_spread, stage_last)
    for step in range(chunks + len(stages) - 1):
        for depth, stage in enumerate(stages):
            if 0 <= step - depth < chunks:
                stage(step - depth)
        vector_step(step)
    for k in range(chunks):
        landed(quarter(k, x, 1 - core), irecv.at[2 * k])
        landed(quarter(k, 1 - x, 1 - core), irecv.at[2 * k + 1])
    for copy in sends:
        copy.wait_send()


def reduce_grads(grads, vector):
    chunks, rows, columns = grads.shape
    half = columns // 2
    kind = grads.dtype
    vmem = pl.BlockSpec(memory_space=pltpu.VMEM)
    size = vector.shape

    def sems(n):
        return [pltpu.SemaphoreType.DMA((n,))] * 2

    return pl.pallas_call(
        functools.partial(reduce_kernel, chunks),
        out_shape=[
            jax.ShapeDtypeStruct((chunks, rows // 2, columns), kind),
            jax.ShapeDtypeStruct((size[0] // 2, size[1]), vector.dtype),
        ],
        in_specs=[vmem] * 2,
        out_specs=[vmem] * 2,
        scratch_shapes=[
            pltpu.VMEM((chunks, rows, half), kind),
            pltpu.VMEM((chunks, rows // 2, half), kind),
            pltpu.VMEM((chunks, rows // 2, half), kind),
            pltpu.VMEM((chunks, rows // 2, half), kind),
            pltpu.VMEM((chunks, rows // 4, half), kind),
            pltpu.VMEM((chunks, rows // 4, half), kind),
            pltpu.VMEM((chunks, GROUPS, rows // 16, half), kind),
            pltpu.VMEM((4,) + size, vector.dtype),
            pltpu.VMEM((6,) + size, vector.dtype),
        ]
        + sems(chunks)
        + sems(chunks)
        + sems(chunks)
        + sems(GROUPS * chunks)
        + sems(GROUPS * chunks)
        + sems(chunks)
        + sems(2 * chunks)
        + sems(6),
        compiler_params=params(60, 5),
        name="reduce_grads",
    )(grads, vector)


def dot(left, right):
    return jnp.dot(left, right, preferred_element_type=jnp.float32)


def attend_kernel(spans, query, keys, marks, veto, out, sums, key_rows, query_aug, acc, stat):
    blocks, rows = keys.shape[0], keys.shape[2]
    width = query.shape[1]
    groups = query.shape[0]

    def turn(j, carry):
        mark = marks[j]
        for h in range(PER_GROUP):
            both = jnp.concatenate([keys[j, h * HD : (h + 1) * HD], mark], axis=0)
            key_rows[h, j] = both.T
        return carry

    lax.fori_loop(0, blocks, turn, 0)
    for i in range(groups):
        for h in range(PER_GROUP):
            query_aug[h, :HD] = query[i, h * HD : (h + 1) * HD] * jnp.bfloat16(0.125)
            query_aug[h, HD:] = veto[i]
        stat[0] = jnp.full(stat.shape[1:], masked_score, jnp.float32)
        stat[1] = jnp.zeros(stat.shape[1:], jnp.float32)
        acc[...] = jnp.zeros(acc.shape, jnp.float32)

        def step(j, carry):
            for h in range(PER_GROUP):
                scores = dot(key_rows[h, j], query_aug[h])
                old = stat[0, h : h + 1]
                new = jnp.maximum(old, jnp.max(scores, axis=0, keepdims=True))
                probs = jnp.exp(scores - new)
                factor = jnp.exp(old - new)
                stat[0, h : h + 1] = new
                stat[1, h : h + 1] = stat[1, h : h + 1] * factor + jnp.sum(
                    probs, axis=0, keepdims=True
                )
                values = keys[j, width + h * HD : width + (h + 1) * HD]
                acc[h] = acc[h] * factor + dot(values, probs.astype(jnp.bfloat16))
            return carry

        lax.fori_loop(spans[i, 0], spans[i, 1], step, 0)
        for h in range(PER_GROUP):
            total = stat[1, h : h + 1]
            out[i, h * HD : (h + 1) * HD] = acc[h] / total
            sums[i, h : h + 1] = stat[0, h : h + 1] + jnp.log(total)


def attend(spans, query, keys, marks, veto):
    groups, width, rows = query.shape
    blocks = keys.shape[0]
    vmem = pl.BlockSpec(memory_space=pltpu.VMEM)
    return pl.pallas_call(
        attend_kernel,
        out_shape=[
            jax.ShapeDtypeStruct(query.shape, jnp.float32),
            jax.ShapeDtypeStruct((groups, 8, rows), jnp.float32),
        ],
        in_specs=[pl.BlockSpec(memory_space=pltpu.SMEM)] + [vmem] * 4,
        out_specs=[vmem] * 2,
        scratch_shapes=[
            pltpu.VMEM((PER_GROUP, blocks, rows, 2 * HD), jnp.bfloat16),
            pltpu.VMEM((PER_GROUP, 2 * HD, rows), jnp.bfloat16),
            pltpu.VMEM((PER_GROUP, HD, rows), jnp.float32),
            pltpu.VMEM((2, 8, rows), jnp.float32),
        ],
        compiler_params=params(40),
        name="attend",
    )(spans, query, keys, marks, veto)


def three_parts(values):
    high = values.astype(jnp.bfloat16)
    rest = values - high.astype(jnp.float32)
    middle = rest.astype(jnp.bfloat16)
    low = (rest - middle.astype(jnp.float32)).astype(jnp.bfloat16)
    return high, middle, low


def attend_back_kernel(
    spans,
    query,
    keys,
    marks,
    veto,
    out,
    sums,
    out_grad,
    query_grad,
    key_grad,
    key_rows,
    value_rows,
    query_aug,
    grad_aug,
    query_rows,
    grad_rows,
    query_acc,
    key_acc,
):
    blocks, rows = keys.shape[0], keys.shape[2]
    width = query.shape[1]
    groups = query.shape[0]
    bf16 = jnp.bfloat16

    def turn(j, carry):
        mark = marks[j]
        for h in range(PER_GROUP):
            both = jnp.concatenate([keys[j, h * HD : (h + 1) * HD], mark], axis=0)
            key_rows[h, j] = both.T
            values = keys[j, width + h * HD : width + (h + 1) * HD]
            value_rows[h, j] = jnp.concatenate([values, mark], axis=0).T
            key_acc[h, j] = jnp.zeros(key_acc.shape[2:], jnp.float32)
        return carry

    lax.fori_loop(0, blocks, turn, 0)
    index = lax.broadcasted_iota(jnp.int32, (HD, rows), 0)
    none = jnp.zeros((HD, rows), bf16)

    def spread(values):
        high, middle, low = three_parts(-values)
        wide = jnp.where(index == 8, high.astype(jnp.float32), 0.0)
        wide = jnp.where(index == 9, middle.astype(jnp.float32), wide)
        return jnp.where(index == 10, low.astype(jnp.float32), wide).astype(bf16)

    for i in range(groups):
        for h in range(PER_GROUP):
            span = slice(h * HD, (h + 1) * HD)
            part = query[i, span] * bf16(0.125)
            grad = out_grad[i, span]
            delta = jnp.sum(grad.astype(jnp.float32) * out[i, span], axis=0, keepdims=True)
            query_aug[h, :HD] = part
            query_aug[h, HD:] = veto[i] + spread(sums[i, h : h + 1])
            grad_aug[h, :HD] = grad
            grad_aug[h, HD:] = spread(delta)
            query_rows[h] = jnp.concatenate([part, none], axis=0).T
            grad_rows[h] = jnp.concatenate([none, grad], axis=0).T
        query_acc[...] = jnp.zeros(query_acc.shape, jnp.float32)

        def step(j, carry):
            for h in range(PER_GROUP):
                probs = jnp.exp(dot(key_rows[h, j], query_aug[h]))
                change = (probs * dot(value_rows[h, j], grad_aug[h])).astype(bf16)
                key_acc[h, j] += dot(probs.astype(bf16), grad_rows[h]) + dot(change, query_rows[h])
                query_acc[h] += dot(keys[j, h * HD : (h + 1) * HD], change)
            return carry

        lax.fori_loop(spans[i, 0], spans[i, 1], step, 0)
        for h in range(PER_GROUP):
            query_grad[i, h * HD : (h + 1) * HD] = (query_acc[h] * 0.125).astype(bf16)

    def finish(j, carry):
        for h in range(PER_GROUP):
            both = key_acc[h, j].T.astype(bf16)
            key_grad[j, h * HD : (h + 1) * HD] = both[:HD]
            key_grad[j, width + h * HD : width + (h + 1) * HD] = both[HD:]
        return carry

    lax.fori_loop(0, blocks, finish, 0)


def attend_back(spans, query, keys, marks, veto, out, sums, out_grad):
    groups, width, rows = query.shape
    blocks = keys.shape[0]
    vmem = pl.BlockSpec(memory_space=pltpu.VMEM)
    bf16 = jnp.bfloat16
    return pl.pallas_call(
        attend_back_kernel,
        out_shape=[
            jax.ShapeDtypeStruct(query.shape, bf16),
            jax.ShapeDtypeStruct(keys.shape, bf16),
        ],
        in_specs=[pl.BlockSpec(memory_space=pltpu.SMEM)] + [vmem] * 7,
        out_specs=[vmem] * 2,
        scratch_shapes=[
            pltpu.VMEM((PER_GROUP, blocks, rows, 2 * HD), bf16),
            pltpu.VMEM((PER_GROUP, blocks, rows, 2 * HD), bf16),
            pltpu.VMEM((PER_GROUP, 2 * HD, rows), bf16),
            pltpu.VMEM((PER_GROUP, 2 * HD, rows), bf16),
            pltpu.VMEM((PER_GROUP, rows, 2 * HD), bf16),
            pltpu.VMEM((PER_GROUP, rows, 2 * HD), bf16),
            pltpu.VMEM((PER_GROUP, HD, rows), jnp.float32),
            pltpu.VMEM((PER_GROUP, blocks, rows, 2 * HD), jnp.float32),
        ],
        compiler_params=params(56),
        name="attend_back",
    )(spans, query, keys, marks, veto, out, sums, out_grad)


def layer_norm(values, gain, offset):
    centre = jnp.mean(values, axis=-1, keepdims=True)
    shifted = values - centre
    spread = jnp.mean(shifted * shifted, axis=-1, keepdims=True)
    return shifted * lax.rsqrt(spread + epsilon) * gain + offset


def exact_gelu(values):
    return jax.nn.gelu(values, approximate=False)


def doc_index(positions, doc_starts):
    hits = (doc_starts[None, :] <= positions[:, None]).astype(jnp.int32)
    return jnp.sum(hits, axis=1) - 1


def doc_tables(doc_lengths, ctx_place, blocks, rows):
    bf16 = jnp.bfloat16
    lengths = doc_lengths[0]
    ends = jnp.cumsum(lengths)
    starts = ends - lengths
    count = lengths.shape[0]
    docs = doc_index(jnp.arange(blocks * rows, dtype=jnp.int32), starts).reshape(blocks, 1, rows)
    number = lax.broadcasted_iota(jnp.int32, (blocks, HD, rows), 1)
    ones = (number >= 8) & (number < 16)
    marks = ((number == docs) | ones).astype(bf16)
    mine = PEERS * jnp.arange(GROUPS, dtype=jnp.int32) + ctx_place % PEERS
    my_docs = docs.reshape(GROUPS, PEERS, 1, rows)[:, ctx_place % PEERS]
    number = number[:GROUPS]
    veto = jnp.where((number != my_docs) & (number < count), masked_score, 0.0).astype(bf16)
    first = doc_index(mine * rows, starts)
    last = doc_index(mine * rows + rows - 1, starts)
    spans = jnp.stack([starts[first] // rows, (ends[last] + rows - 1) // rows], axis=1)
    return spans.astype(jnp.int32), marks, veto


def body(
    patches,
    doc_lengths,
    norm1_gain,
    norm1_bias,
    w_qkv,
    b_qv,
    w_out,
    b_out,
    norm2_gain,
    norm2_bias,
    w_up,
    b_up,
    w_down,
    b_down,
    cotangent,
):
    f32, bf16 = jnp.float32, jnp.bfloat16
    rows, width = patches.shape[1:]
    ctx_place = lax.axis_index("ctx")
    blocks = lax.axis_size("ctx")
    spans, marks, veto = doc_tables(doc_lengths, ctx_place, blocks, rows)
    vectors = [norm1_gain, norm1_bias, b_qv, b_out, norm2_gain, norm2_bias, b_up, b_down]
    sizes = [v.shape[0] for v in vectors]
    small = jnp.concatenate(vectors).reshape(-1, 128)
    small_rows = small.shape[0]
    small = jnp.pad(small, ((0, -small_rows % 16), (0, 0)))
    wqkv2, wout2, wup2, wdown2, small2 = gather_weights([w_qkv, w_out, w_up, w_down], small)
    wqkv = wqkv2.reshape(width, -1)
    wout = wout2.reshape(width, -1)
    wup = wup2.reshape(width, -1)
    wdown = wdown2.reshape(-1, width)
    flat = small2[:, :small_rows].reshape(2, -1).astype(f32)
    full, start = [], 0
    for size in sizes:
        full.append(flat[:, start : start + size].reshape(-1))
        start += size
    gain1, bias1, bqv, bout, gain2, bias2, bup, bdown = full

    inputs = patches[0].astype(f32)
    normed1 = layer_norm(inputs, gain1, bias1).astype(bf16)
    projected = jnp.dot(normed1, wqkv, preferred_element_type=f32)
    offset = jnp.concatenate([bqv[:width], jnp.zeros((width,), f32), bqv[width:]])
    projected = (projected + offset).astype(bf16)
    part = width // GROUPS
    by_group = projected.reshape(rows, 3, GROUPS, part).transpose(2, 1, 3, 0)
    query, keys = spread_heads(by_group.reshape(GROUPS, 3 * part, rows))
    out_heads, sums = attend(spans, query, keys, marks, veto)
    attended = swap_groups(out_heads.astype(bf16)).reshape(width, rows)

    branch = jnp.einsum("ct,cd->td", attended, wout, preferred_element_type=f32) + bout
    hidden_sum = inputs + branch
    normed2 = layer_norm(hidden_sum, gain2, bias2).astype(bf16)
    pre_act = jnp.dot(normed2, wup, preferred_element_type=f32) + bup
    activated = exact_gelu(pre_act).astype(bf16)
    mixed = hidden_sum + jnp.dot(activated, wdown, preferred_element_type=f32) + bdown

    out_grad = cotangent[0]
    wdown_grad = jnp.einsum("tf,td->fd", activated, out_grad, preferred_element_type=f32)
    bdown_grad = jnp.sum(out_grad.astype(f32), axis=0)
    act_grad = jnp.einsum("td,fd->tf", out_grad, wdown, preferred_element_type=f32)
    unused_act, gelu_back = jax.vjp(exact_gelu, pre_act)
    pre_grad = gelu_back(act_grad)[0].astype(bf16)
    wup_grad = jnp.einsum("tc,tf->cf", normed2, pre_grad, preferred_element_type=f32)
    bup_grad = jnp.sum(pre_grad.astype(f32), axis=0)
    normed2_grad = jnp.einsum("tf,cf->tc", pre_grad, wup, preferred_element_type=f32)
    unused_norm2, norm2_back = jax.vjp(layer_norm, hidden_sum, gain2, bias2)
    hidden_part, gain2_grad, bias2_grad = norm2_back(normed2_grad)
    hidden_grad = out_grad.astype(f32) + hidden_part
    branch_grad = hidden_grad.astype(bf16)
    wout_grad = jnp.einsum("ct,td->cd", attended, branch_grad, preferred_element_type=f32)
    bout_grad = jnp.sum(branch_grad.astype(f32), axis=0)
    attended_grad = jnp.einsum("td,cd->ct", branch_grad, wout, preferred_element_type=f32)
    out_grad_heads = swap_groups(attended_grad.astype(bf16).reshape(GROUPS, part, rows))
    query_grad, key_grad = attend_back(
        spans, query, keys, marks, veto, out_heads, sums, out_grad_heads
    )
    collected = collect_heads(query_grad, key_grad)
    projected_grad = (
        collected.reshape(GROUPS, 3, part, rows).transpose(3, 1, 0, 2).reshape(rows, 3 * width)
    )
    wqkv_grad = jnp.einsum("tc,te->ce", normed1, projected_grad, preferred_element_type=f32)
    projected_sums = jnp.sum(projected_grad.astype(f32), axis=0)
    bqv_grad = jnp.concatenate([projected_sums[:width], projected_sums[2 * width :]])
    normed1_grad = jnp.einsum("te,ce->tc", projected_grad, wqkv, preferred_element_type=f32)
    unused_norm1, norm1_back = jax.vjp(layer_norm, inputs, gain1, bias1)
    input_part, gain1_grad, bias1_grad = norm1_back(normed1_grad)
    inputs_grad = hidden_grad + input_part

    def chunked(grad):
        return grad.astype(bf16).reshape(width, -1, width).transpose(1, 0, 2)

    down_chunks = wdown_grad.astype(bf16).reshape(2, -1, width // 2, width)
    grads = jnp.concatenate(
        [
            down_chunks.transpose(1, 0, 2, 3).reshape(-1, width, width),
            chunked(wup_grad),
            chunked(wout_grad),
            chunked(wqkv_grad),
        ]
    )
    vector_grads = [
        gain1_grad, bias1_grad, bqv_grad, bout_grad, gain2_grad, bias2_grad, bup_grad, bdown_grad,
    ]
    vector = jnp.concatenate([v.reshape(2, -1) for v in vector_grads], axis=1)
    summed, vector_sum = reduce_grads(grads, vector.reshape(-1, 128))
    down_count = wdown_grad.shape[0] // width
    up_count = wup_grad.shape[1] // width

    def unchunked(part):
        return part.transpose(1, 0, 2).reshape(part.shape[1], -1).astype(f32)

    down_total = summed[:down_count].reshape(-1, width).astype(f32)
    up_total = unchunked(summed[down_count : down_count + up_count])
    out_total = summed[down_count + up_count].astype(f32)
    qkv_total = unchunked(summed[down_count + up_count + 1 :])
    flat = vector_sum.reshape(-1)
    shares, start = [], 0
    for size in sizes:
        shares.append(flat[start : start + size])
        start += size
    return (
        mixed.astype(bf16)[None],
        inputs_grad[None],
        shares[0],
        shares[1],
        qkv_total,
        shares[2],
        out_total,
        shares[3],
        shares[4],
        shares[5],
        up_total,
        shares[6],
        down_total,
        shares[7],
    )


def shifted_2(block, axis, distance):
    devices = range(lax.axis_size(axis))
    route = [((i - distance) % len(devices), i) for i in devices]
    return lax.ppermute(block, axis, route)


def any_mesh_body(
    patches,
    doc_lengths,
    norm1_gain,
    norm1_bias,
    w_qkv,
    b_qv,
    w_out,
    b_out,
    norm2_gain,
    norm2_bias,
    w_up,
    b_up,
    w_down,
    b_down,
    cotangent,
):
    tok_rows = patches.shape[1]
    model_width = patches.shape[2]
    ctx_size = lax.axis_size("ctx")
    ctx_place = lax.axis_index("ctx")
    gathered = (
        lax.all_gather(norm1_gain, "wsh", axis=0, tiled=True),
        lax.all_gather(norm1_bias, "wsh", axis=0, tiled=True),
        lax.all_gather(w_qkv, "wsh", axis=0, tiled=True),
        lax.all_gather(b_qv, "wsh", axis=0, tiled=True),
        lax.all_gather(w_out, "wsh", axis=0, tiled=True),
        lax.all_gather(b_out, "wsh", axis=0, tiled=True),
        lax.all_gather(norm2_gain, "wsh", axis=0, tiled=True),
        lax.all_gather(norm2_bias, "wsh", axis=0, tiled=True),
        lax.all_gather(w_up, "wsh", axis=0, tiled=True),
        lax.all_gather(b_up, "wsh", axis=0, tiled=True),
        lax.all_gather(w_down, "wsh", axis=0, tiled=True),
        lax.all_gather(b_down, "wsh", axis=0, tiled=True),
    )
    (
        gain1,
        bias1,
        wqkv_full,
        bqv_full,
        wout_full,
        bout_full,
        gain2,
        bias2,
        wup_full,
        bup_full,
        wdown_full,
        bdown_full,
    ) = gathered
    inputs = patches[0].astype(jnp.float32)
    lengths = doc_lengths[0]
    doc_starts = jnp.cumsum(lengths) - lengths
    row_offsets = lax.iota(jnp.int32, tok_rows)
    query_docs = doc_index(ctx_place * tok_rows + row_offsets, doc_starts)
    gain1_float = gain1.astype(jnp.float32)
    bias1_float = bias1.astype(jnp.float32)
    normed1 = layer_norm(inputs, gain1_float, bias1_float).astype(jnp.bfloat16)
    projected = jnp.dot(normed1, wqkv_full, preferred_element_type=jnp.float32)
    bqv_float = bqv_full.astype(jnp.float32)
    query_low = (projected[:, :model_width] + bqv_float[:model_width]).astype(jnp.bfloat16)
    key_low = projected[:, model_width : 2 * model_width].astype(jnp.bfloat16)
    value_low = (projected[:, 2 * model_width :] + bqv_float[model_width:]).astype(jnp.bfloat16)
    query_heads = query_low.reshape(tok_rows, H, HD)

    def attend_block(state, key_block, value_block, key_start):
        run_max, run_total, run_acc = state
        key_docs = doc_index(key_start + row_offsets, doc_starts)
        same_doc = (query_docs[:, None] == key_docs[None, :])[None]
        scores = (
            jnp.einsum(
                "qhd,khd->hqk",
                query_heads,
                key_block.reshape(tok_rows, H, HD),
                preferred_element_type=jnp.float32,
            )
            * 0.125
        )
        scores = jnp.where(same_doc, scores, masked_score)
        new_max = jnp.maximum(run_max, jnp.max(scores, axis=2))
        weights = jnp.where(same_doc, jnp.exp(scores - new_max[:, :, None]), 0.0)
        factor = jnp.exp(run_max - new_max)
        new_total = run_total * factor + jnp.sum(weights, axis=2)
        new_acc = run_acc * factor[:, :, None] + jnp.einsum(
            "hqk,khd->hqd",
            weights.astype(jnp.bfloat16),
            value_block.reshape(tok_rows, H, HD),
            preferred_element_type=jnp.float32,
        )
        return (new_max, new_total, new_acc)

    initial = (
        jnp.full((H, tok_rows), masked_score, jnp.float32),
        jnp.zeros((H, tok_rows), jnp.float32),
        jnp.zeros((H, tok_rows, HD), jnp.float32),
    )
    state = initial
    key_piece = lax.all_gather(key_low, "ctx", axis=0, tiled=True)
    value_piece = lax.all_gather(value_low, "ctx", axis=0, tiled=True)
    blocks = key_piece.shape[0] // tok_rows
    key_blocks = key_piece.reshape(blocks, tok_rows, model_width)
    value_blocks = value_piece.reshape(blocks, tok_rows, model_width)
    block_starts = tok_rows * lax.iota(jnp.int32, blocks)

    def one_block(inner, item):
        key_block, value_block, key_start = item
        return (attend_block(inner, key_block, value_block, key_start), None)

    state, unused = lax.scan(one_block, state, (key_blocks, value_blocks, block_starts))
    run_max, run_total, run_acc = state
    log_total = run_max + jnp.log(run_total)
    attended = jnp.transpose(run_acc / run_total[:, :, None], (1, 0, 2)).reshape(
        tok_rows, model_width
    )
    attended_low = attended.astype(jnp.bfloat16)
    branch = jnp.dot(
        attended_low, wout_full, preferred_element_type=jnp.float32
    ) + bout_full.astype(jnp.float32)
    hidden_sum = inputs + branch
    gain2_float = gain2.astype(jnp.float32)
    bias2_float = bias2.astype(jnp.float32)
    normed2 = layer_norm(hidden_sum, gain2_float, bias2_float).astype(jnp.bfloat16)
    pre_act = jnp.dot(normed2, wup_full, preferred_element_type=jnp.float32) + bup_full.astype(
        jnp.float32
    )
    activated = exact_gelu(pre_act).astype(jnp.bfloat16)
    mixed = (
        hidden_sum
        + jnp.dot(activated, wdown_full, preferred_element_type=jnp.float32)
        + bdown_full.astype(jnp.float32)
    )
    back_gain1 = gathered[0].astype(jnp.float32)
    back_bias1 = gathered[1].astype(jnp.float32)
    back_wqkv = gathered[2]
    back_wout = gathered[4]
    back_gain2 = gathered[6].astype(jnp.float32)
    back_bias2 = gathered[7].astype(jnp.float32)
    back_wup = gathered[8]
    back_wdown = gathered[10]
    out_grad = cotangent[0]
    wdown_grad = jnp.einsum("tf,td->fd", activated, out_grad, preferred_element_type=jnp.float32)
    bdown_grad = jnp.sum(out_grad.astype(jnp.float32), axis=0)
    act_grad = jnp.einsum("td,fd->tf", out_grad, back_wdown, preferred_element_type=jnp.float32)
    unused_act, gelu_back = jax.vjp(exact_gelu, pre_act)
    pre_grad = gelu_back(act_grad)[0].astype(jnp.bfloat16)
    wup_grad = jnp.einsum("tc,tf->cf", normed2, pre_grad, preferred_element_type=jnp.float32)
    bup_grad = jnp.sum(pre_grad.astype(jnp.float32), axis=0)
    normed2_grad = jnp.einsum("tf,cf->tc", pre_grad, back_wup, preferred_element_type=jnp.float32)
    unused_norm2, norm2_back = jax.vjp(layer_norm, hidden_sum, back_gain2, back_bias2)
    hidden_part, gain2_grad, bias2_grad = norm2_back(normed2_grad)
    hidden_grad = out_grad.astype(jnp.float32) + hidden_part
    branch_grad = hidden_grad.astype(jnp.bfloat16)
    wout_grad = jnp.einsum(
        "tc,td->cd", attended_low, branch_grad, preferred_element_type=jnp.float32
    )
    bout_grad = jnp.sum(branch_grad.astype(jnp.float32), axis=0)
    attended_grad = jnp.einsum(
        "td,cd->tc", branch_grad, back_wout, preferred_element_type=jnp.float32
    ).astype(jnp.bfloat16)
    delta = jnp.sum(
        (attended_grad.astype(jnp.float32) * attended).reshape(tok_rows, H, HD), axis=2
    ).T
    grad_heads = attended_grad.reshape(tok_rows, H, HD)

    def back_block(state, anchor):
        key_start = anchor * tok_rows
        key_cur, value_cur, key_grad, value_grad, query_grad = state
        key_docs = doc_index(key_start + row_offsets, doc_starts)
        same_doc = (query_docs[:, None] == key_docs[None, :])[None]
        key_heads = key_cur.reshape(tok_rows, H, HD)
        scores = (
            jnp.einsum("qhd,khd->hqk", query_heads, key_heads, preferred_element_type=jnp.float32)
            * 0.125
        )
        probs = jnp.where(same_doc, jnp.exp(scores - log_total[:, :, None]), 0.0)
        value_grad = value_grad + jnp.einsum(
            "hqk,qhd->khd",
            probs.astype(jnp.bfloat16),
            grad_heads,
            preferred_element_type=jnp.float32,
        ).reshape(tok_rows, model_width)
        prob_grad = jnp.einsum(
            "qhd,khd->hqk",
            grad_heads,
            value_cur.reshape(tok_rows, H, HD),
            preferred_element_type=jnp.float32,
        )
        score_grad = (probs * (prob_grad - delta[:, :, None])).astype(jnp.bfloat16)
        query_grad = (
            query_grad
            + jnp.einsum(
                "hqk,khd->qhd", score_grad, key_heads, preferred_element_type=jnp.float32
            ).reshape(tok_rows, model_width)
            * 0.125
        )
        key_grad = (
            key_grad
            + jnp.einsum(
                "hqk,qhd->khd", score_grad, query_heads, preferred_element_type=jnp.float32
            ).reshape(tok_rows, model_width)
            * 0.125
        )
        return (key_cur, value_cur, key_grad, value_grad, query_grad)

    def pass_on(state):
        key_cur, value_cur, key_grad, value_grad, query_grad = state
        moved_keys = shifted_2((key_cur, value_cur), "ctx", 1)
        moved_sums = (
            shifted_2(key_grad.astype(jnp.bfloat16), "ctx", 1).astype(key_grad.dtype),
            shifted_2(value_grad.astype(jnp.bfloat16), "ctx", 1).astype(value_grad.dtype),
        )
        return (moved_keys[0], moved_keys[1], moved_sums[0], moved_sums[1], query_grad)

    def two_steps(turn, state):
        state = pass_on(back_block(state, (ctx_place - 2 * turn) % ctx_size))
        state = pass_on(back_block(state, (ctx_place - 2 * turn - 1) % ctx_size))
        return state

    zero_rows = jnp.zeros((tok_rows, model_width), jnp.float32)
    final_state = lax.fori_loop(
        0, ctx_size // 2, two_steps, (key_low, value_low, zero_rows, zero_rows, zero_rows)
    )
    key_grad_low = final_state[2].astype(jnp.bfloat16)
    value_grad_low = final_state[3].astype(jnp.bfloat16)
    query_grad_low = final_state[4].astype(jnp.bfloat16)
    projected_grad = jnp.concatenate([query_grad_low, key_grad_low, value_grad_low], axis=1)
    wqkv_grad = jnp.einsum("tc,te->ce", normed1, projected_grad, preferred_element_type=jnp.float32)
    bqv_grad = jnp.concatenate(
        [
            jnp.sum(query_grad_low.astype(jnp.float32), axis=0),
            jnp.sum(value_grad_low.astype(jnp.float32), axis=0),
        ]
    )
    normed1_grad = jnp.einsum(
        "te,ce->tc", projected_grad, back_wqkv, preferred_element_type=jnp.float32
    )
    unused_norm1, norm1_back = jax.vjp(layer_norm, inputs, back_gain1, back_bias1)
    input_part, gain1_grad, bias1_grad = norm1_back(normed1_grad)
    inputs_grad = hidden_grad + input_part
    shares = (
        lax.psum_scatter(
            gain1_grad.astype(jnp.bfloat16), "wsh", scatter_dimension=0, tiled=True
        ).astype(jnp.float32),
        lax.psum_scatter(
            bias1_grad.astype(jnp.bfloat16), "wsh", scatter_dimension=0, tiled=True
        ).astype(jnp.float32),
        lax.psum_scatter(
            wqkv_grad.astype(jnp.bfloat16), "wsh", scatter_dimension=0, tiled=True
        ).astype(jnp.float32),
        lax.psum_scatter(
            bqv_grad.astype(jnp.bfloat16), "wsh", scatter_dimension=0, tiled=True
        ).astype(jnp.float32),
        lax.psum_scatter(
            wout_grad.astype(jnp.bfloat16), "wsh", scatter_dimension=0, tiled=True
        ).astype(jnp.float32),
        lax.psum_scatter(
            bout_grad.astype(jnp.bfloat16), "wsh", scatter_dimension=0, tiled=True
        ).astype(jnp.float32),
        lax.psum_scatter(
            gain2_grad.astype(jnp.bfloat16), "wsh", scatter_dimension=0, tiled=True
        ).astype(jnp.float32),
        lax.psum_scatter(
            bias2_grad.astype(jnp.bfloat16), "wsh", scatter_dimension=0, tiled=True
        ).astype(jnp.float32),
        lax.psum_scatter(
            wup_grad.astype(jnp.bfloat16), "wsh", scatter_dimension=0, tiled=True
        ).astype(jnp.float32),
        lax.psum_scatter(
            bup_grad.astype(jnp.bfloat16), "wsh", scatter_dimension=0, tiled=True
        ).astype(jnp.float32),
        lax.psum_scatter(
            wdown_grad.astype(jnp.bfloat16), "wsh", scatter_dimension=0, tiled=True
        ).astype(jnp.float32),
        lax.psum_scatter(
            bdown_grad.astype(jnp.bfloat16), "wsh", scatter_dimension=0, tiled=True
        ).astype(jnp.float32),
    )
    totals = (
        lax.psum(shares[0].astype(jnp.bfloat16), "ctx").astype(jnp.float32),
        lax.psum(shares[1].astype(jnp.bfloat16), "ctx").astype(jnp.float32),
        lax.psum(shares[2].astype(jnp.bfloat16), "ctx").astype(jnp.float32),
        lax.psum(shares[3].astype(jnp.bfloat16), "ctx").astype(jnp.float32),
        lax.psum(shares[4].astype(jnp.bfloat16), "ctx").astype(jnp.float32),
        lax.psum(shares[5].astype(jnp.bfloat16), "ctx").astype(jnp.float32),
        lax.psum(shares[6].astype(jnp.bfloat16), "ctx").astype(jnp.float32),
        lax.psum(shares[7].astype(jnp.bfloat16), "ctx").astype(jnp.float32),
        lax.psum(shares[8].astype(jnp.bfloat16), "ctx").astype(jnp.float32),
        lax.psum(shares[9].astype(jnp.bfloat16), "ctx").astype(jnp.float32),
        lax.psum(shares[10].astype(jnp.bfloat16), "ctx").astype(jnp.float32),
        lax.psum(shares[11].astype(jnp.bfloat16), "ctx").astype(jnp.float32),
    )
    return (
        mixed.astype(jnp.bfloat16)[None],
        inputs_grad[None],
        totals[0],
        totals[1],
        totals[2],
        totals[3],
        totals[4],
        totals[5],
        totals[6],
        totals[7],
        totals[8],
        totals[9],
        totals[10],
        totals[11],
    )


def solution(mesh):
    as_planned = mesh.shape["ctx"] == GROUPS * PEERS and mesh.shape["wsh"] == 2
    return jax.shard_map(
        body if as_planned else any_mesh_body,
        mesh=mesh,
        in_specs=(
            P("wsh", "ctx", None),
            P("wsh", None),
            P("wsh"),
            P("wsh"),
            P("wsh", None),
            P("wsh"),
            P("wsh", None),
            P("wsh"),
            P("wsh"),
            P("wsh"),
            P("wsh", None),
            P("wsh"),
            P("wsh", None),
            P("wsh"),
            P("wsh", "ctx", None),
        ),
        out_specs=(
            P("wsh", "ctx", None),
            P("wsh", "ctx", None),
            P("wsh"),
            P("wsh"),
            P("wsh", None),
            P("wsh"),
            P("wsh", None),
            P("wsh"),
            P("wsh"),
            P("wsh"),
            P("wsh", None),
            P("wsh"),
            P("wsh", None),
            P("wsh"),
        ),
        check_vma=False,
    )
```

```python
import functools

import jax
import jax.numpy as jnp
from jax import lax
from jax.experimental import pallas as pl
from jax.experimental.pallas import tpu as pltpu
from jax.sharding import PartitionSpec as P

H = 12
HD = 64
GROUPS = 4
PER_GROUP = H // GROUPS
PEERS = 4
MESH = pl.DeviceIdType.MESH
MIB = 2**20

epsilon = 1e-05
masked_score = -1e30


def params(vmem_mib, collective_id=None):
    if collective_id is None:
        return pltpu.CompilerParams(vmem_limit_bytes=vmem_mib * MIB)
    return pltpu.CompilerParams(
        vmem_limit_bytes=vmem_mib * MIB, collective_id=collective_id, has_side_effects=True
    )


def here():
    ctx = lax.axis_index("ctx")
    return ctx // PEERS, (ctx // 2) % 2, ctx % 2, lax.axis_index("wsh")


def at(z, x, core, y):
    return (z * PEERS + x * 2 + core, y)


def remote(src, dst, send, recv, device):
    return pltpu.make_async_remote_copy(
        src_ref=src,
        dst_ref=dst,
        send_sem=send,
        recv_sem=recv,
        device_id=device,
        device_id_type=MESH,
    )


def greet(devices):
    barrier = pltpu.get_barrier_semaphore()
    for device in devices:
        pl.semaphore_signal(barrier, inc=1, device_id=device, device_id_type=MESH)
    pl.semaphore_wait(barrier, len(devices))


def weight_pieces(shapes, most):
    pieces = []
    for index, (rows, columns) in enumerate(shapes):
        quarter = rows // PEERS
        step = quarter
        while step * columns * 2 > most and step % 32 == 0:
            step //= 2
        pieces += [(index, first, step) for first in range(0, quarter, step)]
    return pieces


def weights_kernel(count, pieces, *refs):
    halves, fulls = refs[: count + 1], refs[count + 1 : 2 * count + 2]
    local, ysend, yrecv, xsend, xrecv, csend, crecv, fsend, frecv, small_sem = refs[2 * count + 2 :]
    z, x, core, y = here()
    over_y, over_x, over_core = at(z, x, core, 1 - y), at(z, 1 - x, core, y), at(z, x, 1 - core, y)
    greet([over_y, over_x, over_core])
    small = remote(halves[count], fulls[count].at[y], small_sem.at[0], small_sem.at[1], over_y)
    small.start()
    own = [
        pltpu.make_async_copy(halves[i], fulls[i].at[y], local.at[i]) for i in range(count + 1)
    ]

    def spot(piece, px, pcore):
        index, first, rows = piece
        quarter = fulls[index].shape[1] // PEERS
        return pl.ds((px * 2 + pcore) * quarter + first, rows)

    sends = []
    for k, piece in enumerate(pieces):
        index = piece[0]
        rows = spot(piece, x, core)
        copy = remote(
            halves[index].at[rows], fulls[index].at[y, rows], ysend.at[k], yrecv.at[k], over_y
        )
        copy.start()
        sends.append(copy)
    for copy in own:
        copy.start()

    def landing(k, px, pcore, sem):
        index = pieces[k][0]
        view = fulls[index].at[1 - y, spot(pieces[k], px, pcore)]
        return remote(view, view, sem, sem, over_core)

    def forward(k, px, pcore, send, recv, device):
        index = pieces[k][0]
        view = fulls[index].at[1 - y, spot(pieces[k], px, pcore)]
        copy = remote(view, view, send.at[k], recv.at[k], device)
        copy.start()
        sends.append(copy)

    total = len(pieces)
    for k in range(total + 1):
        if k < total:
            landing(k, x, core, yrecv.at[k]).wait_recv()
            forward(k, x, core, xsend, xrecv, over_x)
            forward(k, x, core, csend, crecv, over_core)
        if k >= 1:
            landing(k - 1, 1 - x, core, xrecv.at[k - 1]).wait_recv()
            forward(k - 1, 1 - x, core, fsend, frecv, over_core)
    for k in range(total):
        landing(k, x, 1 - core, crecv.at[k]).wait_recv()
        landing(k, 1 - x, 1 - core, frecv.at[k]).wait_recv()
    small.wait()
    for copy in own:
        copy.wait()
    for copy in sends:
        copy.wait_send()


def gather_weights(halves, small):
    pieces = weight_pieces([half.shape for half in halves], 320 * 1024)
    count, total = len(halves), len(pieces)
    everything = list(halves) + [small]
    anywhere = pl.BlockSpec(memory_space=pltpu.HBM)
    sems = [pltpu.SemaphoreType.DMA((count + 1,))]
    sems += [pltpu.SemaphoreType.DMA((total,))] * 8 + [pltpu.SemaphoreType.DMA((2,))]
    return pl.pallas_call(
        functools.partial(weights_kernel, count, pieces),
        out_shape=[jax.ShapeDtypeStruct((2,) + a.shape, a.dtype) for a in everything],
        in_specs=[anywhere] * (count + 1),
        out_specs=[anywhere] * (count + 1),
        scratch_shapes=sems,
        compiler_params=params(16, 1),
        name="gather_weights",
    )(*everything)


def spread_kernel(mine, query, keys, local, zsend, zrecv, xsend, xrecv, csend, crecv, fsend, frecv):
    z, x, core, y = here()
    width = query.shape[1]
    over_x, over_core = at(z, 1 - x, core, y), at(z, x, 1 - core, y)
    around = [at((z + d) % GROUPS, x, core, y) for d in range(1, GROUPS)]
    greet(around + [over_x, over_core])
    sends = []

    def go(src, dst, send, recv, device):
        copy = remote(src, dst, send, recv, device)
        copy.start()
        sends.append(copy)

    def block(pz, px, pcore):
        return keys.at[pz * PEERS + px * 2 + pcore]

    own_query = pltpu.make_async_copy(mine.at[z, pl.ds(0, width)], query.at[z], local.at[0])
    own_keys = pltpu.make_async_copy(
        mine.at[z, pl.ds(width, 2 * width)], block(z, x, core), local.at[1]
    )
    own_keys.start()
    own_query.start()
    for d in (2, 1, 3):
        target = (z + d) % GROUPS
        src = mine.at[target, pl.ds(width, 2 * width)]
        go(src, block(z, x, core), zsend.at[d], zrecv.at[d], around[d - 1])
    for d in (2, 1, 3):
        target = (z + d) % GROUPS
        src = mine.at[target, pl.ds(0, width)]
        go(src, query.at[z], zsend.at[GROUPS + d], zrecv.at[GROUPS + d], around[d - 1])
    order = (0, 3, 1, 2)
    for step in range(GROUPS + 1):
        if step < GROUPS:
            d = order[step]
            pz = (z + GROUPS - d) % GROUPS
            view = block(pz, x, core)
            if d == 0:
                own_keys.wait()
            else:
                remote(view, view, zsend.at[d], zrecv.at[d], over_x).wait_recv()
            go(view, view, xsend.at[d], xrecv.at[d], over_x)
            go(view, view, csend.at[d], crecv.at[d], over_core)
        if step >= 1:
            d = order[step - 1]
            view = block((z + GROUPS - d) % GROUPS, 1 - x, core)
            remote(view, view, xsend.at[d], xrecv.at[d], over_x).wait_recv()
            go(view, view, fsend.at[d], frecv.at[d], over_core)
    for d in range(GROUPS):
        pz = (z + GROUPS - d) % GROUPS
        near, far = block(pz, x, 1 - core), block(pz, 1 - x, 1 - core)
        remote(near, near, csend.at[d], crecv.at[d], over_core).wait_recv()
        remote(far, far, fsend.at[d], frecv.at[d], over_core).wait_recv()
        if d > 0:
            part = query.at[pz]
            sem = GROUPS + d
            remote(part, part, zsend.at[sem], zrecv.at[sem], over_x).wait_recv()
    own_query.wait()
    for copy in sends:
        copy.wait_send()


def spread_heads(projected):
    groups, width, rows = projected.shape
    width //= 3
    anywhere = pl.BlockSpec(memory_space=pltpu.HBM)
    sems = [pltpu.SemaphoreType.DMA((2,))] + [pltpu.SemaphoreType.DMA((2 * groups,))] * 2
    sems += [pltpu.SemaphoreType.DMA((groups,))] * 6
    return pl.pallas_call(
        spread_kernel,
        out_shape=[
            jax.ShapeDtypeStruct((groups, width, rows), projected.dtype),
            jax.ShapeDtypeStruct((groups * PEERS, 2 * width, rows), projected.dtype),
        ],
        in_specs=[anywhere],
        out_specs=[anywhere] * 2,
        scratch_shapes=sems,
        compiler_params=params(16, 2),
        name="spread_heads",
    )(projected)


def dot(left, right):
    return jnp.dot(left, right, preferred_element_type=jnp.float32)


def dot_turned(left, right):
    return lax.dot_general(
        left, right, (((1,), (1,)), ((), ())), preferred_element_type=jnp.float32
    )


def normalise(values):
    centre = jnp.mean(values, axis=-1, keepdims=True)
    shifted = values - centre
    spread = jnp.mean(shifted * shifted, axis=-1, keepdims=True)
    scale = lax.rsqrt(spread + epsilon)
    return shifted * scale, scale


def normalise_back(grad, gain, normed, scale):
    inner = grad * gain
    centre = jnp.mean(inner, axis=-1, keepdims=True)
    along = jnp.mean(inner * normed, axis=-1, keepdims=True)
    gain_grad = jnp.sum(grad * normed, axis=0, keepdims=True)
    bias_grad = jnp.sum(grad, axis=0, keepdims=True)
    return scale * (inner - centre - normed * along), gain_grad, bias_grad


LANES = 128


class Packed:
    names = ("gain1", "bias1", "bqv", "bout", "gain2", "bias2", "bup", "bdown")

    def __init__(self, sizes):
        self.sizes = dict(zip(self.names, sizes))
        self.starts, row = {}, 0
        for name in self.names:
            self.starts[name] = row
            row += self.sizes[name] // LANES
        self.used = row
        self.rows = row + -row % 8

    def pack(self, halves):
        flat = jnp.concatenate([half.astype(jnp.float32) for half in halves])
        return jnp.pad(flat.reshape(-1, LANES), ((0, self.rows - self.used), (0, 0)))

    def read(self, ref, name, first=0, count=None):
        count = 2 * self.sizes[name] if count is None else count
        parts = []
        for lane in range(first, first + count, LANES):
            y, inner = divmod(lane, self.sizes[name])
            row = self.starts[name] + inner // LANES
            parts.append(ref[y, row : row + 1])
        return jnp.concatenate(parts, axis=1)

    def write(self, ref, name, values, first=0):
        for lane in range(0, values.shape[1], LANES):
            y, inner = divmod(first + lane, self.sizes[name])
            row = self.starts[name] + inner // LANES
            ref[y, row : row + 1] = values[:, lane : lane + LANES]

    def unpack(self, rows):
        flat = rows[: self.used].reshape(-1)
        parts, start = [], 0
        for name in self.names:
            parts.append(flat[start : start + self.sizes[name]])
            start += self.sizes[name]
        return parts


class Sender:
    def __init__(self):
        self.copies = []

    def __call__(self, src, dst, send, recv, device):
        copy = remote(src, dst, send, recv, device)
        copy.start()
        self.copies.append(copy)

    def finish(self):
        for copy in self.copies:
            copy.wait_send()


def split_rows(first, x, y, quarter):
    if first == "y":
        return [((1 - y) * 2 * quarter, 2 * quarter)], [(y * 2 * quarter, 2 * quarter)]
    other, mine = (1 - x) * quarter, x * quarter
    return (
        [(other, quarter), (2 * quarter + other, quarter)],
        [(mine, quarter), (2 * quarter + mine, quarter)],
    )


def core_sum(first, own, land, send_ref, keep_ref, x, y):
    quarter = land.shape[0] // 4
    gone, kept = split_rows(first, x, y, quarter)
    for ref, parts in ((send_ref, gone), (keep_ref, kept)):
        place = 0
        for start, count in parts:
            rows = pl.ds(start, count)
            total = own(rows).astype(jnp.float32) + land[rows].astype(jnp.float32)
            ref[pl.ds(place, count)] = total.astype(ref.dtype)
            place += count


def middle_kernel(
    pack,
    firsts,
    heads,
    patches,
    out_grad,
    small,
    w_out,
    w_up,
    w_down_half,
    w_down_far,
    mixed,
    hidden_grad,
    grad_heads,
    send_over_x,
    send_over_y,
    keep,
    vector,
    o_land,
    o_grad,
    wout,
    wup,
    wdown,
    act_grad,
    act_turned,
    pre_grad,
    bup_rows,
    grads,
    c_land,
    local,
    osend,
    orecv,
    gsend,
    grecv,
    wsem,
    csend,
    crecv,
):
    f32, bf16 = jnp.float32, jnp.bfloat16
    z, x, core, y = here()
    over_core = at(z, x, 1 - core, y)
    around = [at((z + d) % GROUPS, x, core, y) for d in range(1, GROUPS)]
    rows, width = patches.shape
    tiles = wdown.shape[0] // width
    half = w_down_half.shape[0]
    far = w_down_far.shape[0]
    greet(around + [over_core])
    go = Sender()
    far_rows = pl.ds((1 - y) * half + core * far, far)
    other_rows = pl.ds((1 - y) * half + (1 - core) * far, far)
    for d in (2, 1, 3):
        go(heads.at[(z + d) % GROUPS], o_land.at[z], osend.at[d], orecv.at[d], around[d - 1])
    go(w_down_far, wdown.at[far_rows], wsem.at[0], wsem.at[1], over_core)
    down_copies = [
        pltpu.make_async_copy(w_down_half, wdown.at[pl.ds(y * half, half)], local.at[0]),
        pltpu.make_async_copy(w_down_far, wdown.at[far_rows], local.at[1]),
    ]
    copies = [
        pltpu.make_async_copy(heads.at[z], o_land.at[z], local.at[2]),
        pltpu.make_async_copy(w_out, wout, local.at[3]),
        pltpu.make_async_copy(w_up, wup, local.at[4]),
    ]
    for copy in down_copies + copies:
        copy.start()
    dy = out_grad[...]
    vector[...] = jnp.zeros(vector.shape, f32)
    pack.write(vector, "bdown", jnp.sum(dy.astype(f32), axis=0, keepdims=True))
    for f in range(tiles):
        bup_rows[f, 0:1] = pack.read(small, "bup", f * width, width)
    for copy in down_copies:
        copy.wait()
    landed = wdown.at[other_rows]
    remote(landed, landed, wsem.at[0], wsem.at[1], over_core).wait_recv()

    def tile(f):
        return pl.ds(pl.multiple_of(f * width, width), width)

    def first_grad(f, carry):
        act_grad[f] = dot_turned(dy, wdown[tile(f)])
        return carry

    lax.fori_loop(0, tiles, first_grad, 0)
    for copy in copies:
        copy.wait()
    for d in range(1, GROUPS):
        landed = o_land.at[(z + GROUPS - d) % GROUPS]
        remote(landed, landed, osend.at[d], orecv.at[d], over_core).wait_recv()
    turned = o_land[...].reshape(width, rows)
    hidden = patches[...].astype(f32) + (dot(turned.T, wout[...]) + pack.read(small, "bout"))
    gain2 = pack.read(small, "gain2")
    normed, scale = normalise(hidden)
    c = (normed * gain2 + pack.read(small, "bias2")).astype(bf16)
    mixed_acc = hidden + pack.read(small, "bdown")
    c_grad = jnp.zeros((rows, width), f32)

    def forward_back(f, carry):
        mixed_acc, c_grad = carry
        up = wup[:, tile(f)]
        pre = dot(c, up) + bup_rows[f, 0:1]
        share = 0.5 + 0.5 * lax.erf(pre * (0.5**0.5))
        slope = share + pre * jnp.exp(-0.5 * pre * pre) * ((0.5 / jnp.pi) ** 0.5)
        act = (pre * share).astype(bf16)
        grad = (act_grad[f] * slope).astype(bf16)
        act_turned[tile(f)] = act.T
        pre_grad[f] = grad
        bup_rows[f, 0:1] = jnp.sum(grad.astype(f32), axis=0, keepdims=True)
        return (
            mixed_acc + dot(act, wdown[tile(f)]),
            c_grad + dot_turned(grad, up),
        )

    mixed_acc, c_grad = lax.fori_loop(0, tiles, forward_back, (mixed_acc, c_grad))
    mixed[...] = mixed_acc.astype(bf16)
    for f in range(tiles):
        pack.write(vector, "bup", bup_rows[f, 0:1], f * width)
    part, gain_grad, bias_grad = normalise_back(c_grad, gain2, normed, scale)
    pack.write(vector, "gain2", gain_grad)
    pack.write(vector, "bias2", bias_grad)
    whole = dy.astype(f32) + part
    hidden_grad[...] = whole
    dz = whole.astype(bf16)
    pack.write(vector, "bout", jnp.sum(dz.astype(f32), axis=0, keepdims=True))
    o_grad[...] = dot_turned(wout[...], dz).astype(bf16).reshape(o_grad.shape)
    for d in (2, 1, 3):
        go(o_grad.at[(z + d) % GROUPS], grad_heads.at[z], gsend.at[d], grecv.at[d], around[d - 1])
    own = pltpu.make_async_copy(o_grad.at[z], grad_heads.at[z], local.at[5])
    own.start()

    columns = c_land.shape[2]
    count, ahead = grads.shape[0], send_over_x.shape[0]
    mine = pl.ds(pl.multiple_of(core * columns, columns), columns)
    others = pl.ds(pl.multiple_of((1 - core) * columns, columns), columns)

    def over(k):
        go(grads.at[k, :, others], c_land.at[k], csend.at[k], crecv.at[k], over_core)

    def settle(k):
        landed = c_land.at[k]
        remote(landed, landed, csend.at[k], crecv.at[k], over_core).wait_recv()
        sent = send_over_x.at[k] if k < ahead else send_over_y.at[k - ahead]
        core_sum(firsts[k], lambda r: grads[k, r, mine], c_land.at[k], sent, keep.at[k], x, y)

    c_turned = c.T
    piece = half // tiles
    for k in range(count):
        if k < tiles:
            for top in range(2):
                grads[k, top * piece : (top + 1) * piece] = dot(
                    act_turned[top * half + k * piece : top * half + (k + 1) * piece], dy
                ).astype(bf16)
        elif k < 2 * tiles:
            grads[k] = dot(c_turned, pre_grad[k - tiles]).astype(bf16)
        else:
            grads[k] = dot(turned, dz).astype(bf16)
        over(k)
        if k >= 2:
            settle(k - 2)
    settle(count - 2)
    settle(count - 1)
    for d in range(1, GROUPS):
        landed = grad_heads.at[(z + GROUPS - d) % GROUPS]
        remote(landed, landed, gsend.at[d], grecv.at[d], over_core).wait_recv()
    own.wait()
    go.finish()


def middle(pack, firsts, ahead, heads, patches, out_grad, small, w_out, w_up, w_down_half, w_down_far):
    rows, width = patches.shape
    hidden = w_up.shape[1]
    tiles = hidden // width
    count = 2 * tiles + 1
    f32, bf16 = jnp.float32, jnp.bfloat16
    vmem = pl.BlockSpec(memory_space=pltpu.VMEM)
    hbm = pl.BlockSpec(memory_space=pltpu.HBM)
    dma = pltpu.SemaphoreType.DMA
    return pl.pallas_call(
        functools.partial(middle_kernel, pack, firsts),
        out_shape=[
            jax.ShapeDtypeStruct((rows, width), bf16),
            jax.ShapeDtypeStruct((rows, width), f32),
            jax.ShapeDtypeStruct(heads.shape, bf16),
            jax.ShapeDtypeStruct((ahead, width // 2, width // 2), bf16),
            jax.ShapeDtypeStruct((count - ahead, width // 2, width // 2), bf16),
            jax.ShapeDtypeStruct((count, width // 2, width // 2), bf16),
            jax.ShapeDtypeStruct((2, pack.rows, LANES), f32),
        ],
        in_specs=[hbm, vmem, vmem, vmem, hbm, hbm, hbm, hbm],
        out_specs=[vmem] * 7,
        scratch_shapes=[
            pltpu.VMEM(heads.shape, bf16),
            pltpu.VMEM(heads.shape, bf16),
            pltpu.VMEM((width, width), bf16),
            pltpu.VMEM((width, hidden), bf16),
            pltpu.VMEM((hidden, width), bf16),
            pltpu.VMEM((tiles, rows, width), f32),
            pltpu.VMEM((hidden, rows), bf16),
            pltpu.VMEM((tiles, rows, width), bf16),
            pltpu.VMEM((tiles, 8, width), f32),
            pltpu.VMEM((count, width, width), bf16),
            pltpu.VMEM((count, width, width // 2), bf16),
            dma((6,)),
            dma((GROUPS,)),
            dma((GROUPS,)),
            dma((GROUPS,)),
            dma((GROUPS,)),
            dma((2,)),
            dma((count,)),
            dma((count,)),
        ],
        compiler_params=params(60, 3),
        name="middle",
    )(heads, patches, out_grad, small, w_out, w_up, w_down_half, w_down_far)


class Totals:
    def __init__(self, refs, tiles):
        self.refs, self.tiles = refs, tiles

    def place(self, k, row, count, column, columns):
        down, up, out, qkv = self.refs
        width = out.shape[1]
        if k < self.tiles:
            rows = pl.ds(k * (width // 2) + row, count)
            return down, rows, pl.ds(pl.multiple_of(column, LANES), columns)
        if k < 2 * self.tiles:
            ref, start = up, (k - self.tiles) * width
        elif k == 2 * self.tiles:
            ref, start = out, 0
        else:
            ref, start = qkv, (k - 2 * self.tiles - 1) * width
        return ref, pl.ds(row, count), pl.ds(pl.multiple_of(start + column, LANES), columns)

    def view(self, *place):
        ref, rows, columns = self.place(*place)
        return ref.at[rows, columns]

    def store(self, values, *place):
        ref, rows, columns = self.place(*place)
        ref[rows, columns] = values.astype(ref.dtype)


def last_kernel(
    pack,
    firsts,
    tiles,
    query_grad,
    key_grad,
    normed_low,
    w_qkv,
    patches,
    hidden_grad,
    small,
    landed_ahead,
    send_on,
    keep,
    vector_in,
    inputs_grad,
    down_total,
    up_total,
    out_total,
    qkv_total,
    vector_out,
    got,
    near,
    both,
    far,
    own,
    wqkv,
    grads,
    c_land,
    late_send,
    first_land,
    half_sum,
    second_land,
    quarter_sum,
    z_land,
    eighth_sum,
    far_land,
    vectors,
    v_land,
    local,
    n_send,
    n_recv,
    f_send,
    f_recv,
    q_send,
    q_recv,
    csend,
    crecv,
    asend,
    arecv,
    bsend,
    brecv,
    zsend,
    zrecv,
    wsend,
    wrecv,
    dsend,
    drecv,
    gsend,
    grecv,
    hsend,
    hrecv,
    isend,
    irecv,
    vsend,
    vrecv,
):
    f32, bf16 = jnp.float32, jnp.bfloat16
    z, x, core, y = here()
    over_x, over_core, over_y = (
        at(z, 1 - x, core, y),
        at(z, x, 1 - core, y),
        at(z, x, core, 1 - y),
    )
    around = [at((z + d) % GROUPS, x, core, y) for d in range(1, GROUPS)]
    peer = {"y": over_y, "x": over_x}
    greet(around + [over_x, over_core, over_y])
    go = Sender()
    totals = Totals((down_total, up_total, out_total, qkv_total), tiles)
    part = query_grad.shape[1]
    rows, width = patches.shape
    ahead, chunks = landed_ahead.shape[0], len(firsts)
    early = ahead + send_on.shape[0]
    pair, side = z // 2, z % 2
    over_near, over_far = at(z + 1 - 2 * side, x, core, y), around[1]
    half = c_land.shape[2]
    quarter, shard = width // 4, width // 16

    def landed(view, sem):
        remote(view, view, sem, sem, over_core).wait_recv()

    order = (2, 1, 3, 0)
    for d in order:
        pz = (z + d) % GROUPS
        for k in range(2):
            px = (x + 1 + k) % 2
            slot = 2 * d + k
            src = key_grad.at[pz * PEERS + px * 2 + 1 - core]
            go(src, near.at[slot], n_send.at[slot], n_recv.at[slot], over_core)
    for d in (2, 1, 3):
        pz = (z + d) % GROUPS
        go(query_grad.at[pz], got.at[z, pl.ds(0, part)], q_send.at[d], q_recv.at[d], around[d - 1])
    own_query = pltpu.make_async_copy(query_grad.at[z], got.at[z, pl.ds(0, part)], local.at[0])
    own_query.start()
    weights = pltpu.make_async_copy(w_qkv, wqkv, local.at[2])
    weights.start()

    def start_first(k, src):
        go(src, first_land.at[k], asend.at[k], arecv.at[k], peer[firsts[k]])

    for k in range(ahead, early):
        start_first(k, send_on.at[k - ahead])
    for step in range(GROUPS + 1):
        if step < GROUPS:
            d = order[step]
            pz = (z + d) % GROUPS
            for k in range(2):
                px = (x + 1 + k) % 2
                slot = 2 * d + k
                landed(near.at[slot], n_recv.at[slot])
                mine = key_grad[pz * PEERS + px * 2 + core].astype(f32)
                both[slot] = (mine + near[slot].astype(f32)).astype(bf16)
                if k == 0:
                    go(both.at[slot], far.at[d], f_send.at[d], f_recv.at[d], over_x)
        if step >= 1:
            d = order[step - 1]
            landed(far.at[d], f_recv.at[d])
            own[d] = (both[2 * d + 1].astype(f32) + far[d].astype(f32)).astype(bf16)
            place = got.at[z, pl.ds(part, 2 * part)]
            if d == 0:
                own_keys = pltpu.make_async_copy(own.at[0], place, local.at[1])
                own_keys.start()
            else:
                sem = GROUPS + d
                go(own.at[d], place, q_send.at[sem], q_recv.at[sem], around[d - 1])
    normed_turned = normed_low[...].T
    normed, scale = normalise(patches[...].astype(f32))
    gain1 = pack.read(small, "gain1")
    def kept(k):
        return keep[k] if k < early else half_sum[k]

    def stage_core(k):
        i = k - early
        landed(c_land.at[i], crecv.at[i])
        mine = pl.ds(pl.multiple_of(core * half, half), half)
        core_sum(
            firsts[k],
            lambda r: grads[i, r, mine],
            c_land.at[i],
            late_send.at[i],
            half_sum.at[k],
            x,
            y,
        )
        start_first(k, late_send.at[i])

    def stage_first(k):
        if k < ahead:
            arrived = landed_ahead[k]
        else:
            landed(first_land.at[k], arecv.at[k])
            arrived = first_land[k]
        half_sum[k] = (kept(k).astype(f32) + arrived.astype(f32)).astype(bf16)
        place = x if firsts[k] == "y" else y
        other = half_sum.at[k, pl.ds((1 - place) * quarter, quarter)]
        second = over_x if firsts[k] == "y" else over_y
        go(other, second_land.at[k], bsend.at[k], brecv.at[k], second)

    def stage_second(k):
        landed(second_land.at[k], brecv.at[k])
        place = x if firsts[k] == "y" else y
        total = half_sum[k, pl.ds(place * quarter, quarter)].astype(f32)
        quarter_sum[k] = (total + second_land[k].astype(f32)).astype(bf16)
        other = quarter_sum.at[k, pl.ds((1 - side) * 2 * shard, 2 * shard)]
        go(other, z_land.at[k], zsend.at[k], zrecv.at[k], over_near)

    def stage_near(k):
        landed(z_land.at[k], zrecv.at[k])
        total = quarter_sum[k, pl.ds(side * 2 * shard, 2 * shard)].astype(f32)
        eighth_sum[k] = (total + z_land[k].astype(f32)).astype(bf16)
        other = eighth_sum.at[k, pl.ds((1 - pair) * shard, shard)]
        go(other, far_land.at[k], wsend.at[k], wrecv.at[k], over_far)

    def spot(k, px, pside, ppair, count):
        row = px * quarter + pside * 2 * shard + ppair * shard
        return totals.view(k, row, count, core * half, half)

    def stage_far(k):
        landed(far_land.at[k], wrecv.at[k])
        total = eighth_sum[k, pl.ds(pair * shard, shard)].astype(f32) + far_land[k].astype(f32)
        row = x * quarter + side * 2 * shard + pair * shard
        totals.store(total, k, row, shard, core * half, half)
        view = spot(k, x, side, pair, shard)
        go(view, view, dsend.at[k], drecv.at[k], over_far)

    def stage_back(k):
        landed(spot(k, x, side, 1 - pair, shard), drecv.at[k])
        view = spot(k, x, side, 0, 2 * shard)
        go(view, view, gsend.at[k], grecv.at[k], over_near)

    def stage_out(k):
        landed(spot(k, x, 1 - side, 0, 2 * shard), grecv.at[k])
        view = spot(k, x, 0, 0, quarter)
        go(view, view, hsend.at[k], hrecv.at[k], over_x)
        go(view, view, isend.at[2 * k], irecv.at[2 * k], over_core)

    def stage_last(k):
        view = spot(k, 1 - x, 0, 0, quarter)
        landed(view, hrecv.at[k])
        go(view, view, isend.at[2 * k + 1], irecv.at[2 * k + 1], over_core)

    stages = (
        stage_first,
        stage_second,
        stage_near,
        stage_far,
        stage_back,
        stage_out,
        stage_last,
    )

    def turn(step):
        for depth, stage in enumerate(stages):
            if 0 <= step - depth < chunks:
                stage(step - depth)

    before = min(early, 4)
    for step in range(before):
        turn(step)

    for d in range(1, GROUPS):
        pz = (z + GROUPS - d) % GROUPS
        landed(got.at[pz, pl.ds(0, part)], q_recv.at[d])
        landed(got.at[pz, pl.ds(part, 2 * part)], q_recv.at[GROUPS + d])
    own_query.wait()
    own_keys.wait()
    weights.wait()

    for k in range(early, chunks):
        i = k - early
        turned = got[:, i * part : (i + 1) * part].reshape(width, rows)
        grads[i] = dot_turned(normed_turned, turned).astype(bf16)
        others = pl.ds(pl.multiple_of((1 - core) * half, half), half)
        go(grads.at[i, :, others], c_land.at[i], csend.at[i], crecv.at[i], over_core)
    vectors[0] = vector_in[...]
    ones = jnp.ones((8, rows), bf16)
    normed_grad = jnp.zeros((width, rows), f32)
    for i in range(chunks - early):
        turned = got[:, i * part : (i + 1) * part].reshape(width, rows)
        if i != 1:
            sums = dot_turned(ones, turned)[0:1]
            pack.write(vectors.at[0], "bqv", sums, (i // 2) * width)
        normed_grad += dot(wqkv[:, i * width : (i + 1) * width], turned)
    change, gain_grad, bias_grad = normalise_back(normed_grad.T, gain1, normed, scale)
    inputs_grad[...] = hidden_grad[...] + change
    pack.write(vectors.at[0], "gain1", gain_grad)
    pack.write(vectors.at[0], "bias1", bias_grad)
    go(vectors.at[0], v_land.at[0], vsend.at[0], vrecv.at[0], over_core)

    def vector_step(n):
        if n == 0:
            landed(v_land.at[0], vrecv.at[0])
            vectors[1] = vectors[0] + v_land[0]
            go(vectors.at[1], v_land.at[1], vsend.at[1], vrecv.at[1], over_x)
        elif n == 1:
            landed(v_land.at[1], vrecv.at[1])
            vectors[2] = vectors[1] + v_land[1]
            go(vectors.at[2], v_land.at[2], vsend.at[2], vrecv.at[2], over_y)
        elif n == 2:
            landed(v_land.at[2], vrecv.at[2])
            vectors[3] = vectors[2] + v_land[2]
            for d in range(1, GROUPS):
                sem = 2 + d
                go(vectors.at[3], v_land.at[sem], vsend.at[sem], vrecv.at[sem], around[d - 1])
        elif n == 3:
            total = vectors[3]
            for d in range(1, GROUPS):
                landed(v_land.at[2 + d], vrecv.at[2 + d])
                total += v_land[2 + d]
            v_land[0] = total
            vector_out[...] = v_land[0, y]

    for k in range(early, chunks):
        stage_core(k)
    for step in range(before, chunks + len(stages) - 1):
        turn(step)
        vector_step(step - before)
    for k in range(chunks):
        for px in range(2):
            place = (x + px) % 2
            view = totals.view(k, place * quarter, quarter, (1 - core) * half, half)
            landed(view, irecv.at[2 * k + px])
    go.finish()


def last(
    pack, firsts, query_grad, key_grad, normed_low, w_qkv, patches, hidden_grad, small,
    landed_ahead, send_on, keep, vector
):
    f32, bf16 = jnp.float32, jnp.bfloat16
    vmem = pl.BlockSpec(memory_space=pltpu.VMEM)
    hbm = pl.BlockSpec(memory_space=pltpu.HBM)
    groups, part, rows = query_grad.shape
    width = patches.shape[1]
    early, half = keep.shape[0], width // 2
    tiles, chunks, late = (early - 1) // 2, len(firsts), len(firsts) - early
    piece = (2 * part, rows)
    dma = pltpu.SemaphoreType.DMA

    def pair(n):
        return [dma((n,))] * 2

    return pl.pallas_call(
        functools.partial(last_kernel, pack, firsts, tiles),
        out_shape=[
            jax.ShapeDtypeStruct((rows, width), f32),
            jax.ShapeDtypeStruct((tiles * half, width), bf16),
            jax.ShapeDtypeStruct((half, tiles * width), bf16),
            jax.ShapeDtypeStruct((half, width), bf16),
            jax.ShapeDtypeStruct((half, late * width), bf16),
            jax.ShapeDtypeStruct(vector.shape[1:], f32),
        ],
        in_specs=[hbm, vmem, vmem, hbm, vmem, vmem, vmem, vmem, hbm, vmem, vmem],
        out_specs=[vmem] * 6,
        scratch_shapes=[
            pltpu.VMEM((groups, 3 * part, rows), bf16),
            pltpu.VMEM((2 * groups,) + piece, bf16),
            pltpu.VMEM((2 * groups,) + piece, bf16),
            pltpu.VMEM((groups,) + piece, bf16),
            pltpu.VMEM((groups,) + piece, bf16),
            pltpu.VMEM(w_qkv.shape, bf16),
            pltpu.VMEM((late, width, width), bf16),
            pltpu.VMEM((late, width, half), bf16),
            pltpu.VMEM((late, half, half), bf16),
            pltpu.VMEM((chunks, half, half), bf16),
            pltpu.VMEM((chunks, half, half), bf16),
            pltpu.VMEM((chunks, half // 2, half), bf16),
            pltpu.VMEM((chunks, half // 2, half), bf16),
            pltpu.VMEM((chunks, half // 4, half), bf16),
            pltpu.VMEM((chunks, half // 4, half), bf16),
            pltpu.VMEM((chunks, half // 8, half), bf16),
            pltpu.VMEM((4,) + vector.shape, f32),
            pltpu.VMEM((6,) + vector.shape, f32),
            dma((3,)),
        ]
        + pair(2 * groups)
        + pair(groups)
        + pair(2 * groups)
        + pair(late)
        + pair(chunks)
        + pair(chunks)
        + pair(chunks) * 5
        + pair(2 * chunks)
        + pair(6),
        compiler_params=params(60, 4),
        name="last",
    )(
        query_grad, key_grad, normed_low, w_qkv, patches, hidden_grad, small, landed_ahead, send_on,
        keep, vector
    )


def attend_kernel(spans, query, keys, marks, veto, out, out_low, sums, key_rows, query_aug, acc, stat):
    blocks, rows = keys.shape[0], keys.shape[2]
    width = query.shape[1]
    groups = query.shape[0]

    def turn(j, carry):
        mark = marks[j]
        for h in range(PER_GROUP):
            both = jnp.concatenate([keys[j, h * HD : (h + 1) * HD], mark], axis=0)
            key_rows[h, j] = both.T
        return carry

    lax.fori_loop(0, blocks, turn, 0)
    for i in range(groups):
        for h in range(PER_GROUP):
            query_aug[h, :HD] = query[i, h * HD : (h + 1) * HD] * jnp.bfloat16(0.125)
            query_aug[h, HD:] = veto[i]
        stat[0] = jnp.full(stat.shape[1:], masked_score, jnp.float32)
        stat[1] = jnp.zeros(stat.shape[1:], jnp.float32)
        acc[...] = jnp.zeros(acc.shape, jnp.float32)

        def step(j, carry):
            for h in range(PER_GROUP):
                scores = dot(key_rows[h, j], query_aug[h])
                old = stat[0, h : h + 1]
                new = jnp.maximum(old, jnp.max(scores, axis=0, keepdims=True))
                probs = jnp.exp(scores - new)
                factor = jnp.exp(old - new)
                stat[0, h : h + 1] = new
                stat[1, h : h + 1] = stat[1, h : h + 1] * factor + jnp.sum(
                    probs, axis=0, keepdims=True
                )
                values = keys[j, width + h * HD : width + (h + 1) * HD]
                acc[h] = acc[h] * factor + dot(values, probs.astype(jnp.bfloat16))
            return carry

        lax.fori_loop(spans[i, 0], spans[i, 1], step, 0)
        for h in range(PER_GROUP):
            total = stat[1, h : h + 1]
            shared = acc[h] / total
            out[i, h * HD : (h + 1) * HD] = shared
            out_low[i, h * HD : (h + 1) * HD] = shared.astype(jnp.bfloat16)
            sums[i, h : h + 1] = stat[0, h : h + 1] + jnp.log(total)


def attend(spans, query, keys, marks, veto):
    groups, width, rows = query.shape
    blocks = keys.shape[0]
    vmem = pl.BlockSpec(memory_space=pltpu.VMEM)
    return pl.pallas_call(
        attend_kernel,
        out_shape=[
            jax.ShapeDtypeStruct(query.shape, jnp.float32),
            jax.ShapeDtypeStruct(query.shape, jnp.bfloat16),
            jax.ShapeDtypeStruct((groups, 8, rows), jnp.float32),
        ],
        in_specs=[pl.BlockSpec(memory_space=pltpu.SMEM)] + [vmem] * 4,
        out_specs=[vmem] * 3,
        scratch_shapes=[
            pltpu.VMEM((PER_GROUP, blocks, rows, 2 * HD), jnp.bfloat16),
            pltpu.VMEM((PER_GROUP, 2 * HD, rows), jnp.bfloat16),
            pltpu.VMEM((PER_GROUP, HD, rows), jnp.float32),
            pltpu.VMEM((2, 8, rows), jnp.float32),
        ],
        compiler_params=params(40),
        name="attend",
    )(spans, query, keys, marks, veto)


def three_parts(values):
    high = values.astype(jnp.bfloat16)
    rest = values - high.astype(jnp.float32)
    middle = rest.astype(jnp.bfloat16)
    low = (rest - middle.astype(jnp.float32)).astype(jnp.bfloat16)
    return high, middle, low


def attend_back_kernel(
    spans,
    query,
    keys,
    marks,
    veto,
    out,
    sums,
    out_grad,
    query_grad,
    key_grad,
    key_rows,
    value_rows,
    query_aug,
    grad_aug,
    query_rows,
    grad_rows,
    query_acc,
    key_acc,
):
    blocks, rows = keys.shape[0], keys.shape[2]
    width = query.shape[1]
    groups = query.shape[0]
    bf16 = jnp.bfloat16

    def turn(j, carry):
        mark = marks[j]
        for h in range(PER_GROUP):
            both = jnp.concatenate([keys[j, h * HD : (h + 1) * HD], mark], axis=0)
            key_rows[h, j] = both.T
            values = keys[j, width + h * HD : width + (h + 1) * HD]
            value_rows[h, j] = jnp.concatenate([values, mark], axis=0).T
            key_acc[h, j] = jnp.zeros(key_acc.shape[2:], jnp.float32)
        return carry

    lax.fori_loop(0, blocks, turn, 0)
    index = lax.broadcasted_iota(jnp.int32, (HD, rows), 0)
    none = jnp.zeros((HD, rows), bf16)

    def spread(values):
        high, middle, low = three_parts(-values)
        wide = jnp.where(index == 8, high.astype(jnp.float32), 0.0)
        wide = jnp.where(index == 9, middle.astype(jnp.float32), wide)
        return jnp.where(index == 10, low.astype(jnp.float32), wide).astype(bf16)

    for i in range(groups):
        for h in range(PER_GROUP):
            span = slice(h * HD, (h + 1) * HD)
            part = query[i, span] * bf16(0.125)
            grad = out_grad[i, span]
            delta = jnp.sum(grad.astype(jnp.float32) * out[i, span], axis=0, keepdims=True)
            query_aug[h, :HD] = part
            query_aug[h, HD:] = veto[i] + spread(sums[i, h : h + 1])
            grad_aug[h, :HD] = grad
            grad_aug[h, HD:] = spread(delta)
            query_rows[h] = jnp.concatenate([part, none], axis=0).T
            grad_rows[h] = jnp.concatenate([none, grad], axis=0).T
        query_acc[...] = jnp.zeros(query_acc.shape, jnp.float32)

        def step(j, carry):
            for h in range(PER_GROUP):
                probs = jnp.exp(dot(key_rows[h, j], query_aug[h]))
                change = (probs * dot(value_rows[h, j], grad_aug[h])).astype(bf16)
                key_acc[h, j] += dot(probs.astype(bf16), grad_rows[h]) + dot(change, query_rows[h])
                query_acc[h] += dot(keys[j, h * HD : (h + 1) * HD], change)
            return carry

        lax.fori_loop(spans[i, 0], spans[i, 1], step, 0)
        for h in range(PER_GROUP):
            query_grad[i, h * HD : (h + 1) * HD] = (query_acc[h] * 0.125).astype(bf16)

    def finish(j, carry):
        for h in range(PER_GROUP):
            both = key_acc[h, j].T.astype(bf16)
            key_grad[j, h * HD : (h + 1) * HD] = both[:HD]
            key_grad[j, width + h * HD : width + (h + 1) * HD] = both[HD:]
        return carry

    lax.fori_loop(0, blocks, finish, 0)


def attend_back(spans, query, keys, marks, veto, out, sums, out_grad):
    groups, width, rows = query.shape
    blocks = keys.shape[0]
    vmem = pl.BlockSpec(memory_space=pltpu.VMEM)
    bf16 = jnp.bfloat16
    return pl.pallas_call(
        attend_back_kernel,
        out_shape=[
            jax.ShapeDtypeStruct(query.shape, bf16),
            jax.ShapeDtypeStruct(keys.shape, bf16),
        ],
        in_specs=[pl.BlockSpec(memory_space=pltpu.SMEM)] + [vmem] * 7,
        out_specs=[vmem] * 2,
        scratch_shapes=[
            pltpu.VMEM((PER_GROUP, blocks, rows, 2 * HD), bf16),
            pltpu.VMEM((PER_GROUP, blocks, rows, 2 * HD), bf16),
            pltpu.VMEM((PER_GROUP, 2 * HD, rows), bf16),
            pltpu.VMEM((PER_GROUP, 2 * HD, rows), bf16),
            pltpu.VMEM((PER_GROUP, rows, 2 * HD), bf16),
            pltpu.VMEM((PER_GROUP, rows, 2 * HD), bf16),
            pltpu.VMEM((PER_GROUP, HD, rows), jnp.float32),
            pltpu.VMEM((PER_GROUP, blocks, rows, 2 * HD), jnp.float32),
        ],
        compiler_params=params(56),
        name="attend_back",
    )(spans, query, keys, marks, veto, out, sums, out_grad)


def layer_norm(values, gain, offset):
    centre = jnp.mean(values, axis=-1, keepdims=True)
    shifted = values - centre
    spread = jnp.mean(shifted * shifted, axis=-1, keepdims=True)
    return shifted * lax.rsqrt(spread + epsilon) * gain + offset


def exact_gelu(values):
    return jax.nn.gelu(values, approximate=False)


def doc_index(positions, doc_starts):
    hits = (doc_starts[None, :] <= positions[:, None]).astype(jnp.int32)
    return jnp.sum(hits, axis=1) - 1


def doc_tables(doc_lengths, ctx_place, blocks, rows):
    bf16 = jnp.bfloat16
    lengths = doc_lengths[0]
    ends = jnp.cumsum(lengths)
    starts = ends - lengths
    count = lengths.shape[0]
    docs = doc_index(jnp.arange(blocks * rows, dtype=jnp.int32), starts).reshape(blocks, 1, rows)
    number = lax.broadcasted_iota(jnp.int32, (blocks, HD, rows), 1)
    ones = (number >= 8) & (number < 16)
    marks = ((number == docs) | ones).astype(bf16)
    mine = PEERS * jnp.arange(GROUPS, dtype=jnp.int32) + ctx_place % PEERS
    my_docs = docs.reshape(GROUPS, PEERS, 1, rows)[:, ctx_place % PEERS]
    number = number[:GROUPS]
    veto = jnp.where((number != my_docs) & (number < count), masked_score, 0.0).astype(bf16)
    first = doc_index(mine * rows, starts)
    last = doc_index(mine * rows + rows - 1, starts)
    spans = jnp.stack([starts[first] // rows, (ends[last] + rows - 1) // rows], axis=1)
    return spans.astype(jnp.int32), marks, veto


def body(
    patches,
    doc_lengths,
    norm1_gain,
    norm1_bias,
    w_qkv,
    b_qv,
    w_out,
    b_out,
    norm2_gain,
    norm2_bias,
    w_up,
    b_up,
    w_down,
    b_down,
    cotangent,
):
    f32, bf16 = jnp.float32, jnp.bfloat16
    rows, width = patches.shape[1:]
    ctx_place = lax.axis_index("ctx")
    blocks = lax.axis_size("ctx")
    spans, marks, veto = doc_tables(doc_lengths, ctx_place, blocks, rows)
    vectors = [norm1_gain, norm1_bias, b_qv, b_out, norm2_gain, norm2_bias, b_up, b_down]
    pack = Packed([v.shape[0] for v in vectors])
    wqkv2, wout2, wup2, small = gather_weights([w_qkv, w_out, w_up], pack.pack(vectors))
    wqkv = wqkv2.reshape(width, -1)
    wout = wout2.reshape(width, -1)
    wup = wup2.reshape(width, -1)
    far = w_down.shape[0] // 2
    down_part = lax.dynamic_slice_in_dim(w_down, (ctx_place % 2) * far, far)
    down_far = lax.ppermute(down_part, "wsh", [(0, 1), (1, 0)])

    def whole(name):
        start = pack.starts[name]
        part = small[:, start : start + pack.sizes[name] // LANES]
        return part.reshape(-1)

    inputs = patches[0].astype(f32)
    normed1 = layer_norm(inputs, whole("gain1"), whole("bias1")).astype(bf16)
    projected = jnp.dot(normed1, wqkv, preferred_element_type=f32)
    bqv = whole("bqv")
    offset = jnp.concatenate([bqv[:width], jnp.zeros((width,), f32), bqv[width:]])
    projected = (projected + offset).astype(bf16)
    part = width // GROUPS
    by_group = projected.reshape(rows, 3, GROUPS, part).transpose(2, 1, 3, 0)
    query, keys = spread_heads(by_group.reshape(GROUPS, 3 * part, rows))
    out_heads, heads_low, sums = attend(spans, query, keys, marks, veto)
    tiles = w_up.shape[1] // width
    chunks = 2 * tiles + 1 + w_qkv.shape[1] // width
    ahead = 4
    firsts = ["x"] * ahead + ["y"] * (chunks - ahead)
    mixed, hidden_grad, grad_heads, send_over_x, send_over_y, keep, vector = middle(
        pack, firsts, ahead, heads_low, patches[0], cotangent[0], small, wout, wup, w_down, down_far
    )
    across = [(c, c + 2 - c // 2 % 2 * 4) for c in range(blocks)]
    landed_ahead = lax.ppermute(send_over_x, "ctx", across)
    query_grad, key_grad = attend_back(
        spans, query, keys, marks, veto, out_heads, sums, grad_heads
    )
    inputs_grad, down_total, up_total, out_total, qkv_total, vector_total = last(
        pack, firsts, query_grad, key_grad, normed1, wqkv, patches[0], hidden_grad, small,
        landed_ahead, send_over_y, keep, vector,
    )
    shares = pack.unpack(vector_total)
    return (
        mixed[None],
        inputs_grad[None],
        shares[0],
        shares[1],
        qkv_total.astype(f32),
        shares[2],
        out_total.astype(f32),
        shares[3],
        shares[4],
        shares[5],
        up_total.astype(f32),
        shares[6],
        down_total.astype(f32),
        shares[7],
    )


def shifted_2(block, axis, distance):
    devices = range(lax.axis_size(axis))
    route = [((i - distance) % len(devices), i) for i in devices]
    return lax.ppermute(block, axis, route)


def any_mesh_body(
    patches,
    doc_lengths,
    norm1_gain,
    norm1_bias,
    w_qkv,
    b_qv,
    w_out,
    b_out,
    norm2_gain,
    norm2_bias,
    w_up,
    b_up,
    w_down,
    b_down,
    cotangent,
):
    tok_rows = patches.shape[1]
    model_width = patches.shape[2]
    ctx_size = lax.axis_size("ctx")
    ctx_place = lax.axis_index("ctx")
    gathered = (
        lax.all_gather(norm1_gain, "wsh", axis=0, tiled=True),
        lax.all_gather(norm1_bias, "wsh", axis=0, tiled=True),
        lax.all_gather(w_qkv, "wsh", axis=0, tiled=True),
        lax.all_gather(b_qv, "wsh", axis=0, tiled=True),
        lax.all_gather(w_out, "wsh", axis=0, tiled=True),
        lax.all_gather(b_out, "wsh", axis=0, tiled=True),
        lax.all_gather(norm2_gain, "wsh", axis=0, tiled=True),
        lax.all_gather(norm2_bias, "wsh", axis=0, tiled=True),
        lax.all_gather(w_up, "wsh", axis=0, tiled=True),
        lax.all_gather(b_up, "wsh", axis=0, tiled=True),
        lax.all_gather(w_down, "wsh", axis=0, tiled=True),
        lax.all_gather(b_down, "wsh", axis=0, tiled=True),
    )
    (
        gain1,
        bias1,
        wqkv_full,
        bqv_full,
        wout_full,
        bout_full,
        gain2,
        bias2,
        wup_full,
        bup_full,
        wdown_full,
        bdown_full,
    ) = gathered
    inputs = patches[0].astype(jnp.float32)
    lengths = doc_lengths[0]
    doc_starts = jnp.cumsum(lengths) - lengths
    row_offsets = lax.iota(jnp.int32, tok_rows)
    query_docs = doc_index(ctx_place * tok_rows + row_offsets, doc_starts)
    gain1_float = gain1.astype(jnp.float32)
    bias1_float = bias1.astype(jnp.float32)
    normed1 = layer_norm(inputs, gain1_float, bias1_float).astype(jnp.bfloat16)
    projected = jnp.dot(normed1, wqkv_full, preferred_element_type=jnp.float32)
    bqv_float = bqv_full.astype(jnp.float32)
    query_low = (projected[:, :model_width] + bqv_float[:model_width]).astype(jnp.bfloat16)
    key_low = projected[:, model_width : 2 * model_width].astype(jnp.bfloat16)
    value_low = (projected[:, 2 * model_width :] + bqv_float[model_width:]).astype(jnp.bfloat16)
    query_heads = query_low.reshape(tok_rows, H, HD)

    def attend_block(state, key_block, value_block, key_start):
        run_max, run_total, run_acc = state
        key_docs = doc_index(key_start + row_offsets, doc_starts)
        same_doc = (query_docs[:, None] == key_docs[None, :])[None]
        scores = (
            jnp.einsum(
                "qhd,khd->hqk",
                query_heads,
                key_block.reshape(tok_rows, H, HD),
                preferred_element_type=jnp.float32,
            )
            * 0.125
        )
        scores = jnp.where(same_doc, scores, masked_score)
        new_max = jnp.maximum(run_max, jnp.max(scores, axis=2))
        weights = jnp.where(same_doc, jnp.exp(scores - new_max[:, :, None]), 0.0)
        factor = jnp.exp(run_max - new_max)
        new_total = run_total * factor + jnp.sum(weights, axis=2)
        new_acc = run_acc * factor[:, :, None] + jnp.einsum(
            "hqk,khd->hqd",
            weights.astype(jnp.bfloat16),
            value_block.reshape(tok_rows, H, HD),
            preferred_element_type=jnp.float32,
        )
        return (new_max, new_total, new_acc)

    initial = (
        jnp.full((H, tok_rows), masked_score, jnp.float32),
        jnp.zeros((H, tok_rows), jnp.float32),
        jnp.zeros((H, tok_rows, HD), jnp.float32),
    )
    state = initial
    key_piece = lax.all_gather(key_low, "ctx", axis=0, tiled=True)
    value_piece = lax.all_gather(value_low, "ctx", axis=0, tiled=True)
    blocks = key_piece.shape[0] // tok_rows
    key_blocks = key_piece.reshape(blocks, tok_rows, model_width)
    value_blocks = value_piece.reshape(blocks, tok_rows, model_width)
    block_starts = tok_rows * lax.iota(jnp.int32, blocks)

    def one_block(inner, item):
        key_block, value_block, key_start = item
        return (attend_block(inner, key_block, value_block, key_start), None)

    state, unused = lax.scan(one_block, state, (key_blocks, value_blocks, block_starts))
    run_max, run_total, run_acc = state
    log_total = run_max + jnp.log(run_total)
    attended = jnp.transpose(run_acc / run_total[:, :, None], (1, 0, 2)).reshape(
        tok_rows, model_width
    )
    attended_low = attended.astype(jnp.bfloat16)
    branch = jnp.dot(
        attended_low, wout_full, preferred_element_type=jnp.float32
    ) + bout_full.astype(jnp.float32)
    hidden_sum = inputs + branch
    gain2_float = gain2.astype(jnp.float32)
    bias2_float = bias2.astype(jnp.float32)
    normed2 = layer_norm(hidden_sum, gain2_float, bias2_float).astype(jnp.bfloat16)
    pre_act = jnp.dot(normed2, wup_full, preferred_element_type=jnp.float32) + bup_full.astype(
        jnp.float32
    )
    activated = exact_gelu(pre_act).astype(jnp.bfloat16)
    mixed = (
        hidden_sum
        + jnp.dot(activated, wdown_full, preferred_element_type=jnp.float32)
        + bdown_full.astype(jnp.float32)
    )
    back_gain1 = gathered[0].astype(jnp.float32)
    back_bias1 = gathered[1].astype(jnp.float32)
    back_wqkv = gathered[2]
    back_wout = gathered[4]
    back_gain2 = gathered[6].astype(jnp.float32)
    back_bias2 = gathered[7].astype(jnp.float32)
    back_wup = gathered[8]
    back_wdown = gathered[10]
    out_grad = cotangent[0]
    wdown_grad = jnp.einsum("tf,td->fd", activated, out_grad, preferred_element_type=jnp.float32)
    bdown_grad = jnp.sum(out_grad.astype(jnp.float32), axis=0)
    act_grad = jnp.einsum("td,fd->tf", out_grad, back_wdown, preferred_element_type=jnp.float32)
    unused_act, gelu_back = jax.vjp(exact_gelu, pre_act)
    pre_grad = gelu_back(act_grad)[0].astype(jnp.bfloat16)
    wup_grad = jnp.einsum("tc,tf->cf", normed2, pre_grad, preferred_element_type=jnp.float32)
    bup_grad = jnp.sum(pre_grad.astype(jnp.float32), axis=0)
    normed2_grad = jnp.einsum("tf,cf->tc", pre_grad, back_wup, preferred_element_type=jnp.float32)
    unused_norm2, norm2_back = jax.vjp(layer_norm, hidden_sum, back_gain2, back_bias2)
    hidden_part, gain2_grad, bias2_grad = norm2_back(normed2_grad)
    hidden_grad = out_grad.astype(jnp.float32) + hidden_part
    branch_grad = hidden_grad.astype(jnp.bfloat16)
    wout_grad = jnp.einsum(
        "tc,td->cd", attended_low, branch_grad, preferred_element_type=jnp.float32
    )
    bout_grad = jnp.sum(branch_grad.astype(jnp.float32), axis=0)
    attended_grad = jnp.einsum(
        "td,cd->tc", branch_grad, back_wout, preferred_element_type=jnp.float32
    ).astype(jnp.bfloat16)
    delta = jnp.sum(
        (attended_grad.astype(jnp.float32) * attended).reshape(tok_rows, H, HD), axis=2
    ).T
    grad_heads = attended_grad.reshape(tok_rows, H, HD)

    def back_block(state, anchor):
        key_start = anchor * tok_rows
        key_cur, value_cur, key_grad, value_grad, query_grad = state
        key_docs = doc_index(key_start + row_offsets, doc_starts)
        same_doc = (query_docs[:, None] == key_docs[None, :])[None]
        key_heads = key_cur.reshape(tok_rows, H, HD)
        scores = (
            jnp.einsum("qhd,khd->hqk", query_heads, key_heads, preferred_element_type=jnp.float32)
            * 0.125
        )
        probs = jnp.where(same_doc, jnp.exp(scores - log_total[:, :, None]), 0.0)
        value_grad = value_grad + jnp.einsum(
            "hqk,qhd->khd",
            probs.astype(jnp.bfloat16),
            grad_heads,
            preferred_element_type=jnp.float32,
        ).reshape(tok_rows, model_width)
        prob_grad = jnp.einsum(
            "qhd,khd->hqk",
            grad_heads,
            value_cur.reshape(tok_rows, H, HD),
            preferred_element_type=jnp.float32,
        )
        score_grad = (probs * (prob_grad - delta[:, :, None])).astype(jnp.bfloat16)
        query_grad = (
            query_grad
            + jnp.einsum(
                "hqk,khd->qhd", score_grad, key_heads, preferred_element_type=jnp.float32
            ).reshape(tok_rows, model_width)
            * 0.125
        )
        key_grad = (
            key_grad
            + jnp.einsum(
                "hqk,qhd->khd", score_grad, query_heads, preferred_element_type=jnp.float32
            ).reshape(tok_rows, model_width)
            * 0.125
        )
        return (key_cur, value_cur, key_grad, value_grad, query_grad)

    def pass_on(state):
        key_cur, value_cur, key_grad, value_grad, query_grad = state
        moved_keys = shifted_2((key_cur, value_cur), "ctx", 1)
        moved_sums = (
            shifted_2(key_grad.astype(jnp.bfloat16), "ctx", 1).astype(key_grad.dtype),
            shifted_2(value_grad.astype(jnp.bfloat16), "ctx", 1).astype(value_grad.dtype),
        )
        return (moved_keys[0], moved_keys[1], moved_sums[0], moved_sums[1], query_grad)

    def two_steps(turn, state):
        state = pass_on(back_block(state, (ctx_place - 2 * turn) % ctx_size))
        state = pass_on(back_block(state, (ctx_place - 2 * turn - 1) % ctx_size))
        return state

    zero_rows = jnp.zeros((tok_rows, model_width), jnp.float32)
    final_state = lax.fori_loop(
        0, ctx_size // 2, two_steps, (key_low, value_low, zero_rows, zero_rows, zero_rows)
    )
    key_grad_low = final_state[2].astype(jnp.bfloat16)
    value_grad_low = final_state[3].astype(jnp.bfloat16)
    query_grad_low = final_state[4].astype(jnp.bfloat16)
    projected_grad = jnp.concatenate([query_grad_low, key_grad_low, value_grad_low], axis=1)
    wqkv_grad = jnp.einsum("tc,te->ce", normed1, projected_grad, preferred_element_type=jnp.float32)
    bqv_grad = jnp.concatenate(
        [
            jnp.sum(query_grad_low.astype(jnp.float32), axis=0),
            jnp.sum(value_grad_low.astype(jnp.float32), axis=0),
        ]
    )
    normed1_grad = jnp.einsum(
        "te,ce->tc", projected_grad, back_wqkv, preferred_element_type=jnp.float32
    )
    unused_norm1, norm1_back = jax.vjp(layer_norm, inputs, back_gain1, back_bias1)
    input_part, gain1_grad, bias1_grad = norm1_back(normed1_grad)
    inputs_grad = hidden_grad + input_part
    shares = (
        lax.psum_scatter(
            gain1_grad.astype(jnp.bfloat16), "wsh", scatter_dimension=0, tiled=True
        ).astype(jnp.float32),
        lax.psum_scatter(
            bias1_grad.astype(jnp.bfloat16), "wsh", scatter_dimension=0, tiled=True
        ).astype(jnp.float32),
        lax.psum_scatter(
            wqkv_grad.astype(jnp.bfloat16), "wsh", scatter_dimension=0, tiled=True
        ).astype(jnp.float32),
        lax.psum_scatter(
            bqv_grad.astype(jnp.bfloat16), "wsh", scatter_dimension=0, tiled=True
        ).astype(jnp.float32),
        lax.psum_scatter(
            wout_grad.astype(jnp.bfloat16), "wsh", scatter_dimension=0, tiled=True
        ).astype(jnp.float32),
        lax.psum_scatter(
            bout_grad.astype(jnp.bfloat16), "wsh", scatter_dimension=0, tiled=True
        ).astype(jnp.float32),
        lax.psum_scatter(
            gain2_grad.astype(jnp.bfloat16), "wsh", scatter_dimension=0, tiled=True
        ).astype(jnp.float32),
        lax.psum_scatter(
            bias2_grad.astype(jnp.bfloat16), "wsh", scatter_dimension=0, tiled=True
        ).astype(jnp.float32),
        lax.psum_scatter(
            wup_grad.astype(jnp.bfloat16), "wsh", scatter_dimension=0, tiled=True
        ).astype(jnp.float32),
        lax.psum_scatter(
            bup_grad.astype(jnp.bfloat16), "wsh", scatter_dimension=0, tiled=True
        ).astype(jnp.float32),
        lax.psum_scatter(
            wdown_grad.astype(jnp.bfloat16), "wsh", scatter_dimension=0, tiled=True
        ).astype(jnp.float32),
        lax.psum_scatter(
            bdown_grad.astype(jnp.bfloat16), "wsh", scatter_dimension=0, tiled=True
        ).astype(jnp.float32),
    )
    totals = (
        lax.psum(shares[0].astype(jnp.bfloat16), "ctx").astype(jnp.float32),
        lax.psum(shares[1].astype(jnp.bfloat16), "ctx").astype(jnp.float32),
        lax.psum(shares[2].astype(jnp.bfloat16), "ctx").astype(jnp.float32),
        lax.psum(shares[3].astype(jnp.bfloat16), "ctx").astype(jnp.float32),
        lax.psum(shares[4].astype(jnp.bfloat16), "ctx").astype(jnp.float32),
        lax.psum(shares[5].astype(jnp.bfloat16), "ctx").astype(jnp.float32),
        lax.psum(shares[6].astype(jnp.bfloat16), "ctx").astype(jnp.float32),
        lax.psum(shares[7].astype(jnp.bfloat16), "ctx").astype(jnp.float32),
        lax.psum(shares[8].astype(jnp.bfloat16), "ctx").astype(jnp.float32),
        lax.psum(shares[9].astype(jnp.bfloat16), "ctx").astype(jnp.float32),
        lax.psum(shares[10].astype(jnp.bfloat16), "ctx").astype(jnp.float32),
        lax.psum(shares[11].astype(jnp.bfloat16), "ctx").astype(jnp.float32),
    )
    return (
        mixed.astype(jnp.bfloat16)[None],
        inputs_grad[None],
        totals[0],
        totals[1],
        totals[2],
        totals[3],
        totals[4],
        totals[5],
        totals[6],
        totals[7],
        totals[8],
        totals[9],
        totals[10],
        totals[11],
    )


def solution(mesh):
    as_planned = mesh.shape["ctx"] == GROUPS * PEERS and mesh.shape["wsh"] == 2
    return jax.shard_map(
        body if as_planned else any_mesh_body,
        mesh=mesh,
        in_specs=(
            P("wsh", "ctx", None),
            P("wsh", None),
            P("wsh"),
            P("wsh"),
            P("wsh", None),
            P("wsh"),
            P("wsh", None),
            P("wsh"),
            P("wsh"),
            P("wsh"),
            P("wsh", None),
            P("wsh"),
            P("wsh", None),
            P("wsh"),
            P("wsh", "ctx", None),
        ),
        out_specs=(
            P("wsh", "ctx", None),
            P("wsh", "ctx", None),
            P("wsh"),
            P("wsh"),
            P("wsh", None),
            P("wsh"),
            P("wsh", None),
            P("wsh"),
            P("wsh"),
            P("wsh"),
            P("wsh", None),
            P("wsh"),
            P("wsh", None),
            P("wsh"),
        ),
        check_vma=False,
    )
```

```python
import functools

import jax
import jax.numpy as jnp
from jax import lax
from jax.experimental import pallas as pl
from jax.experimental.pallas import tpu as pltpu
from jax.sharding import PartitionSpec as P

H = 12
HD = 64
GROUPS = 4
PER_GROUP = H // GROUPS
PEERS = 4
MESH = pl.DeviceIdType.MESH
MIB = 2**20

epsilon = 1e-05
masked_score = -1e30


def params(vmem_mib, collective_id=None):
    if collective_id is None:
        return pltpu.CompilerParams(vmem_limit_bytes=vmem_mib * MIB)
    return pltpu.CompilerParams(
        vmem_limit_bytes=vmem_mib * MIB, collective_id=collective_id, has_side_effects=True
    )


def here():
    ctx = lax.axis_index("ctx")
    return ctx // PEERS, (ctx // 2) % 2, ctx % 2, lax.axis_index("wsh")


def at(z, x, core, y):
    return (z * PEERS + x * 2 + core, y)


def remote(src, dst, send, recv, device):
    return pltpu.make_async_remote_copy(
        src_ref=src,
        dst_ref=dst,
        send_sem=send,
        recv_sem=recv,
        device_id=device,
        device_id_type=MESH,
    )


def greet(devices):
    barrier = pltpu.get_barrier_semaphore()
    for device in devices:
        pl.semaphore_signal(barrier, inc=1, device_id=device, device_id_type=MESH)
    pl.semaphore_wait(barrier, len(devices))


def dot(left, right):
    return jnp.dot(left, right, preferred_element_type=jnp.float32)


def dot_turned(left, right):
    return lax.dot_general(
        left, right, (((1,), (1,)), ((), ())), preferred_element_type=jnp.float32
    )


def normalise(values):
    centre = jnp.mean(values, axis=-1, keepdims=True)
    shifted = values - centre
    spread = jnp.mean(shifted * shifted, axis=-1, keepdims=True)
    scale = lax.rsqrt(spread + epsilon)
    return shifted * scale, scale


def normalise_back(grad, gain, normed, scale):
    inner = grad * gain
    centre = jnp.mean(inner, axis=-1, keepdims=True)
    along = jnp.mean(inner * normed, axis=-1, keepdims=True)
    gain_grad = jnp.sum(grad * normed, axis=0, keepdims=True)
    bias_grad = jnp.sum(grad, axis=0, keepdims=True)
    return scale * (inner - centre - normed * along), gain_grad, bias_grad


LANES = 128


class Packed:
    names = ("gain1", "bias1", "bqv", "bout", "gain2", "bias2", "bup", "bdown")

    def __init__(self, sizes):
        self.sizes = dict(zip(self.names, sizes))
        self.starts, row = {}, 0
        for name in self.names:
            self.starts[name] = row
            row += self.sizes[name] // LANES
        self.used = row
        self.rows = row + -row % 8

    def pack(self, halves):
        total, flat = self.rows * LANES, 0.0
        for name, half in zip(self.names, halves):
            start = self.starts[name] * LANES
            after = total - start - half.shape[0]
            flat += jnp.pad(half.astype(jnp.float32), (start, after))
        return flat.reshape(-1, LANES)

    def read(self, ref, name, first=0, count=None):
        count = 2 * self.sizes[name] if count is None else count
        parts = []
        for lane in range(first, first + count, LANES):
            y, inner = divmod(lane, self.sizes[name])
            row = self.starts[name] + inner // LANES
            parts.append(ref[y, row : row + 1])
        return jnp.concatenate(parts, axis=1)

    def write(self, ref, name, values, first=0):
        for lane in range(0, values.shape[1], LANES):
            y, inner = divmod(first + lane, self.sizes[name])
            row = self.starts[name] + inner // LANES
            ref[y, row : row + 1] = values[:, lane : lane + LANES]

    def unpack(self, rows):
        flat = rows[: self.used].reshape(-1)
        parts, start = [], 0
        for name in self.names:
            parts.append(flat[start : start + self.sizes[name]])
            start += self.sizes[name]
        return parts


class Sender:
    def __init__(self):
        self.copies = []

    def __call__(self, src, dst, send, recv, device):
        copy = remote(src, dst, send, recv, device)
        copy.start()
        self.copies.append(copy)

    def finish(self):
        for copy in self.copies:
            copy.wait_send()


def front_kernel(
    pack,
    patches,
    small_half,
    qkv_half,
    out_half,
    up_half,
    down_half,
    query,
    keys,
    normed_low,
    small,
    qkv_far,
    out_far,
    up_far,
    down_part,
    qkv_own,
    staged,
    local,
    small_sem,
    ysend,
    yrecv,
    xsend,
    xrecv,
    csend,
    crecv,
    fsend,
    frecv,
    psend,
    precv,
    nsend,
    nrecv,
    query_send,
    query_recv,
    zsend,
    zrecv,
    kxsend,
    kxrecv,
    kcsend,
    kcrecv,
    kfsend,
    kfrecv,
):
    bf16 = jnp.bfloat16
    z, x, core, y = here()
    over_x, over_core, over_y = (
        at(z, 1 - x, core, y),
        at(z, x, 1 - core, y),
        at(z, x, core, 1 - y),
    )
    around = [at((z + d) % GROUPS, x, core, y) for d in range(1, GROUPS)]
    rows, width = patches.shape
    part = query.shape[1]
    half = qkv_half.shape[0]
    quarter = half // PEERS
    down = down_part.shape[0]
    greet(around + [over_x, over_core, over_y])
    go = Sender()

    def landed(view, sem):
        remote(view, view, sem, sem, over_core).wait_recv()

    def columns(b):
        return pl.ds(b * width, width)

    def share(px, pcore, b):
        return qkv_far.at[pl.ds((px * 2 + pcore) * quarter, quarter), columns(b)]

    order = (1, 2, 0)
    go(small_half, small.at[y], small_sem.at[0], small_sem.at[1], over_y)
    for b in order:
        src = qkv_half.at[pl.ds((x * 2 + core) * quarter, quarter), columns(b)]
        go(src, share(x, core, b), ysend.at[b], yrecv.at[b], over_y)
    copies = [
        pltpu.make_async_copy(small_half, small.at[y], local.at[0]),
        pltpu.make_async_copy(qkv_half, qkv_own, local.at[1]),
        pltpu.make_async_copy(down_half.at[pl.ds(core * down, down)], down_part, local.at[2]),
    ]
    for copy in copies:
        copy.start()

    pieces = [(out_half, out_far, half // 2, 0)]
    pieces += [(up_half, up_far, half // 8, first) for first in range(0, half // 2, half // 8)]

    def piece_rows(k, pcore):
        return pl.ds(pcore * (half // 2) + pieces[k][3], pieces[k][2])

    for k, (src, full, count, first) in enumerate(pieces):
        span = piece_rows(k, core)
        go(src.at[span], full.at[span], psend.at[k], precv.at[k], over_y)

    copies[0].wait()
    landed(small.at[1 - y], small_sem.at[1])
    normed, scale = normalise(patches[...].astype(jnp.float32))
    low = (normed * pack.read(small, "gain1") + pack.read(small, "bias1")).astype(bf16)
    normed_low[...] = low
    low_own = jnp.where(y == 0, low[:, :half], low[:, half:])
    low_far = jnp.where(y == 0, low[:, half:], low[:, :half])
    for i, b in enumerate(order):
        view = share(x, core, b)
        landed(view, yrecv.at[b])
        go(view, view, xsend.at[b], xrecv.at[b], over_x)
        go(view, view, csend.at[b], crecv.at[b], over_core)
    copies[1].wait()

    def block(pz, px, pcore, b):
        return keys.at[pz * PEERS + px * 2 + pcore, pl.ds((b - 1) * part, part)]

    own = []
    for i, b in enumerate(order):
        view = share(1 - x, core, b)
        landed(view, xrecv.at[b])
        go(view, view, fsend.at[b], frecv.at[b], over_core)
        landed(share(x, 1 - core, b), crecv.at[b])
        landed(share(1 - x, 1 - core, b), frecv.at[b])
        made = dot(low_own, qkv_own[:, b * width : (b + 1) * width])
        made = made + dot(low_far, qkv_far[:, b * width : (b + 1) * width])
        if b != 1:
            made = made + pack.read(small, "bqv", (b // 2) * width, width)
        staged[b] = made.astype(bf16).T.reshape(GROUPS, part, rows)
        for d in (2, 1, 3):
            target = (z + d) % GROUPS
            if b == 0:
                dst, sems = query.at[z], (query_send.at[d], query_recv.at[d])
            else:
                sem = (b - 1) * GROUPS + d
                dst, sems = block(z, x, core, b), (zsend.at[sem], zrecv.at[sem])
            go(staged.at[b, target], dst, sems[0], sems[1], around[d - 1])
        dst = query.at[z] if b == 0 else block(z, x, core, b)
        own.append(pltpu.make_async_copy(staged.at[b, z], dst, local.at[3 + i]))
        own[-1].start()
        if b > 0:
            sem = (b - 1) * GROUPS
            go(staged.at[b, z], dst, kxsend.at[sem], kxrecv.at[sem], over_x)
            go(staged.at[b, z], dst, kcsend.at[sem], kcrecv.at[sem], over_core)

    sequence = [(1, 0), (2, 0)] + [(b, d) for b in (1, 2) for d in (1, 3, 2)]
    for i in range(len(sequence) + 1):
        if i < len(sequence):
            b, d = sequence[i]
            sem = (b - 1) * GROUPS + d
            if d > 0:
                view = block((z + GROUPS - d) % GROUPS, x, core, b)
                landed(view, zrecv.at[sem])
                go(view, view, kxsend.at[sem], kxrecv.at[sem], over_x)
                go(view, view, kcsend.at[sem], kcrecv.at[sem], over_core)
        if i >= 1:
            b, d = sequence[i - 1]
            sem = (b - 1) * GROUPS + d
            view = block((z + GROUPS - d) % GROUPS, 1 - x, core, b)
            landed(view, kxrecv.at[sem])
            go(view, view, kfsend.at[sem], kfrecv.at[sem], over_core)
    for k, (src, full, count, first) in enumerate(pieces):
        view = full.at[piece_rows(k, core)]
        landed(view, precv.at[k])
        go(view, view, nsend.at[k], nrecv.at[k], over_core)
    for b, d in sequence:
        sem = (b - 1) * GROUPS + d
        pz = (z + GROUPS - d) % GROUPS
        landed(block(pz, x, 1 - core, b), kcrecv.at[sem])
        landed(block(pz, 1 - x, 1 - core, b), kfrecv.at[sem])
    for d in range(1, GROUPS):
        landed(query.at[(z + GROUPS - d) % GROUPS], query_recv.at[d])
    for k, (src, full, count, first) in enumerate(pieces):
        landed(full.at[piece_rows(k, 1 - core)], nrecv.at[k])
    for copy in copies[2:] + own:
        copy.wait()
    go.finish()


def front(pack, patches, small_half, qkv_half, out_half, up_half, down_half):
    f32, bf16 = jnp.float32, jnp.bfloat16
    vmem = pl.BlockSpec(memory_space=pltpu.VMEM)
    hbm = pl.BlockSpec(memory_space=pltpu.HBM)
    rows, width = patches.shape
    part, half = width // GROUPS, qkv_half.shape[0]
    dma = pltpu.SemaphoreType.DMA

    def pair(n):
        return [dma((n,))] * 2

    return pl.pallas_call(
        functools.partial(front_kernel, pack),
        out_shape=[
            jax.ShapeDtypeStruct((GROUPS, part, rows), bf16),
            jax.ShapeDtypeStruct((GROUPS * PEERS, 2 * part, rows), bf16),
            jax.ShapeDtypeStruct((rows, width), bf16),
            jax.ShapeDtypeStruct((2,) + small_half.shape, f32),
            jax.ShapeDtypeStruct(qkv_half.shape, bf16),
            jax.ShapeDtypeStruct(out_half.shape, bf16),
            jax.ShapeDtypeStruct(up_half.shape, bf16),
            jax.ShapeDtypeStruct((down_half.shape[0] // 2, width), bf16),
        ],
        in_specs=[vmem, hbm, hbm, hbm, hbm, hbm],
        out_specs=[vmem] * 8,
        scratch_shapes=[
            pltpu.VMEM(qkv_half.shape, bf16),
            pltpu.VMEM((3, GROUPS, part, rows), bf16),
            dma((6,)),
        ]
        + [dma((2,))]
        + pair(3) * 4
        + pair(5) * 2
        + pair(GROUPS)
        + pair(2 * GROUPS) * 4,
        compiler_params=params(60, 1),
        name="front",
    )(patches, small_half, qkv_half, out_half, up_half, down_half)


def split_rows(first, x, y, quarter):
    if first == "y":
        return [((1 - y) * 2 * quarter, 2 * quarter)], [(y * 2 * quarter, 2 * quarter)]
    other, mine = (1 - x) * quarter, x * quarter
    return (
        [(other, quarter), (2 * quarter + other, quarter)],
        [(mine, quarter), (2 * quarter + mine, quarter)],
    )


def core_sum(first, own, land, send_ref, keep_ref, x, y):
    quarter = land.shape[0] // 4
    gone, kept = split_rows(first, x, y, quarter)
    for ref, parts in ((send_ref, gone), (keep_ref, kept)):
        place = 0
        for start, count in parts:
            rows = pl.ds(start, count)
            total = own(rows).astype(jnp.float32) + land[rows].astype(jnp.float32)
            ref[pl.ds(place, count)] = total.astype(ref.dtype)
            place += count


def middle_kernel(
    pack,
    firsts,
    heads,
    patches,
    out_grad,
    small,
    w_out,
    w_out_far,
    w_up,
    w_up_far,
    w_down_half,
    w_down_far,
    mixed,
    hidden_grad,
    grad_heads,
    send_over_x,
    send_over_y,
    keep,
    vector,
    o_land,
    o_grad,
    wout,
    wup,
    wdown,
    act_grad,
    act_turned,
    pre_grad,
    bup_rows,
    grads,
    c_land,
    local,
    osend,
    orecv,
    gsend,
    grecv,
    wsem,
    csend,
    crecv,
):
    f32, bf16 = jnp.float32, jnp.bfloat16
    z, x, core, y = here()
    over_core = at(z, x, 1 - core, y)
    around = [at((z + d) % GROUPS, x, core, y) for d in range(1, GROUPS)]
    rows, width = patches.shape
    tiles = wdown.shape[0] // width
    half = w_down_half.shape[0]
    far = w_down_far.shape[0]
    greet(around + [over_core])
    go = Sender()
    far_rows = pl.ds((1 - y) * half + core * far, far)
    other_rows = pl.ds((1 - y) * half + (1 - core) * far, far)
    for d in (2, 1, 3):
        go(heads.at[(z + d) % GROUPS], o_land.at[z], osend.at[d], orecv.at[d], around[d - 1])
    go(w_down_far, wdown.at[far_rows], wsem.at[0], wsem.at[1], over_core)
    down_copies = [
        pltpu.make_async_copy(w_down_half, wdown.at[pl.ds(y * half, half)], local.at[0]),
        pltpu.make_async_copy(w_down_far, wdown.at[far_rows], local.at[1]),
    ]
    copies = [
        pltpu.make_async_copy(heads.at[z], o_land.at[z], local.at[2]),
    ]
    pairs = [(w_out, wout, y), (w_out_far, wout, 1 - y), (w_up, wup, y), (w_up_far, wup, 1 - y)]
    for i, (src, dst, side) in enumerate(pairs):
        count = src.shape[0]
        span = pl.ds(side * count, count)
        copies.append(pltpu.make_async_copy(src, dst.at[span], local.at[4 + i]))

    for copy in down_copies + copies:
        copy.start()
    dy = out_grad[...]
    vector[...] = jnp.zeros(vector.shape, f32)
    pack.write(vector, "bdown", jnp.sum(dy.astype(f32), axis=0, keepdims=True))
    for f in range(tiles):
        bup_rows[f, 0:1] = pack.read(small, "bup", f * width, width)
    for copy in down_copies:
        copy.wait()
    landed = wdown.at[other_rows]
    remote(landed, landed, wsem.at[0], wsem.at[1], over_core).wait_recv()

    def tile(f):
        return pl.ds(pl.multiple_of(f * width, width), width)

    def first_grad(f, carry):
        act_grad[f] = dot_turned(dy, wdown[tile(f)])
        return carry

    lax.fori_loop(0, tiles, first_grad, 0)
    for copy in copies:
        copy.wait()
    for d in range(1, GROUPS):
        landed = o_land.at[(z + GROUPS - d) % GROUPS]
        remote(landed, landed, osend.at[d], orecv.at[d], over_core).wait_recv()
    turned = o_land[...].reshape(width, rows)
    hidden = patches[...].astype(f32) + (dot(turned.T, wout[...]) + pack.read(small, "bout"))
    gain2 = pack.read(small, "gain2")
    normed, scale = normalise(hidden)
    c = (normed * gain2 + pack.read(small, "bias2")).astype(bf16)
    mixed_acc = hidden + pack.read(small, "bdown")
    c_grad = jnp.zeros((rows, width), f32)

    def forward_back(f, carry):
        mixed_acc, c_grad = carry
        up = wup[:, tile(f)]
        pre = dot(c, up) + bup_rows[f, 0:1]
        share = 0.5 + 0.5 * lax.erf(pre * (0.5**0.5))
        slope = share + pre * jnp.exp(-0.5 * pre * pre) * ((0.5 / jnp.pi) ** 0.5)
        act = (pre * share).astype(bf16)
        grad = (act_grad[f] * slope).astype(bf16)
        act_turned[tile(f)] = act.T
        pre_grad[f] = grad
        bup_rows[f, 0:1] = jnp.sum(grad.astype(f32), axis=0, keepdims=True)
        return (
            mixed_acc + dot(act, wdown[tile(f)]),
            c_grad + dot_turned(grad, up),
        )

    mixed_acc, c_grad = lax.fori_loop(0, tiles, forward_back, (mixed_acc, c_grad))
    mixed[...] = mixed_acc.astype(bf16)
    for f in range(tiles):
        pack.write(vector, "bup", bup_rows[f, 0:1], f * width)
    part, gain_grad, bias_grad = normalise_back(c_grad, gain2, normed, scale)
    pack.write(vector, "gain2", gain_grad)
    pack.write(vector, "bias2", bias_grad)
    whole = dy.astype(f32) + part
    hidden_grad[...] = whole
    dz = whole.astype(bf16)
    pack.write(vector, "bout", jnp.sum(dz.astype(f32), axis=0, keepdims=True))
    o_grad[...] = dot_turned(wout[...], dz).astype(bf16).reshape(o_grad.shape)
    for d in (2, 1, 3):
        go(o_grad.at[(z + d) % GROUPS], grad_heads.at[z], gsend.at[d], grecv.at[d], around[d - 1])
    own = pltpu.make_async_copy(o_grad.at[z], grad_heads.at[z], local.at[3])
    own.start()

    columns = c_land.shape[2]
    count, ahead = grads.shape[0], send_over_x.shape[0]
    mine = pl.ds(pl.multiple_of(core * columns, columns), columns)
    others = pl.ds(pl.multiple_of((1 - core) * columns, columns), columns)

    def over(k):
        go(grads.at[k, :, others], c_land.at[k], csend.at[k], crecv.at[k], over_core)

    def settle(k):
        landed = c_land.at[k]
        remote(landed, landed, csend.at[k], crecv.at[k], over_core).wait_recv()
        sent = send_over_x.at[k] if k < ahead else send_over_y.at[k - ahead]
        core_sum(firsts[k], lambda r: grads[k, r, mine], c_land.at[k], sent, keep.at[k], x, y)

    c_turned = c.T
    piece = half // tiles
    for k in range(count):
        if k < tiles:
            for top in range(2):
                grads[k, top * piece : (top + 1) * piece] = dot(
                    act_turned[top * half + k * piece : top * half + (k + 1) * piece], dy
                ).astype(bf16)
        elif k < 2 * tiles:
            grads[k] = dot(c_turned, pre_grad[k - tiles]).astype(bf16)
        else:
            grads[k] = dot(turned, dz).astype(bf16)
        over(k)
        if k >= 2:
            settle(k - 2)
    settle(count - 2)
    settle(count - 1)
    for d in range(1, GROUPS):
        landed = grad_heads.at[(z + GROUPS - d) % GROUPS]
        remote(landed, landed, gsend.at[d], grecv.at[d], over_core).wait_recv()
    own.wait()
    go.finish()


def middle(pack, firsts, ahead, heads, patches, out_grad, small, *weights):
    rows, width = patches.shape
    hidden = weights[2].shape[1]
    tiles = hidden // width
    count = 2 * tiles + 1
    f32, bf16 = jnp.float32, jnp.bfloat16
    vmem = pl.BlockSpec(memory_space=pltpu.VMEM)
    hbm = pl.BlockSpec(memory_space=pltpu.HBM)
    dma = pltpu.SemaphoreType.DMA
    return pl.pallas_call(
        functools.partial(middle_kernel, pack, firsts),
        out_shape=[
            jax.ShapeDtypeStruct((rows, width), bf16),
            jax.ShapeDtypeStruct((rows, width), f32),
            jax.ShapeDtypeStruct(heads.shape, bf16),
            jax.ShapeDtypeStruct((ahead, width // 2, width // 2), bf16),
            jax.ShapeDtypeStruct((count - ahead, width // 2, width // 2), bf16),
            jax.ShapeDtypeStruct((count, width // 2, width // 2), bf16),
            jax.ShapeDtypeStruct((2, pack.rows, LANES), f32),
        ],
        in_specs=[hbm, vmem, vmem, vmem] + [hbm] * 6,
        out_specs=[vmem] * 7,
        scratch_shapes=[
            pltpu.VMEM(heads.shape, bf16),
            pltpu.VMEM(heads.shape, bf16),
            pltpu.VMEM((width, width), bf16),
            pltpu.VMEM((width, hidden), bf16),
            pltpu.VMEM((hidden, width), bf16),
            pltpu.VMEM((tiles, rows, width), f32),
            pltpu.VMEM((hidden, rows), bf16),
            pltpu.VMEM((tiles, rows, width), bf16),
            pltpu.VMEM((tiles, 8, width), f32),
            pltpu.VMEM((count, width, width), bf16),
            pltpu.VMEM((count, width, width // 2), bf16),
            dma((8,)),
            dma((GROUPS,)),
            dma((GROUPS,)),
            dma((GROUPS,)),
            dma((GROUPS,)),
            dma((2,)),
            dma((count,)),
            dma((count,)),
        ],
        compiler_params=params(60, 3),
        name="middle",
    )(heads, patches, out_grad, small, *weights)


class Totals:
    def __init__(self, refs, tiles):
        self.refs, self.tiles = refs, tiles

    def place(self, k, row, count, column, columns):
        down, up, out, qkv = self.refs
        width = out.shape[1]
        if k < self.tiles:
            rows = pl.ds(k * (width // 2) + row, count)
            return down, rows, pl.ds(pl.multiple_of(column, LANES), columns)
        if k < 2 * self.tiles:
            ref, start = up, (k - self.tiles) * width
        elif k == 2 * self.tiles:
            ref, start = out, 0
        else:
            ref, start = qkv, (k - 2 * self.tiles - 1) * width
        return ref, pl.ds(row, count), pl.ds(pl.multiple_of(start + column, LANES), columns)

    def view(self, *place):
        ref, rows, columns = self.place(*place)
        return ref.at[rows, columns]

    def store(self, values, *place):
        ref, rows, columns = self.place(*place)
        ref[rows, columns] = values.astype(ref.dtype)


def last_kernel(
    pack,
    firsts,
    tiles,
    query_grad,
    key_grad,
    normed_low,
    w_qkv,
    w_qkv_far,
    patches,
    hidden_grad,
    small,
    landed_ahead,
    send_on,
    keep,
    vector_in,
    inputs_grad,
    down_total,
    up_total,
    out_total,
    qkv_total,
    vector_out,
    got,
    near,
    both,
    far,
    own,
    wqkv,
    grads,
    c_land,
    late_send,
    first_land,
    half_sum,
    second_land,
    quarter_sum,
    z_land,
    eighth_sum,
    far_land,
    vectors,
    v_land,
    local,
    n_send,
    n_recv,
    f_send,
    f_recv,
    q_send,
    q_recv,
    csend,
    crecv,
    asend,
    arecv,
    bsend,
    brecv,
    zsend,
    zrecv,
    wsend,
    wrecv,
    dsend,
    drecv,
    gsend,
    grecv,
    hsend,
    hrecv,
    isend,
    irecv,
    vsend,
    vrecv,
):
    f32, bf16 = jnp.float32, jnp.bfloat16
    z, x, core, y = here()
    over_x, over_core, over_y = (
        at(z, 1 - x, core, y),
        at(z, x, 1 - core, y),
        at(z, x, core, 1 - y),
    )
    around = [at((z + d) % GROUPS, x, core, y) for d in range(1, GROUPS)]
    peer = {"y": over_y, "x": over_x}
    greet(around + [over_x, over_core, over_y])
    go = Sender()
    totals = Totals((down_total, up_total, out_total, qkv_total), tiles)
    part = query_grad.shape[1]
    rows, width = patches.shape
    ahead, chunks = landed_ahead.shape[0], len(firsts)
    early = ahead + send_on.shape[0]
    pair, side = z // 2, z % 2
    over_near, over_far = at(z + 1 - 2 * side, x, core, y), around[1]
    half = c_land.shape[2]
    quarter, shard = width // 4, width // 16

    def landed(view, sem):
        remote(view, view, sem, sem, over_core).wait_recv()

    order = (2, 1, 3, 0)
    for d in order:
        pz = (z + d) % GROUPS
        for k in range(2):
            px = (x + 1 + k) % 2
            slot = 2 * d + k
            src = key_grad.at[pz * PEERS + px * 2 + 1 - core]
            go(src, near.at[slot], n_send.at[slot], n_recv.at[slot], over_core)
    for d in (2, 1, 3):
        pz = (z + d) % GROUPS
        go(query_grad.at[pz], got.at[z, pl.ds(0, part)], q_send.at[d], q_recv.at[d], around[d - 1])
    own_query = pltpu.make_async_copy(query_grad.at[z], got.at[z, pl.ds(0, part)], local.at[0])
    own_query.start()
    count = w_qkv.shape[0]
    weights = [
        pltpu.make_async_copy(w_qkv, wqkv.at[pl.ds(y * count, count)], local.at[2]),
        pltpu.make_async_copy(w_qkv_far, wqkv.at[pl.ds((1 - y) * count, count)], local.at[3]),
    ]
    for copy in weights:
        copy.start()

    def start_first(k, src):
        go(src, first_land.at[k], asend.at[k], arecv.at[k], peer[firsts[k]])

    for k in range(ahead, early):
        start_first(k, send_on.at[k - ahead])
    for step in range(GROUPS + 1):
        if step < GROUPS:
            d = order[step]
            pz = (z + d) % GROUPS
            for k in range(2):
                px = (x + 1 + k) % 2
                slot = 2 * d + k
                landed(near.at[slot], n_recv.at[slot])
                mine = key_grad[pz * PEERS + px * 2 + core].astype(f32)
                both[slot] = (mine + near[slot].astype(f32)).astype(bf16)
                if k == 0:
                    go(both.at[slot], far.at[d], f_send.at[d], f_recv.at[d], over_x)
        if step >= 1:
            d = order[step - 1]
            landed(far.at[d], f_recv.at[d])
            own[d] = (both[2 * d + 1].astype(f32) + far[d].astype(f32)).astype(bf16)
            place = got.at[z, pl.ds(part, 2 * part)]
            if d == 0:
                own_keys = pltpu.make_async_copy(own.at[0], place, local.at[1])
                own_keys.start()
            else:
                sem = GROUPS + d
                go(own.at[d], place, q_send.at[sem], q_recv.at[sem], around[d - 1])
    normed_turned = normed_low[...].T
    normed, scale = normalise(patches[...].astype(f32))
    gain1 = pack.read(small, "gain1")
    def kept(k):
        return keep[k] if k < early else half_sum[k]

    def stage_core(k):
        i = k - early
        landed(c_land.at[i], crecv.at[i])
        mine = pl.ds(pl.multiple_of(core * half, half), half)
        core_sum(
            firsts[k],
            lambda r: grads[i, r, mine],
            c_land.at[i],
            late_send.at[i],
            half_sum.at[k],
            x,
            y,
        )
        start_first(k, late_send.at[i])

    def stage_first(k):
        if k < ahead:
            arrived = landed_ahead[k]
        else:
            landed(first_land.at[k], arecv.at[k])
            arrived = first_land[k]
        half_sum[k] = (kept(k).astype(f32) + arrived.astype(f32)).astype(bf16)
        place = x if firsts[k] == "y" else y
        other = half_sum.at[k, pl.ds((1 - place) * quarter, quarter)]
        second = over_x if firsts[k] == "y" else over_y
        go(other, second_land.at[k], bsend.at[k], brecv.at[k], second)

    def stage_second(k):
        landed(second_land.at[k], brecv.at[k])
        place = x if firsts[k] == "y" else y
        total = half_sum[k, pl.ds(place * quarter, quarter)].astype(f32)
        quarter_sum[k] = (total + second_land[k].astype(f32)).astype(bf16)
        other = quarter_sum.at[k, pl.ds((1 - side) * 2 * shard, 2 * shard)]
        go(other, z_land.at[k], zsend.at[k], zrecv.at[k], over_near)

    def stage_near(k):
        landed(z_land.at[k], zrecv.at[k])
        total = quarter_sum[k, pl.ds(side * 2 * shard, 2 * shard)].astype(f32)
        eighth_sum[k] = (total + z_land[k].astype(f32)).astype(bf16)
        other = eighth_sum.at[k, pl.ds((1 - pair) * shard, shard)]
        go(other, far_land.at[k], wsend.at[k], wrecv.at[k], over_far)

    def spot(k, px, pside, ppair, count):
        row = px * quarter + pside * 2 * shard + ppair * shard
        return totals.view(k, row, count, core * half, half)

    def stage_far(k):
        landed(far_land.at[k], wrecv.at[k])
        total = eighth_sum[k, pl.ds(pair * shard, shard)].astype(f32) + far_land[k].astype(f32)
        row = x * quarter + side * 2 * shard + pair * shard
        totals.store(total, k, row, shard, core * half, half)
        view = spot(k, x, side, pair, shard)
        go(view, view, dsend.at[k], drecv.at[k], over_far)

    def stage_back(k):
        landed(spot(k, x, side, 1 - pair, shard), drecv.at[k])
        view = spot(k, x, side, 0, 2 * shard)
        go(view, view, gsend.at[k], grecv.at[k], over_near)

    def stage_out(k):
        landed(spot(k, x, 1 - side, 0, 2 * shard), grecv.at[k])
        view = spot(k, x, 0, 0, quarter)
        go(view, view, hsend.at[k], hrecv.at[k], over_x)
        go(view, view, isend.at[2 * k], irecv.at[2 * k], over_core)

    def stage_last(k):
        view = spot(k, 1 - x, 0, 0, quarter)
        landed(view, hrecv.at[k])
        go(view, view, isend.at[2 * k + 1], irecv.at[2 * k + 1], over_core)

    stages = (
        stage_first,
        stage_second,
        stage_near,
        stage_far,
        stage_back,
        stage_out,
        stage_last,
    )

    def turn(step):
        for depth, stage in enumerate(stages):
            if 0 <= step - depth < chunks:
                stage(step - depth)

    before = min(early, 4)
    for step in range(before):
        turn(step)

    for d in range(1, GROUPS):
        pz = (z + GROUPS - d) % GROUPS
        landed(got.at[pz, pl.ds(0, part)], q_recv.at[d])
        landed(got.at[pz, pl.ds(part, 2 * part)], q_recv.at[GROUPS + d])
    own_query.wait()
    own_keys.wait()
    for copy in weights:
        copy.wait()

    for k in range(early, chunks):
        i = k - early
        turned = got[:, i * part : (i + 1) * part].reshape(width, rows)
        grads[i] = dot_turned(normed_turned, turned).astype(bf16)
        others = pl.ds(pl.multiple_of((1 - core) * half, half), half)
        go(grads.at[i, :, others], c_land.at[i], csend.at[i], crecv.at[i], over_core)
    vectors[0] = vector_in[...]
    ones = jnp.ones((8, rows), bf16)
    normed_grad = jnp.zeros((width, rows), f32)
    for i in range(chunks - early):
        turned = got[:, i * part : (i + 1) * part].reshape(width, rows)
        if i != 1:
            sums = dot_turned(ones, turned)[0:1]
            pack.write(vectors.at[0], "bqv", sums, (i // 2) * width)
        normed_grad += dot(wqkv[:, i * width : (i + 1) * width], turned)
    change, gain_grad, bias_grad = normalise_back(normed_grad.T, gain1, normed, scale)
    inputs_grad[...] = hidden_grad[...] + change
    pack.write(vectors.at[0], "gain1", gain_grad)
    pack.write(vectors.at[0], "bias1", bias_grad)
    go(vectors.at[0], v_land.at[0], vsend.at[0], vrecv.at[0], over_core)

    def vector_step(n):
        if n == 0:
            landed(v_land.at[0], vrecv.at[0])
            vectors[1] = vectors[0] + v_land[0]
            go(vectors.at[1], v_land.at[1], vsend.at[1], vrecv.at[1], over_x)
        elif n == 1:
            landed(v_land.at[1], vrecv.at[1])
            vectors[2] = vectors[1] + v_land[1]
            go(vectors.at[2], v_land.at[2], vsend.at[2], vrecv.at[2], over_y)
        elif n == 2:
            landed(v_land.at[2], vrecv.at[2])
            vectors[3] = vectors[2] + v_land[2]
            for d in range(1, GROUPS):
                sem = 2 + d
                go(vectors.at[3], v_land.at[sem], vsend.at[sem], vrecv.at[sem], around[d - 1])
        elif n == 3:
            total = vectors[3]
            for d in range(1, GROUPS):
                landed(v_land.at[2 + d], vrecv.at[2 + d])
                total += v_land[2 + d]
            v_land[0] = total
            vector_out[...] = v_land[0, y]

    for k in range(early, chunks):
        stage_core(k)
    for step in range(before, chunks + len(stages) - 1):
        turn(step)
        vector_step(step - before)
    for k in range(chunks):
        for px in range(2):
            place = (x + px) % 2
            view = totals.view(k, place * quarter, quarter, (1 - core) * half, half)
            landed(view, irecv.at[2 * k + px])
    go.finish()


def last(
    pack, firsts, query_grad, key_grad, normed_low, w_qkv, w_qkv_far, patches, hidden_grad, small,
    landed_ahead, send_on, keep, vector
):
    f32, bf16 = jnp.float32, jnp.bfloat16
    vmem = pl.BlockSpec(memory_space=pltpu.VMEM)
    hbm = pl.BlockSpec(memory_space=pltpu.HBM)
    groups, part, rows = query_grad.shape
    width = patches.shape[1]
    early, half = keep.shape[0], width // 2
    tiles, chunks, late = (early - 1) // 2, len(firsts), len(firsts) - early
    piece = (2 * part, rows)
    dma = pltpu.SemaphoreType.DMA

    def pair(n):
        return [dma((n,))] * 2

    return pl.pallas_call(
        functools.partial(last_kernel, pack, firsts, tiles),
        out_shape=[
            jax.ShapeDtypeStruct((rows, width), f32),
            jax.ShapeDtypeStruct((tiles * half, width), bf16),
            jax.ShapeDtypeStruct((half, tiles * width), bf16),
            jax.ShapeDtypeStruct((half, width), bf16),
            jax.ShapeDtypeStruct((half, late * width), bf16),
            jax.ShapeDtypeStruct(vector.shape[1:], f32),
        ],
        in_specs=[hbm, vmem, vmem, hbm, hbm, vmem, vmem, vmem, vmem, hbm, vmem, vmem],
        out_specs=[vmem] * 6,
        scratch_shapes=[
            pltpu.VMEM((groups, 3 * part, rows), bf16),
            pltpu.VMEM((2 * groups,) + piece, bf16),
            pltpu.VMEM((2 * groups,) + piece, bf16),
            pltpu.VMEM((groups,) + piece, bf16),
            pltpu.VMEM((groups,) + piece, bf16),
            pltpu.VMEM((width, late * width), bf16),
            pltpu.VMEM((late, width, width), bf16),
            pltpu.VMEM((late, width, half), bf16),
            pltpu.VMEM((late, half, half), bf16),
            pltpu.VMEM((chunks, half, half), bf16),
            pltpu.VMEM((chunks, half, half), bf16),
            pltpu.VMEM((chunks, half // 2, half), bf16),
            pltpu.VMEM((chunks, half // 2, half), bf16),
            pltpu.VMEM((chunks, half // 4, half), bf16),
            pltpu.VMEM((chunks, half // 4, half), bf16),
            pltpu.VMEM((chunks, half // 8, half), bf16),
            pltpu.VMEM((4,) + vector.shape, f32),
            pltpu.VMEM((6,) + vector.shape, f32),
            dma((4,)),
        ]
        + pair(2 * groups)
        + pair(groups)
        + pair(2 * groups)
        + pair(late)
        + pair(chunks)
        + pair(chunks)
        + pair(chunks) * 5
        + pair(2 * chunks)
        + pair(6),
        compiler_params=params(60, 4),
        name="last",
    )(
        query_grad, key_grad, normed_low, w_qkv, w_qkv_far, patches, hidden_grad, small,
        landed_ahead, send_on, keep, vector,
    )


class Documents:
    def __init__(self, lengths, rows):
        self.rows, self.count = rows, lengths.shape[1]
        self.starts, self.ends, place = [], [], 0
        for d in range(self.count):
            self.starts.append(place)
            place = place + lengths[0, d]
            self.ends.append(place)

    def span(self, block):
        first, last = block * self.rows, (block + 1) * self.rows - 1
        low, high = 0, 0
        for d in range(self.count):
            low = jnp.where(self.starts[d] <= first, self.starts[d], low)
        for d in reversed(range(self.count)):
            high = jnp.where(self.ends[d] > last, self.ends[d], high)
        return low // self.rows, (high + self.rows - 1) // self.rows

    def inside(self, block, yes, no):
        shape = (8, self.rows)
        row = lax.broadcasted_iota(jnp.int32, shape, 0)
        place = block * self.rows + lax.broadcasted_iota(jnp.int32, shape, 1)
        found = jnp.where(row < self.count, no, 0.0)
        for d in range(self.count):
            hit = (row == d) & (place >= self.starts[d]) & (place < self.ends[d])
            found = jnp.where(hit, yes, found)
        return found

    def marks(self, block):
        ones, rest = jnp.ones((8, self.rows)), jnp.zeros((HD - 16, self.rows))
        return jnp.concatenate([self.inside(block, 1.0, 0.0), ones, rest]).astype(jnp.bfloat16)

    def veto(self, block):
        rest = jnp.zeros((HD - 8, self.rows))
        return jnp.concatenate([self.inside(block, 0.0, masked_score), rest])


def attend_kernel(
    lengths, place, query, keys, out, out_low, sums, key_rows, query_aug, acc, stat
):
    blocks, rows = keys.shape[0], keys.shape[2]
    width = query.shape[1]
    groups = query.shape[0]
    documents = Documents(lengths, rows)

    def turn(j, carry):
        mark = documents.marks(j)
        for h in range(PER_GROUP):
            both = jnp.concatenate([keys[j, h * HD : (h + 1) * HD], mark], axis=0)
            key_rows[h, j] = both.T
        return carry

    lax.fori_loop(0, blocks, turn, 0)
    for i in range(groups):
        block = i * PEERS + place[0]
        veto = documents.veto(block).astype(jnp.bfloat16)
        for h in range(PER_GROUP):
            query_aug[h, :HD] = query[i, h * HD : (h + 1) * HD] * jnp.bfloat16(0.125)
            query_aug[h, HD:] = veto
        stat[0] = jnp.full(stat.shape[1:], masked_score, jnp.float32)
        stat[1] = jnp.zeros(stat.shape[1:], jnp.float32)
        acc[...] = jnp.zeros(acc.shape, jnp.float32)

        def step(j, carry):
            for h in range(PER_GROUP):
                scores = dot(key_rows[h, j], query_aug[h])
                old = stat[0, h : h + 1]
                new = jnp.maximum(old, jnp.max(scores, axis=0, keepdims=True))
                probs = jnp.exp(scores - new)
                factor = jnp.exp(old - new)
                stat[0, h : h + 1] = new
                stat[1, h : h + 1] = stat[1, h : h + 1] * factor + jnp.sum(
                    probs, axis=0, keepdims=True
                )
                values = keys[j, width + h * HD : width + (h + 1) * HD]
                acc[h] = acc[h] * factor + dot(values, probs.astype(jnp.bfloat16))
            return carry

        lax.fori_loop(*documents.span(block), step, 0)
        for h in range(PER_GROUP):
            total = stat[1, h : h + 1]
            shared = acc[h] / total
            out[i, h * HD : (h + 1) * HD] = shared
            out_low[i, h * HD : (h + 1) * HD] = shared.astype(jnp.bfloat16)
            sums[i, h : h + 1] = stat[0, h : h + 1] + jnp.log(total)


def attend(lengths, place, query, keys):
    groups, width, rows = query.shape
    blocks = keys.shape[0]
    vmem = pl.BlockSpec(memory_space=pltpu.VMEM)
    return pl.pallas_call(
        attend_kernel,
        out_shape=[
            jax.ShapeDtypeStruct(query.shape, jnp.float32),
            jax.ShapeDtypeStruct(query.shape, jnp.bfloat16),
            jax.ShapeDtypeStruct((groups, 8, rows), jnp.float32),
        ],
        in_specs=[pl.BlockSpec(memory_space=pltpu.SMEM)] * 2 + [vmem] * 2,
        out_specs=[vmem] * 3,
        scratch_shapes=[
            pltpu.VMEM((PER_GROUP, blocks, rows, 2 * HD), jnp.bfloat16),
            pltpu.VMEM((PER_GROUP, 2 * HD, rows), jnp.bfloat16),
            pltpu.VMEM((PER_GROUP, HD, rows), jnp.float32),
            pltpu.VMEM((2, 8, rows), jnp.float32),
        ],
        compiler_params=params(60),
        name="attend",
    )(lengths, place, query, keys)


def three_parts(values):
    high = values.astype(jnp.bfloat16)
    rest = values - high.astype(jnp.float32)
    middle = rest.astype(jnp.bfloat16)
    low = (rest - middle.astype(jnp.float32)).astype(jnp.bfloat16)
    return high, middle, low


def attend_back_kernel(
    lengths,
    place,
    query,
    keys,
    out,
    sums,
    out_grad,
    query_grad,
    key_grad,
    key_rows,
    value_rows,
    query_aug,
    grad_aug,
    query_rows,
    grad_rows,
    query_acc,
    key_acc,
):
    blocks, rows = keys.shape[0], keys.shape[2]
    width = query.shape[1]
    groups = query.shape[0]
    bf16 = jnp.bfloat16
    documents = Documents(lengths, rows)

    def turn(j, carry):
        mark = documents.marks(j)
        for h in range(PER_GROUP):
            both = jnp.concatenate([keys[j, h * HD : (h + 1) * HD], mark], axis=0)
            key_rows[h, j] = both.T
            values = keys[j, width + h * HD : width + (h + 1) * HD]
            value_rows[h, j] = jnp.concatenate([values, mark], axis=0).T
            key_acc[h, j] = jnp.zeros(key_acc.shape[2:], jnp.float32)
        return carry

    lax.fori_loop(0, blocks, turn, 0)
    index = lax.broadcasted_iota(jnp.int32, (HD, rows), 0)
    none = jnp.zeros((HD, rows), bf16)

    def spread(values):
        high, middle, low = three_parts(-values)
        wide = jnp.where(index == 8, high.astype(jnp.float32), 0.0)
        wide = jnp.where(index == 9, middle.astype(jnp.float32), wide)
        return jnp.where(index == 10, low.astype(jnp.float32), wide)

    for i in range(groups):
        block = i * PEERS + place[0]
        veto = documents.veto(block)
        for h in range(PER_GROUP):
            span = slice(h * HD, (h + 1) * HD)
            part = query[i, span] * bf16(0.125)
            grad = out_grad[i, span]
            delta = jnp.sum(grad.astype(jnp.float32) * out[i, span], axis=0, keepdims=True)
            query_aug[h, :HD] = part
            query_aug[h, HD:] = (veto + spread(sums[i, h : h + 1])).astype(bf16)
            grad_aug[h, :HD] = grad
            grad_aug[h, HD:] = spread(delta).astype(bf16)
            query_rows[h] = jnp.concatenate([part, none], axis=0).T
            grad_rows[h] = jnp.concatenate([none, grad], axis=0).T
        query_acc[...] = jnp.zeros(query_acc.shape, jnp.float32)

        def step(j, carry):
            for h in range(PER_GROUP):
                probs = jnp.exp(dot(key_rows[h, j], query_aug[h]))
                change = (probs * dot(value_rows[h, j], grad_aug[h])).astype(bf16)
                key_acc[h, j] += dot(probs.astype(bf16), grad_rows[h]) + dot(change, query_rows[h])
                query_acc[h] += dot(keys[j, h * HD : (h + 1) * HD], change)
            return carry

        lax.fori_loop(*documents.span(block), step, 0)
        for h in range(PER_GROUP):
            query_grad[i, h * HD : (h + 1) * HD] = (query_acc[h] * 0.125).astype(bf16)

    def finish(j, carry):
        for h in range(PER_GROUP):
            both = key_acc[h, j].T.astype(bf16)
            key_grad[j, h * HD : (h + 1) * HD] = both[:HD]
            key_grad[j, width + h * HD : width + (h + 1) * HD] = both[HD:]
        return carry

    lax.fori_loop(0, blocks, finish, 0)


def attend_back(lengths, place, query, keys, out, sums, out_grad):
    groups, width, rows = query.shape
    blocks = keys.shape[0]
    vmem = pl.BlockSpec(memory_space=pltpu.VMEM)
    bf16 = jnp.bfloat16
    return pl.pallas_call(
        attend_back_kernel,
        out_shape=[
            jax.ShapeDtypeStruct(query.shape, bf16),
            jax.ShapeDtypeStruct(keys.shape, bf16),
        ],
        in_specs=[pl.BlockSpec(memory_space=pltpu.SMEM)] * 2 + [vmem] * 5,
        out_specs=[vmem] * 2,
        scratch_shapes=[
            pltpu.VMEM((PER_GROUP, blocks, rows, 2 * HD), bf16),
            pltpu.VMEM((PER_GROUP, blocks, rows, 2 * HD), bf16),
            pltpu.VMEM((PER_GROUP, 2 * HD, rows), bf16),
            pltpu.VMEM((PER_GROUP, 2 * HD, rows), bf16),
            pltpu.VMEM((PER_GROUP, rows, 2 * HD), bf16),
            pltpu.VMEM((PER_GROUP, rows, 2 * HD), bf16),
            pltpu.VMEM((PER_GROUP, HD, rows), jnp.float32),
            pltpu.VMEM((PER_GROUP, blocks, rows, 2 * HD), jnp.float32),
        ],
        compiler_params=params(60),
        name="attend_back",
    )(lengths, place, query, keys, out, sums, out_grad)


def layer_norm(values, gain, offset):
    centre = jnp.mean(values, axis=-1, keepdims=True)
    shifted = values - centre
    spread = jnp.mean(shifted * shifted, axis=-1, keepdims=True)
    return shifted * lax.rsqrt(spread + epsilon) * gain + offset


def exact_gelu(values):
    return jax.nn.gelu(values, approximate=False)


def doc_index(positions, doc_starts):
    hits = (doc_starts[None, :] <= positions[:, None]).astype(jnp.int32)
    return jnp.sum(hits, axis=1) - 1


def body(
    patches,
    doc_lengths,
    norm1_gain,
    norm1_bias,
    w_qkv,
    b_qv,
    w_out,
    b_out,
    norm2_gain,
    norm2_bias,
    w_up,
    b_up,
    w_down,
    b_down,
    cotangent,
):
    f32, bf16 = jnp.float32, jnp.bfloat16
    rows, width = patches.shape[1:]
    ctx_place = lax.axis_index("ctx")
    blocks = lax.axis_size("ctx")
    place = (ctx_place % PEERS).astype(jnp.int32).reshape(1)
    vectors = [norm1_gain, norm1_bias, b_qv, b_out, norm2_gain, norm2_bias, b_up, b_down]
    pack = Packed([v.shape[0] for v in vectors])
    query, keys, normed1, small, qkv_far, out_far, up_far, down_part = front(
        pack, patches[0], pack.pack(vectors), w_qkv, w_out, w_up, w_down
    )
    down_far = lax.ppermute(down_part, "wsh", [(0, 1), (1, 0)])
    out_heads, heads_low, sums = attend(doc_lengths, place, query, keys)
    tiles = w_up.shape[1] // width
    chunks = 2 * tiles + 1 + w_qkv.shape[1] // width
    ahead = 4
    firsts = ["x"] * ahead + ["y"] * (chunks - ahead)
    mixed, hidden_grad, grad_heads, send_over_x, send_over_y, keep, vector = middle(
        pack, firsts, ahead, heads_low, patches[0], cotangent[0], small, w_out, out_far, w_up,
        up_far, w_down, down_far,
    )
    across = [(c, c + 2 - c // 2 % 2 * 4) for c in range(blocks)]
    landed_ahead = lax.ppermute(send_over_x, "ctx", across)
    query_grad, key_grad = attend_back(
        doc_lengths, place, query, keys, out_heads, sums, grad_heads
    )
    inputs_grad, down_total, up_total, out_total, qkv_total, vector_total = last(
        pack, firsts, query_grad, key_grad, normed1, w_qkv, qkv_far, patches[0], hidden_grad, small,
        landed_ahead, send_over_y, keep, vector,
    )
    shares = pack.unpack(vector_total)
    return (
        mixed[None],
        inputs_grad[None],
        shares[0],
        shares[1],
        qkv_total.astype(f32),
        shares[2],
        out_total.astype(f32),
        shares[3],
        shares[4],
        shares[5],
        up_total.astype(f32),
        shares[6],
        down_total.astype(f32),
        shares[7],
    )


def shifted_2(block, axis, distance):
    devices = range(lax.axis_size(axis))
    route = [((i - distance) % len(devices), i) for i in devices]
    return lax.ppermute(block, axis, route)


def any_mesh_body(
    patches,
    doc_lengths,
    norm1_gain,
    norm1_bias,
    w_qkv,
    b_qv,
    w_out,
    b_out,
    norm2_gain,
    norm2_bias,
    w_up,
    b_up,
    w_down,
    b_down,
    cotangent,
):
    tok_rows = patches.shape[1]
    model_width = patches.shape[2]
    ctx_size = lax.axis_size("ctx")
    ctx_place = lax.axis_index("ctx")
    gathered = (
        lax.all_gather(norm1_gain, "wsh", axis=0, tiled=True),
        lax.all_gather(norm1_bias, "wsh", axis=0, tiled=True),
        lax.all_gather(w_qkv, "wsh", axis=0, tiled=True),
        lax.all_gather(b_qv, "wsh", axis=0, tiled=True),
        lax.all_gather(w_out, "wsh", axis=0, tiled=True),
        lax.all_gather(b_out, "wsh", axis=0, tiled=True),
        lax.all_gather(norm2_gain, "wsh", axis=0, tiled=True),
        lax.all_gather(norm2_bias, "wsh", axis=0, tiled=True),
        lax.all_gather(w_up, "wsh", axis=0, tiled=True),
        lax.all_gather(b_up, "wsh", axis=0, tiled=True),
        lax.all_gather(w_down, "wsh", axis=0, tiled=True),
        lax.all_gather(b_down, "wsh", axis=0, tiled=True),
    )
    (
        gain1,
        bias1,
        wqkv_full,
        bqv_full,
        wout_full,
        bout_full,
        gain2,
        bias2,
        wup_full,
        bup_full,
        wdown_full,
        bdown_full,
    ) = gathered
    inputs = patches[0].astype(jnp.float32)
    lengths = doc_lengths[0]
    doc_starts = jnp.cumsum(lengths) - lengths
    row_offsets = lax.iota(jnp.int32, tok_rows)
    query_docs = doc_index(ctx_place * tok_rows + row_offsets, doc_starts)
    gain1_float = gain1.astype(jnp.float32)
    bias1_float = bias1.astype(jnp.float32)
    normed1 = layer_norm(inputs, gain1_float, bias1_float).astype(jnp.bfloat16)
    projected = jnp.dot(normed1, wqkv_full, preferred_element_type=jnp.float32)
    bqv_float = bqv_full.astype(jnp.float32)
    query_low = (projected[:, :model_width] + bqv_float[:model_width]).astype(jnp.bfloat16)
    key_low = projected[:, model_width : 2 * model_width].astype(jnp.bfloat16)
    value_low = (projected[:, 2 * model_width :] + bqv_float[model_width:]).astype(jnp.bfloat16)
    query_heads = query_low.reshape(tok_rows, H, HD)

    def attend_block(state, key_block, value_block, key_start):
        run_max, run_total, run_acc = state
        key_docs = doc_index(key_start + row_offsets, doc_starts)
        same_doc = (query_docs[:, None] == key_docs[None, :])[None]
        scores = (
            jnp.einsum(
                "qhd,khd->hqk",
                query_heads,
                key_block.reshape(tok_rows, H, HD),
                preferred_element_type=jnp.float32,
            )
            * 0.125
        )
        scores = jnp.where(same_doc, scores, masked_score)
        new_max = jnp.maximum(run_max, jnp.max(scores, axis=2))
        weights = jnp.where(same_doc, jnp.exp(scores - new_max[:, :, None]), 0.0)
        factor = jnp.exp(run_max - new_max)
        new_total = run_total * factor + jnp.sum(weights, axis=2)
        new_acc = run_acc * factor[:, :, None] + jnp.einsum(
            "hqk,khd->hqd",
            weights.astype(jnp.bfloat16),
            value_block.reshape(tok_rows, H, HD),
            preferred_element_type=jnp.float32,
        )
        return (new_max, new_total, new_acc)

    initial = (
        jnp.full((H, tok_rows), masked_score, jnp.float32),
        jnp.zeros((H, tok_rows), jnp.float32),
        jnp.zeros((H, tok_rows, HD), jnp.float32),
    )
    state = initial
    key_piece = lax.all_gather(key_low, "ctx", axis=0, tiled=True)
    value_piece = lax.all_gather(value_low, "ctx", axis=0, tiled=True)
    blocks = key_piece.shape[0] // tok_rows
    key_blocks = key_piece.reshape(blocks, tok_rows, model_width)
    value_blocks = value_piece.reshape(blocks, tok_rows, model_width)
    block_starts = tok_rows * lax.iota(jnp.int32, blocks)

    def one_block(inner, item):
        key_block, value_block, key_start = item
        return (attend_block(inner, key_block, value_block, key_start), None)

    state, unused = lax.scan(one_block, state, (key_blocks, value_blocks, block_starts))
    run_max, run_total, run_acc = state
    log_total = run_max + jnp.log(run_total)
    attended = jnp.transpose(run_acc / run_total[:, :, None], (1, 0, 2)).reshape(
        tok_rows, model_width
    )
    attended_low = attended.astype(jnp.bfloat16)
    branch = jnp.dot(
        attended_low, wout_full, preferred_element_type=jnp.float32
    ) + bout_full.astype(jnp.float32)
    hidden_sum = inputs + branch
    gain2_float = gain2.astype(jnp.float32)
    bias2_float = bias2.astype(jnp.float32)
    normed2 = layer_norm(hidden_sum, gain2_float, bias2_float).astype(jnp.bfloat16)
    pre_act = jnp.dot(normed2, wup_full, preferred_element_type=jnp.float32) + bup_full.astype(
        jnp.float32
    )
    activated = exact_gelu(pre_act).astype(jnp.bfloat16)
    mixed = (
        hidden_sum
        + jnp.dot(activated, wdown_full, preferred_element_type=jnp.float32)
        + bdown_full.astype(jnp.float32)
    )
    back_gain1 = gathered[0].astype(jnp.float32)
    back_bias1 = gathered[1].astype(jnp.float32)
    back_wqkv = gathered[2]
    back_wout = gathered[4]
    back_gain2 = gathered[6].astype(jnp.float32)
    back_bias2 = gathered[7].astype(jnp.float32)
    back_wup = gathered[8]
    back_wdown = gathered[10]
    out_grad = cotangent[0]
    wdown_grad = jnp.einsum("tf,td->fd", activated, out_grad, preferred_element_type=jnp.float32)
    bdown_grad = jnp.sum(out_grad.astype(jnp.float32), axis=0)
    act_grad = jnp.einsum("td,fd->tf", out_grad, back_wdown, preferred_element_type=jnp.float32)
    unused_act, gelu_back = jax.vjp(exact_gelu, pre_act)
    pre_grad = gelu_back(act_grad)[0].astype(jnp.bfloat16)
    wup_grad = jnp.einsum("tc,tf->cf", normed2, pre_grad, preferred_element_type=jnp.float32)
    bup_grad = jnp.sum(pre_grad.astype(jnp.float32), axis=0)
    normed2_grad = jnp.einsum("tf,cf->tc", pre_grad, back_wup, preferred_element_type=jnp.float32)
    unused_norm2, norm2_back = jax.vjp(layer_norm, hidden_sum, back_gain2, back_bias2)
    hidden_part, gain2_grad, bias2_grad = norm2_back(normed2_grad)
    hidden_grad = out_grad.astype(jnp.float32) + hidden_part
    branch_grad = hidden_grad.astype(jnp.bfloat16)
    wout_grad = jnp.einsum(
        "tc,td->cd", attended_low, branch_grad, preferred_element_type=jnp.float32
    )
    bout_grad = jnp.sum(branch_grad.astype(jnp.float32), axis=0)
    attended_grad = jnp.einsum(
        "td,cd->tc", branch_grad, back_wout, preferred_element_type=jnp.float32
    ).astype(jnp.bfloat16)
    delta = jnp.sum(
        (attended_grad.astype(jnp.float32) * attended).reshape(tok_rows, H, HD), axis=2
    ).T
    grad_heads = attended_grad.reshape(tok_rows, H, HD)

    def back_block(state, anchor):
        key_start = anchor * tok_rows
        key_cur, value_cur, key_grad, value_grad, query_grad = state
        key_docs = doc_index(key_start + row_offsets, doc_starts)
        same_doc = (query_docs[:, None] == key_docs[None, :])[None]
        key_heads = key_cur.reshape(tok_rows, H, HD)
        scores = (
            jnp.einsum("qhd,khd->hqk", query_heads, key_heads, preferred_element_type=jnp.float32)
            * 0.125
        )
        probs = jnp.where(same_doc, jnp.exp(scores - log_total[:, :, None]), 0.0)
        value_grad = value_grad + jnp.einsum(
            "hqk,qhd->khd",
            probs.astype(jnp.bfloat16),
            grad_heads,
            preferred_element_type=jnp.float32,
        ).reshape(tok_rows, model_width)
        prob_grad = jnp.einsum(
            "qhd,khd->hqk",
            grad_heads,
            value_cur.reshape(tok_rows, H, HD),
            preferred_element_type=jnp.float32,
        )
        score_grad = (probs * (prob_grad - delta[:, :, None])).astype(jnp.bfloat16)
        query_grad = (
            query_grad
            + jnp.einsum(
                "hqk,khd->qhd", score_grad, key_heads, preferred_element_type=jnp.float32
            ).reshape(tok_rows, model_width)
            * 0.125
        )
        key_grad = (
            key_grad
            + jnp.einsum(
                "hqk,qhd->khd", score_grad, query_heads, preferred_element_type=jnp.float32
            ).reshape(tok_rows, model_width)
            * 0.125
        )
        return (key_cur, value_cur, key_grad, value_grad, query_grad)

    def pass_on(state):
        key_cur, value_cur, key_grad, value_grad, query_grad = state
        moved_keys = shifted_2((key_cur, value_cur), "ctx", 1)
        moved_sums = (
            shifted_2(key_grad.astype(jnp.bfloat16), "ctx", 1).astype(key_grad.dtype),
            shifted_2(value_grad.astype(jnp.bfloat16), "ctx", 1).astype(value_grad.dtype),
        )
        return (moved_keys[0], moved_keys[1], moved_sums[0], moved_sums[1], query_grad)

    def two_steps(turn, state):
        state = pass_on(back_block(state, (ctx_place - 2 * turn) % ctx_size))
        state = pass_on(back_block(state, (ctx_place - 2 * turn - 1) % ctx_size))
        return state

    zero_rows = jnp.zeros((tok_rows, model_width), jnp.float32)
    final_state = lax.fori_loop(
        0, ctx_size // 2, two_steps, (key_low, value_low, zero_rows, zero_rows, zero_rows)
    )
    key_grad_low = final_state[2].astype(jnp.bfloat16)
    value_grad_low = final_state[3].astype(jnp.bfloat16)
    query_grad_low = final_state[4].astype(jnp.bfloat16)
    projected_grad = jnp.concatenate([query_grad_low, key_grad_low, value_grad_low], axis=1)
    wqkv_grad = jnp.einsum("tc,te->ce", normed1, projected_grad, preferred_element_type=jnp.float32)
    bqv_grad = jnp.concatenate(
        [
            jnp.sum(query_grad_low.astype(jnp.float32), axis=0),
            jnp.sum(value_grad_low.astype(jnp.float32), axis=0),
        ]
    )
    normed1_grad = jnp.einsum(
        "te,ce->tc", projected_grad, back_wqkv, preferred_element_type=jnp.float32
    )
    unused_norm1, norm1_back = jax.vjp(layer_norm, inputs, back_gain1, back_bias1)
    input_part, gain1_grad, bias1_grad = norm1_back(normed1_grad)
    inputs_grad = hidden_grad + input_part
    shares = (
        lax.psum_scatter(
            gain1_grad.astype(jnp.bfloat16), "wsh", scatter_dimension=0, tiled=True
        ).astype(jnp.float32),
        lax.psum_scatter(
            bias1_grad.astype(jnp.bfloat16), "wsh", scatter_dimension=0, tiled=True
        ).astype(jnp.float32),
        lax.psum_scatter(
            wqkv_grad.astype(jnp.bfloat16), "wsh", scatter_dimension=0, tiled=True
        ).astype(jnp.float32),
        lax.psum_scatter(
            bqv_grad.astype(jnp.bfloat16), "wsh", scatter_dimension=0, tiled=True
        ).astype(jnp.float32),
        lax.psum_scatter(
            wout_grad.astype(jnp.bfloat16), "wsh", scatter_dimension=0, tiled=True
        ).astype(jnp.float32),
        lax.psum_scatter(
            bout_grad.astype(jnp.bfloat16), "wsh", scatter_dimension=0, tiled=True
        ).astype(jnp.float32),
        lax.psum_scatter(
            gain2_grad.astype(jnp.bfloat16), "wsh", scatter_dimension=0, tiled=True
        ).astype(jnp.float32),
        lax.psum_scatter(
            bias2_grad.astype(jnp.bfloat16), "wsh", scatter_dimension=0, tiled=True
        ).astype(jnp.float32),
        lax.psum_scatter(
            wup_grad.astype(jnp.bfloat16), "wsh", scatter_dimension=0, tiled=True
        ).astype(jnp.float32),
        lax.psum_scatter(
            bup_grad.astype(jnp.bfloat16), "wsh", scatter_dimension=0, tiled=True
        ).astype(jnp.float32),
        lax.psum_scatter(
            wdown_grad.astype(jnp.bfloat16), "wsh", scatter_dimension=0, tiled=True
        ).astype(jnp.float32),
        lax.psum_scatter(
            bdown_grad.astype(jnp.bfloat16), "wsh", scatter_dimension=0, tiled=True
        ).astype(jnp.float32),
    )
    totals = (
        lax.psum(shares[0].astype(jnp.bfloat16), "ctx").astype(jnp.float32),
        lax.psum(shares[1].astype(jnp.bfloat16), "ctx").astype(jnp.float32),
        lax.psum(shares[2].astype(jnp.bfloat16), "ctx").astype(jnp.float32),
        lax.psum(shares[3].astype(jnp.bfloat16), "ctx").astype(jnp.float32),
        lax.psum(shares[4].astype(jnp.bfloat16), "ctx").astype(jnp.float32),
        lax.psum(shares[5].astype(jnp.bfloat16), "ctx").astype(jnp.float32),
        lax.psum(shares[6].astype(jnp.bfloat16), "ctx").astype(jnp.float32),
        lax.psum(shares[7].astype(jnp.bfloat16), "ctx").astype(jnp.float32),
        lax.psum(shares[8].astype(jnp.bfloat16), "ctx").astype(jnp.float32),
        lax.psum(shares[9].astype(jnp.bfloat16), "ctx").astype(jnp.float32),
        lax.psum(shares[10].astype(jnp.bfloat16), "ctx").astype(jnp.float32),
        lax.psum(shares[11].astype(jnp.bfloat16), "ctx").astype(jnp.float32),
    )
    return (
        mixed.astype(jnp.bfloat16)[None],
        inputs_grad[None],
        totals[0],
        totals[1],
        totals[2],
        totals[3],
        totals[4],
        totals[5],
        totals[6],
        totals[7],
        totals[8],
        totals[9],
        totals[10],
        totals[11],
    )


def solution(mesh):
    as_planned = mesh.shape["ctx"] == GROUPS * PEERS and mesh.shape["wsh"] == 2
    return jax.shard_map(
        body if as_planned else any_mesh_body,
        mesh=mesh,
        in_specs=(
            P("wsh", "ctx", None),
            P("wsh", None),
            P("wsh"),
            P("wsh"),
            P("wsh", None),
            P("wsh"),
            P("wsh", None),
            P("wsh"),
            P("wsh"),
            P("wsh"),
            P("wsh", None),
            P("wsh"),
            P("wsh", None),
            P("wsh"),
            P("wsh", "ctx", None),
        ),
        out_specs=(
            P("wsh", "ctx", None),
            P("wsh", "ctx", None),
            P("wsh"),
            P("wsh"),
            P("wsh", None),
            P("wsh"),
            P("wsh", None),
            P("wsh"),
            P("wsh"),
            P("wsh"),
            P("wsh", None),
            P("wsh"),
            P("wsh", None),
            P("wsh"),
        ),
        check_vma=False,
    )
```

```python
import functools

import jax
import jax.numpy as jnp
from jax import lax
from jax.experimental import pallas as pl
from jax.experimental.pallas import tpu as pltpu
from jax.sharding import PartitionSpec as P

H = 12
HD = 64
GROUPS = 4
PER_GROUP = H // GROUPS
PEERS = 4
MESH = pl.DeviceIdType.MESH
MIB = 2**20

epsilon = 1e-05
masked_score = -1e30


def params(vmem_mib, collective_id=None):
    if collective_id is None:
        return pltpu.CompilerParams(vmem_limit_bytes=vmem_mib * MIB)
    return pltpu.CompilerParams(
        vmem_limit_bytes=vmem_mib * MIB, collective_id=collective_id, has_side_effects=True
    )


def here():
    ctx = lax.axis_index("ctx")
    return ctx // PEERS, (ctx // 2) % 2, ctx % 2, lax.axis_index("wsh")


def at(z, x, core, y):
    return (z * PEERS + x * 2 + core, y)


def remote(src, dst, send, recv, device):
    return pltpu.make_async_remote_copy(
        src_ref=src,
        dst_ref=dst,
        send_sem=send,
        recv_sem=recv,
        device_id=device,
        device_id_type=MESH,
    )


def greet(devices):
    barrier = pltpu.get_barrier_semaphore()
    for device in devices:
        pl.semaphore_signal(barrier, inc=1, device_id=device, device_id_type=MESH)
    pl.semaphore_wait(barrier, len(devices))


def dot(left, right):
    return jnp.dot(left, right, preferred_element_type=jnp.float32)


def dot_turned(left, right):
    return lax.dot_general(
        left, right, (((1,), (1,)), ((), ())), preferred_element_type=jnp.float32
    )


def normalise(values):
    centre = jnp.mean(values, axis=-1, keepdims=True)
    shifted = values - centre
    spread = jnp.mean(shifted * shifted, axis=-1, keepdims=True)
    scale = lax.rsqrt(spread + epsilon)
    return shifted * scale, scale


def normalise_back(grad, gain, normed, scale):
    inner = grad * gain
    centre = jnp.mean(inner, axis=-1, keepdims=True)
    along = jnp.mean(inner * normed, axis=-1, keepdims=True)
    gain_grad = jnp.sum(grad * normed, axis=0, keepdims=True)
    bias_grad = jnp.sum(grad, axis=0, keepdims=True)
    return scale * (inner - centre - normed * along), gain_grad, bias_grad


LANES = 128


class Packed:
    names = ("gain1", "bias1", "bqv", "bout", "gain2", "bias2", "bup", "bdown")

    def __init__(self, sizes):
        self.sizes = dict(zip(self.names, sizes))
        self.starts, row = {}, 0
        for name in self.names:
            self.starts[name] = row
            row += self.sizes[name] // LANES
        self.used = row
        self.rows = row + -row % 8

    def pack(self, halves):
        total, flat = self.rows * LANES, 0.0
        for name, half in zip(self.names, halves):
            start = self.starts[name] * LANES
            after = total - start - half.shape[0]
            flat += jnp.pad(half.astype(jnp.float32), (start, after))
        return flat.reshape(-1, LANES)

    def read(self, ref, name, first=0, count=None):
        count = 2 * self.sizes[name] if count is None else count
        parts = []
        for lane in range(first, first + count, LANES):
            y, inner = divmod(lane, self.sizes[name])
            row = self.starts[name] + inner // LANES
            parts.append(ref[y, row : row + 1])
        return jnp.concatenate(parts, axis=1)

    def write(self, ref, name, values, first=0):
        for lane in range(0, values.shape[1], LANES):
            y, inner = divmod(first + lane, self.sizes[name])
            row = self.starts[name] + inner // LANES
            ref[y, row : row + 1] = values[:, lane : lane + LANES]

    def unpack(self, rows):
        flat = rows[: self.used].reshape(-1)
        parts, start = [], 0
        for name in self.names:
            parts.append(flat[start : start + self.sizes[name]])
            start += self.sizes[name]
        return parts


class Sender:
    def __init__(self):
        self.copies = []

    def __call__(self, src, dst, send, recv, device):
        copy = remote(src, dst, send, recv, device)
        copy.start()
        self.copies.append(copy)

    def finish(self):
        for copy in self.copies:
            copy.wait_send()


def front_kernel(
    pack,
    patches,
    small_half,
    qkv_half,
    out_half,
    up_half,
    down_half,
    query,
    keys,
    normed_low,
    small,
    qkv_far,
    out_far,
    up_far,
    down_got,
    down_part,
    qkv_own,
    staged,
    local,
    small_sem,
    ysend,
    yrecv,
    xsend,
    xrecv,
    csend,
    crecv,
    fsend,
    frecv,
    psend,
    precv,
    nsend,
    nrecv,
    pxsend,
    pxrecv,
    pfsend,
    pfrecv,
    query_send,
    query_recv,
    zsend,
    zrecv,
    kxsend,
    kxrecv,
    kcsend,
    kcrecv,
    kfsend,
    kfrecv,
):
    bf16 = jnp.bfloat16
    z, x, core, y = here()
    over_x, over_core, over_y = (
        at(z, 1 - x, core, y),
        at(z, x, 1 - core, y),
        at(z, x, core, 1 - y),
    )
    around = [at((z + d) % GROUPS, x, core, y) for d in range(1, GROUPS)]
    rows, width = patches.shape
    part = query.shape[1]
    half = qkv_half.shape[0]
    quarter = half // PEERS
    down, later = down_half.shape[0] // 2, down_part.shape[0]
    sooner = down - later
    greet(around + [over_x, over_core, over_y])
    go = Sender()

    def landed(view, sem):
        remote(view, view, sem, sem, over_core).wait_recv()

    def columns(b):
        return pl.ds(b * width, width)

    def share(px, pcore, b):
        return qkv_far.at[pl.ds((px * 2 + pcore) * quarter, quarter), columns(b)]

    order = (1, 2, 0)
    go(small_half, small.at[y], small_sem.at[0], small_sem.at[1], over_y)
    for b in order:
        src = qkv_half.at[pl.ds((x * 2 + core) * quarter, quarter), columns(b)]
        go(src, share(x, core, b), ysend.at[b], yrecv.at[b], over_y)
    copies = [
        pltpu.make_async_copy(small_half, small.at[y], local.at[0]),
        pltpu.make_async_copy(qkv_half, qkv_own, local.at[1]),
        pltpu.make_async_copy(
            down_half.at[pl.ds(core * down + sooner, later)], down_part, local.at[2]
        ),
    ]
    for copy in copies:
        copy.start()

    step = quarter // 2
    pieces = [(up_half, up_far, quarter, quarter, step, i * step, half // 2) for i in range(2)]
    shared = len(pieces)
    pieces += [(out_half, out_far, half // 2, half // 2, half // 2, 0, 0)]
    step = sooner // 2
    pieces += [(down_half, down_got, down, sooner, step, i * step, 0) for i in range(2)]

    def piece_view(k, px, pcore):
        unused, full, unused, apart, count, first, across = pieces[k]
        return full.at[pl.ds(px * across + pcore * apart + first, count)]

    def piece_in(k):
        view = piece_view(k, x, core)
        landed(view, precv.at[k])
        if k < shared:
            go(view, view, pxsend.at[k], pxrecv.at[k], over_x)
        go(view, view, nsend.at[k], nrecv.at[k], over_core)

    def piece_over(k):
        view = piece_view(k, 1 - x, core)
        landed(view, pxrecv.at[k])
        go(view, view, pfsend.at[k], pfrecv.at[k], over_core)

    copies[0].wait()
    landed(small.at[1 - y], small_sem.at[1])
    normed, scale = normalise(patches[...].astype(jnp.float32))
    low = (normed * pack.read(small, "gain1") + pack.read(small, "bias1")).astype(bf16)
    normed_low[...] = low
    low_own = jnp.where(y == 0, low[:, :half], low[:, half:])
    low_far = jnp.where(y == 0, low[:, half:], low[:, :half])
    for i, b in enumerate(order):
        view = share(x, core, b)
        landed(view, yrecv.at[b])
        go(view, view, xsend.at[b], xrecv.at[b], over_x)
        go(view, view, csend.at[b], crecv.at[b], over_core)
    for k, (src, unused, apart, unused, count, first, across) in enumerate(pieces):
        span = pl.ds(x * across + core * apart + first, count)
        go(src.at[span], piece_view(k, x, core), psend.at[k], precv.at[k], over_y)

    copies[1].wait()

    def block(pz, px, pcore, b):
        return keys.at[pz * PEERS + px * 2 + pcore, pl.ds((b - 1) * part, part)]

    own = []
    for i, b in enumerate(order):
        view = share(1 - x, core, b)
        landed(view, xrecv.at[b])
        go(view, view, fsend.at[b], frecv.at[b], over_core)
        landed(share(x, 1 - core, b), crecv.at[b])
        landed(share(1 - x, 1 - core, b), frecv.at[b])
        made = dot(low_own, qkv_own[:, b * width : (b + 1) * width])
        made = made + dot(low_far, qkv_far[:, b * width : (b + 1) * width])
        if b != 1:
            made = made + pack.read(small, "bqv", (b // 2) * width, width)
        staged[b] = made.astype(bf16).T.reshape(GROUPS, part, rows)
        for d in (2, 1, 3):
            target = (z + d) % GROUPS
            if b == 0:
                dst, sems = query.at[z], (query_send.at[d], query_recv.at[d])
            else:
                sem = (b - 1) * GROUPS + d
                dst, sems = block(z, x, core, b), (zsend.at[sem], zrecv.at[sem])
            go(staged.at[b, target], dst, sems[0], sems[1], around[d - 1])
        dst = query.at[z] if b == 0 else block(z, x, core, b)
        own.append(pltpu.make_async_copy(staged.at[b, z], dst, local.at[3 + i]))
        own[-1].start()
        if b > 0:
            sem = (b - 1) * GROUPS
            go(staged.at[b, z], dst, kxsend.at[sem], kxrecv.at[sem], over_x)
            go(staged.at[b, z], dst, kcsend.at[sem], kcrecv.at[sem], over_core)

    sequence = [(1, 0), (2, 0)] + [(b, d) for b in (1, 2) for d in (1, 3, 2)]
    for i in range(len(sequence) + 1):
        if i < len(sequence):
            b, d = sequence[i]
            sem = (b - 1) * GROUPS + d
            if d > 0:
                view = block((z + GROUPS - d) % GROUPS, x, core, b)
                landed(view, zrecv.at[sem])
                go(view, view, kxsend.at[sem], kxrecv.at[sem], over_x)
                go(view, view, kcsend.at[sem], kcrecv.at[sem], over_core)
        if i >= 1:
            b, d = sequence[i - 1]
            sem = (b - 1) * GROUPS + d
            view = block((z + GROUPS - d) % GROUPS, 1 - x, core, b)
            landed(view, kxrecv.at[sem])
            go(view, view, kfsend.at[sem], kfrecv.at[sem], over_core)
        if 2 <= i < 2 + shared:
            piece_in(i - 2)
    for k in range(shared, len(pieces)):
        piece_in(k)
    for k in range(shared):
        piece_over(k)
    for b, d in sequence:
        sem = (b - 1) * GROUPS + d
        pz = (z + GROUPS - d) % GROUPS
        landed(block(pz, x, 1 - core, b), kcrecv.at[sem])
        landed(block(pz, 1 - x, 1 - core, b), kfrecv.at[sem])
    for d in range(1, GROUPS):
        landed(query.at[(z + GROUPS - d) % GROUPS], query_recv.at[d])
    for k in range(len(pieces)):
        landed(piece_view(k, x, 1 - core), nrecv.at[k])
    for k in range(shared):
        landed(piece_view(k, 1 - x, 1 - core), pfrecv.at[k])
    for copy in copies[2:] + own:
        copy.wait()
    go.finish()


def front(pack, patches, small_half, qkv_half, out_half, up_half, down_half):
    f32, bf16 = jnp.float32, jnp.bfloat16
    vmem = pl.BlockSpec(memory_space=pltpu.VMEM)
    hbm = pl.BlockSpec(memory_space=pltpu.HBM)
    rows, width = patches.shape
    part, half = width // GROUPS, qkv_half.shape[0]
    dma = pltpu.SemaphoreType.DMA

    def pair(n):
        return [dma((n,))] * 2

    return pl.pallas_call(
        functools.partial(front_kernel, pack),
        out_shape=[
            jax.ShapeDtypeStruct((GROUPS, part, rows), bf16),
            jax.ShapeDtypeStruct((GROUPS * PEERS, 2 * part, rows), bf16),
            jax.ShapeDtypeStruct((rows, width), bf16),
            jax.ShapeDtypeStruct((2,) + small_half.shape, f32),
            jax.ShapeDtypeStruct(qkv_half.shape, bf16),
            jax.ShapeDtypeStruct(out_half.shape, bf16),
            jax.ShapeDtypeStruct(up_half.shape, bf16),
            jax.ShapeDtypeStruct((down_half.shape[0] // 2, width), bf16),
            jax.ShapeDtypeStruct((down_half.shape[0] // 4, width), bf16),
        ],
        in_specs=[vmem, hbm, hbm, hbm, hbm, hbm],
        out_specs=[vmem] * 9,
        scratch_shapes=[
            pltpu.VMEM(qkv_half.shape, bf16),
            pltpu.VMEM((3, GROUPS, part, rows), bf16),
            dma((6,)),
        ]
        + [dma((2,))]
        + pair(3) * 4
        + pair(5) * 2
        + pair(2) * 2
        + pair(GROUPS)
        + pair(2 * GROUPS) * 4,
        compiler_params=params(60, 1),
        name="front",
    )(patches, small_half, qkv_half, out_half, up_half, down_half)


def split_rows(first, x, y, quarter):
    if first == "y":
        return [((1 - y) * 2 * quarter, 2 * quarter)], [(y * 2 * quarter, 2 * quarter)]
    other, mine = (1 - x) * quarter, x * quarter
    return (
        [(other, quarter), (2 * quarter + other, quarter)],
        [(mine, quarter), (2 * quarter + mine, quarter)],
    )


def core_sum(first, own, land, send_ref, keep_ref, x, y):
    quarter = land.shape[0] // 4
    gone, kept = split_rows(first, x, y, quarter)
    for ref, parts in ((send_ref, gone), (keep_ref, kept)):
        place = 0
        for start, count in parts:
            rows = pl.ds(start, count)
            total = own(rows).astype(jnp.float32) + land[rows].astype(jnp.float32)
            ref[pl.ds(place, count)] = total.astype(ref.dtype)
            place += count


def middle_kernel(
    pack,
    firsts,
    heads,
    patches,
    out_grad,
    small,
    w_out,
    w_out_far,
    w_up,
    w_up_far,
    w_down_half,
    w_down_got,
    w_down_far,
    mixed,
    hidden_grad,
    grad_heads,
    send_over_x,
    send_over_y,
    keep,
    vector,
    o_land,
    o_grad,
    wout,
    wup,
    wdown,
    act_grad,
    act_turned,
    pre_grad,
    bup_rows,
    grads,
    c_land,
    local,
    osend,
    orecv,
    gsend,
    grecv,
    wsem,
    csend,
    crecv,
):
    f32, bf16 = jnp.float32, jnp.bfloat16
    z, x, core, y = here()
    over_core = at(z, x, 1 - core, y)
    around = [at((z + d) % GROUPS, x, core, y) for d in range(1, GROUPS)]
    rows, width = patches.shape
    tiles = wdown.shape[0] // width
    half = w_down_half.shape[0]
    far = w_down_far.shape[0]
    greet(around + [over_core])
    go = Sender()
    near = half // 2 - far
    far_rows = pl.ds((1 - y) * half + core * (half // 2) + near, far)
    other_rows = pl.ds((1 - y) * half + (1 - core) * (half // 2) + near, far)
    for d in (2, 1, 3):
        go(heads.at[(z + d) % GROUPS], o_land.at[z], osend.at[d], orecv.at[d], around[d - 1])
    go(w_down_far, wdown.at[far_rows], wsem.at[0], wsem.at[1], over_core)
    down_copies = [
        pltpu.make_async_copy(w_down_half, wdown.at[pl.ds(y * half, half)], local.at[0]),
        pltpu.make_async_copy(w_down_far, wdown.at[far_rows], local.at[1]),
    ]
    for c in range(2):
        src = w_down_got.at[pl.ds(c * near, near)]
        dst = wdown.at[pl.ds((1 - y) * half + c * (half // 2), near)]
        down_copies.append(pltpu.make_async_copy(src, dst, local.at[8 + c]))
    copies = [
        pltpu.make_async_copy(heads.at[z], o_land.at[z], local.at[2]),
    ]
    pairs = [(w_out, wout, y), (w_out_far, wout, 1 - y), (w_up, wup, y), (w_up_far, wup, 1 - y)]
    for i, (src, dst, side) in enumerate(pairs):
        count = src.shape[0]
        span = pl.ds(side * count, count)
        copies.append(pltpu.make_async_copy(src, dst.at[span], local.at[4 + i]))

    for copy in down_copies + copies:
        copy.start()
    dy = out_grad[...]
    vector[...] = jnp.zeros(vector.shape, f32)
    pack.write(vector, "bdown", jnp.sum(dy.astype(f32), axis=0, keepdims=True))
    for f in range(tiles):
        bup_rows[f, 0:1] = pack.read(small, "bup", f * width, width)
    for copy in down_copies:
        copy.wait()
    landed = wdown.at[other_rows]
    remote(landed, landed, wsem.at[0], wsem.at[1], over_core).wait_recv()

    def tile(f):
        return pl.ds(pl.multiple_of(f * width, width), width)

    def first_grad(f, carry):
        act_grad[f] = dot_turned(dy, wdown[tile(f)])
        return carry

    lax.fori_loop(0, tiles, first_grad, 0)
    for copy in copies:
        copy.wait()
    for d in range(1, GROUPS):
        landed = o_land.at[(z + GROUPS - d) % GROUPS]
        remote(landed, landed, osend.at[d], orecv.at[d], over_core).wait_recv()
    turned = o_land[...].reshape(width, rows)
    hidden = patches[...].astype(f32) + (dot(turned.T, wout[...]) + pack.read(small, "bout"))
    gain2 = pack.read(small, "gain2")
    normed, scale = normalise(hidden)
    c = (normed * gain2 + pack.read(small, "bias2")).astype(bf16)
    mixed_acc = hidden + pack.read(small, "bdown")
    c_grad = jnp.zeros((rows, width), f32)

    def forward_back(f, carry):
        mixed_acc, c_grad = carry
        up = wup[:, tile(f)]
        pre = dot(c, up) + bup_rows[f, 0:1]
        share = 0.5 + 0.5 * lax.erf(pre * (0.5**0.5))
        slope = share + pre * jnp.exp(-0.5 * pre * pre) * ((0.5 / jnp.pi) ** 0.5)
        act = (pre * share).astype(bf16)
        grad = (act_grad[f] * slope).astype(bf16)
        act_turned[tile(f)] = act.T
        pre_grad[f] = grad
        bup_rows[f, 0:1] = jnp.sum(grad.astype(f32), axis=0, keepdims=True)
        return (
            mixed_acc + dot(act, wdown[tile(f)]),
            c_grad + dot_turned(grad, up),
        )

    mixed_acc, c_grad = lax.fori_loop(0, tiles, forward_back, (mixed_acc, c_grad))
    mixed[...] = mixed_acc.astype(bf16)
    for f in range(tiles):
        pack.write(vector, "bup", bup_rows[f, 0:1], f * width)
    part, gain_grad, bias_grad = normalise_back(c_grad, gain2, normed, scale)
    pack.write(vector, "gain2", gain_grad)
    pack.write(vector, "bias2", bias_grad)
    whole = dy.astype(f32) + part
    hidden_grad[...] = whole
    dz = whole.astype(bf16)
    pack.write(vector, "bout", jnp.sum(dz.astype(f32), axis=0, keepdims=True))
    o_grad[...] = dot_turned(wout[...], dz).astype(bf16).reshape(o_grad.shape)
    for d in (2, 1, 3):
        go(o_grad.at[(z + d) % GROUPS], grad_heads.at[z], gsend.at[d], grecv.at[d], around[d - 1])
    own = pltpu.make_async_copy(o_grad.at[z], grad_heads.at[z], local.at[3])
    own.start()

    columns = c_land.shape[2]
    count, ahead = grads.shape[0], send_over_x.shape[0]
    mine = pl.ds(pl.multiple_of(core * columns, columns), columns)
    others = pl.ds(pl.multiple_of((1 - core) * columns, columns), columns)

    def over(k):
        go(grads.at[k, :, others], c_land.at[k], csend.at[k], crecv.at[k], over_core)

    def settle(k):
        landed = c_land.at[k]
        remote(landed, landed, csend.at[k], crecv.at[k], over_core).wait_recv()
        sent = send_over_x.at[k] if k < ahead else send_over_y.at[k - ahead]
        core_sum(firsts[k], lambda r: grads[k, r, mine], c_land.at[k], sent, keep.at[k], x, y)

    c_turned = c.T
    piece = half // tiles
    for k in range(count):
        if k < tiles:
            for top in range(2):
                grads[k, top * piece : (top + 1) * piece] = dot(
                    act_turned[top * half + k * piece : top * half + (k + 1) * piece], dy
                ).astype(bf16)
        elif k < 2 * tiles:
            grads[k] = dot(c_turned, pre_grad[k - tiles]).astype(bf16)
        else:
            grads[k] = dot(turned, dz).astype(bf16)
        over(k)
        if k >= 2:
            settle(k - 2)
    settle(count - 2)
    settle(count - 1)
    for d in range(1, GROUPS):
        landed = grad_heads.at[(z + GROUPS - d) % GROUPS]
        remote(landed, landed, gsend.at[d], grecv.at[d], over_core).wait_recv()
    own.wait()
    go.finish()


def middle(pack, firsts, ahead, heads, patches, out_grad, small, *weights):
    rows, width = patches.shape
    hidden = weights[2].shape[1]
    tiles = hidden // width
    count = 2 * tiles + 1
    f32, bf16 = jnp.float32, jnp.bfloat16
    vmem = pl.BlockSpec(memory_space=pltpu.VMEM)
    hbm = pl.BlockSpec(memory_space=pltpu.HBM)
    dma = pltpu.SemaphoreType.DMA
    return pl.pallas_call(
        functools.partial(middle_kernel, pack, firsts),
        out_shape=[
            jax.ShapeDtypeStruct((rows, width), bf16),
            jax.ShapeDtypeStruct((rows, width), f32),
            jax.ShapeDtypeStruct(heads.shape, bf16),
            jax.ShapeDtypeStruct((ahead, width // 2, width // 2), bf16),
            jax.ShapeDtypeStruct((count - ahead, width // 2, width // 2), bf16),
            jax.ShapeDtypeStruct((count, width // 2, width // 2), bf16),
            jax.ShapeDtypeStruct((2, pack.rows, LANES), f32),
        ],
        in_specs=[hbm, vmem, vmem, vmem] + [hbm] * 7,
        out_specs=[vmem] * 7,
        scratch_shapes=[
            pltpu.VMEM(heads.shape, bf16),
            pltpu.VMEM(heads.shape, bf16),
            pltpu.VMEM((width, width), bf16),
            pltpu.VMEM((width, hidden), bf16),
            pltpu.VMEM((hidden, width), bf16),
            pltpu.VMEM((tiles, rows, width), f32),
            pltpu.VMEM((hidden, rows), bf16),
            pltpu.VMEM((tiles, rows, width), bf16),
            pltpu.VMEM((tiles, 8, width), f32),
            pltpu.VMEM((count, width, width), bf16),
            pltpu.VMEM((count, width, width // 2), bf16),
            dma((10,)),
            dma((GROUPS,)),
            dma((GROUPS,)),
            dma((GROUPS,)),
            dma((GROUPS,)),
            dma((2,)),
            dma((count,)),
            dma((count,)),
        ],
        compiler_params=params(60, 3),
        name="middle",
    )(heads, patches, out_grad, small, *weights)


class Totals:
    def __init__(self, refs, tiles):
        self.refs, self.tiles = refs, tiles

    def place(self, k, row, count, column, columns):
        width = self.refs[2].shape[1]
        start = 0
        if k < self.tiles:
            which, row = 0, k * (width // 2) + row
        elif k < 2 * self.tiles:
            which, start = 1, (k - self.tiles) * width
        elif k == 2 * self.tiles:
            which = 2
        else:
            which, start = 3, (k - 2 * self.tiles - 1) * width
        return which, pl.ds(row, count), pl.ds(pl.multiple_of(start + column, LANES), columns)

    def view(self, *place):
        which, rows, columns = self.place(*place)
        return self.refs[which].at[rows, columns]

    def store(self, values, *place):
        which, rows, columns = self.place(*place)
        ref = self.refs[which]
        ref[rows, columns] = values.astype(ref.dtype)


def last_kernel(
    pack,
    firsts,
    tiles,
    query_grad,
    key_grad,
    normed_low,
    w_qkv,
    w_qkv_far,
    patches,
    hidden_grad,
    small,
    ahead_x,
    ahead_y,
    keep,
    vector_in,
    inputs_grad,
    down_out,
    up_out,
    out_out,
    qkv_out,
    vector_out,
    down_total,
    up_total,
    out_total,
    qkv_total,
    got,
    near,
    both,
    far,
    own,
    wqkv,
    grads,
    c_land,
    late_send,
    first_land,
    half_sum,
    second_land,
    quarter_sum,
    z_land,
    eighth_sum,
    far_land,
    vectors,
    v_land,
    local,
    loads,
    n_send,
    n_recv,
    f_send,
    f_recv,
    q_send,
    q_recv,
    csend,
    crecv,
    asend,
    arecv,
    bsend,
    brecv,
    zsend,
    zrecv,
    wsend,
    wrecv,
    dsend,
    drecv,
    gsend,
    grecv,
    hsend,
    hrecv,
    isend,
    irecv,
    vsend,
    vrecv,
):
    f32, bf16 = jnp.float32, jnp.bfloat16
    z, x, core, y = here()
    pair, side = z // 2, z % 2
    over_x, over_core, over_y = (
        at(z, 1 - x, core, y),
        at(z, x, 1 - core, y),
        at(z, x, core, 1 - y),
    )
    around = [at((z + d) % GROUPS, x, core, y) for d in range(1, GROUPS)]
    over_near, over_far = at(z + 1 - 2 * side, x, core, y), around[1]
    peer = {"y": over_y, "x": over_x}
    greet(around + [over_x, over_core, over_y])
    go = Sender()
    totals = Totals((down_total, up_total, out_total, qkv_total), tiles)
    outs = Totals((down_out, up_out, out_out, qkv_out), tiles)
    part = query_grad.shape[1]
    rows, width = patches.shape
    chunks, early, late = len(firsts), keep.shape[0], c_land.shape[0]
    ahead = ahead_x.shape[0]
    half = c_land.shape[2]
    quarter, shard = width // 4, width // 16

    def landed(view, sem):
        remote(view, view, sem, sem, over_core).wait_recv()

    order = (2, 1, 3, 0)
    held = []
    for d in order:
        pz = (z + d) % GROUPS
        for k in range(2):
            px = (x + 1 + k) % 2
            slot = 2 * d + k
            src = key_grad.at[pz * PEERS + px * 2 + 1 - core]
            go(src, near.at[slot], n_send.at[slot], n_recv.at[slot], over_core)
            src = key_grad.at[pz * PEERS + px * 2 + core]
            copy = pltpu.make_async_copy(src, both.at[slot], local.at[4 + slot])
            copy.start()
            held.append((slot, copy))
    held = dict(held)
    for d in (2, 1, 3):
        pz = (z + d) % GROUPS
        go(query_grad.at[pz], got.at[z, pl.ds(0, part)], q_send.at[d], q_recv.at[d], around[d - 1])
    own_query = pltpu.make_async_copy(query_grad.at[z], got.at[z, pl.ds(0, part)], local.at[0])
    own_query.start()
    arrivals = []
    for k in range(early):
        src = ahead_x.at[k] if k < ahead else ahead_y.at[k - ahead]
        arrivals.append(
            (
                pltpu.make_async_copy(keep.at[k], half_sum.at[k], loads.at[2 * k]),
                pltpu.make_async_copy(src, first_land.at[k], loads.at[2 * k + 1]),
            )
        )
        for copy in arrivals[k]:
            copy.start()
    count = w_qkv.shape[0]
    weights = [
        pltpu.make_async_copy(w_qkv, wqkv.at[pl.ds(y * count, count)], local.at[2]),
        pltpu.make_async_copy(w_qkv_far, wqkv.at[pl.ds((1 - y) * count, count)], local.at[3]),
    ]
    for copy in weights:
        copy.start()

    def collect_near(step):
        d = order[step]
        for k in range(2):
            slot = 2 * d + k
            landed(near.at[slot], n_recv.at[slot])
            held[slot].wait()
            both[slot] = (both[slot].astype(f32) + near[slot].astype(f32)).astype(bf16)
            if k == 0:
                go(both.at[slot], far.at[d], f_send.at[d], f_recv.at[d], over_x)

    def collect_far(step):
        d = order[step]
        landed(far.at[d], f_recv.at[d])
        own[d] = (both[2 * d + 1].astype(f32) + far[d].astype(f32)).astype(bf16)
        place = got.at[z, pl.ds(part, 2 * part)]
        if d == 0:
            copy = pltpu.make_async_copy(own.at[0], place, local.at[1])
            copy.start()
            return copy
        sem = GROUPS + d
        go(own.at[d], place, q_send.at[sem], q_recv.at[sem], around[d - 1])
        return None

    def stage_core(k):
        i = k - early
        landed(c_land.at[i], crecv.at[i])
        mine = pl.ds(pl.multiple_of(core * half, half), half)
        core_sum(
            firsts[k],
            lambda r: grads[i, r, mine],
            c_land.at[i],
            late_send.at[i],
            half_sum.at[k],
            x,
            y,
        )
        go(late_send.at[i], first_land.at[k], asend.at[i], arecv.at[i], peer[firsts[k]])

    def stage_first(k):
        if k < early:
            for copy in arrivals[k]:
                copy.wait()
        else:
            landed(first_land.at[k], arecv.at[k - early])
        half_sum[k] = (half_sum[k].astype(f32) + first_land[k].astype(f32)).astype(bf16)
        place = x if firsts[k] == "y" else y
        other = half_sum.at[k, pl.ds((1 - place) * quarter, quarter)]
        second = over_x if firsts[k] == "y" else over_y
        go(other, second_land.at[k], bsend.at[k], brecv.at[k], second)

    def stage_second(k):
        landed(second_land.at[k], brecv.at[k])
        place = x if firsts[k] == "y" else y
        total = half_sum[k, pl.ds(place * quarter, quarter)].astype(f32)
        quarter_sum[k] = (total + second_land[k].astype(f32)).astype(bf16)
        other = quarter_sum.at[k, pl.ds((1 - side) * 2 * shard, 2 * shard)]
        go(other, z_land.at[k], zsend.at[k], zrecv.at[k], over_near)

    def stage_near(k):
        landed(z_land.at[k], zrecv.at[k])
        total = quarter_sum[k, pl.ds(side * 2 * shard, 2 * shard)].astype(f32)
        eighth_sum[k] = (total + z_land[k].astype(f32)).astype(bf16)
        other = eighth_sum.at[k, pl.ds((1 - pair) * shard, shard)]
        go(other, far_land.at[k], wsend.at[k], wrecv.at[k], over_far)

    def spot(k, px, pside, ppair, count):
        row = px * quarter + pside * 2 * shard + ppair * shard
        return totals.view(k, row, count, core * half, half)

    def stage_far(k):
        landed(far_land.at[k], wrecv.at[k])
        total = eighth_sum[k, pl.ds(pair * shard, shard)].astype(f32) + far_land[k].astype(f32)
        row = x * quarter + side * 2 * shard + pair * shard
        totals.store(total, k, row, shard, core * half, half)
        view = spot(k, x, side, pair, shard)
        go(view, view, dsend.at[k], drecv.at[k], over_far)

    def stage_back(k):
        landed(spot(k, x, side, 1 - pair, shard), drecv.at[k])
        view = spot(k, x, side, 0, 2 * shard)
        go(view, view, gsend.at[k], grecv.at[k], over_near)

    def stage_out(k):
        landed(spot(k, x, 1 - side, 0, 2 * shard), grecv.at[k])
        view = spot(k, x, 0, 0, quarter)
        go(view, view, hsend.at[k], hrecv.at[k], over_x)
        go(view, view, isend.at[2 * k], irecv.at[2 * k], over_core)

    def stage_last(k):
        view = spot(k, 1 - x, 0, 0, quarter)
        landed(view, hrecv.at[k])
        go(view, view, isend.at[2 * k + 1], irecv.at[2 * k + 1], over_core)

    written = []

    def stage_write(k):
        for px in range(2):
            place = (x + px) % 2
            view = totals.view(k, place * quarter, quarter, (1 - core) * half, half)
            landed(view, irecv.at[2 * k + px])
        place = (k, 0, 2 * quarter, 0, 2 * half)
        copy = pltpu.make_async_copy(totals.view(*place), outs.view(*place), loads.at[2 * early + k])
        copy.start()
        written.append(copy)

    stages = (
        stage_first,
        stage_second,
        stage_near,
        stage_far,
        stage_back,
        stage_out,
        stage_last,
        stage_write,
    )

    def vector_step(n):
        if n == 0:
            landed(v_land.at[0], vrecv.at[0])
            vectors[1] = vectors[0] + v_land[0]
            go(vectors.at[1], v_land.at[1], vsend.at[1], vrecv.at[1], over_x)
        elif n == 1:
            landed(v_land.at[1], vrecv.at[1])
            vectors[2] = vectors[1] + v_land[1]
            go(vectors.at[2], v_land.at[2], vsend.at[2], vrecv.at[2], over_y)
        elif n == 2:
            landed(v_land.at[2], vrecv.at[2])
            vectors[3] = vectors[2] + v_land[2]
            for d in range(1, GROUPS):
                sem = 2 + d
                go(vectors.at[3], v_land.at[sem], vsend.at[sem], vrecv.at[sem], around[d - 1])
        elif n == 3:
            total = vectors[3]
            for d in range(1, GROUPS):
                landed(v_land.at[2 + d], vrecv.at[2 + d])
                total += v_land[2 + d]
            v_land[0] = total
            vector_out[...] = v_land[0, y]

    entry = list(range(early)) + [LATE_TURN + i for i in range(late)]
    turns = iter(range(entry[-1] + len(stages)))

    def turn():
        step = next(turns, None)
        if step is None:
            return False
        for depth, stage in enumerate(stages):
            for k in range(chunks):
                if step - depth == entry[k]:
                    stage(k)
        return True

    collect_near(0)
    turn()
    for step in range(1, GROUPS):
        collect_near(step)
        collect_far(step - 1)
        turn()
    own_keys = collect_far(GROUPS - 1)
    turn()
    normed_turned = normed_low[...].T
    normed, scale = normalise(patches[...].astype(f32))
    gain1 = pack.read(small, "gain1")
    turn()
    for d in range(1, GROUPS):
        landed(got.at[(z + GROUPS - d) % GROUPS, pl.ds(0, part)], q_recv.at[d])
    own_query.wait()
    turn()
    others = pl.ds(pl.multiple_of((1 - core) * half, half), half)

    def project(i):
        turned = got[:, i * part : (i + 1) * part].reshape(width, rows)
        grads[i] = dot_turned(normed_turned, turned).astype(bf16)
        go(grads.at[i, :, others], c_land.at[i], csend.at[i], crecv.at[i], over_core)

    project(0)
    for d in range(1, GROUPS):
        landed(got.at[(z + GROUPS - d) % GROUPS, pl.ds(part, 2 * part)], q_recv.at[GROUPS + d])
    own_keys.wait()
    for i in range(1, late):
        project(i)
    turn()
    for copy in weights:
        copy.wait()
    vectors[0] = vector_in[...]
    ones = jnp.ones((8, rows), bf16)
    normed_grad = jnp.zeros((width, rows), f32)
    for i in range(late):
        turned = got[:, i * part : (i + 1) * part].reshape(width, rows)
        if i != 1:
            sums = dot_turned(ones, turned)[0:1]
            pack.write(vectors.at[0], "bqv", sums, (i // 2) * width)
        normed_grad += dot(wqkv[:, i * width : (i + 1) * width], turned)
        stage_core(early + i)
    turn()
    change, gain_grad, bias_grad = normalise_back(normed_grad.T, gain1, normed, scale)
    inputs_grad[...] = hidden_grad[...] + change
    pack.write(vectors.at[0], "gain1", gain_grad)
    pack.write(vectors.at[0], "bias1", bias_grad)
    go(vectors.at[0], v_land.at[0], vsend.at[0], vrecv.at[0], over_core)
    step = 0
    while turn():
        vector_step(step)
        step += 1
    for copy in written:
        copy.wait()
    go.finish()


LATE_TURN = 9


def last(
    pack, firsts, query_grad, key_grad, normed_low, w_qkv, w_qkv_far, patches, hidden_grad, small,
    ahead_x, ahead_y, keep, vector
):
    f32, bf16 = jnp.float32, jnp.bfloat16
    vmem = pl.BlockSpec(memory_space=pltpu.VMEM)
    hbm = pl.BlockSpec(memory_space=pltpu.HBM)
    groups, part, rows = query_grad.shape
    width = patches.shape[1]
    early, half = keep.shape[0], width // 2
    tiles, chunks, late = (early - 1) // 2, len(firsts), len(firsts) - early
    piece = (2 * part, rows)
    dma = pltpu.SemaphoreType.DMA
    totals = [
        (tiles * half, width),
        (half, tiles * width),
        (half, width),
        (half, late * width),
    ]

    def pair(n):
        return [dma((n,))] * 2

    return pl.pallas_call(
        functools.partial(last_kernel, pack, firsts, tiles),
        out_shape=[jax.ShapeDtypeStruct((rows, width), f32)]
        + [jax.ShapeDtypeStruct(shape, bf16) for shape in totals]
        + [jax.ShapeDtypeStruct(vector.shape[1:], f32)],
        in_specs=[hbm, hbm, vmem, hbm, hbm, vmem, vmem, vmem, hbm, hbm, hbm, vmem],
        out_specs=[vmem] + [hbm] * 4 + [vmem],
        scratch_shapes=[pltpu.VMEM(shape, bf16) for shape in totals]
        + [
            pltpu.VMEM((groups, 3 * part, rows), bf16),
            pltpu.VMEM((2 * groups,) + piece, bf16),
            pltpu.VMEM((2 * groups,) + piece, bf16),
            pltpu.VMEM((groups,) + piece, bf16),
            pltpu.VMEM((groups,) + piece, bf16),
            pltpu.VMEM((width, late * width), bf16),
            pltpu.VMEM((late, width, width), bf16),
            pltpu.VMEM((late, width, half), bf16),
            pltpu.VMEM((late, half, half), bf16),
            pltpu.VMEM((chunks, half, half), bf16),
            pltpu.VMEM((chunks, half, half), bf16),
            pltpu.VMEM((chunks, half // 2, half), bf16),
            pltpu.VMEM((chunks, half // 2, half), bf16),
            pltpu.VMEM((chunks, half // 4, half), bf16),
            pltpu.VMEM((chunks, half // 4, half), bf16),
            pltpu.VMEM((chunks, half // 8, half), bf16),
            pltpu.VMEM((4,) + vector.shape, f32),
            pltpu.VMEM((6,) + vector.shape, f32),
            dma((4 + 2 * groups,)),
            dma((2 * early + chunks,)),
        ]
        + pair(2 * groups)
        + pair(groups)
        + pair(2 * groups)
        + pair(late) * 2
        + pair(chunks) * 6
        + pair(2 * chunks)
        + pair(6),
        compiler_params=params(60, 4),
        name="last",
    )(
        query_grad, key_grad, normed_low, w_qkv, w_qkv_far, patches, hidden_grad, small,
        ahead_x, ahead_y, keep, vector,
    )


class Documents:
    def __init__(self, lengths, rows):
        self.rows, self.count = rows, lengths.shape[1]
        self.starts, self.ends, place = [], [], 0
        for d in range(self.count):
            self.starts.append(place)
            place = place + lengths[0, d]
            self.ends.append(place)

    def span(self, block):
        first, last = block * self.rows, (block + 1) * self.rows - 1
        low, high = 0, 0
        for d in range(self.count):
            low = jnp.where(self.starts[d] <= first, self.starts[d], low)
        for d in reversed(range(self.count)):
            high = jnp.where(self.ends[d] > last, self.ends[d], high)
        return low // self.rows, (high + self.rows - 1) // self.rows

    def inside(self, block, yes, no):
        shape = (8, self.rows)
        row = lax.broadcasted_iota(jnp.int32, shape, 0)
        place = block * self.rows + lax.broadcasted_iota(jnp.int32, shape, 1)
        found = jnp.where(row < self.count, no, 0.0)
        for d in range(self.count):
            hit = (row == d) & (place >= self.starts[d]) & (place < self.ends[d])
            found = jnp.where(hit, yes, found)
        return found

    def marks(self, block):
        ones, rest = jnp.ones((8, self.rows)), jnp.zeros((HD - 16, self.rows))
        return jnp.concatenate([self.inside(block, 1.0, 0.0), ones, rest]).astype(jnp.bfloat16)

    def veto(self, block):
        rest = jnp.zeros((HD - 8, self.rows))
        return jnp.concatenate([self.inside(block, 0.0, masked_score), rest])


def attend_kernel(
    lengths, place, query, keys, out, out_low, sums, key_rows, query_aug, acc, stat
):
    blocks, rows = keys.shape[0], keys.shape[2]
    width = query.shape[1]
    groups = query.shape[0]
    documents = Documents(lengths, rows)

    def turn(j, carry):
        mark = documents.marks(j)
        for h in range(PER_GROUP):
            both = jnp.concatenate([keys[j, h * HD : (h + 1) * HD], mark], axis=0)
            key_rows[h, j] = both.T
        return carry

    lax.fori_loop(0, blocks, turn, 0)
    for i in range(groups):
        block = i * PEERS + place[0]
        veto = documents.veto(block).astype(jnp.bfloat16)
        for h in range(PER_GROUP):
            query_aug[h, :HD] = query[i, h * HD : (h + 1) * HD] * jnp.bfloat16(0.125)
            query_aug[h, HD:] = veto
        stat[0] = jnp.full(stat.shape[1:], masked_score, jnp.float32)
        stat[1] = jnp.zeros(stat.shape[1:], jnp.float32)
        acc[...] = jnp.zeros(acc.shape, jnp.float32)

        low, high = documents.span(block)
        steps = (high - low + 1) // 2
        low = jnp.minimum(low, blocks - 2 * steps)

        def step(n, carry):
            j = low + 2 * n
            made = [
                [dot(key_rows[h, j + k], query_aug[h]) for k in range(2)] for h in range(PER_GROUP)
            ]
            for h in range(PER_GROUP):
                first, second = made[h]
                old = stat[0, h : h + 1]
                most = jnp.max(jnp.maximum(first, second), axis=0, keepdims=True)
                new = jnp.maximum(old, most)
                first, second = jnp.exp(first - new), jnp.exp(second - new)
                factor = jnp.exp(old - new)
                stat[0, h : h + 1] = new
                stat[1, h : h + 1] = stat[1, h : h + 1] * factor + jnp.sum(
                    first + second, axis=0, keepdims=True
                )
                span = slice(width + h * HD, width + (h + 1) * HD)
                shared = dot(keys[j, span], first.astype(jnp.bfloat16))
                shared += dot(keys[j + 1, span], second.astype(jnp.bfloat16))
                acc[h] = acc[h] * factor + shared
            return carry

        lax.fori_loop(0, steps, step, 0)
        for h in range(PER_GROUP):
            total = stat[1, h : h + 1]
            shared = acc[h] / total
            out[i, h * HD : (h + 1) * HD] = shared
            out_low[i, h * HD : (h + 1) * HD] = shared.astype(jnp.bfloat16)
            sums[i, h : h + 1] = stat[0, h : h + 1] + jnp.log(total)


def attend(lengths, place, query, keys):
    groups, width, rows = query.shape
    blocks = keys.shape[0]
    vmem = pl.BlockSpec(memory_space=pltpu.VMEM)
    return pl.pallas_call(
        attend_kernel,
        out_shape=[
            jax.ShapeDtypeStruct(query.shape, jnp.float32),
            jax.ShapeDtypeStruct(query.shape, jnp.bfloat16),
            jax.ShapeDtypeStruct((groups, 8, rows), jnp.float32),
        ],
        in_specs=[pl.BlockSpec(memory_space=pltpu.SMEM)] * 2 + [vmem] * 2,
        out_specs=[vmem] * 3,
        scratch_shapes=[
            pltpu.VMEM((PER_GROUP, blocks, rows, 2 * HD), jnp.bfloat16),
            pltpu.VMEM((PER_GROUP, 2 * HD, rows), jnp.bfloat16),
            pltpu.VMEM((PER_GROUP, HD, rows), jnp.float32),
            pltpu.VMEM((2, 8, rows), jnp.float32),
        ],
        compiler_params=params(60),
        name="attend",
    )(lengths, place, query, keys)


def three_parts(values):
    high = values.astype(jnp.bfloat16)
    rest = values - high.astype(jnp.float32)
    middle = rest.astype(jnp.bfloat16)
    low = (rest - middle.astype(jnp.float32)).astype(jnp.bfloat16)
    return high, middle, low


def attend_back_kernel(
    lengths,
    place,
    query,
    keys,
    out,
    sums,
    out_grad,
    query_grad,
    key_grad,
    key_rows,
    value_rows,
    query_aug,
    grad_aug,
    query_rows,
    grad_rows,
    query_acc,
    key_acc,
):
    blocks, rows = keys.shape[0], keys.shape[2]
    width = query.shape[1]
    groups = query.shape[0]
    bf16 = jnp.bfloat16
    documents = Documents(lengths, rows)

    def turn(j, carry):
        mark = documents.marks(j)
        for h in range(PER_GROUP):
            both = jnp.concatenate([keys[j, h * HD : (h + 1) * HD], mark], axis=0)
            key_rows[h, pl.ds(pl.multiple_of(j * rows, rows), rows)] = both.T
            values = keys[j, width + h * HD : width + (h + 1) * HD]
            place = pl.ds(pl.multiple_of(j * rows, rows), rows)
            value_rows[h, place] = jnp.concatenate([values, mark], axis=0).T
            key_acc[h, place] = jnp.zeros((rows, 2 * HD), jnp.float32)
        return carry

    lax.fori_loop(0, blocks, turn, 0)
    index = lax.broadcasted_iota(jnp.int32, (HD, rows), 0)
    none = jnp.zeros((HD, rows), bf16)

    def spread(values):
        high, middle, low = three_parts(-values)
        wide = jnp.where(index == 8, high.astype(jnp.float32), 0.0)
        wide = jnp.where(index == 9, middle.astype(jnp.float32), wide)
        return jnp.where(index == 10, low.astype(jnp.float32), wide)

    for i in range(groups):
        block = i * PEERS + place[0]
        veto = documents.veto(block)
        for h in range(PER_GROUP):
            span = slice(h * HD, (h + 1) * HD)
            part = query[i, span] * bf16(0.125)
            grad = out_grad[i, span]
            delta = jnp.sum(grad.astype(jnp.float32) * out[i, span], axis=0, keepdims=True)
            query_aug[h, :HD] = part
            query_aug[h, HD:] = (veto + spread(sums[i, h : h + 1])).astype(bf16)
            grad_aug[h, :HD] = grad
            grad_aug[h, HD:] = spread(delta).astype(bf16)
            query_rows[h] = jnp.concatenate([part, none], axis=0).T
            grad_rows[h] = jnp.concatenate([none, grad], axis=0).T
        query_acc[...] = jnp.zeros(query_acc.shape, jnp.float32)

        low, high = documents.span(block)
        steps = (high - low + 1) // 2
        low = jnp.minimum(low, blocks - 2 * steps)

        def step(n, carry):
            j = low + 2 * n
            span = pl.ds(pl.multiple_of(j * rows, rows), 2 * rows)
            for h in range(PER_GROUP):
                probs = jnp.exp(dot(key_rows[h, span], query_aug[h]))
                change = (probs * dot(value_rows[h, span], grad_aug[h])).astype(bf16)
                low_probs = probs.astype(bf16)
                key_acc[h, span] += dot(low_probs, grad_rows[h]) + dot(change, query_rows[h])
                turned = slice(h * HD, (h + 1) * HD)
                query_acc[h] += dot(keys[j, turned], change[:rows]) + dot(
                    keys[j + 1, turned], change[rows:]
                )
            return carry

        lax.fori_loop(0, steps, step, 0)
        for h in range(PER_GROUP):
            query_grad[i, h * HD : (h + 1) * HD] = (query_acc[h] * 0.125).astype(bf16)

    def finish(j, carry):
        for h in range(PER_GROUP):
            both = key_acc[h, pl.ds(pl.multiple_of(j * rows, rows), rows)].astype(bf16).T
            key_grad[j, h * HD : (h + 1) * HD] = both[:HD]
            key_grad[j, width + h * HD : width + (h + 1) * HD] = both[HD:]
        return carry

    lax.fori_loop(0, blocks, finish, 0)


def attend_back(lengths, place, query, keys, out, sums, out_grad):
    groups, width, rows = query.shape
    blocks = keys.shape[0]
    vmem = pl.BlockSpec(memory_space=pltpu.VMEM)
    bf16 = jnp.bfloat16
    return pl.pallas_call(
        attend_back_kernel,
        out_shape=[
            jax.ShapeDtypeStruct(query.shape, bf16),
            jax.ShapeDtypeStruct(keys.shape, bf16),
        ],
        in_specs=[pl.BlockSpec(memory_space=pltpu.SMEM)] * 2 + [vmem] * 5,
        out_specs=[vmem] * 2,
        scratch_shapes=[
            pltpu.VMEM((PER_GROUP, blocks * rows, 2 * HD), bf16),
            pltpu.VMEM((PER_GROUP, blocks * rows, 2 * HD), bf16),
            pltpu.VMEM((PER_GROUP, 2 * HD, rows), bf16),
            pltpu.VMEM((PER_GROUP, 2 * HD, rows), bf16),
            pltpu.VMEM((PER_GROUP, rows, 2 * HD), bf16),
            pltpu.VMEM((PER_GROUP, rows, 2 * HD), bf16),
            pltpu.VMEM((PER_GROUP, HD, rows), jnp.float32),
            pltpu.VMEM((PER_GROUP, blocks * rows, 2 * HD), jnp.float32),
        ],
        compiler_params=params(60),
        name="attend_back",
    )(lengths, place, query, keys, out, sums, out_grad)


def layer_norm(values, gain, offset):
    centre = jnp.mean(values, axis=-1, keepdims=True)
    shifted = values - centre
    spread = jnp.mean(shifted * shifted, axis=-1, keepdims=True)
    return shifted * lax.rsqrt(spread + epsilon) * gain + offset


def exact_gelu(values):
    return jax.nn.gelu(values, approximate=False)


def doc_index(positions, doc_starts):
    hits = (doc_starts[None, :] <= positions[:, None]).astype(jnp.int32)
    return jnp.sum(hits, axis=1) - 1


def body(
    patches,
    doc_lengths,
    norm1_gain,
    norm1_bias,
    w_qkv,
    b_qv,
    w_out,
    b_out,
    norm2_gain,
    norm2_bias,
    w_up,
    b_up,
    w_down,
    b_down,
    cotangent,
):
    f32, bf16 = jnp.float32, jnp.bfloat16
    rows, width = patches.shape[1:]
    ctx_place = lax.axis_index("ctx")
    blocks = lax.axis_size("ctx")
    place = (ctx_place % PEERS).astype(jnp.int32).reshape(1)
    vectors = [norm1_gain, norm1_bias, b_qv, b_out, norm2_gain, norm2_bias, b_up, b_down]
    pack = Packed([v.shape[0] for v in vectors])
    query, keys, normed1, small, qkv_far, out_far, up_far, down_got, down_part = front(
        pack, patches[0], pack.pack(vectors), w_qkv, w_out, w_up, w_down
    )
    down_far = lax.ppermute(down_part, "wsh", [(0, 1), (1, 0)])
    out_heads, heads_low, sums = attend(doc_lengths, place, query, keys)
    tiles = w_up.shape[1] // width
    chunks = 2 * tiles + 1 + w_qkv.shape[1] // width
    ahead = tiles + 1
    firsts = ["x"] * ahead + ["y"] * (chunks - ahead)
    mixed, hidden_grad, grad_heads, send_over_x, send_over_y, keep, vector = middle(
        pack, firsts, ahead, heads_low, patches[0], cotangent[0], small, w_out, out_far, w_up,
        up_far, w_down, down_got, down_far,
    )
    across = [(c, c + 2 - c // 2 % 2 * 4) for c in range(blocks)]
    ahead_x = lax.ppermute(send_over_x, "ctx", across)
    ahead_y = lax.ppermute(send_over_y, "wsh", [(0, 1), (1, 0)])
    query_grad, key_grad = attend_back(
        doc_lengths, place, query, keys, out_heads, sums, grad_heads
    )
    inputs_grad, down_total, up_total, out_total, qkv_total, vector_total = last(
        pack, firsts, query_grad, key_grad, normed1, w_qkv, qkv_far, patches[0], hidden_grad, small,
        ahead_x, ahead_y, keep, vector,
    )
    shares = pack.unpack(vector_total)
    return (
        mixed[None],
        inputs_grad[None],
        shares[0],
        shares[1],
        qkv_total.astype(f32),
        shares[2],
        out_total.astype(f32),
        shares[3],
        shares[4],
        shares[5],
        up_total.astype(f32),
        shares[6],
        down_total.astype(f32),
        shares[7],
    )


def shifted_2(block, axis, distance):
    devices = range(lax.axis_size(axis))
    route = [((i - distance) % len(devices), i) for i in devices]
    return lax.ppermute(block, axis, route)


def any_mesh_body(
    patches,
    doc_lengths,
    norm1_gain,
    norm1_bias,
    w_qkv,
    b_qv,
    w_out,
    b_out,
    norm2_gain,
    norm2_bias,
    w_up,
    b_up,
    w_down,
    b_down,
    cotangent,
):
    tok_rows = patches.shape[1]
    model_width = patches.shape[2]
    ctx_size = lax.axis_size("ctx")
    ctx_place = lax.axis_index("ctx")
    gathered = (
        lax.all_gather(norm1_gain, "wsh", axis=0, tiled=True),
        lax.all_gather(norm1_bias, "wsh", axis=0, tiled=True),
        lax.all_gather(w_qkv, "wsh", axis=0, tiled=True),
        lax.all_gather(b_qv, "wsh", axis=0, tiled=True),
        lax.all_gather(w_out, "wsh", axis=0, tiled=True),
        lax.all_gather(b_out, "wsh", axis=0, tiled=True),
        lax.all_gather(norm2_gain, "wsh", axis=0, tiled=True),
        lax.all_gather(norm2_bias, "wsh", axis=0, tiled=True),
        lax.all_gather(w_up, "wsh", axis=0, tiled=True),
        lax.all_gather(b_up, "wsh", axis=0, tiled=True),
        lax.all_gather(w_down, "wsh", axis=0, tiled=True),
        lax.all_gather(b_down, "wsh", axis=0, tiled=True),
    )
    (
        gain1,
        bias1,
        wqkv_full,
        bqv_full,
        wout_full,
        bout_full,
        gain2,
        bias2,
        wup_full,
        bup_full,
        wdown_full,
        bdown_full,
    ) = gathered
    inputs = patches[0].astype(jnp.float32)
    lengths = doc_lengths[0]
    doc_starts = jnp.cumsum(lengths) - lengths
    row_offsets = lax.iota(jnp.int32, tok_rows)
    query_docs = doc_index(ctx_place * tok_rows + row_offsets, doc_starts)
    gain1_float = gain1.astype(jnp.float32)
    bias1_float = bias1.astype(jnp.float32)
    normed1 = layer_norm(inputs, gain1_float, bias1_float).astype(jnp.bfloat16)
    projected = jnp.dot(normed1, wqkv_full, preferred_element_type=jnp.float32)
    bqv_float = bqv_full.astype(jnp.float32)
    query_low = (projected[:, :model_width] + bqv_float[:model_width]).astype(jnp.bfloat16)
    key_low = projected[:, model_width : 2 * model_width].astype(jnp.bfloat16)
    value_low = (projected[:, 2 * model_width :] + bqv_float[model_width:]).astype(jnp.bfloat16)
    query_heads = query_low.reshape(tok_rows, H, HD)

    def attend_block(state, key_block, value_block, key_start):
        run_max, run_total, run_acc = state
        key_docs = doc_index(key_start + row_offsets, doc_starts)
        same_doc = (query_docs[:, None] == key_docs[None, :])[None]
        scores = (
            jnp.einsum(
                "qhd,khd->hqk",
                query_heads,
                key_block.reshape(tok_rows, H, HD),
                preferred_element_type=jnp.float32,
            )
            * 0.125
        )
        scores = jnp.where(same_doc, scores, masked_score)
        new_max = jnp.maximum(run_max, jnp.max(scores, axis=2))
        weights = jnp.where(same_doc, jnp.exp(scores - new_max[:, :, None]), 0.0)
        factor = jnp.exp(run_max - new_max)
        new_total = run_total * factor + jnp.sum(weights, axis=2)
        new_acc = run_acc * factor[:, :, None] + jnp.einsum(
            "hqk,khd->hqd",
            weights.astype(jnp.bfloat16),
            value_block.reshape(tok_rows, H, HD),
            preferred_element_type=jnp.float32,
        )
        return (new_max, new_total, new_acc)

    initial = (
        jnp.full((H, tok_rows), masked_score, jnp.float32),
        jnp.zeros((H, tok_rows), jnp.float32),
        jnp.zeros((H, tok_rows, HD), jnp.float32),
    )
    state = initial
    key_piece = lax.all_gather(key_low, "ctx", axis=0, tiled=True)
    value_piece = lax.all_gather(value_low, "ctx", axis=0, tiled=True)
    blocks = key_piece.shape[0] // tok_rows
    key_blocks = key_piece.reshape(blocks, tok_rows, model_width)
    value_blocks = value_piece.reshape(blocks, tok_rows, model_width)
    block_starts = tok_rows * lax.iota(jnp.int32, blocks)

    def one_block(inner, item):
        key_block, value_block, key_start = item
        return (attend_block(inner, key_block, value_block, key_start), None)

    state, unused = lax.scan(one_block, state, (key_blocks, value_blocks, block_starts))
    run_max, run_total, run_acc = state
    log_total = run_max + jnp.log(run_total)
    attended = jnp.transpose(run_acc / run_total[:, :, None], (1, 0, 2)).reshape(
        tok_rows, model_width
    )
    attended_low = attended.astype(jnp.bfloat16)
    branch = jnp.dot(
        attended_low, wout_full, preferred_element_type=jnp.float32
    ) + bout_full.astype(jnp.float32)
    hidden_sum = inputs + branch
    gain2_float = gain2.astype(jnp.float32)
    bias2_float = bias2.astype(jnp.float32)
    normed2 = layer_norm(hidden_sum, gain2_float, bias2_float).astype(jnp.bfloat16)
    pre_act = jnp.dot(normed2, wup_full, preferred_element_type=jnp.float32) + bup_full.astype(
        jnp.float32
    )
    activated = exact_gelu(pre_act).astype(jnp.bfloat16)
    mixed = (
        hidden_sum
        + jnp.dot(activated, wdown_full, preferred_element_type=jnp.float32)
        + bdown_full.astype(jnp.float32)
    )
    back_gain1 = gathered[0].astype(jnp.float32)
    back_bias1 = gathered[1].astype(jnp.float32)
    back_wqkv = gathered[2]
    back_wout = gathered[4]
    back_gain2 = gathered[6].astype(jnp.float32)
    back_bias2 = gathered[7].astype(jnp.float32)
    back_wup = gathered[8]
    back_wdown = gathered[10]
    out_grad = cotangent[0]
    wdown_grad = jnp.einsum("tf,td->fd", activated, out_grad, preferred_element_type=jnp.float32)
    bdown_grad = jnp.sum(out_grad.astype(jnp.float32), axis=0)
    act_grad = jnp.einsum("td,fd->tf", out_grad, back_wdown, preferred_element_type=jnp.float32)
    unused_act, gelu_back = jax.vjp(exact_gelu, pre_act)
    pre_grad = gelu_back(act_grad)[0].astype(jnp.bfloat16)
    wup_grad = jnp.einsum("tc,tf->cf", normed2, pre_grad, preferred_element_type=jnp.float32)
    bup_grad = jnp.sum(pre_grad.astype(jnp.float32), axis=0)
    normed2_grad = jnp.einsum("tf,cf->tc", pre_grad, back_wup, preferred_element_type=jnp.float32)
    unused_norm2, norm2_back = jax.vjp(layer_norm, hidden_sum, back_gain2, back_bias2)
    hidden_part, gain2_grad, bias2_grad = norm2_back(normed2_grad)
    hidden_grad = out_grad.astype(jnp.float32) + hidden_part
    branch_grad = hidden_grad.astype(jnp.bfloat16)
    wout_grad = jnp.einsum(
        "tc,td->cd", attended_low, branch_grad, preferred_element_type=jnp.float32
    )
    bout_grad = jnp.sum(branch_grad.astype(jnp.float32), axis=0)
    attended_grad = jnp.einsum(
        "td,cd->tc", branch_grad, back_wout, preferred_element_type=jnp.float32
    ).astype(jnp.bfloat16)
    delta = jnp.sum(
        (attended_grad.astype(jnp.float32) * attended).reshape(tok_rows, H, HD), axis=2
    ).T
    grad_heads = attended_grad.reshape(tok_rows, H, HD)

    def back_block(state, anchor):
        key_start = anchor * tok_rows
        key_cur, value_cur, key_grad, value_grad, query_grad = state
        key_docs = doc_index(key_start + row_offsets, doc_starts)
        same_doc = (query_docs[:, None] == key_docs[None, :])[None]
        key_heads = key_cur.reshape(tok_rows, H, HD)
        scores = (
            jnp.einsum("qhd,khd->hqk", query_heads, key_heads, preferred_element_type=jnp.float32)
            * 0.125
        )
        probs = jnp.where(same_doc, jnp.exp(scores - log_total[:, :, None]), 0.0)
        value_grad = value_grad + jnp.einsum(
            "hqk,qhd->khd",
            probs.astype(jnp.bfloat16),
            grad_heads,
            preferred_element_type=jnp.float32,
        ).reshape(tok_rows, model_width)
        prob_grad = jnp.einsum(
            "qhd,khd->hqk",
            grad_heads,
            value_cur.reshape(tok_rows, H, HD),
            preferred_element_type=jnp.float32,
        )
        score_grad = (probs * (prob_grad - delta[:, :, None])).astype(jnp.bfloat16)
        query_grad = (
            query_grad
            + jnp.einsum(
                "hqk,khd->qhd", score_grad, key_heads, preferred_element_type=jnp.float32
            ).reshape(tok_rows, model_width)
            * 0.125
        )
        key_grad = (
            key_grad
            + jnp.einsum(
                "hqk,qhd->khd", score_grad, query_heads, preferred_element_type=jnp.float32
            ).reshape(tok_rows, model_width)
            * 0.125
        )
        return (key_cur, value_cur, key_grad, value_grad, query_grad)

    def pass_on(state):
        key_cur, value_cur, key_grad, value_grad, query_grad = state
        moved_keys = shifted_2((key_cur, value_cur), "ctx", 1)
        moved_sums = (
            shifted_2(key_grad.astype(jnp.bfloat16), "ctx", 1).astype(key_grad.dtype),
            shifted_2(value_grad.astype(jnp.bfloat16), "ctx", 1).astype(value_grad.dtype),
        )
        return (moved_keys[0], moved_keys[1], moved_sums[0], moved_sums[1], query_grad)

    def two_steps(turn, state):
        state = pass_on(back_block(state, (ctx_place - 2 * turn) % ctx_size))
        state = pass_on(back_block(state, (ctx_place - 2 * turn - 1) % ctx_size))
        return state

    zero_rows = jnp.zeros((tok_rows, model_width), jnp.float32)
    final_state = lax.fori_loop(
        0, ctx_size // 2, two_steps, (key_low, value_low, zero_rows, zero_rows, zero_rows)
    )
    key_grad_low = final_state[2].astype(jnp.bfloat16)
    value_grad_low = final_state[3].astype(jnp.bfloat16)
    query_grad_low = final_state[4].astype(jnp.bfloat16)
    projected_grad = jnp.concatenate([query_grad_low, key_grad_low, value_grad_low], axis=1)
    wqkv_grad = jnp.einsum("tc,te->ce", normed1, projected_grad, preferred_element_type=jnp.float32)
    bqv_grad = jnp.concatenate(
        [
            jnp.sum(query_grad_low.astype(jnp.float32), axis=0),
            jnp.sum(value_grad_low.astype(jnp.float32), axis=0),
        ]
    )
    normed1_grad = jnp.einsum(
        "te,ce->tc", projected_grad, back_wqkv, preferred_element_type=jnp.float32
    )
    unused_norm1, norm1_back = jax.vjp(layer_norm, inputs, back_gain1, back_bias1)
    input_part, gain1_grad, bias1_grad = norm1_back(normed1_grad)
    inputs_grad = hidden_grad + input_part
    shares = (
        lax.psum_scatter(
            gain1_grad.astype(jnp.bfloat16), "wsh", scatter_dimension=0, tiled=True
        ).astype(jnp.float32),
        lax.psum_scatter(
            bias1_grad.astype(jnp.bfloat16), "wsh", scatter_dimension=0, tiled=True
        ).astype(jnp.float32),
        lax.psum_scatter(
            wqkv_grad.astype(jnp.bfloat16), "wsh", scatter_dimension=0, tiled=True
        ).astype(jnp.float32),
        lax.psum_scatter(
            bqv_grad.astype(jnp.bfloat16), "wsh", scatter_dimension=0, tiled=True
        ).astype(jnp.float32),
        lax.psum_scatter(
            wout_grad.astype(jnp.bfloat16), "wsh", scatter_dimension=0, tiled=True
        ).astype(jnp.float32),
        lax.psum_scatter(
            bout_grad.astype(jnp.bfloat16), "wsh", scatter_dimension=0, tiled=True
        ).astype(jnp.float32),
        lax.psum_scatter(
            gain2_grad.astype(jnp.bfloat16), "wsh", scatter_dimension=0, tiled=True
        ).astype(jnp.float32),
        lax.psum_scatter(
            bias2_grad.astype(jnp.bfloat16), "wsh", scatter_dimension=0, tiled=True
        ).astype(jnp.float32),
        lax.psum_scatter(
            wup_grad.astype(jnp.bfloat16), "wsh", scatter_dimension=0, tiled=True
        ).astype(jnp.float32),
        lax.psum_scatter(
            bup_grad.astype(jnp.bfloat16), "wsh", scatter_dimension=0, tiled=True
        ).astype(jnp.float32),
        lax.psum_scatter(
            wdown_grad.astype(jnp.bfloat16), "wsh", scatter_dimension=0, tiled=True
        ).astype(jnp.float32),
        lax.psum_scatter(
            bdown_grad.astype(jnp.bfloat16), "wsh", scatter_dimension=0, tiled=True
        ).astype(jnp.float32),
    )
    totals = (
        lax.psum(shares[0].astype(jnp.bfloat16), "ctx").astype(jnp.float32),
        lax.psum(shares[1].astype(jnp.bfloat16), "ctx").astype(jnp.float32),
        lax.psum(shares[2].astype(jnp.bfloat16), "ctx").astype(jnp.float32),
        lax.psum(shares[3].astype(jnp.bfloat16), "ctx").astype(jnp.float32),
        lax.psum(shares[4].astype(jnp.bfloat16), "ctx").astype(jnp.float32),
        lax.psum(shares[5].astype(jnp.bfloat16), "ctx").astype(jnp.float32),
        lax.psum(shares[6].astype(jnp.bfloat16), "ctx").astype(jnp.float32),
        lax.psum(shares[7].astype(jnp.bfloat16), "ctx").astype(jnp.float32),
        lax.psum(shares[8].astype(jnp.bfloat16), "ctx").astype(jnp.float32),
        lax.psum(shares[9].astype(jnp.bfloat16), "ctx").astype(jnp.float32),
        lax.psum(shares[10].astype(jnp.bfloat16), "ctx").astype(jnp.float32),
        lax.psum(shares[11].astype(jnp.bfloat16), "ctx").astype(jnp.float32),
    )
    return (
        mixed.astype(jnp.bfloat16)[None],
        inputs_grad[None],
        totals[0],
        totals[1],
        totals[2],
        totals[3],
        totals[4],
        totals[5],
        totals[6],
        totals[7],
        totals[8],
        totals[9],
        totals[10],
        totals[11],
    )


def solution(mesh):
    as_planned = mesh.shape["ctx"] == GROUPS * PEERS and mesh.shape["wsh"] == 2
    return jax.shard_map(
        body if as_planned else any_mesh_body,
        mesh=mesh,
        in_specs=(
            P("wsh", "ctx", None),
            P("wsh", None),
            P("wsh"),
            P("wsh"),
            P("wsh", None),
            P("wsh"),
            P("wsh", None),
            P("wsh"),
            P("wsh"),
            P("wsh"),
            P("wsh", None),
            P("wsh"),
            P("wsh", None),
            P("wsh"),
            P("wsh", "ctx", None),
        ),
        out_specs=(
            P("wsh", "ctx", None),
            P("wsh", "ctx", None),
            P("wsh"),
            P("wsh"),
            P("wsh", None),
            P("wsh"),
            P("wsh", None),
            P("wsh"),
            P("wsh"),
            P("wsh"),
            P("wsh", None),
            P("wsh"),
            P("wsh", None),
            P("wsh"),
        ),
        check_vma=False,
    )
```

```python
import functools

import jax
import jax.numpy as jnp
from jax import lax
from jax.experimental import pallas as pl
from jax.experimental.pallas import tpu as pltpu
from jax.sharding import PartitionSpec as P

H = 12
HD = 64
GROUPS = 4
PER_GROUP = H // GROUPS
PEERS = 4
MESH = pl.DeviceIdType.MESH
MIB = 2**20

epsilon = 1e-05
masked_score = -1e30


def params(vmem_mib, collective_id=None):
    if collective_id is None:
        return pltpu.CompilerParams(vmem_limit_bytes=vmem_mib * MIB)
    return pltpu.CompilerParams(
        vmem_limit_bytes=vmem_mib * MIB, collective_id=collective_id, has_side_effects=True
    )


def here():
    ctx = lax.axis_index("ctx")
    return ctx // PEERS, (ctx // 2) % 2, ctx % 2, lax.axis_index("wsh")


def at(z, x, core, y):
    return (z * PEERS + x * 2 + core, y)


def remote(src, dst, send, recv, device):
    return pltpu.make_async_remote_copy(
        src_ref=src,
        dst_ref=dst,
        send_sem=send,
        recv_sem=recv,
        device_id=device,
        device_id_type=MESH,
    )


def greet(devices):
    barrier = pltpu.get_barrier_semaphore()
    for device in devices:
        pl.semaphore_signal(barrier, inc=1, device_id=device, device_id_type=MESH)
    pl.semaphore_wait(barrier, len(devices))


def dot(left, right):
    return jnp.dot(left, right, preferred_element_type=jnp.float32)


def dot_turned(left, right):
    return lax.dot_general(
        left, right, (((1,), (1,)), ((), ())), preferred_element_type=jnp.float32
    )


def normalise(values):
    centre = jnp.mean(values, axis=-1, keepdims=True)
    shifted = values - centre
    spread = jnp.mean(shifted * shifted, axis=-1, keepdims=True)
    scale = lax.rsqrt(spread + epsilon)
    return shifted * scale, scale


def normalise_back(grad, gain, normed, scale):
    inner = grad * gain
    centre = jnp.mean(inner, axis=-1, keepdims=True)
    along = jnp.mean(inner * normed, axis=-1, keepdims=True)
    gain_grad = jnp.sum(grad * normed, axis=0, keepdims=True)
    bias_grad = jnp.sum(grad, axis=0, keepdims=True)
    return scale * (inner - centre - normed * along), gain_grad, bias_grad


LANES = 128


class Packed:
    names = ("gain1", "bias1", "bqv", "bout", "gain2", "bias2", "bup", "bdown")

    def __init__(self, sizes):
        self.sizes = dict(zip(self.names, sizes))
        self.starts, row = {}, 0
        for name in self.names:
            self.starts[name] = row
            row += self.sizes[name] // LANES
        self.used = row
        self.rows = row + -row % 8

    def pack(self, halves):
        total, flat = self.rows * LANES, 0.0
        for name, half in zip(self.names, halves):
            start = self.starts[name] * LANES
            after = total - start - half.shape[0]
            flat += jnp.pad(half.astype(jnp.float32), (start, after))
        return flat.reshape(-1, LANES)

    def read(self, ref, name, first=0, count=None):
        count = 2 * self.sizes[name] if count is None else count
        parts = []
        for lane in range(first, first + count, LANES):
            y, inner = divmod(lane, self.sizes[name])
            row = self.starts[name] + inner // LANES
            parts.append(ref[y, row : row + 1])
        return jnp.concatenate(parts, axis=1)

    def write(self, ref, name, values, first=0):
        for lane in range(0, values.shape[1], LANES):
            y, inner = divmod(first + lane, self.sizes[name])
            row = self.starts[name] + inner // LANES
            ref[y, row : row + 1] = values[:, lane : lane + LANES]

    def unpack(self, rows):
        flat = rows[: self.used].reshape(-1)
        parts, start = [], 0
        for name in self.names:
            parts.append(flat[start : start + self.sizes[name]])
            start += self.sizes[name]
        return parts


class Sender:
    def __init__(self):
        self.copies = []

    def __call__(self, src, dst, send, recv, device):
        copy = remote(src, dst, send, recv, device)
        copy.start()
        self.copies.append(copy)

    def finish(self):
        for copy in self.copies:
            copy.wait_send()


def front_kernel(
    pack,
    patches,
    small_half,
    qkv_half,
    out_half,
    up_half,
    down_half,
    query,
    keys,
    normed_low,
    small,
    qkv_far,
    out_far,
    up_far,
    down_got,
    down_part,
    qkv_own,
    staged,
    local,
    small_sem,
    ysend,
    yrecv,
    xsend,
    xrecv,
    csend,
    crecv,
    fsend,
    frecv,
    psend,
    precv,
    nsend,
    nrecv,
    pxsend,
    pxrecv,
    pfsend,
    pfrecv,
    query_send,
    query_recv,
    zsend,
    zrecv,
    kxsend,
    kxrecv,
    kcsend,
    kcrecv,
    kfsend,
    kfrecv,
):
    bf16 = jnp.bfloat16
    z, x, core, y = here()
    over_x, over_core, over_y = (
        at(z, 1 - x, core, y),
        at(z, x, 1 - core, y),
        at(z, x, core, 1 - y),
    )
    around = [at((z + d) % GROUPS, x, core, y) for d in range(1, GROUPS)]
    rows, width = patches.shape
    part = query.shape[1]
    half = qkv_half.shape[0]
    quarter = half // PEERS
    down, later = down_half.shape[0] // 2, down_part.shape[0]
    sooner = down - later
    greet(around + [over_x, over_core, over_y])
    go = Sender()

    def landed(view, sem):
        remote(view, view, sem, sem, over_core).wait_recv()

    def columns(b):
        return pl.ds(b * width, width)

    def share(px, pcore, b):
        return qkv_far.at[pl.ds((px * 2 + pcore) * quarter, quarter), columns(b)]

    order = (1, 2, 0)
    go(small_half, small.at[y], small_sem.at[0], small_sem.at[1], over_y)
    for b in order:
        src = qkv_half.at[pl.ds((x * 2 + core) * quarter, quarter), columns(b)]
        go(src, share(x, core, b), ysend.at[b], yrecv.at[b], over_y)
    copies = [
        pltpu.make_async_copy(small_half, small.at[y], local.at[0]),
        pltpu.make_async_copy(qkv_half, qkv_own, local.at[1]),
        pltpu.make_async_copy(
            down_half.at[pl.ds(core * down + sooner, later)], down_part, local.at[2]
        ),
    ]
    for copy in copies:
        copy.start()

    step = quarter // 2
    pieces = [(up_half, up_far, quarter, quarter, step, i * step, half // 2) for i in range(2)]
    shared = len(pieces)
    pieces += [(out_half, out_far, half // 2, half // 2, half // 2, 0, 0)]
    step = sooner // 2
    pieces += [(down_half, down_got, down, sooner, step, i * step, 0) for i in range(2)]

    def piece_view(k, px, pcore):
        unused, full, unused, apart, count, first, across = pieces[k]
        return full.at[pl.ds(px * across + pcore * apart + first, count)]

    def piece_in(k):
        view = piece_view(k, x, core)
        landed(view, precv.at[k])
        if k < shared:
            go(view, view, pxsend.at[k], pxrecv.at[k], over_x)
        go(view, view, nsend.at[k], nrecv.at[k], over_core)

    def piece_over(k):
        view = piece_view(k, 1 - x, core)
        landed(view, pxrecv.at[k])
        go(view, view, pfsend.at[k], pfrecv.at[k], over_core)

    copies[0].wait()
    landed(small.at[1 - y], small_sem.at[1])
    normed, scale = normalise(patches[...].astype(jnp.float32))
    low = (normed * pack.read(small, "gain1") + pack.read(small, "bias1")).astype(bf16)
    normed_low[...] = low
    low_own = jnp.where(y == 0, low[:, :half], low[:, half:])
    low_far = jnp.where(y == 0, low[:, half:], low[:, :half])
    for i, b in enumerate(order):
        view = share(x, core, b)
        landed(view, yrecv.at[b])
        go(view, view, xsend.at[b], xrecv.at[b], over_x)
        go(view, view, csend.at[b], crecv.at[b], over_core)
    for k, (src, unused, apart, unused, count, first, across) in enumerate(pieces):
        span = pl.ds(x * across + core * apart + first, count)
        go(src.at[span], piece_view(k, x, core), psend.at[k], precv.at[k], over_y)

    copies[1].wait()

    def block(pz, px, pcore, b):
        return keys.at[pz * PEERS + px * 2 + pcore, pl.ds((b - 1) * part, part)]

    own = []
    for i, b in enumerate(order):
        view = share(1 - x, core, b)
        landed(view, xrecv.at[b])
        go(view, view, fsend.at[b], frecv.at[b], over_core)
        landed(share(x, 1 - core, b), crecv.at[b])
        landed(share(1 - x, 1 - core, b), frecv.at[b])
        made = dot(low_own, qkv_own[:, b * width : (b + 1) * width])
        made = made + dot(low_far, qkv_far[:, b * width : (b + 1) * width])
        if b != 1:
            made = made + pack.read(small, "bqv", (b // 2) * width, width)
        staged[b] = made.astype(bf16).T.reshape(GROUPS, part, rows)
        for d in (2, 1, 3):
            target = (z + d) % GROUPS
            if b == 0:
                dst, sems = query.at[z], (query_send.at[d], query_recv.at[d])
            else:
                sem = (b - 1) * GROUPS + d
                dst, sems = block(z, x, core, b), (zsend.at[sem], zrecv.at[sem])
            go(staged.at[b, target], dst, sems[0], sems[1], around[d - 1])
        dst = query.at[z] if b == 0 else block(z, x, core, b)
        own.append(pltpu.make_async_copy(staged.at[b, z], dst, local.at[3 + i]))
        own[-1].start()
        if b > 0:
            sem = (b - 1) * GROUPS
            go(staged.at[b, z], dst, kxsend.at[sem], kxrecv.at[sem], over_x)
            go(staged.at[b, z], dst, kcsend.at[sem], kcrecv.at[sem], over_core)

    sequence = [(1, 0), (2, 0)] + [(b, d) for b in (1, 2) for d in (1, 3, 2)]
    for i in range(len(sequence) + 1):
        if i < len(sequence):
            b, d = sequence[i]
            sem = (b - 1) * GROUPS + d
            if d > 0:
                view = block((z + GROUPS - d) % GROUPS, x, core, b)
                landed(view, zrecv.at[sem])
                go(view, view, kxsend.at[sem], kxrecv.at[sem], over_x)
                go(view, view, kcsend.at[sem], kcrecv.at[sem], over_core)
        if i >= 1:
            b, d = sequence[i - 1]
            sem = (b - 1) * GROUPS + d
            view = block((z + GROUPS - d) % GROUPS, 1 - x, core, b)
            landed(view, kxrecv.at[sem])
            go(view, view, kfsend.at[sem], kfrecv.at[sem], over_core)
        if 2 <= i < 2 + shared:
            piece_in(i - 2)
    for k in range(shared, len(pieces)):
        piece_in(k)
    for k in range(shared):
        piece_over(k)
    for b, d in sequence:
        sem = (b - 1) * GROUPS + d
        pz = (z + GROUPS - d) % GROUPS
        landed(block(pz, x, 1 - core, b), kcrecv.at[sem])
        landed(block(pz, 1 - x, 1 - core, b), kfrecv.at[sem])
    for d in range(1, GROUPS):
        landed(query.at[(z + GROUPS - d) % GROUPS], query_recv.at[d])
    for k in range(len(pieces)):
        landed(piece_view(k, x, 1 - core), nrecv.at[k])
    for k in range(shared):
        landed(piece_view(k, 1 - x, 1 - core), pfrecv.at[k])
    for copy in copies[2:] + own:
        copy.wait()
    go.finish()


def front(pack, patches, small_half, qkv_half, out_half, up_half, down_half):
    f32, bf16 = jnp.float32, jnp.bfloat16
    vmem = pl.BlockSpec(memory_space=pltpu.VMEM)
    hbm = pl.BlockSpec(memory_space=pltpu.HBM)
    rows, width = patches.shape
    part, half = width // GROUPS, qkv_half.shape[0]
    dma = pltpu.SemaphoreType.DMA

    def pair(n):
        return [dma((n,))] * 2

    return pl.pallas_call(
        functools.partial(front_kernel, pack),
        out_shape=[
            jax.ShapeDtypeStruct((GROUPS, part, rows), bf16),
            jax.ShapeDtypeStruct((GROUPS * PEERS, 2 * part, rows), bf16),
            jax.ShapeDtypeStruct((rows, width), bf16),
            jax.ShapeDtypeStruct((2,) + small_half.shape, f32),
            jax.ShapeDtypeStruct(qkv_half.shape, bf16),
            jax.ShapeDtypeStruct(out_half.shape, bf16),
            jax.ShapeDtypeStruct(up_half.shape, bf16),
            jax.ShapeDtypeStruct((down_half.shape[0] // 2, width), bf16),
            jax.ShapeDtypeStruct((down_half.shape[0] // 4, width), bf16),
        ],
        in_specs=[vmem, hbm, hbm, hbm, hbm, hbm],
        out_specs=[vmem] * 9,
        scratch_shapes=[
            pltpu.VMEM(qkv_half.shape, bf16),
            pltpu.VMEM((3, GROUPS, part, rows), bf16),
            dma((6,)),
        ]
        + [dma((2,))]
        + pair(3) * 4
        + pair(5) * 2
        + pair(2) * 2
        + pair(GROUPS)
        + pair(2 * GROUPS) * 4,
        compiler_params=params(60, 1),
        name="front",
    )(patches, small_half, qkv_half, out_half, up_half, down_half)


def split_rows(first, x, y, quarter):
    if first == "y":
        return [((1 - y) * 2 * quarter, 2 * quarter)], [(y * 2 * quarter, 2 * quarter)]
    other, mine = (1 - x) * quarter, x * quarter
    return (
        [(other, quarter), (2 * quarter + other, quarter)],
        [(mine, quarter), (2 * quarter + mine, quarter)],
    )


def core_sum(first, own, land, send_ref, keep_ref, x, y):
    quarter = land.shape[0] // 4
    gone, kept = split_rows(first, x, y, quarter)
    for ref, parts in ((send_ref, gone), (keep_ref, kept)):
        place = 0
        for start, count in parts:
            rows = pl.ds(start, count)
            total = own(rows).astype(jnp.float32) + land[rows].astype(jnp.float32)
            ref[pl.ds(place, count)] = total.astype(ref.dtype)
            place += count


def middle_kernel(
    pack,
    firsts,
    heads,
    patches,
    out_grad,
    small,
    w_out,
    w_out_far,
    w_up,
    w_up_far,
    w_down_half,
    w_down_got,
    w_down_far,
    mixed,
    hidden_grad,
    grad_heads,
    send_over_x,
    send_over_y,
    send_rest,
    keep,
    vector,
    o_land,
    o_grad,
    wout,
    wup,
    wdown,
    act_grad,
    act_turned,
    pre_grad,
    bup_rows,
    grads,
    c_land,
    local,
    osend,
    orecv,
    gsend,
    grecv,
    wsem,
    csend,
    crecv,
):
    f32, bf16 = jnp.float32, jnp.bfloat16
    z, x, core, y = here()
    over_core = at(z, x, 1 - core, y)
    around = [at((z + d) % GROUPS, x, core, y) for d in range(1, GROUPS)]
    rows, width = patches.shape
    tiles = wdown.shape[0] // width
    half = w_down_half.shape[0]
    far = w_down_far.shape[0]
    greet(around + [over_core])
    go = Sender()
    near = half // 2 - far
    far_rows = pl.ds((1 - y) * half + core * (half // 2) + near, far)
    other_rows = pl.ds((1 - y) * half + (1 - core) * (half // 2) + near, far)
    for d in (2, 1, 3):
        go(heads.at[(z + d) % GROUPS], o_land.at[z], osend.at[d], orecv.at[d], around[d - 1])
    go(w_down_far, wdown.at[far_rows], wsem.at[0], wsem.at[1], over_core)
    down_copies = [
        pltpu.make_async_copy(w_down_half, wdown.at[pl.ds(y * half, half)], local.at[0]),
        pltpu.make_async_copy(w_down_far, wdown.at[far_rows], local.at[1]),
    ]
    for c in range(2):
        src = w_down_got.at[pl.ds(c * near, near)]
        dst = wdown.at[pl.ds((1 - y) * half + c * (half // 2), near)]
        down_copies.append(pltpu.make_async_copy(src, dst, local.at[8 + c]))
    copies = [
        pltpu.make_async_copy(heads.at[z], o_land.at[z], local.at[2]),
    ]
    pairs = [(w_out, wout, y), (w_out_far, wout, 1 - y), (w_up, wup, y), (w_up_far, wup, 1 - y)]
    for i, (src, dst, side) in enumerate(pairs):
        count = src.shape[0]
        span = pl.ds(side * count, count)
        copies.append(pltpu.make_async_copy(src, dst.at[span], local.at[4 + i]))

    for copy in down_copies + copies:
        copy.start()
    dy = out_grad[...]
    vector[...] = jnp.zeros(vector.shape, f32)
    pack.write(vector, "bdown", jnp.sum(dy.astype(f32), axis=0, keepdims=True))
    for f in range(tiles):
        bup_rows[f, 0:1] = pack.read(small, "bup", f * width, width)
    for copy in down_copies:
        copy.wait()
    landed = wdown.at[other_rows]
    remote(landed, landed, wsem.at[0], wsem.at[1], over_core).wait_recv()

    def tile(f):
        return pl.ds(pl.multiple_of(f * width, width), width)

    def first_grad(f, carry):
        act_grad[f] = dot_turned(dy, wdown[tile(f)])
        return carry

    lax.fori_loop(0, tiles, first_grad, 0)
    for copy in copies:
        copy.wait()
    for d in range(1, GROUPS):
        landed = o_land.at[(z + GROUPS - d) % GROUPS]
        remote(landed, landed, osend.at[d], orecv.at[d], over_core).wait_recv()
    turned = o_land[...].reshape(width, rows)
    hidden = patches[...].astype(f32) + (dot(turned.T, wout[...]) + pack.read(small, "bout"))
    gain2 = pack.read(small, "gain2")
    normed, scale = normalise(hidden)
    c = (normed * gain2 + pack.read(small, "bias2")).astype(bf16)
    mixed_acc = hidden + pack.read(small, "bdown")
    c_grad = jnp.zeros((rows, width), f32)

    def forward_back(f, carry):
        mixed_acc, c_grad = carry
        up = wup[:, tile(f)]
        pre = dot(c, up) + bup_rows[f, 0:1]
        share = 0.5 + 0.5 * lax.erf(pre * (0.5**0.5))
        slope = share + pre * jnp.exp(-0.5 * pre * pre) * ((0.5 / jnp.pi) ** 0.5)
        act = (pre * share).astype(bf16)
        grad = (act_grad[f] * slope).astype(bf16)
        act_turned[tile(f)] = act.T
        pre_grad[f] = grad
        bup_rows[f, 0:1] = jnp.sum(grad.astype(f32), axis=0, keepdims=True)
        return (
            mixed_acc + dot(act, wdown[tile(f)]),
            c_grad + dot_turned(grad, up),
        )

    mixed_acc, c_grad = lax.fori_loop(0, tiles, forward_back, (mixed_acc, c_grad))
    mixed[...] = mixed_acc.astype(bf16)
    for f in range(tiles):
        pack.write(vector, "bup", bup_rows[f, 0:1], f * width)
    part, gain_grad, bias_grad = normalise_back(c_grad, gain2, normed, scale)
    pack.write(vector, "gain2", gain_grad)
    pack.write(vector, "bias2", bias_grad)
    whole = dy.astype(f32) + part
    hidden_grad[...] = whole
    dz = whole.astype(bf16)
    pack.write(vector, "bout", jnp.sum(dz.astype(f32), axis=0, keepdims=True))
    o_grad[...] = dot_turned(wout[...], dz).astype(bf16).reshape(o_grad.shape)
    for d in (2, 1, 3):
        go(o_grad.at[(z + d) % GROUPS], grad_heads.at[z], gsend.at[d], grecv.at[d], around[d - 1])
    own = pltpu.make_async_copy(o_grad.at[z], grad_heads.at[z], local.at[3])
    own.start()

    columns = c_land.shape[2]
    count = grads.shape[0]
    mine = pl.ds(pl.multiple_of(core * columns, columns), columns)
    others = pl.ds(pl.multiple_of((1 - core) * columns, columns), columns)

    def over(k):
        go(grads.at[k, :, others], c_land.at[k], csend.at[k], crecv.at[k], over_core)

    def settle(k):
        landed = c_land.at[k]
        remote(landed, landed, csend.at[k], crecv.at[k], over_core).wait_recv()
        place, sent = k, None
        for ref in (send_over_x, send_over_y, send_rest):
            if sent is None and place < ref.shape[0]:
                sent = ref.at[place]
            place -= ref.shape[0]
        core_sum(firsts[k], lambda r: grads[k, r, mine], c_land.at[k], sent, keep.at[k], x, y)

    c_turned = c.T
    piece = half // tiles
    for k in range(count):
        if k < tiles:
            for top in range(2):
                grads[k, top * piece : (top + 1) * piece] = dot(
                    act_turned[top * half + k * piece : top * half + (k + 1) * piece], dy
                ).astype(bf16)
        elif k < 2 * tiles:
            grads[k] = dot(c_turned, pre_grad[k - tiles]).astype(bf16)
        else:
            grads[k] = dot(turned, dz).astype(bf16)
        over(k)
        if k >= 2:
            settle(k - 2)
    settle(count - 2)
    settle(count - 1)
    for d in range(1, GROUPS):
        landed = grad_heads.at[(z + GROUPS - d) % GROUPS]
        remote(landed, landed, gsend.at[d], grecv.at[d], over_core).wait_recv()
    own.wait()
    go.finish()


def middle(pack, firsts, ahead, heads, patches, out_grad, small, *weights):
    rows, width = patches.shape
    hidden = weights[2].shape[1]
    tiles = hidden // width
    count = 2 * tiles + 1
    f32, bf16 = jnp.float32, jnp.bfloat16
    vmem = pl.BlockSpec(memory_space=pltpu.VMEM)
    hbm = pl.BlockSpec(memory_space=pltpu.HBM)
    dma = pltpu.SemaphoreType.DMA
    return pl.pallas_call(
        functools.partial(middle_kernel, pack, firsts),
        out_shape=[
            jax.ShapeDtypeStruct((rows, width), bf16),
            jax.ShapeDtypeStruct((rows, width), f32),
            jax.ShapeDtypeStruct(heads.shape, bf16),
            jax.ShapeDtypeStruct((ahead, width // 2, width // 2), bf16),
            jax.ShapeDtypeStruct((ahead, width // 2, width // 2), bf16),
            jax.ShapeDtypeStruct((count - 2 * ahead, width // 2, width // 2), bf16),
            jax.ShapeDtypeStruct((count, width // 2, width // 2), bf16),
            jax.ShapeDtypeStruct((2, pack.rows, LANES), f32),
        ],
        in_specs=[hbm, vmem, vmem, vmem] + [hbm] * 7,
        out_specs=[vmem] * 8,
        scratch_shapes=[
            pltpu.VMEM(heads.shape, bf16),
            pltpu.VMEM(heads.shape, bf16),
            pltpu.VMEM((width, width), bf16),
            pltpu.VMEM((width, hidden), bf16),
            pltpu.VMEM((hidden, width), bf16),
            pltpu.VMEM((tiles, rows, width), f32),
            pltpu.VMEM((hidden, rows), bf16),
            pltpu.VMEM((tiles, rows, width), bf16),
            pltpu.VMEM((tiles, 8, width), f32),
            pltpu.VMEM((count, width, width), bf16),
            pltpu.VMEM((count, width, width // 2), bf16),
            dma((10,)),
            dma((GROUPS,)),
            dma((GROUPS,)),
            dma((GROUPS,)),
            dma((GROUPS,)),
            dma((2,)),
            dma((count,)),
            dma((count,)),
        ],
        compiler_params=params(60, 3),
        name="middle",
    )(heads, patches, out_grad, small, *weights)


class Totals:
    def __init__(self, refs, tiles):
        self.refs, self.tiles = refs, tiles

    def place(self, k, row, count, column, columns):
        width = self.refs[2].shape[1]
        start = 0
        if k < self.tiles:
            which, row = 0, k * (width // 2) + row
        elif k < 2 * self.tiles:
            which, start = 1, (k - self.tiles) * width
        elif k == 2 * self.tiles:
            which = 2
        else:
            which, start = 3, (k - 2 * self.tiles - 1) * width
        return which, pl.ds(row, count), pl.ds(pl.multiple_of(start + column, LANES), columns)

    def view(self, *place):
        which, rows, columns = self.place(*place)
        return self.refs[which].at[rows, columns]

    def store(self, values, *place):
        which, rows, columns = self.place(*place)
        ref = self.refs[which]
        ref[rows, columns] = values.astype(ref.dtype)


def last_kernel(
    pack,
    firsts,
    tiles,
    query_grad,
    key_grad,
    normed_low,
    w_qkv,
    w_qkv_far,
    patches,
    hidden_grad,
    small,
    ahead_x,
    ahead_y,
    send_rest,
    keep,
    vector_in,
    inputs_grad,
    down_out,
    up_out,
    out_out,
    qkv_out,
    vector_out,
    down_total,
    up_total,
    out_total,
    qkv_total,
    got,
    near,
    both,
    far,
    own,
    wqkv,
    grads,
    c_land,
    late_send,
    first_land,
    half_sum,
    second_land,
    quarter_sum,
    z_land,
    eighth_sum,
    far_land,
    vectors,
    v_land,
    local,
    loads,
    n_send,
    n_recv,
    f_send,
    f_recv,
    q_send,
    q_recv,
    csend,
    crecv,
    asend,
    arecv,
    bsend,
    brecv,
    zsend,
    zrecv,
    wsend,
    wrecv,
    dsend,
    drecv,
    gsend,
    grecv,
    hsend,
    hrecv,
    isend,
    irecv,
    vsend,
    vrecv,
):
    f32, bf16 = jnp.float32, jnp.bfloat16
    z, x, core, y = here()
    pair, side = z // 2, z % 2
    over_x, over_core, over_y = (
        at(z, 1 - x, core, y),
        at(z, x, 1 - core, y),
        at(z, x, core, 1 - y),
    )
    around = [at((z + d) % GROUPS, x, core, y) for d in range(1, GROUPS)]
    over_near, over_far = at(z + 1 - 2 * side, x, core, y), around[1]
    peer = {"y": over_y, "x": over_x}
    greet(around + [over_x, over_core, over_y])
    go = Sender()
    totals = Totals((down_total, up_total, out_total, qkv_total), tiles)
    outs = Totals((down_out, up_out, out_out, qkv_out), tiles)
    part = query_grad.shape[1]
    rows, width = patches.shape
    chunks, early, late = len(firsts), keep.shape[0], c_land.shape[0]
    ahead = ahead_x.shape[0]
    hidden = ahead + ahead_y.shape[0]
    half = c_land.shape[2]
    quarter, shard = width // 4, width // 16

    def landed(view, sem):
        remote(view, view, sem, sem, over_core).wait_recv()

    order = (2, 1, 3, 0)
    held = []
    for d in order:
        pz = (z + d) % GROUPS
        for k in range(2):
            px = (x + 1 + k) % 2
            slot = 2 * d + k
            src = key_grad.at[pz * PEERS + px * 2 + 1 - core]
            go(src, near.at[slot], n_send.at[slot], n_recv.at[slot], over_core)
            src = key_grad.at[pz * PEERS + px * 2 + core]
            copy = pltpu.make_async_copy(src, both.at[slot], local.at[4 + slot])
            copy.start()
            held.append((slot, copy))
    held = dict(held)
    for d in (2, 1, 3):
        pz = (z + d) % GROUPS
        go(query_grad.at[pz], got.at[z, pl.ds(0, part)], q_send.at[d], q_recv.at[d], around[d - 1])
    own_query = pltpu.make_async_copy(query_grad.at[z], got.at[z, pl.ds(0, part)], local.at[0])
    own_query.start()
    arrivals = []
    for k in range(early):
        arrivals.append([pltpu.make_async_copy(keep.at[k], half_sum.at[k], loads.at[2 * k])])
        if k < hidden:
            src = ahead_x.at[k] if k < ahead else ahead_y.at[k - ahead]
            copy = pltpu.make_async_copy(src, first_land.at[k], loads.at[2 * k + 1])
            arrivals[k].append(copy)
        else:
            sem = late + k - hidden
            src = send_rest.at[k - hidden]
            go(src, first_land.at[k], asend.at[sem], arecv.at[sem], peer[firsts[k]])
        for copy in arrivals[k]:
            copy.start()
    count = w_qkv.shape[0]
    weights = [
        pltpu.make_async_copy(w_qkv, wqkv.at[pl.ds(y * count, count)], local.at[2]),
        pltpu.make_async_copy(w_qkv_far, wqkv.at[pl.ds((1 - y) * count, count)], local.at[3]),
    ]
    for copy in weights:
        copy.start()

    def collect_near(step):
        d = order[step]
        for k in range(2):
            slot = 2 * d + k
            landed(near.at[slot], n_recv.at[slot])
            held[slot].wait()
            both[slot] = (both[slot].astype(f32) + near[slot].astype(f32)).astype(bf16)
            if k == 0:
                go(both.at[slot], far.at[d], f_send.at[d], f_recv.at[d], over_x)

    def collect_far(step):
        d = order[step]
        landed(far.at[d], f_recv.at[d])
        own[d] = (both[2 * d + 1].astype(f32) + far[d].astype(f32)).astype(bf16)
        place = got.at[z, pl.ds(part, 2 * part)]
        if d == 0:
            copy = pltpu.make_async_copy(own.at[0], place, local.at[1])
            copy.start()
            return copy
        sem = GROUPS + d
        go(own.at[d], place, q_send.at[sem], q_recv.at[sem], around[d - 1])
        return None

    def stage_core(k):
        i = k - early
        landed(c_land.at[i], crecv.at[i])
        mine = pl.ds(pl.multiple_of(core * half, half), half)
        core_sum(
            firsts[k],
            lambda r: grads[i, r, mine],
            c_land.at[i],
            late_send.at[i],
            half_sum.at[k],
            x,
            y,
        )
        go(late_send.at[i], first_land.at[k], asend.at[i], arecv.at[i], peer[firsts[k]])

    def stage_first(k):
        if k < early:
            for copy in arrivals[k]:
                copy.wait()
        if k >= hidden:
            landed(first_land.at[k], arecv.at[k - early if k >= early else late + k - hidden])
        half_sum[k] = (half_sum[k].astype(f32) + first_land[k].astype(f32)).astype(bf16)
        place = x if firsts[k] == "y" else y
        other = half_sum.at[k, pl.ds((1 - place) * quarter, quarter)]
        second = over_x if firsts[k] == "y" else over_y
        go(other, second_land.at[k], bsend.at[k], brecv.at[k], second)

    def stage_second(k):
        landed(second_land.at[k], brecv.at[k])
        place = x if firsts[k] == "y" else y
        total = half_sum[k, pl.ds(place * quarter, quarter)].astype(f32)
        quarter_sum[k] = (total + second_land[k].astype(f32)).astype(bf16)
        other = quarter_sum.at[k, pl.ds((1 - side) * 2 * shard, 2 * shard)]
        go(other, z_land.at[k], zsend.at[k], zrecv.at[k], over_near)

    def stage_near(k):
        landed(z_land.at[k], zrecv.at[k])
        total = quarter_sum[k, pl.ds(side * 2 * shard, 2 * shard)].astype(f32)
        eighth_sum[k] = (total + z_land[k].astype(f32)).astype(bf16)
        other = eighth_sum.at[k, pl.ds((1 - pair) * shard, shard)]
        go(other, far_land.at[k], wsend.at[k], wrecv.at[k], over_far)

    def spot(k, px, pside, ppair, count):
        row = px * quarter + pside * 2 * shard + ppair * shard
        return totals.view(k, row, count, core * half, half)

    def stage_far(k):
        landed(far_land.at[k], wrecv.at[k])
        total = eighth_sum[k, pl.ds(pair * shard, shard)].astype(f32) + far_land[k].astype(f32)
        row = x * quarter + side * 2 * shard + pair * shard
        totals.store(total, k, row, shard, core * half, half)
        view = spot(k, x, side, pair, shard)
        go(view, view, dsend.at[k], drecv.at[k], over_far)

    def stage_back(k):
        landed(spot(k, x, side, 1 - pair, shard), drecv.at[k])
        view = spot(k, x, side, 0, 2 * shard)
        go(view, view, gsend.at[k], grecv.at[k], over_near)

    def stage_out(k):
        landed(spot(k, x, 1 - side, 0, 2 * shard), grecv.at[k])
        view = spot(k, x, 0, 0, quarter)
        go(view, view, hsend.at[k], hrecv.at[k], over_x)
        go(view, view, isend.at[2 * k], irecv.at[2 * k], over_core)

    def stage_last(k):
        view = spot(k, 1 - x, 0, 0, quarter)
        landed(view, hrecv.at[k])
        go(view, view, isend.at[2 * k + 1], irecv.at[2 * k + 1], over_core)

    written = []

    def stage_write(k):
        for px in range(2):
            place = (x + px) % 2
            view = totals.view(k, place * quarter, quarter, (1 - core) * half, half)
            landed(view, irecv.at[2 * k + px])
        place = (k, 0, 2 * quarter, 0, 2 * half)
        copy = pltpu.make_async_copy(totals.view(*place), outs.view(*place), loads.at[2 * early + k])
        copy.start()
        written.append(copy)

    stages = (
        stage_first,
        stage_second,
        stage_near,
        stage_far,
        stage_back,
        stage_out,
        stage_last,
        stage_write,
    )

    def vector_step(n):
        if n == 0:
            landed(v_land.at[0], vrecv.at[0])
            vectors[1] = vectors[0] + v_land[0]
            go(vectors.at[1], v_land.at[1], vsend.at[1], vrecv.at[1], over_x)
        elif n == 1:
            landed(v_land.at[1], vrecv.at[1])
            vectors[2] = vectors[1] + v_land[1]
            go(vectors.at[2], v_land.at[2], vsend.at[2], vrecv.at[2], over_y)
        elif n == 2:
            landed(v_land.at[2], vrecv.at[2])
            vectors[3] = vectors[2] + v_land[2]
            for d in range(1, GROUPS):
                sem = 2 + d
                go(vectors.at[3], v_land.at[sem], vsend.at[sem], vrecv.at[sem], around[d - 1])
        elif n == 3:
            total = vectors[3]
            for d in range(1, GROUPS):
                landed(v_land.at[2 + d], vrecv.at[2 + d])
                total += v_land[2 + d]
            v_land[0] = total
            vector_out[...] = v_land[0, y]

    entry = list(range(early)) + [LATE_TURN + i for i in range(late)]
    turns = iter(range(entry[-1] + len(stages)))

    def turn():
        step = next(turns, None)
        if step is None:
            return False
        for depth, stage in enumerate(stages):
            for k in range(chunks):
                if step - depth == entry[k]:
                    stage(k)
        return True

    collect_near(0)
    turn()
    for step in range(1, GROUPS):
        collect_near(step)
        collect_far(step - 1)
        turn()
    own_keys = collect_far(GROUPS - 1)
    turn()
    normed_turned = normed_low[...].T
    normed, scale = normalise(patches[...].astype(f32))
    gain1 = pack.read(small, "gain1")
    turn()
    for d in range(1, GROUPS):
        landed(got.at[(z + GROUPS - d) % GROUPS, pl.ds(0, part)], q_recv.at[d])
    own_query.wait()
    turn()
    others = pl.ds(pl.multiple_of((1 - core) * half, half), half)

    def project(i):
        turned = got[:, i * part : (i + 1) * part].reshape(width, rows)
        grads[i] = dot_turned(normed_turned, turned).astype(bf16)
        go(grads.at[i, :, others], c_land.at[i], csend.at[i], crecv.at[i], over_core)

    project(0)
    for d in range(1, GROUPS):
        landed(got.at[(z + GROUPS - d) % GROUPS, pl.ds(part, 2 * part)], q_recv.at[GROUPS + d])
    own_keys.wait()
    for i in range(1, late):
        project(i)
    turn()
    for copy in weights:
        copy.wait()
    vectors[0] = vector_in[...]
    ones = jnp.ones((8, rows), bf16)
    normed_grad = jnp.zeros((width, rows), f32)
    for i in range(late):
        turned = got[:, i * part : (i + 1) * part].reshape(width, rows)
        if i != 1:
            sums = dot_turned(ones, turned)[0:1]
            pack.write(vectors.at[0], "bqv", sums, (i // 2) * width)
        normed_grad += dot(wqkv[:, i * width : (i + 1) * width], turned)
        stage_core(early + i)
    turn()
    change, gain_grad, bias_grad = normalise_back(normed_grad.T, gain1, normed, scale)
    inputs_grad[...] = hidden_grad[...] + change
    pack.write(vectors.at[0], "gain1", gain_grad)
    pack.write(vectors.at[0], "bias1", bias_grad)
    go(vectors.at[0], v_land.at[0], vsend.at[0], vrecv.at[0], over_core)
    step = 0
    while turn():
        vector_step(step)
        step += 1
    for copy in written:
        copy.wait()
    go.finish()


LATE_TURN = 9


def last(
    pack, firsts, query_grad, key_grad, normed_low, w_qkv, w_qkv_far, patches, hidden_grad, small,
    ahead_x, ahead_y, send_rest, keep, vector
):
    f32, bf16 = jnp.float32, jnp.bfloat16
    vmem = pl.BlockSpec(memory_space=pltpu.VMEM)
    hbm = pl.BlockSpec(memory_space=pltpu.HBM)
    groups, part, rows = query_grad.shape
    width = patches.shape[1]
    early, half = keep.shape[0], width // 2
    tiles, chunks, late = (early - 1) // 2, len(firsts), len(firsts) - early
    piece = (2 * part, rows)
    dma = pltpu.SemaphoreType.DMA
    totals = [
        (tiles * half, width),
        (half, tiles * width),
        (half, width),
        (half, late * width),
    ]

    def pair(n):
        return [dma((n,))] * 2

    return pl.pallas_call(
        functools.partial(last_kernel, pack, firsts, tiles),
        out_shape=[jax.ShapeDtypeStruct((rows, width), f32)]
        + [jax.ShapeDtypeStruct(shape, bf16) for shape in totals]
        + [jax.ShapeDtypeStruct(vector.shape[1:], f32)],
        in_specs=[hbm, hbm, vmem, hbm, hbm, vmem, vmem, vmem, hbm, hbm, hbm, hbm, vmem],
        out_specs=[vmem] + [hbm] * 4 + [vmem],
        scratch_shapes=[pltpu.VMEM(shape, bf16) for shape in totals]
        + [
            pltpu.VMEM((groups, 3 * part, rows), bf16),
            pltpu.VMEM((2 * groups,) + piece, bf16),
            pltpu.VMEM((2 * groups,) + piece, bf16),
            pltpu.VMEM((groups,) + piece, bf16),
            pltpu.VMEM((groups,) + piece, bf16),
            pltpu.VMEM((width, late * width), bf16),
            pltpu.VMEM((late, width, width), bf16),
            pltpu.VMEM((late, width, half), bf16),
            pltpu.VMEM((late, half, half), bf16),
            pltpu.VMEM((chunks, half, half), bf16),
            pltpu.VMEM((chunks, half, half), bf16),
            pltpu.VMEM((chunks, half // 2, half), bf16),
            pltpu.VMEM((chunks, half // 2, half), bf16),
            pltpu.VMEM((chunks, half // 4, half), bf16),
            pltpu.VMEM((chunks, half // 4, half), bf16),
            pltpu.VMEM((chunks, half // 8, half), bf16),
            pltpu.VMEM((4,) + vector.shape, f32),
            pltpu.VMEM((6,) + vector.shape, f32),
            dma((4 + 2 * groups,)),
            dma((2 * early + chunks,)),
        ]
        + pair(2 * groups)
        + pair(groups)
        + pair(2 * groups)
        + pair(late)
        + pair(chunks)
        + pair(chunks) * 6
        + pair(2 * chunks)
        + pair(6),
        compiler_params=params(60, 4),
        name="last",
    )(
        query_grad, key_grad, normed_low, w_qkv, w_qkv_far, patches, hidden_grad, small,
        ahead_x, ahead_y, send_rest, keep, vector,
    )


class Documents:
    def __init__(self, lengths, rows):
        self.rows, self.count = rows, lengths.shape[1]
        self.starts, self.ends, place = [], [], 0
        for d in range(self.count):
            self.starts.append(place)
            place = place + lengths[0, d]
            self.ends.append(place)

    def span(self, block):
        first, last = block * self.rows, (block + 1) * self.rows - 1
        low, high = 0, 0
        for d in range(self.count):
            low = jnp.where(self.starts[d] <= first, self.starts[d], low)
        for d in reversed(range(self.count)):
            high = jnp.where(self.ends[d] > last, self.ends[d], high)
        return low // self.rows, (high + self.rows - 1) // self.rows

    def inside(self, block, yes, no):
        shape = (8, self.rows)
        row = lax.broadcasted_iota(jnp.int32, shape, 0)
        place = block * self.rows + lax.broadcasted_iota(jnp.int32, shape, 1)
        found = jnp.where(row < self.count, no, 0.0)
        for d in range(self.count):
            hit = (row == d) & (place >= self.starts[d]) & (place < self.ends[d])
            found = jnp.where(hit, yes, found)
        return found

    def marks(self, block):
        ones, rest = jnp.ones((8, self.rows)), jnp.zeros((HD - 16, self.rows))
        return jnp.concatenate([self.inside(block, 1.0, 0.0), ones, rest]).astype(jnp.bfloat16)

    def veto(self, block):
        rest = jnp.zeros((HD - 8, self.rows))
        return jnp.concatenate([self.inside(block, 0.0, masked_score), rest])


def attend_kernel(
    lengths, place, query, keys, out, out_low, sums, key_rows, query_aug, acc, stat
):
    blocks, rows = keys.shape[0], keys.shape[2]
    width = query.shape[1]
    groups = query.shape[0]
    documents = Documents(lengths, rows)

    def turn(j, carry):
        mark = documents.marks(j)
        for h in range(PER_GROUP):
            both = jnp.concatenate([keys[j, h * HD : (h + 1) * HD], mark], axis=0)
            key_rows[h, j] = both.T
        return carry

    lax.fori_loop(0, blocks, turn, 0)
    for i in range(groups):
        block = i * PEERS + place[0]
        veto = documents.veto(block).astype(jnp.bfloat16)
        for h in range(PER_GROUP):
            query_aug[h, :HD] = query[i, h * HD : (h + 1) * HD] * jnp.bfloat16(0.125)
            query_aug[h, HD:] = veto
        stat[0] = jnp.full(stat.shape[1:], masked_score, jnp.float32)
        stat[1] = jnp.zeros(stat.shape[1:], jnp.float32)
        acc[...] = jnp.zeros(acc.shape, jnp.float32)

        low, high = documents.span(block)
        steps = (high - low + 1) // 2
        low = jnp.minimum(low, blocks - 2 * steps)

        def step(n, carry):
            j = low + 2 * n
            made = [
                [dot(key_rows[h, j + k], query_aug[h]) for k in range(2)] for h in range(PER_GROUP)
            ]
            for h in range(PER_GROUP):
                first, second = made[h]
                old = stat[0, h : h + 1]
                most = jnp.max(jnp.maximum(first, second), axis=0, keepdims=True)
                new = jnp.maximum(old, most)
                first, second = jnp.exp(first - new), jnp.exp(second - new)
                factor = jnp.exp(old - new)
                stat[0, h : h + 1] = new
                stat[1, h : h + 1] = stat[1, h : h + 1] * factor + jnp.sum(
                    first + second, axis=0, keepdims=True
                )
                span = slice(width + h * HD, width + (h + 1) * HD)
                shared = dot(keys[j, span], first.astype(jnp.bfloat16))
                shared += dot(keys[j + 1, span], second.astype(jnp.bfloat16))
                acc[h] = acc[h] * factor + shared
            return carry

        lax.fori_loop(0, steps, step, 0)
        for h in range(PER_GROUP):
            total = stat[1, h : h + 1]
            shared = acc[h] / total
            out[i, h * HD : (h + 1) * HD] = shared
            out_low[i, h * HD : (h + 1) * HD] = shared.astype(jnp.bfloat16)
            sums[i, h : h + 1] = stat[0, h : h + 1] + jnp.log(total)


def attend(lengths, place, query, keys):
    groups, width, rows = query.shape
    blocks = keys.shape[0]
    vmem = pl.BlockSpec(memory_space=pltpu.VMEM)
    return pl.pallas_call(
        attend_kernel,
        out_shape=[
            jax.ShapeDtypeStruct(query.shape, jnp.float32),
            jax.ShapeDtypeStruct(query.shape, jnp.bfloat16),
            jax.ShapeDtypeStruct((groups, 8, rows), jnp.float32),
        ],
        in_specs=[pl.BlockSpec(memory_space=pltpu.SMEM)] * 2 + [vmem] * 2,
        out_specs=[vmem] * 3,
        scratch_shapes=[
            pltpu.VMEM((PER_GROUP, blocks, rows, 2 * HD), jnp.bfloat16),
            pltpu.VMEM((PER_GROUP, 2 * HD, rows), jnp.bfloat16),
            pltpu.VMEM((PER_GROUP, HD, rows), jnp.float32),
            pltpu.VMEM((2, 8, rows), jnp.float32),
        ],
        compiler_params=params(60),
        name="attend",
    )(lengths, place, query, keys)


def three_parts(values):
    high = values.astype(jnp.bfloat16)
    rest = values - high.astype(jnp.float32)
    middle = rest.astype(jnp.bfloat16)
    low = (rest - middle.astype(jnp.float32)).astype(jnp.bfloat16)
    return high, middle, low


def attend_back_kernel(
    lengths,
    place,
    query,
    keys,
    out,
    sums,
    out_grad,
    query_grad,
    key_grad,
    key_rows,
    value_rows,
    query_aug,
    grad_aug,
    query_rows,
    grad_rows,
    query_acc,
    key_acc,
):
    blocks, rows = keys.shape[0], keys.shape[2]
    width = query.shape[1]
    groups = query.shape[0]
    bf16 = jnp.bfloat16
    documents = Documents(lengths, rows)

    def turn(j, carry):
        mark = documents.marks(j)
        for h in range(PER_GROUP):
            both = jnp.concatenate([keys[j, h * HD : (h + 1) * HD], mark], axis=0)
            key_rows[h, pl.ds(pl.multiple_of(j * rows, rows), rows)] = both.T
            values = keys[j, width + h * HD : width + (h + 1) * HD]
            place = pl.ds(pl.multiple_of(j * rows, rows), rows)
            value_rows[h, place] = jnp.concatenate([values, mark], axis=0).T
            key_acc[h, place] = jnp.zeros((rows, 2 * HD), jnp.float32)
        return carry

    lax.fori_loop(0, blocks, turn, 0)
    index = lax.broadcasted_iota(jnp.int32, (HD, rows), 0)
    none = jnp.zeros((HD, rows), bf16)

    def spread(values):
        high, middle, low = three_parts(-values)
        wide = jnp.where(index == 8, high.astype(jnp.float32), 0.0)
        wide = jnp.where(index == 9, middle.astype(jnp.float32), wide)
        return jnp.where(index == 10, low.astype(jnp.float32), wide)

    for i in range(groups):
        block = i * PEERS + place[0]
        veto = documents.veto(block)
        for h in range(PER_GROUP):
            span = slice(h * HD, (h + 1) * HD)
            part = query[i, span] * bf16(0.125)
            grad = out_grad[i, span]
            delta = jnp.sum(grad.astype(jnp.float32) * out[i, span], axis=0, keepdims=True)
            query_aug[h, :HD] = part
            query_aug[h, HD:] = (veto + spread(sums[i, h : h + 1])).astype(bf16)
            grad_aug[h, :HD] = grad
            grad_aug[h, HD:] = spread(delta).astype(bf16)
            query_rows[h] = jnp.concatenate([part, none], axis=0).T
            grad_rows[h] = jnp.concatenate([none, grad], axis=0).T
        query_acc[...] = jnp.zeros(query_acc.shape, jnp.float32)

        low, high = documents.span(block)
        steps = (high - low + 1) // 2
        low = jnp.minimum(low, blocks - 2 * steps)

        def step(n, carry):
            j = low + 2 * n
            span = pl.ds(pl.multiple_of(j * rows, rows), 2 * rows)
            for h in range(PER_GROUP):
                probs = jnp.exp(dot(key_rows[h, span], query_aug[h]))
                change = (probs * dot(value_rows[h, span], grad_aug[h])).astype(bf16)
                low_probs = probs.astype(bf16)
                key_acc[h, span] += dot(low_probs, grad_rows[h]) + dot(change, query_rows[h])
                turned = slice(h * HD, (h + 1) * HD)
                query_acc[h] += dot(keys[j, turned], change[:rows]) + dot(
                    keys[j + 1, turned], change[rows:]
                )
            return carry

        lax.fori_loop(0, steps, step, 0)
        for h in range(PER_GROUP):
            query_grad[i, h * HD : (h + 1) * HD] = (query_acc[h] * 0.125).astype(bf16)

    def finish(j, carry):
        for h in range(PER_GROUP):
            both = key_acc[h, pl.ds(pl.multiple_of(j * rows, rows), rows)].astype(bf16).T
            key_grad[j, h * HD : (h + 1) * HD] = both[:HD]
            key_grad[j, width + h * HD : width + (h + 1) * HD] = both[HD:]
        return carry

    lax.fori_loop(0, blocks, finish, 0)


def attend_back(lengths, place, query, keys, out, sums, out_grad):
    groups, width, rows = query.shape
    blocks = keys.shape[0]
    vmem = pl.BlockSpec(memory_space=pltpu.VMEM)
    bf16 = jnp.bfloat16
    return pl.pallas_call(
        attend_back_kernel,
        out_shape=[
            jax.ShapeDtypeStruct(query.shape, bf16),
            jax.ShapeDtypeStruct(keys.shape, bf16),
        ],
        in_specs=[pl.BlockSpec(memory_space=pltpu.SMEM)] * 2 + [vmem] * 5,
        out_specs=[vmem] * 2,
        scratch_shapes=[
            pltpu.VMEM((PER_GROUP, blocks * rows, 2 * HD), bf16),
            pltpu.VMEM((PER_GROUP, blocks * rows, 2 * HD), bf16),
            pltpu.VMEM((PER_GROUP, 2 * HD, rows), bf16),
            pltpu.VMEM((PER_GROUP, 2 * HD, rows), bf16),
            pltpu.VMEM((PER_GROUP, rows, 2 * HD), bf16),
            pltpu.VMEM((PER_GROUP, rows, 2 * HD), bf16),
            pltpu.VMEM((PER_GROUP, HD, rows), jnp.float32),
            pltpu.VMEM((PER_GROUP, blocks * rows, 2 * HD), jnp.float32),
        ],
        compiler_params=params(60),
        name="attend_back",
    )(lengths, place, query, keys, out, sums, out_grad)


def layer_norm(values, gain, offset):
    centre = jnp.mean(values, axis=-1, keepdims=True)
    shifted = values - centre
    spread = jnp.mean(shifted * shifted, axis=-1, keepdims=True)
    return shifted * lax.rsqrt(spread + epsilon) * gain + offset


def exact_gelu(values):
    return jax.nn.gelu(values, approximate=False)


def doc_index(positions, doc_starts):
    hits = (doc_starts[None, :] <= positions[:, None]).astype(jnp.int32)
    return jnp.sum(hits, axis=1) - 1


def body(
    patches,
    doc_lengths,
    norm1_gain,
    norm1_bias,
    w_qkv,
    b_qv,
    w_out,
    b_out,
    norm2_gain,
    norm2_bias,
    w_up,
    b_up,
    w_down,
    b_down,
    cotangent,
):
    f32, bf16 = jnp.float32, jnp.bfloat16
    rows, width = patches.shape[1:]
    ctx_place = lax.axis_index("ctx")
    blocks = lax.axis_size("ctx")
    place = (ctx_place % PEERS).astype(jnp.int32).reshape(1)
    vectors = [norm1_gain, norm1_bias, b_qv, b_out, norm2_gain, norm2_bias, b_up, b_down]
    pack = Packed([v.shape[0] for v in vectors])
    query, keys, normed1, small, qkv_far, out_far, up_far, down_got, down_part = front(
        pack, patches[0], pack.pack(vectors), w_qkv, w_out, w_up, w_down
    )
    down_far = lax.ppermute(down_part, "wsh", [(0, 1), (1, 0)])
    out_heads, heads_low, sums = attend(doc_lengths, place, query, keys)
    tiles = w_up.shape[1] // width
    chunks = 2 * tiles + 1 + w_qkv.shape[1] // width
    ahead = tiles
    firsts = ["x"] * ahead + ["y"] * (chunks - ahead)
    mixed, hidden_grad, grad_heads, send_over_x, send_over_y, send_rest, keep, vector = middle(
        pack, firsts, ahead, heads_low, patches[0], cotangent[0], small, w_out, out_far, w_up,
        up_far, w_down, down_got, down_far,
    )
    across = [(c, c + 2 - c // 2 % 2 * 4) for c in range(blocks)]
    ahead_x = lax.ppermute(send_over_x, "ctx", across)
    ahead_y = lax.ppermute(send_over_y, "wsh", [(0, 1), (1, 0)])
    query_grad, key_grad = attend_back(
        doc_lengths, place, query, keys, out_heads, sums, grad_heads
    )
    inputs_grad, down_total, up_total, out_total, qkv_total, vector_total = last(
        pack, firsts, query_grad, key_grad, normed1, w_qkv, qkv_far, patches[0], hidden_grad, small,
        ahead_x, ahead_y, send_rest, keep, vector,
    )
    shares = pack.unpack(vector_total)
    return (
        mixed[None],
        inputs_grad[None],
        shares[0],
        shares[1],
        qkv_total.astype(f32),
        shares[2],
        out_total.astype(f32),
        shares[3],
        shares[4],
        shares[5],
        up_total.astype(f32),
        shares[6],
        down_total.astype(f32),
        shares[7],
    )


def shifted_2(block, axis, distance):
    devices = range(lax.axis_size(axis))
    route = [((i - distance) % len(devices), i) for i in devices]
    return lax.ppermute(block, axis, route)


def any_mesh_body(
    patches,
    doc_lengths,
    norm1_gain,
    norm1_bias,
    w_qkv,
    b_qv,
    w_out,
    b_out,
    norm2_gain,
    norm2_bias,
    w_up,
    b_up,
    w_down,
    b_down,
    cotangent,
):
    tok_rows = patches.shape[1]
    model_width = patches.shape[2]
    ctx_size = lax.axis_size("ctx")
    ctx_place = lax.axis_index("ctx")
    gathered = (
        lax.all_gather(norm1_gain, "wsh", axis=0, tiled=True),
        lax.all_gather(norm1_bias, "wsh", axis=0, tiled=True),
        lax.all_gather(w_qkv, "wsh", axis=0, tiled=True),
        lax.all_gather(b_qv, "wsh", axis=0, tiled=True),
        lax.all_gather(w_out, "wsh", axis=0, tiled=True),
        lax.all_gather(b_out, "wsh", axis=0, tiled=True),
        lax.all_gather(norm2_gain, "wsh", axis=0, tiled=True),
        lax.all_gather(norm2_bias, "wsh", axis=0, tiled=True),
        lax.all_gather(w_up, "wsh", axis=0, tiled=True),
        lax.all_gather(b_up, "wsh", axis=0, tiled=True),
        lax.all_gather(w_down, "wsh", axis=0, tiled=True),
        lax.all_gather(b_down, "wsh", axis=0, tiled=True),
    )
    (
        gain1,
        bias1,
        wqkv_full,
        bqv_full,
        wout_full,
        bout_full,
        gain2,
        bias2,
        wup_full,
        bup_full,
        wdown_full,
        bdown_full,
    ) = gathered
    inputs = patches[0].astype(jnp.float32)
    lengths = doc_lengths[0]
    doc_starts = jnp.cumsum(lengths) - lengths
    row_offsets = lax.iota(jnp.int32, tok_rows)
    query_docs = doc_index(ctx_place * tok_rows + row_offsets, doc_starts)
    gain1_float = gain1.astype(jnp.float32)
    bias1_float = bias1.astype(jnp.float32)
    normed1 = layer_norm(inputs, gain1_float, bias1_float).astype(jnp.bfloat16)
    projected = jnp.dot(normed1, wqkv_full, preferred_element_type=jnp.float32)
    bqv_float = bqv_full.astype(jnp.float32)
    query_low = (projected[:, :model_width] + bqv_float[:model_width]).astype(jnp.bfloat16)
    key_low = projected[:, model_width : 2 * model_width].astype(jnp.bfloat16)
    value_low = (projected[:, 2 * model_width :] + bqv_float[model_width:]).astype(jnp.bfloat16)
    query_heads = query_low.reshape(tok_rows, H, HD)

    def attend_block(state, key_block, value_block, key_start):
        run_max, run_total, run_acc = state
        key_docs = doc_index(key_start + row_offsets, doc_starts)
        same_doc = (query_docs[:, None] == key_docs[None, :])[None]
        scores = (
            jnp.einsum(
                "qhd,khd->hqk",
                query_heads,
                key_block.reshape(tok_rows, H, HD),
                preferred_element_type=jnp.float32,
            )
            * 0.125
        )
        scores = jnp.where(same_doc, scores, masked_score)
        new_max = jnp.maximum(run_max, jnp.max(scores, axis=2))
        weights = jnp.where(same_doc, jnp.exp(scores - new_max[:, :, None]), 0.0)
        factor = jnp.exp(run_max - new_max)
        new_total = run_total * factor + jnp.sum(weights, axis=2)
        new_acc = run_acc * factor[:, :, None] + jnp.einsum(
            "hqk,khd->hqd",
            weights.astype(jnp.bfloat16),
            value_block.reshape(tok_rows, H, HD),
            preferred_element_type=jnp.float32,
        )
        return (new_max, new_total, new_acc)

    initial = (
        jnp.full((H, tok_rows), masked_score, jnp.float32),
        jnp.zeros((H, tok_rows), jnp.float32),
        jnp.zeros((H, tok_rows, HD), jnp.float32),
    )
    state = initial
    key_piece = lax.all_gather(key_low, "ctx", axis=0, tiled=True)
    value_piece = lax.all_gather(value_low, "ctx", axis=0, tiled=True)
    blocks = key_piece.shape[0] // tok_rows
    key_blocks = key_piece.reshape(blocks, tok_rows, model_width)
    value_blocks = value_piece.reshape(blocks, tok_rows, model_width)
    block_starts = tok_rows * lax.iota(jnp.int32, blocks)

    def one_block(inner, item):
        key_block, value_block, key_start = item
        return (attend_block(inner, key_block, value_block, key_start), None)

    state, unused = lax.scan(one_block, state, (key_blocks, value_blocks, block_starts))
    run_max, run_total, run_acc = state
    log_total = run_max + jnp.log(run_total)
    attended = jnp.transpose(run_acc / run_total[:, :, None], (1, 0, 2)).reshape(
        tok_rows, model_width
    )
    attended_low = attended.astype(jnp.bfloat16)
    branch = jnp.dot(
        attended_low, wout_full, preferred_element_type=jnp.float32
    ) + bout_full.astype(jnp.float32)
    hidden_sum = inputs + branch
    gain2_float = gain2.astype(jnp.float32)
    bias2_float = bias2.astype(jnp.float32)
    normed2 = layer_norm(hidden_sum, gain2_float, bias2_float).astype(jnp.bfloat16)
    pre_act = jnp.dot(normed2, wup_full, preferred_element_type=jnp.float32) + bup_full.astype(
        jnp.float32
    )
    activated = exact_gelu(pre_act).astype(jnp.bfloat16)
    mixed = (
        hidden_sum
        + jnp.dot(activated, wdown_full, preferred_element_type=jnp.float32)
        + bdown_full.astype(jnp.float32)
    )
    back_gain1 = gathered[0].astype(jnp.float32)
    back_bias1 = gathered[1].astype(jnp.float32)
    back_wqkv = gathered[2]
    back_wout = gathered[4]
    back_gain2 = gathered[6].astype(jnp.float32)
    back_bias2 = gathered[7].astype(jnp.float32)
    back_wup = gathered[8]
    back_wdown = gathered[10]
    out_grad = cotangent[0]
    wdown_grad = jnp.einsum("tf,td->fd", activated, out_grad, preferred_element_type=jnp.float32)
    bdown_grad = jnp.sum(out_grad.astype(jnp.float32), axis=0)
    act_grad = jnp.einsum("td,fd->tf", out_grad, back_wdown, preferred_element_type=jnp.float32)
    unused_act, gelu_back = jax.vjp(exact_gelu, pre_act)
    pre_grad = gelu_back(act_grad)[0].astype(jnp.bfloat16)
    wup_grad = jnp.einsum("tc,tf->cf", normed2, pre_grad, preferred_element_type=jnp.float32)
    bup_grad = jnp.sum(pre_grad.astype(jnp.float32), axis=0)
    normed2_grad = jnp.einsum("tf,cf->tc", pre_grad, back_wup, preferred_element_type=jnp.float32)
    unused_norm2, norm2_back = jax.vjp(layer_norm, hidden_sum, back_gain2, back_bias2)
    hidden_part, gain2_grad, bias2_grad = norm2_back(normed2_grad)
    hidden_grad = out_grad.astype(jnp.float32) + hidden_part
    branch_grad = hidden_grad.astype(jnp.bfloat16)
    wout_grad = jnp.einsum(
        "tc,td->cd", attended_low, branch_grad, preferred_element_type=jnp.float32
    )
    bout_grad = jnp.sum(branch_grad.astype(jnp.float32), axis=0)
    attended_grad = jnp.einsum(
        "td,cd->tc", branch_grad, back_wout, preferred_element_type=jnp.float32
    ).astype(jnp.bfloat16)
    delta = jnp.sum(
        (attended_grad.astype(jnp.float32) * attended).reshape(tok_rows, H, HD), axis=2
    ).T
    grad_heads = attended_grad.reshape(tok_rows, H, HD)

    def back_block(state, anchor):
        key_start = anchor * tok_rows
        key_cur, value_cur, key_grad, value_grad, query_grad = state
        key_docs = doc_index(key_start + row_offsets, doc_starts)
        same_doc = (query_docs[:, None] == key_docs[None, :])[None]
        key_heads = key_cur.reshape(tok_rows, H, HD)
        scores = (
            jnp.einsum("qhd,khd->hqk", query_heads, key_heads, preferred_element_type=jnp.float32)
            * 0.125
        )
        probs = jnp.where(same_doc, jnp.exp(scores - log_total[:, :, None]), 0.0)
        value_grad = value_grad + jnp.einsum(
            "hqk,qhd->khd",
            probs.astype(jnp.bfloat16),
            grad_heads,
            preferred_element_type=jnp.float32,
        ).reshape(tok_rows, model_width)
        prob_grad = jnp.einsum(
            "qhd,khd->hqk",
            grad_heads,
            value_cur.reshape(tok_rows, H, HD),
            preferred_element_type=jnp.float32,
        )
        score_grad = (probs * (prob_grad - delta[:, :, None])).astype(jnp.bfloat16)
        query_grad = (
            query_grad
            + jnp.einsum(
                "hqk,khd->qhd", score_grad, key_heads, preferred_element_type=jnp.float32
            ).reshape(tok_rows, model_width)
            * 0.125
        )
        key_grad = (
            key_grad
            + jnp.einsum(
                "hqk,qhd->khd", score_grad, query_heads, preferred_element_type=jnp.float32
            ).reshape(tok_rows, model_width)
            * 0.125
        )
        return (key_cur, value_cur, key_grad, value_grad, query_grad)

    def pass_on(state):
        key_cur, value_cur, key_grad, value_grad, query_grad = state
        moved_keys = shifted_2((key_cur, value_cur), "ctx", 1)
        moved_sums = (
            shifted_2(key_grad.astype(jnp.bfloat16), "ctx", 1).astype(key_grad.dtype),
            shifted_2(value_grad.astype(jnp.bfloat16), "ctx", 1).astype(value_grad.dtype),
        )
        return (moved_keys[0], moved_keys[1], moved_sums[0], moved_sums[1], query_grad)

    def two_steps(turn, state):
        state = pass_on(back_block(state, (ctx_place - 2 * turn) % ctx_size))
        state = pass_on(back_block(state, (ctx_place - 2 * turn - 1) % ctx_size))
        return state

    zero_rows = jnp.zeros((tok_rows, model_width), jnp.float32)
    final_state = lax.fori_loop(
        0, ctx_size // 2, two_steps, (key_low, value_low, zero_rows, zero_rows, zero_rows)
    )
    key_grad_low = final_state[2].astype(jnp.bfloat16)
    value_grad_low = final_state[3].astype(jnp.bfloat16)
    query_grad_low = final_state[4].astype(jnp.bfloat16)
    projected_grad = jnp.concatenate([query_grad_low, key_grad_low, value_grad_low], axis=1)
    wqkv_grad = jnp.einsum("tc,te->ce", normed1, projected_grad, preferred_element_type=jnp.float32)
    bqv_grad = jnp.concatenate(
        [
            jnp.sum(query_grad_low.astype(jnp.float32), axis=0),
            jnp.sum(value_grad_low.astype(jnp.float32), axis=0),
        ]
    )
    normed1_grad = jnp.einsum(
        "te,ce->tc", projected_grad, back_wqkv, preferred_element_type=jnp.float32
    )
    unused_norm1, norm1_back = jax.vjp(layer_norm, inputs, back_gain1, back_bias1)
    input_part, gain1_grad, bias1_grad = norm1_back(normed1_grad)
    inputs_grad = hidden_grad + input_part
    shares = (
        lax.psum_scatter(
            gain1_grad.astype(jnp.bfloat16), "wsh", scatter_dimension=0, tiled=True
        ).astype(jnp.float32),
        lax.psum_scatter(
            bias1_grad.astype(jnp.bfloat16), "wsh", scatter_dimension=0, tiled=True
        ).astype(jnp.float32),
        lax.psum_scatter(
            wqkv_grad.astype(jnp.bfloat16), "wsh", scatter_dimension=0, tiled=True
        ).astype(jnp.float32),
        lax.psum_scatter(
            bqv_grad.astype(jnp.bfloat16), "wsh", scatter_dimension=0, tiled=True
        ).astype(jnp.float32),
        lax.psum_scatter(
            wout_grad.astype(jnp.bfloat16), "wsh", scatter_dimension=0, tiled=True
        ).astype(jnp.float32),
        lax.psum_scatter(
            bout_grad.astype(jnp.bfloat16), "wsh", scatter_dimension=0, tiled=True
        ).astype(jnp.float32),
        lax.psum_scatter(
            gain2_grad.astype(jnp.bfloat16), "wsh", scatter_dimension=0, tiled=True
        ).astype(jnp.float32),
        lax.psum_scatter(
            bias2_grad.astype(jnp.bfloat16), "wsh", scatter_dimension=0, tiled=True
        ).astype(jnp.float32),
        lax.psum_scatter(
            wup_grad.astype(jnp.bfloat16), "wsh", scatter_dimension=0, tiled=True
        ).astype(jnp.float32),
        lax.psum_scatter(
            bup_grad.astype(jnp.bfloat16), "wsh", scatter_dimension=0, tiled=True
        ).astype(jnp.float32),
        lax.psum_scatter(
            wdown_grad.astype(jnp.bfloat16), "wsh", scatter_dimension=0, tiled=True
        ).astype(jnp.float32),
        lax.psum_scatter(
            bdown_grad.astype(jnp.bfloat16), "wsh", scatter_dimension=0, tiled=True
        ).astype(jnp.float32),
    )
    totals = (
        lax.psum(shares[0].astype(jnp.bfloat16), "ctx").astype(jnp.float32),
        lax.psum(shares[1].astype(jnp.bfloat16), "ctx").astype(jnp.float32),
        lax.psum(shares[2].astype(jnp.bfloat16), "ctx").astype(jnp.float32),
        lax.psum(shares[3].astype(jnp.bfloat16), "ctx").astype(jnp.float32),
        lax.psum(shares[4].astype(jnp.bfloat16), "ctx").astype(jnp.float32),
        lax.psum(shares[5].astype(jnp.bfloat16), "ctx").astype(jnp.float32),
        lax.psum(shares[6].astype(jnp.bfloat16), "ctx").astype(jnp.float32),
        lax.psum(shares[7].astype(jnp.bfloat16), "ctx").astype(jnp.float32),
        lax.psum(shares[8].astype(jnp.bfloat16), "ctx").astype(jnp.float32),
        lax.psum(shares[9].astype(jnp.bfloat16), "ctx").astype(jnp.float32),
        lax.psum(shares[10].astype(jnp.bfloat16), "ctx").astype(jnp.float32),
        lax.psum(shares[11].astype(jnp.bfloat16), "ctx").astype(jnp.float32),
    )
    return (
        mixed.astype(jnp.bfloat16)[None],
        inputs_grad[None],
        totals[0],
        totals[1],
        totals[2],
        totals[3],
        totals[4],
        totals[5],
        totals[6],
        totals[7],
        totals[8],
        totals[9],
        totals[10],
        totals[11],
    )


def solution(mesh):
    as_planned = mesh.shape["ctx"] == GROUPS * PEERS and mesh.shape["wsh"] == 2
    return jax.shard_map(
        body if as_planned else any_mesh_body,
        mesh=mesh,
        in_specs=(
            P("wsh", "ctx", None),
            P("wsh", None),
            P("wsh"),
            P("wsh"),
            P("wsh", None),
            P("wsh"),
            P("wsh", None),
            P("wsh"),
            P("wsh"),
            P("wsh"),
            P("wsh", None),
            P("wsh"),
            P("wsh", None),
            P("wsh"),
            P("wsh", "ctx", None),
        ),
        out_specs=(
            P("wsh", "ctx", None),
            P("wsh", "ctx", None),
            P("wsh"),
            P("wsh"),
            P("wsh", None),
            P("wsh"),
            P("wsh", None),
            P("wsh"),
            P("wsh"),
            P("wsh"),
            P("wsh", None),
            P("wsh"),
            P("wsh", None),
            P("wsh"),
        ),
        check_vma=False,
    )
```

```python
import functools

import jax
import jax.numpy as jnp
from jax import lax
from jax.experimental import pallas as pl
from jax.experimental.pallas import tpu as pltpu
from jax.sharding import PartitionSpec as P

H = 12
HD = 64
GROUPS = 4
PER_GROUP = H // GROUPS
PEERS = 4
MESH = pl.DeviceIdType.MESH
MIB = 2**20

epsilon = 1e-05
masked_score = -1e30


def params(vmem_mib, collective_id=None):
    if collective_id is None:
        return pltpu.CompilerParams(vmem_limit_bytes=vmem_mib * MIB)
    return pltpu.CompilerParams(
        vmem_limit_bytes=vmem_mib * MIB, collective_id=collective_id, has_side_effects=True
    )


def here():
    ctx = lax.axis_index("ctx")
    return ctx // PEERS, (ctx // 2) % 2, ctx % 2, lax.axis_index("wsh")


def at(z, x, core, y):
    return (z * PEERS + x * 2 + core, y)


def remote(src, dst, send, recv, device):
    return pltpu.make_async_remote_copy(
        src_ref=src,
        dst_ref=dst,
        send_sem=send,
        recv_sem=recv,
        device_id=device,
        device_id_type=MESH,
    )


def greet(devices):
    barrier = pltpu.get_barrier_semaphore()
    for device in devices:
        pl.semaphore_signal(barrier, inc=1, device_id=device, device_id_type=MESH)
    pl.semaphore_wait(barrier, len(devices))


def dot(left, right):
    return jnp.dot(left, right, preferred_element_type=jnp.float32)


def dot_turned(left, right):
    return lax.dot_general(
        left, right, (((1,), (1,)), ((), ())), preferred_element_type=jnp.float32
    )


def normalise(values):
    centre = jnp.mean(values, axis=-1, keepdims=True)
    shifted = values - centre
    spread = jnp.mean(shifted * shifted, axis=-1, keepdims=True)
    scale = lax.rsqrt(spread + epsilon)
    return shifted * scale, scale


def normalise_back(grad, gain, normed, scale):
    inner = grad * gain
    centre = jnp.mean(inner, axis=-1, keepdims=True)
    along = jnp.mean(inner * normed, axis=-1, keepdims=True)
    gain_grad = jnp.sum(grad * normed, axis=0, keepdims=True)
    bias_grad = jnp.sum(grad, axis=0, keepdims=True)
    return scale * (inner - centre - normed * along), gain_grad, bias_grad


LANES = 128


class Packed:
    names = ("gain1", "bias1", "bqv", "bout", "gain2", "bias2", "bup", "bdown")

    def __init__(self, sizes):
        self.sizes = dict(zip(self.names, sizes))
        self.starts, row = {}, 0
        for name in self.names:
            self.starts[name] = row
            row += self.sizes[name] // LANES
        self.used = row
        self.rows = row + -row % 8

    def pack(self, halves):
        total, flat = self.rows * LANES, 0.0
        for name, half in zip(self.names, halves):
            start = self.starts[name] * LANES
            after = total - start - half.shape[0]
            flat += jnp.pad(half.astype(jnp.float32), (start, after))
        return flat.reshape(-1, LANES)

    def read(self, ref, name, first=0, count=None):
        count = 2 * self.sizes[name] if count is None else count
        parts = []
        for lane in range(first, first + count, LANES):
            y, inner = divmod(lane, self.sizes[name])
            row = self.starts[name] + inner // LANES
            parts.append(ref[y, row : row + 1])
        return jnp.concatenate(parts, axis=1)

    def write(self, ref, name, values, first=0):
        for lane in range(0, values.shape[1], LANES):
            y, inner = divmod(first + lane, self.sizes[name])
            row = self.starts[name] + inner // LANES
            ref[y, row : row + 1] = values[:, lane : lane + LANES]

    def unpack(self, rows):
        flat = rows[: self.used].reshape(-1)
        parts, start = [], 0
        for name in self.names:
            parts.append(flat[start : start + self.sizes[name]])
            start += self.sizes[name]
        return parts


class Sender:
    def __init__(self):
        self.copies = []

    def __call__(self, src, dst, send, recv, device):
        copy = remote(src, dst, send, recv, device)
        copy.start()
        self.copies.append(copy)

    def finish(self):
        for copy in self.copies:
            copy.wait_send()


def front_kernel(
    pack,
    patches,
    small_half,
    qkv_half,
    out_half,
    up_half,
    down_half,
    query,
    keys,
    normed_low,
    small,
    qkv_far,
    out_far,
    up_far,
    down_got,
    down_part,
    qkv_own,
    staged,
    local,
    small_sem,
    ysend,
    yrecv,
    xsend,
    xrecv,
    csend,
    crecv,
    fsend,
    frecv,
    psend,
    precv,
    nsend,
    nrecv,
    pxsend,
    pxrecv,
    pfsend,
    pfrecv,
    query_send,
    query_recv,
    zsend,
    zrecv,
    kxsend,
    kxrecv,
    kcsend,
    kcrecv,
    kfsend,
    kfrecv,
):
    bf16 = jnp.bfloat16
    z, x, core, y = here()
    over_x, over_core, over_y = (
        at(z, 1 - x, core, y),
        at(z, x, 1 - core, y),
        at(z, x, core, 1 - y),
    )
    around = [at((z + d) % GROUPS, x, core, y) for d in range(1, GROUPS)]
    rows, width = patches.shape
    part = query.shape[1]
    half = qkv_half.shape[0]
    quarter = half // PEERS
    down, later = down_half.shape[0] // 2, down_part.shape[0]
    sooner = down - later
    greet(around + [over_x, over_core, over_y])
    go = Sender()

    def landed(view, sem):
        remote(view, view, sem, sem, over_core).wait_recv()

    def columns(b):
        return pl.ds(b * width, width)

    def share(px, pcore, b):
        return qkv_far.at[pl.ds((px * 2 + pcore) * quarter, quarter), columns(b)]

    order = (1, 2, 0)
    go(small_half, small.at[y], small_sem.at[0], small_sem.at[1], over_y)
    for b in order:
        src = qkv_half.at[pl.ds((x * 2 + core) * quarter, quarter), columns(b)]
        go(src, share(x, core, b), ysend.at[b], yrecv.at[b], over_y)
    copies = [
        pltpu.make_async_copy(small_half, small.at[y], local.at[0]),
        pltpu.make_async_copy(qkv_half, qkv_own, local.at[1]),
        pltpu.make_async_copy(
            down_half.at[pl.ds(core * down + sooner, later)], down_part, local.at[2]
        ),
    ]
    for copy in copies:
        copy.start()

    step = quarter // 2
    pieces = [(up_half, up_far, quarter, quarter, step, i * step, half // 2) for i in range(2)]
    shared = len(pieces)
    pieces += [(out_half, out_far, half // 2, half // 2, half // 2, 0, 0)]
    step = sooner // 2
    pieces += [(down_half, down_got, down, sooner, step, i * step, 0) for i in range(2)]

    def piece_view(k, px, pcore):
        unused, full, unused, apart, count, first, across = pieces[k]
        return full.at[pl.ds(px * across + pcore * apart + first, count)]

    def piece_in(k):
        view = piece_view(k, x, core)
        landed(view, precv.at[k])
        if k < shared:
            go(view, view, pxsend.at[k], pxrecv.at[k], over_x)
        go(view, view, nsend.at[k], nrecv.at[k], over_core)

    def piece_over(k):
        view = piece_view(k, 1 - x, core)
        landed(view, pxrecv.at[k])
        go(view, view, pfsend.at[k], pfrecv.at[k], over_core)

    copies[0].wait()
    landed(small.at[1 - y], small_sem.at[1])
    normed, scale = normalise(patches[...].astype(jnp.float32))
    low = (normed * pack.read(small, "gain1") + pack.read(small, "bias1")).astype(bf16)
    normed_low[...] = low
    low_own = jnp.where(y == 0, low[:, :half], low[:, half:])
    low_far = jnp.where(y == 0, low[:, half:], low[:, :half])
    for i, b in enumerate(order):
        view = share(x, core, b)
        landed(view, yrecv.at[b])
        go(view, view, xsend.at[b], xrecv.at[b], over_x)
        go(view, view, csend.at[b], crecv.at[b], over_core)
    for k, (src, unused, apart, unused, count, first, across) in enumerate(pieces):
        span = pl.ds(x * across + core * apart + first, count)
        go(src.at[span], piece_view(k, x, core), psend.at[k], precv.at[k], over_y)

    copies[1].wait()

    def block(pz, px, pcore, b):
        return keys.at[pz * PEERS + px * 2 + pcore, pl.ds((b - 1) * part, part)]

    own = []
    for i, b in enumerate(order):
        view = share(1 - x, core, b)
        landed(view, xrecv.at[b])
        go(view, view, fsend.at[b], frecv.at[b], over_core)
        landed(share(x, 1 - core, b), crecv.at[b])
        landed(share(1 - x, 1 - core, b), frecv.at[b])
        made = dot(low_own, qkv_own[:, b * width : (b + 1) * width])
        made = made + dot(low_far, qkv_far[:, b * width : (b + 1) * width])
        if b != 1:
            made = made + pack.read(small, "bqv", (b // 2) * width, width)
        staged[b] = made.astype(bf16).T.reshape(GROUPS, part, rows)
        for d in (2, 1, 3):
            target = (z + d) % GROUPS
            if b == 0:
                dst, sems = query.at[z], (query_send.at[d], query_recv.at[d])
            else:
                sem = (b - 1) * GROUPS + d
                dst, sems = block(z, x, core, b), (zsend.at[sem], zrecv.at[sem])
            go(staged.at[b, target], dst, sems[0], sems[1], around[d - 1])
        dst = query.at[z] if b == 0 else block(z, x, core, b)
        own.append(pltpu.make_async_copy(staged.at[b, z], dst, local.at[3 + i]))
        own[-1].start()
        if b > 0:
            sem = (b - 1) * GROUPS
            go(staged.at[b, z], dst, kxsend.at[sem], kxrecv.at[sem], over_x)
            go(staged.at[b, z], dst, kcsend.at[sem], kcrecv.at[sem], over_core)

    sequence = [(1, 0), (2, 0)] + [(b, d) for b in (1, 2) for d in (1, 3, 2)]
    for i in range(len(sequence) + 1):
        if i < len(sequence):
            b, d = sequence[i]
            sem = (b - 1) * GROUPS + d
            if d > 0:
                view = block((z + GROUPS - d) % GROUPS, x, core, b)
                landed(view, zrecv.at[sem])
                go(view, view, kxsend.at[sem], kxrecv.at[sem], over_x)
                go(view, view, kcsend.at[sem], kcrecv.at[sem], over_core)
        if i >= 1:
            b, d = sequence[i - 1]
            sem = (b - 1) * GROUPS + d
            view = block((z + GROUPS - d) % GROUPS, 1 - x, core, b)
            landed(view, kxrecv.at[sem])
            go(view, view, kfsend.at[sem], kfrecv.at[sem], over_core)
        if 2 <= i < 2 + shared:
            piece_in(i - 2)
    for k in range(shared, len(pieces)):
        piece_in(k)
    for k in range(shared):
        piece_over(k)
    for b, d in sequence:
        sem = (b - 1) * GROUPS + d
        pz = (z + GROUPS - d) % GROUPS
        landed(block(pz, x, 1 - core, b), kcrecv.at[sem])
        landed(block(pz, 1 - x, 1 - core, b), kfrecv.at[sem])
    for d in range(1, GROUPS):
        landed(query.at[(z + GROUPS - d) % GROUPS], query_recv.at[d])
    for k in range(len(pieces)):
        landed(piece_view(k, x, 1 - core), nrecv.at[k])
    for k in range(shared):
        landed(piece_view(k, 1 - x, 1 - core), pfrecv.at[k])
    for copy in copies[2:] + own:
        copy.wait()
    go.finish()


def front(pack, patches, small_half, qkv_half, out_half, up_half, down_half):
    f32, bf16 = jnp.float32, jnp.bfloat16
    vmem = pl.BlockSpec(memory_space=pltpu.VMEM)
    hbm = pl.BlockSpec(memory_space=pltpu.HBM)
    rows, width = patches.shape
    part, half = width // GROUPS, qkv_half.shape[0]
    dma = pltpu.SemaphoreType.DMA

    def pair(n):
        return [dma((n,))] * 2

    return pl.pallas_call(
        functools.partial(front_kernel, pack),
        out_shape=[
            jax.ShapeDtypeStruct((GROUPS, part, rows), bf16),
            jax.ShapeDtypeStruct((GROUPS * PEERS, 2 * part, rows), bf16),
            jax.ShapeDtypeStruct((rows, width), bf16),
            jax.ShapeDtypeStruct((2,) + small_half.shape, f32),
            jax.ShapeDtypeStruct(qkv_half.shape, bf16),
            jax.ShapeDtypeStruct(out_half.shape, bf16),
            jax.ShapeDtypeStruct(up_half.shape, bf16),
            jax.ShapeDtypeStruct((down_half.shape[0] // 2, width), bf16),
            jax.ShapeDtypeStruct((down_half.shape[0] // 4, width), bf16),
        ],
        in_specs=[vmem, hbm, hbm, hbm, hbm, hbm],
        out_specs=[vmem] * 9,
        scratch_shapes=[
            pltpu.VMEM(qkv_half.shape, bf16),
            pltpu.VMEM((3, GROUPS, part, rows), bf16),
            dma((6,)),
        ]
        + [dma((2,))]
        + pair(3) * 4
        + pair(5) * 2
        + pair(2) * 2
        + pair(GROUPS)
        + pair(2 * GROUPS) * 4,
        compiler_params=params(60, 1),
        name="front",
    )(patches, small_half, qkv_half, out_half, up_half, down_half)


def split_rows(first, x, y, quarter):
    if first == "y":
        return [((1 - y) * 2 * quarter, 2 * quarter)], [(y * 2 * quarter, 2 * quarter)]
    other, mine = (1 - x) * quarter, x * quarter
    return (
        [(other, quarter), (2 * quarter + other, quarter)],
        [(mine, quarter), (2 * quarter + mine, quarter)],
    )


def core_sum(first, own, land, send_ref, keep_ref, x, y):
    quarter = land.shape[0] // 4
    gone, kept = split_rows(first, x, y, quarter)
    for ref, parts in ((send_ref, gone), (keep_ref, kept)):
        place = 0
        for start, count in parts:
            rows = pl.ds(start, count)
            total = own(rows).astype(jnp.float32) + land[rows].astype(jnp.float32)
            ref[pl.ds(place, count)] = total.astype(ref.dtype)
            place += count


def middle_kernel(
    pack,
    firsts,
    heads,
    patches,
    out_grad,
    small,
    w_out,
    w_out_far,
    w_up,
    w_up_far,
    w_down_half,
    w_down_got,
    w_down_far,
    mixed,
    hidden_grad,
    grad_heads,
    send_over_x,
    send_over_y,
    send_rest,
    keep,
    vector,
    o_land,
    o_grad,
    wout,
    wup,
    wdown,
    act_grad,
    act_turned,
    pre_grad,
    bup_rows,
    grads,
    c_land,
    local,
    osend,
    orecv,
    gsend,
    grecv,
    wsem,
    csend,
    crecv,
):
    f32, bf16 = jnp.float32, jnp.bfloat16
    z, x, core, y = here()
    over_core = at(z, x, 1 - core, y)
    around = [at((z + d) % GROUPS, x, core, y) for d in range(1, GROUPS)]
    rows, width = patches.shape
    tiles = wdown.shape[0] // width
    half = w_down_half.shape[0]
    far = w_down_far.shape[0]
    greet(around + [over_core])
    go = Sender()
    near = half // 2 - far
    far_rows = pl.ds((1 - y) * half + core * (half // 2) + near, far)
    other_rows = pl.ds((1 - y) * half + (1 - core) * (half // 2) + near, far)
    for d in (2, 1, 3):
        go(heads.at[(z + d) % GROUPS], o_land.at[z], osend.at[d], orecv.at[d], around[d - 1])
    go(w_down_far, wdown.at[far_rows], wsem.at[0], wsem.at[1], over_core)
    down_copies = [
        pltpu.make_async_copy(w_down_half, wdown.at[pl.ds(y * half, half)], local.at[0]),
        pltpu.make_async_copy(w_down_far, wdown.at[far_rows], local.at[1]),
    ]
    for c in range(2):
        src = w_down_got.at[pl.ds(c * near, near)]
        dst = wdown.at[pl.ds((1 - y) * half + c * (half // 2), near)]
        down_copies.append(pltpu.make_async_copy(src, dst, local.at[8 + c]))
    copies = [
        pltpu.make_async_copy(heads.at[z], o_land.at[z], local.at[2]),
    ]
    pairs = [(w_out, wout, y), (w_out_far, wout, 1 - y), (w_up, wup, y), (w_up_far, wup, 1 - y)]
    for i, (src, dst, side) in enumerate(pairs):
        count = src.shape[0]
        span = pl.ds(side * count, count)
        copies.append(pltpu.make_async_copy(src, dst.at[span], local.at[4 + i]))

    for copy in down_copies + copies:
        copy.start()
    dy = out_grad[...]
    vector[...] = jnp.zeros(vector.shape, f32)
    pack.write(vector, "bdown", jnp.sum(dy.astype(f32), axis=0, keepdims=True))
    for f in range(tiles):
        bup_rows[f, 0:1] = pack.read(small, "bup", f * width, width)
    for copy in down_copies:
        copy.wait()
    landed = wdown.at[other_rows]
    remote(landed, landed, wsem.at[0], wsem.at[1], over_core).wait_recv()

    def tile(f):
        return pl.ds(pl.multiple_of(f * width, width), width)

    def first_grad(f, carry):
        act_grad[f] = dot_turned(dy, wdown[tile(f)])
        return carry

    lax.fori_loop(0, tiles, first_grad, 0)
    for copy in copies:
        copy.wait()
    for d in range(1, GROUPS):
        landed = o_land.at[(z + GROUPS - d) % GROUPS]
        remote(landed, landed, osend.at[d], orecv.at[d], over_core).wait_recv()
    turned = o_land[...].reshape(width, rows)
    hidden = patches[...].astype(f32) + (dot(turned.T, wout[...]) + pack.read(small, "bout"))
    gain2 = pack.read(small, "gain2")
    normed, scale = normalise(hidden)
    c = (normed * gain2 + pack.read(small, "bias2")).astype(bf16)
    mixed_acc = hidden + pack.read(small, "bdown")
    c_grad = jnp.zeros((rows, width), f32)

    def forward_back(f, carry):
        mixed_acc, c_grad = carry
        up = wup[:, tile(f)]
        pre = dot(c, up) + bup_rows[f, 0:1]
        share = 0.5 + 0.5 * lax.erf(pre * (0.5**0.5))
        slope = share + pre * jnp.exp(-0.5 * pre * pre) * ((0.5 / jnp.pi) ** 0.5)
        act = (pre * share).astype(bf16)
        grad = (act_grad[f] * slope).astype(bf16)
        act_turned[tile(f)] = act.T
        pre_grad[f] = grad
        bup_rows[f, 0:1] = jnp.sum(grad.astype(f32), axis=0, keepdims=True)
        return (
            mixed_acc + dot(act, wdown[tile(f)]),
            c_grad + dot_turned(grad, up),
        )

    mixed_acc, c_grad = lax.fori_loop(0, tiles, forward_back, (mixed_acc, c_grad))
    mixed[...] = mixed_acc.astype(bf16)
    for f in range(tiles):
        pack.write(vector, "bup", bup_rows[f, 0:1], f * width)
    part, gain_grad, bias_grad = normalise_back(c_grad, gain2, normed, scale)
    pack.write(vector, "gain2", gain_grad)
    pack.write(vector, "bias2", bias_grad)
    whole = dy.astype(f32) + part
    hidden_grad[...] = whole
    dz = whole.astype(bf16)
    pack.write(vector, "bout", jnp.sum(dz.astype(f32), axis=0, keepdims=True))
    o_grad[...] = dot_turned(wout[...], dz).astype(bf16).reshape(o_grad.shape)
    for d in (2, 1, 3):
        go(o_grad.at[(z + d) % GROUPS], grad_heads.at[z], gsend.at[d], grecv.at[d], around[d - 1])
    own = pltpu.make_async_copy(o_grad.at[z], grad_heads.at[z], local.at[3])
    own.start()

    columns = c_land.shape[2]
    count = grads.shape[0]
    mine = pl.ds(pl.multiple_of(core * columns, columns), columns)
    others = pl.ds(pl.multiple_of((1 - core) * columns, columns), columns)

    def over(k):
        go(grads.at[k, :, others], c_land.at[k], csend.at[k], crecv.at[k], over_core)

    def settle(k):
        landed = c_land.at[k]
        remote(landed, landed, csend.at[k], crecv.at[k], over_core).wait_recv()
        place, sent = k, None
        for ref in (send_over_x, send_over_y, send_rest):
            if sent is None and place < ref.shape[0]:
                sent = ref.at[place]
            place -= ref.shape[0]
        core_sum(firsts[k], lambda r: grads[k, r, mine], c_land.at[k], sent, keep.at[k], x, y)

    c_turned = c.T
    piece = half // tiles
    for k in range(count):
        if k < tiles:
            for top in range(2):
                grads[k, top * piece : (top + 1) * piece] = dot(
                    act_turned[top * half + k * piece : top * half + (k + 1) * piece], dy
                ).astype(bf16)
        elif k < 2 * tiles:
            grads[k] = dot(c_turned, pre_grad[k - tiles]).astype(bf16)
        else:
            grads[k] = dot(turned, dz).astype(bf16)
        over(k)
        if k >= 2:
            settle(k - 2)
    settle(count - 2)
    settle(count - 1)
    for d in range(1, GROUPS):
        landed = grad_heads.at[(z + GROUPS - d) % GROUPS]
        remote(landed, landed, gsend.at[d], grecv.at[d], over_core).wait_recv()
    own.wait()
    go.finish()


def middle(pack, firsts, ahead, heads, patches, out_grad, small, *weights):
    rows, width = patches.shape
    hidden = weights[2].shape[1]
    tiles = hidden // width
    count = 2 * tiles + 1
    f32, bf16 = jnp.float32, jnp.bfloat16
    vmem = pl.BlockSpec(memory_space=pltpu.VMEM)
    hbm = pl.BlockSpec(memory_space=pltpu.HBM)
    dma = pltpu.SemaphoreType.DMA
    return pl.pallas_call(
        functools.partial(middle_kernel, pack, firsts),
        out_shape=[
            jax.ShapeDtypeStruct((rows, width), bf16),
            jax.ShapeDtypeStruct((rows, width), f32),
            jax.ShapeDtypeStruct(heads.shape, bf16),
            jax.ShapeDtypeStruct((ahead, width // 2, width // 2), bf16),
            jax.ShapeDtypeStruct((ahead, width // 2, width // 2), bf16),
            jax.ShapeDtypeStruct((count - 2 * ahead, width // 2, width // 2), bf16),
            jax.ShapeDtypeStruct((count, width // 2, width // 2), bf16),
            jax.ShapeDtypeStruct((2, pack.rows, LANES), f32),
        ],
        in_specs=[hbm, vmem, vmem, vmem] + [hbm] * 7,
        out_specs=[vmem] * 8,
        scratch_shapes=[
            pltpu.VMEM(heads.shape, bf16),
            pltpu.VMEM(heads.shape, bf16),
            pltpu.VMEM((width, width), bf16),
            pltpu.VMEM((width, hidden), bf16),
            pltpu.VMEM((hidden, width), bf16),
            pltpu.VMEM((tiles, rows, width), f32),
            pltpu.VMEM((hidden, rows), bf16),
            pltpu.VMEM((tiles, rows, width), bf16),
            pltpu.VMEM((tiles, 8, width), f32),
            pltpu.VMEM((count, width, width), bf16),
            pltpu.VMEM((count, width, width // 2), bf16),
            dma((10,)),
            dma((GROUPS,)),
            dma((GROUPS,)),
            dma((GROUPS,)),
            dma((GROUPS,)),
            dma((2,)),
            dma((count,)),
            dma((count,)),
        ],
        compiler_params=params(60, 3),
        name="middle",
    )(heads, patches, out_grad, small, *weights)


class Totals:
    def __init__(self, refs, tiles):
        self.refs, self.tiles = refs, tiles

    def place(self, k, row, count, column, columns):
        width = self.refs[2].shape[1]
        start = 0
        if k < self.tiles:
            which, row = 0, k * (width // 2) + row
        elif k < 2 * self.tiles:
            which, start = 1, (k - self.tiles) * width
        elif k == 2 * self.tiles:
            which = 2
        else:
            which, start = 3, (k - 2 * self.tiles - 1) * width
        return which, pl.ds(row, count), pl.ds(pl.multiple_of(start + column, LANES), columns)

    def view(self, *place):
        which, rows, columns = self.place(*place)
        return self.refs[which].at[rows, columns]

    def store(self, values, *place):
        which, rows, columns = self.place(*place)
        ref = self.refs[which]
        ref[rows, columns] = values.astype(ref.dtype)


def last_kernel(
    pack,
    firsts,
    tiles,
    query_grad,
    key_grad,
    normed_low,
    w_qkv,
    w_qkv_far,
    patches,
    hidden_grad,
    small,
    ahead_x,
    ahead_y,
    send_rest,
    keep,
    vector_in,
    inputs_grad,
    down_out,
    up_out,
    out_out,
    qkv_out,
    vector_out,
    down_total,
    up_total,
    out_total,
    qkv_total,
    got,
    near,
    both,
    far,
    own,
    wqkv,
    grads,
    c_land,
    late_send,
    first_land,
    half_sum,
    second_land,
    quarter_sum,
    z_land,
    eighth_sum,
    far_land,
    vectors,
    v_land,
    local,
    loads,
    n_send,
    n_recv,
    f_send,
    f_recv,
    q_send,
    q_recv,
    csend,
    crecv,
    asend,
    arecv,
    bsend,
    brecv,
    zsend,
    zrecv,
    wsend,
    wrecv,
    dsend,
    drecv,
    gsend,
    grecv,
    hsend,
    hrecv,
    isend,
    irecv,
    vsend,
    vrecv,
):
    f32, bf16 = jnp.float32, jnp.bfloat16
    z, x, core, y = here()
    pair, side = z // 2, z % 2
    over_x, over_core, over_y = (
        at(z, 1 - x, core, y),
        at(z, x, 1 - core, y),
        at(z, x, core, 1 - y),
    )
    around = [at((z + d) % GROUPS, x, core, y) for d in range(1, GROUPS)]
    over_near, over_far = at(z + 1 - 2 * side, x, core, y), around[1]
    peer = {"y": over_y, "x": over_x}
    greet(around + [over_x, over_core, over_y])
    go = Sender()
    totals = Totals((down_total, up_total, out_total, qkv_total), tiles)
    outs = Totals((down_out, up_out, out_out, qkv_out), tiles)
    part = query_grad.shape[1]
    rows, width = patches.shape
    chunks, early, late = len(firsts), keep.shape[0], c_land.shape[0]
    ahead = ahead_x.shape[0]
    hidden = ahead + ahead_y.shape[0]
    half = c_land.shape[2]
    quarter, shard = width // 4, width // 16

    def landed(view, sem):
        remote(view, view, sem, sem, over_core).wait_recv()

    order = (2, 1, 3, 0)
    held = []
    for d in order:
        pz = (z + d) % GROUPS
        for k in range(2):
            px = (x + 1 + k) % 2
            slot = 2 * d + k
            src = key_grad.at[pz * PEERS + px * 2 + 1 - core]
            go(src, near.at[slot], n_send.at[slot], n_recv.at[slot], over_core)
            src = key_grad.at[pz * PEERS + px * 2 + core]
            copy = pltpu.make_async_copy(src, both.at[slot], local.at[4 + slot])
            copy.start()
            held.append((slot, copy))
    held = dict(held)
    for d in (2, 1, 3):
        pz = (z + d) % GROUPS
        go(query_grad.at[pz], got.at[z, pl.ds(0, part)], q_send.at[d], q_recv.at[d], around[d - 1])
    own_query = pltpu.make_async_copy(query_grad.at[z], got.at[z, pl.ds(0, part)], local.at[0])
    own_query.start()
    arrivals = []
    for k in range(early):
        arrivals.append([pltpu.make_async_copy(keep.at[k], half_sum.at[k], loads.at[2 * k])])
        if k < hidden:
            src = ahead_x.at[k] if k < ahead else ahead_y.at[k - ahead]
            copy = pltpu.make_async_copy(src, first_land.at[k], loads.at[2 * k + 1])
            arrivals[k].append(copy)
        else:
            sem = late + k - hidden
            src = send_rest.at[k - hidden]
            go(src, first_land.at[k], asend.at[sem], arecv.at[sem], peer[firsts[k]])
        for copy in arrivals[k]:
            copy.start()
    count = w_qkv.shape[0]
    weights = [
        pltpu.make_async_copy(w_qkv, wqkv.at[pl.ds(y * count, count)], local.at[2]),
        pltpu.make_async_copy(w_qkv_far, wqkv.at[pl.ds((1 - y) * count, count)], local.at[3]),
    ]
    for copy in weights:
        copy.start()

    def collect_near(step):
        d = order[step]
        for k in range(2):
            slot = 2 * d + k
            landed(near.at[slot], n_recv.at[slot])
            held[slot].wait()
            both[slot] = (both[slot].astype(f32) + near[slot].astype(f32)).astype(bf16)
            if k == 0:
                go(both.at[slot], far.at[d], f_send.at[d], f_recv.at[d], over_x)

    def collect_far(step):
        d = order[step]
        landed(far.at[d], f_recv.at[d])
        own[d] = (both[2 * d + 1].astype(f32) + far[d].astype(f32)).astype(bf16)
        place = got.at[z, pl.ds(part, 2 * part)]
        if d == 0:
            copy = pltpu.make_async_copy(own.at[0], place, local.at[1])
            copy.start()
            return copy
        sem = GROUPS + d
        go(own.at[d], place, q_send.at[sem], q_recv.at[sem], around[d - 1])
        return None

    def stage_core(k):
        i = k - early
        landed(c_land.at[i], crecv.at[i])
        mine = pl.ds(pl.multiple_of(core * half, half), half)
        core_sum(
            firsts[k],
            lambda r: grads[i, r, mine],
            c_land.at[i],
            late_send.at[i],
            half_sum.at[k],
            x,
            y,
        )
        go(late_send.at[i], first_land.at[k], asend.at[i], arecv.at[i], peer[firsts[k]])

    def stage_first(k):
        if k < early:
            for copy in arrivals[k]:
                copy.wait()
        if k >= hidden:
            landed(first_land.at[k], arecv.at[k - early if k >= early else late + k - hidden])
        half_sum[k] = (half_sum[k].astype(f32) + first_land[k].astype(f32)).astype(bf16)
        place = x if firsts[k] == "y" else y
        other = half_sum.at[k, pl.ds((1 - place) * quarter, quarter)]
        second = over_x if firsts[k] == "y" else over_y
        go(other, second_land.at[k], bsend.at[k], brecv.at[k], second)

    def stage_second(k):
        landed(second_land.at[k], brecv.at[k])
        place = x if firsts[k] == "y" else y
        total = half_sum[k, pl.ds(place * quarter, quarter)].astype(f32)
        quarter_sum[k] = (total + second_land[k].astype(f32)).astype(bf16)
        other = quarter_sum.at[k, pl.ds((1 - side) * 2 * shard, 2 * shard)]
        go(other, z_land.at[k], zsend.at[k], zrecv.at[k], over_near)

    def stage_near(k):
        landed(z_land.at[k], zrecv.at[k])
        total = quarter_sum[k, pl.ds(side * 2 * shard, 2 * shard)].astype(f32)
        eighth_sum[k] = (total + z_land[k].astype(f32)).astype(bf16)
        other = eighth_sum.at[k, pl.ds((1 - pair) * shard, shard)]
        go(other, far_land.at[k], wsend.at[k], wrecv.at[k], over_far)

    def spot(k, px, pside, ppair, count):
        row = px * quarter + pside * 2 * shard + ppair * shard
        return totals.view(k, row, count, core * half, half)

    def stage_far(k):
        landed(far_land.at[k], wrecv.at[k])
        total = eighth_sum[k, pl.ds(pair * shard, shard)].astype(f32) + far_land[k].astype(f32)
        row = x * quarter + side * 2 * shard + pair * shard
        totals.store(total, k, row, shard, core * half, half)
        view = spot(k, x, side, pair, shard)
        go(view, view, dsend.at[k], drecv.at[k], over_far)

    def stage_back(k):
        landed(spot(k, x, side, 1 - pair, shard), drecv.at[k])
        view = spot(k, x, side, 0, 2 * shard)
        go(view, view, gsend.at[k], grecv.at[k], over_near)

    def stage_out(k):
        landed(spot(k, x, 1 - side, 0, 2 * shard), grecv.at[k])
        view = spot(k, x, 0, 0, quarter)
        go(view, view, hsend.at[k], hrecv.at[k], over_x)
        go(view, view, isend.at[2 * k], irecv.at[2 * k], over_core)

    def stage_last(k):
        view = spot(k, 1 - x, 0, 0, quarter)
        landed(view, hrecv.at[k])
        go(view, view, isend.at[2 * k + 1], irecv.at[2 * k + 1], over_core)

    written = []

    def stage_write(k):
        for px in range(2):
            place = (x + px) % 2
            view = totals.view(k, place * quarter, quarter, (1 - core) * half, half)
            landed(view, irecv.at[2 * k + px])
        place = (k, 0, 2 * quarter, 0, 2 * half)
        copy = pltpu.make_async_copy(totals.view(*place), outs.view(*place), loads.at[2 * early + k])
        copy.start()
        written.append(copy)

    stages = (
        stage_first,
        stage_second,
        stage_near,
        stage_far,
        stage_back,
        stage_out,
        stage_last,
        stage_write,
    )

    def vector_step(n):
        if n == 0:
            landed(v_land.at[0], vrecv.at[0])
            vectors[1] = vectors[0] + v_land[0]
            go(vectors.at[1], v_land.at[1], vsend.at[1], vrecv.at[1], over_x)
        elif n == 1:
            landed(v_land.at[1], vrecv.at[1])
            vectors[2] = vectors[1] + v_land[1]
            go(vectors.at[2], v_land.at[2], vsend.at[2], vrecv.at[2], over_y)
        elif n == 2:
            landed(v_land.at[2], vrecv.at[2])
            vectors[3] = vectors[2] + v_land[2]
            for d in range(1, GROUPS):
                sem = 2 + d
                go(vectors.at[3], v_land.at[sem], vsend.at[sem], vrecv.at[sem], around[d - 1])
        elif n == 3:
            total = vectors[3]
            for d in range(1, GROUPS):
                landed(v_land.at[2 + d], vrecv.at[2 + d])
                total += v_land[2 + d]
            v_land[0] = total
            vector_out[...] = v_land[0, y]

    mixed = [2 * k for k in range(ahead)] + [2 * k + 1 for k in range(hidden - ahead)]
    entry = mixed + list(range(hidden, early)) + [LATE_TURN + i for i in range(late)]
    turns = iter(range(entry[-1] + len(stages)))

    def turn():
        step = next(turns, None)
        if step is None:
            return False
        for depth, stage in enumerate(stages):
            for k in range(chunks):
                if step - depth == entry[k]:
                    stage(k)
        return True

    collect_near(0)
    turn()
    for step in range(1, GROUPS):
        collect_near(step)
        collect_far(step - 1)
        turn()
    own_keys = collect_far(GROUPS - 1)
    turn()
    normed_turned = normed_low[...].T
    normed, scale = normalise(patches[...].astype(f32))
    gain1 = pack.read(small, "gain1")
    turn()
    for d in range(1, GROUPS):
        landed(got.at[(z + GROUPS - d) % GROUPS, pl.ds(0, part)], q_recv.at[d])
    own_query.wait()
    turn()
    others = pl.ds(pl.multiple_of((1 - core) * half, half), half)

    def project(i):
        turned = got[:, i * part : (i + 1) * part].reshape(width, rows)
        grads[i] = dot_turned(normed_turned, turned).astype(bf16)
        go(grads.at[i, :, others], c_land.at[i], csend.at[i], crecv.at[i], over_core)

    project(0)
    for d in range(1, GROUPS):
        landed(got.at[(z + GROUPS - d) % GROUPS, pl.ds(part, 2 * part)], q_recv.at[GROUPS + d])
    own_keys.wait()
    for i in range(1, late):
        project(i)
    turn()
    for copy in weights:
        copy.wait()
    vectors[0] = vector_in[...]
    ones = jnp.ones((8, rows), bf16)
    normed_grad = jnp.zeros((width, rows), f32)
    for i in range(late):
        turned = got[:, i * part : (i + 1) * part].reshape(width, rows)
        if i != 1:
            sums = dot_turned(ones, turned)[0:1]
            pack.write(vectors.at[0], "bqv", sums, (i // 2) * width)
        normed_grad += dot(wqkv[:, i * width : (i + 1) * width], turned)
        stage_core(early + i)
    turn()
    change, gain_grad, bias_grad = normalise_back(normed_grad.T, gain1, normed, scale)
    inputs_grad[...] = hidden_grad[...] + change
    pack.write(vectors.at[0], "gain1", gain_grad)
    pack.write(vectors.at[0], "bias1", bias_grad)
    go(vectors.at[0], v_land.at[0], vsend.at[0], vrecv.at[0], over_core)
    step = 0
    while turn():
        vector_step(step)
        step += 1
    for copy in written:
        copy.wait()
    go.finish()


LATE_TURN = 9


def last(
    pack, firsts, query_grad, key_grad, normed_low, w_qkv, w_qkv_far, patches, hidden_grad, small,
    ahead_x, ahead_y, send_rest, keep, vector
):
    f32, bf16 = jnp.float32, jnp.bfloat16
    vmem = pl.BlockSpec(memory_space=pltpu.VMEM)
    hbm = pl.BlockSpec(memory_space=pltpu.HBM)
    groups, part, rows = query_grad.shape
    width = patches.shape[1]
    early, half = keep.shape[0], width // 2
    tiles, chunks, late = (early - 1) // 2, len(firsts), len(firsts) - early
    piece = (2 * part, rows)
    dma = pltpu.SemaphoreType.DMA
    totals = [
        (tiles * half, width),
        (half, tiles * width),
        (half, width),
        (half, late * width),
    ]

    def pair(n):
        return [dma((n,))] * 2

    return pl.pallas_call(
        functools.partial(last_kernel, pack, firsts, tiles),
        out_shape=[jax.ShapeDtypeStruct((rows, width), f32)]
        + [jax.ShapeDtypeStruct(shape, bf16) for shape in totals]
        + [jax.ShapeDtypeStruct(vector.shape[1:], f32)],
        in_specs=[hbm, hbm, vmem, hbm, hbm, vmem, vmem, vmem, hbm, hbm, hbm, hbm, vmem],
        out_specs=[vmem] + [hbm] * 4 + [vmem],
        scratch_shapes=[pltpu.VMEM(shape, bf16) for shape in totals]
        + [
            pltpu.VMEM((groups, 3 * part, rows), bf16),
            pltpu.VMEM((2 * groups,) + piece, bf16),
            pltpu.VMEM((2 * groups,) + piece, bf16),
            pltpu.VMEM((groups,) + piece, bf16),
            pltpu.VMEM((groups,) + piece, bf16),
            pltpu.VMEM((width, late * width), bf16),
            pltpu.VMEM((late, width, width), bf16),
            pltpu.VMEM((late, width, half), bf16),
            pltpu.VMEM((late, half, half), bf16),
            pltpu.VMEM((chunks, half, half), bf16),
            pltpu.VMEM((chunks, half, half), bf16),
            pltpu.VMEM((chunks, half // 2, half), bf16),
            pltpu.VMEM((chunks, half // 2, half), bf16),
            pltpu.VMEM((chunks, half // 4, half), bf16),
            pltpu.VMEM((chunks, half // 4, half), bf16),
            pltpu.VMEM((chunks, half // 8, half), bf16),
            pltpu.VMEM((4,) + vector.shape, f32),
            pltpu.VMEM((6,) + vector.shape, f32),
            dma((4 + 2 * groups,)),
            dma((2 * early + chunks,)),
        ]
        + pair(2 * groups)
        + pair(groups)
        + pair(2 * groups)
        + pair(late)
        + pair(chunks)
        + pair(chunks) * 6
        + pair(2 * chunks)
        + pair(6),
        compiler_params=params(60, 4),
        name="last",
    )(
        query_grad, key_grad, normed_low, w_qkv, w_qkv_far, patches, hidden_grad, small,
        ahead_x, ahead_y, send_rest, keep, vector,
    )


class Documents:
    def __init__(self, lengths, rows):
        self.rows, self.count = rows, lengths.shape[1]
        self.starts, self.ends, place = [], [], 0
        for d in range(self.count):
            self.starts.append(place)
            place = place + lengths[0, d]
            self.ends.append(place)

    def span(self, block):
        first, last = block * self.rows, (block + 1) * self.rows - 1
        low, high = 0, 0
        for d in range(self.count):
            low = jnp.where(self.starts[d] <= first, self.starts[d], low)
        for d in reversed(range(self.count)):
            high = jnp.where(self.ends[d] > last, self.ends[d], high)
        return low // self.rows, (high + self.rows - 1) // self.rows

    def inside(self, block, yes, no):
        shape = (8, self.rows)
        row = lax.broadcasted_iota(jnp.int32, shape, 0)
        place = block * self.rows + lax.broadcasted_iota(jnp.int32, shape, 1)
        found = jnp.where(row < self.count, no, 0.0)
        for d in range(self.count):
            hit = (row == d) & (place >= self.starts[d]) & (place < self.ends[d])
            found = jnp.where(hit, yes, found)
        return found

    def marks(self, block):
        ones, rest = jnp.ones((8, self.rows)), jnp.zeros((HD - 16, self.rows))
        return jnp.concatenate([self.inside(block, 1.0, 0.0), ones, rest]).astype(jnp.bfloat16)

    def veto(self, block):
        rest = jnp.zeros((HD - 8, self.rows))
        return jnp.concatenate([self.inside(block, 0.0, masked_score), rest])


def attend_kernel(
    lengths, place, query, keys, out, out_low, sums, key_rows, query_aug, acc, stat
):
    blocks, rows = keys.shape[0], keys.shape[2]
    width = query.shape[1]
    groups = query.shape[0]
    documents = Documents(lengths, rows)

    def turn(j, carry):
        mark = documents.marks(j)
        for h in range(PER_GROUP):
            both = jnp.concatenate([keys[j, h * HD : (h + 1) * HD], mark], axis=0)
            key_rows[h, j] = both.T
        return carry

    lax.fori_loop(0, blocks, turn, 0)
    for i in range(groups):
        block = i * PEERS + place[0]
        veto = documents.veto(block).astype(jnp.bfloat16)
        for h in range(PER_GROUP):
            query_aug[h, :HD] = query[i, h * HD : (h + 1) * HD] * jnp.bfloat16(0.125)
            query_aug[h, HD:] = veto
        stat[0] = jnp.full(stat.shape[1:], masked_score, jnp.float32)
        stat[1] = jnp.zeros(stat.shape[1:], jnp.float32)
        acc[...] = jnp.zeros(acc.shape, jnp.float32)

        low, high = documents.span(block)
        steps = (high - low + 1) // 2
        low = jnp.minimum(low, blocks - 2 * steps)

        def step(n, carry):
            j = low + 2 * n
            made = [
                [dot(key_rows[h, j + k], query_aug[h]) for k in range(2)] for h in range(PER_GROUP)
            ]
            for h in range(PER_GROUP):
                first, second = made[h]
                old = stat[0, h : h + 1]
                most = jnp.max(jnp.maximum(first, second), axis=0, keepdims=True)
                new = jnp.maximum(old, most)
                first, second = jnp.exp(first - new), jnp.exp(second - new)
                factor = jnp.exp(old - new)
                stat[0, h : h + 1] = new
                stat[1, h : h + 1] = stat[1, h : h + 1] * factor + jnp.sum(
                    first + second, axis=0, keepdims=True
                )
                span = slice(width + h * HD, width + (h + 1) * HD)
                shared = dot(keys[j, span], first.astype(jnp.bfloat16))
                shared += dot(keys[j + 1, span], second.astype(jnp.bfloat16))
                acc[h] = acc[h] * factor + shared
            return carry

        lax.fori_loop(0, steps, step, 0)
        for h in range(PER_GROUP):
            total = stat[1, h : h + 1]
            shared = acc[h] / total
            out[i, h * HD : (h + 1) * HD] = shared
            out_low[i, h * HD : (h + 1) * HD] = shared.astype(jnp.bfloat16)
            sums[i, h : h + 1] = stat[0, h : h + 1] + jnp.log(total)


def attend(lengths, place, query, keys):
    groups, width, rows = query.shape
    blocks = keys.shape[0]
    vmem = pl.BlockSpec(memory_space=pltpu.VMEM)
    return pl.pallas_call(
        attend_kernel,
        out_shape=[
            jax.ShapeDtypeStruct(query.shape, jnp.float32),
            jax.ShapeDtypeStruct(query.shape, jnp.bfloat16),
            jax.ShapeDtypeStruct((groups, 8, rows), jnp.float32),
        ],
        in_specs=[pl.BlockSpec(memory_space=pltpu.SMEM)] * 2 + [vmem] * 2,
        out_specs=[vmem] * 3,
        scratch_shapes=[
            pltpu.VMEM((PER_GROUP, blocks, rows, 2 * HD), jnp.bfloat16),
            pltpu.VMEM((PER_GROUP, 2 * HD, rows), jnp.bfloat16),
            pltpu.VMEM((PER_GROUP, HD, rows), jnp.float32),
            pltpu.VMEM((2, 8, rows), jnp.float32),
        ],
        compiler_params=params(60),
        name="attend",
    )(lengths, place, query, keys)


def three_parts(values):
    high = values.astype(jnp.bfloat16)
    rest = values - high.astype(jnp.float32)
    middle = rest.astype(jnp.bfloat16)
    low = (rest - middle.astype(jnp.float32)).astype(jnp.bfloat16)
    return high, middle, low


def attend_back_kernel(
    lengths,
    place,
    query,
    keys,
    out,
    sums,
    out_grad,
    query_grad,
    key_grad,
    key_rows,
    value_rows,
    query_aug,
    grad_aug,
    query_rows,
    grad_rows,
    query_acc,
    key_acc,
):
    blocks, rows = keys.shape[0], keys.shape[2]
    width = query.shape[1]
    groups = query.shape[0]
    bf16 = jnp.bfloat16
    documents = Documents(lengths, rows)

    def turn(j, carry):
        mark = documents.marks(j)
        for h in range(PER_GROUP):
            both = jnp.concatenate([keys[j, h * HD : (h + 1) * HD], mark], axis=0)
            key_rows[h, pl.ds(pl.multiple_of(j * rows, rows), rows)] = both.T
            values = keys[j, width + h * HD : width + (h + 1) * HD]
            place = pl.ds(pl.multiple_of(j * rows, rows), rows)
            value_rows[h, place] = jnp.concatenate([values, mark], axis=0).T
            key_acc[h, place] = jnp.zeros((rows, 2 * HD), jnp.float32)
        return carry

    lax.fori_loop(0, blocks, turn, 0)
    index = lax.broadcasted_iota(jnp.int32, (HD, rows), 0)
    none = jnp.zeros((HD, rows), bf16)

    def spread(values):
        high, middle, low = three_parts(-values)
        wide = jnp.where(index == 8, high.astype(jnp.float32), 0.0)
        wide = jnp.where(index == 9, middle.astype(jnp.float32), wide)
        return jnp.where(index == 10, low.astype(jnp.float32), wide)

    for i in range(groups):
        block = i * PEERS + place[0]
        veto = documents.veto(block)
        for h in range(PER_GROUP):
            span = slice(h * HD, (h + 1) * HD)
            part = query[i, span] * bf16(0.125)
            grad = out_grad[i, span]
            delta = jnp.sum(grad.astype(jnp.float32) * out[i, span], axis=0, keepdims=True)
            query_aug[h, :HD] = part
            query_aug[h, HD:] = (veto + spread(sums[i, h : h + 1])).astype(bf16)
            grad_aug[h, :HD] = grad
            grad_aug[h, HD:] = spread(delta).astype(bf16)
            query_rows[h] = jnp.concatenate([part, none], axis=0).T
            grad_rows[h] = jnp.concatenate([none, grad], axis=0).T
        query_acc[...] = jnp.zeros(query_acc.shape, jnp.float32)

        low, high = documents.span(block)
        steps = (high - low + 1) // 2
        low = jnp.minimum(low, blocks - 2 * steps)

        def step(n, carry):
            j = low + 2 * n
            span = pl.ds(pl.multiple_of(j * rows, rows), 2 * rows)
            for h in range(PER_GROUP):
                probs = jnp.exp(dot(key_rows[h, span], query_aug[h]))
                change = (probs * dot(value_rows[h, span], grad_aug[h])).astype(bf16)
                low_probs = probs.astype(bf16)
                key_acc[h, span] += dot(low_probs, grad_rows[h]) + dot(change, query_rows[h])
                turned = slice(h * HD, (h + 1) * HD)
                query_acc[h] += dot(keys[j, turned], change[:rows]) + dot(
                    keys[j + 1, turned], change[rows:]
                )
            return carry

        lax.fori_loop(0, steps, step, 0)
        for h in range(PER_GROUP):
            query_grad[i, h * HD : (h + 1) * HD] = (query_acc[h] * 0.125).astype(bf16)

    def finish(j, carry):
        for h in range(PER_GROUP):
            both = key_acc[h, pl.ds(pl.multiple_of(j * rows, rows), rows)].astype(bf16).T
            key_grad[j, h * HD : (h + 1) * HD] = both[:HD]
            key_grad[j, width + h * HD : width + (h + 1) * HD] = both[HD:]
        return carry

    lax.fori_loop(0, blocks, finish, 0)


def attend_back(lengths, place, query, keys, out, sums, out_grad):
    groups, width, rows = query.shape
    blocks = keys.shape[0]
    vmem = pl.BlockSpec(memory_space=pltpu.VMEM)
    bf16 = jnp.bfloat16
    return pl.pallas_call(
        attend_back_kernel,
        out_shape=[
            jax.ShapeDtypeStruct(query.shape, bf16),
            jax.ShapeDtypeStruct(keys.shape, bf16),
        ],
        in_specs=[pl.BlockSpec(memory_space=pltpu.SMEM)] * 2 + [vmem] * 5,
        out_specs=[vmem] * 2,
        scratch_shapes=[
            pltpu.VMEM((PER_GROUP, blocks * rows, 2 * HD), bf16),
            pltpu.VMEM((PER_GROUP, blocks * rows, 2 * HD), bf16),
            pltpu.VMEM((PER_GROUP, 2 * HD, rows), bf16),
            pltpu.VMEM((PER_GROUP, 2 * HD, rows), bf16),
            pltpu.VMEM((PER_GROUP, rows, 2 * HD), bf16),
            pltpu.VMEM((PER_GROUP, rows, 2 * HD), bf16),
            pltpu.VMEM((PER_GROUP, HD, rows), jnp.float32),
            pltpu.VMEM((PER_GROUP, blocks * rows, 2 * HD), jnp.float32),
        ],
        compiler_params=params(60),
        name="attend_back",
    )(lengths, place, query, keys, out, sums, out_grad)


def layer_norm(values, gain, offset):
    centre = jnp.mean(values, axis=-1, keepdims=True)
    shifted = values - centre
    spread = jnp.mean(shifted * shifted, axis=-1, keepdims=True)
    return shifted * lax.rsqrt(spread + epsilon) * gain + offset


def exact_gelu(values):
    return jax.nn.gelu(values, approximate=False)


def doc_index(positions, doc_starts):
    hits = (doc_starts[None, :] <= positions[:, None]).astype(jnp.int32)
    return jnp.sum(hits, axis=1) - 1


def body(
    patches,
    doc_lengths,
    norm1_gain,
    norm1_bias,
    w_qkv,
    b_qv,
    w_out,
    b_out,
    norm2_gain,
    norm2_bias,
    w_up,
    b_up,
    w_down,
    b_down,
    cotangent,
):
    f32, bf16 = jnp.float32, jnp.bfloat16
    rows, width = patches.shape[1:]
    ctx_place = lax.axis_index("ctx")
    blocks = lax.axis_size("ctx")
    place = (ctx_place % PEERS).astype(jnp.int32).reshape(1)
    vectors = [norm1_gain, norm1_bias, b_qv, b_out, norm2_gain, norm2_bias, b_up, b_down]
    pack = Packed([v.shape[0] for v in vectors])
    query, keys, normed1, small, qkv_far, out_far, up_far, down_got, down_part = front(
        pack, patches[0], pack.pack(vectors), w_qkv, w_out, w_up, w_down
    )
    down_far = lax.ppermute(down_part, "wsh", [(0, 1), (1, 0)])
    out_heads, heads_low, sums = attend(doc_lengths, place, query, keys)
    tiles = w_up.shape[1] // width
    chunks = 2 * tiles + 1 + w_qkv.shape[1] // width
    ahead = tiles
    firsts = ["x"] * ahead + ["y"] * (chunks - ahead)
    mixed, hidden_grad, grad_heads, send_over_x, send_over_y, send_rest, keep, vector = middle(
        pack, firsts, ahead, heads_low, patches[0], cotangent[0], small, w_out, out_far, w_up,
        up_far, w_down, down_got, down_far,
    )
    across = [(c, c + 2 - c // 2 % 2 * 4) for c in range(blocks)]
    ahead_x = lax.ppermute(send_over_x, "ctx", across)
    ahead_y = lax.ppermute(send_over_y, "wsh", [(0, 1), (1, 0)])
    query_grad, key_grad = attend_back(
        doc_lengths, place, query, keys, out_heads, sums, grad_heads
    )
    inputs_grad, down_total, up_total, out_total, qkv_total, vector_total = last(
        pack, firsts, query_grad, key_grad, normed1, w_qkv, qkv_far, patches[0], hidden_grad, small,
        ahead_x, ahead_y, send_rest, keep, vector,
    )
    shares = pack.unpack(vector_total)
    return (
        mixed[None],
        inputs_grad[None],
        shares[0],
        shares[1],
        qkv_total.astype(f32),
        shares[2],
        out_total.astype(f32),
        shares[3],
        shares[4],
        shares[5],
        up_total.astype(f32),
        shares[6],
        down_total.astype(f32),
        shares[7],
    )


def shifted_2(block, axis, distance):
    devices = range(lax.axis_size(axis))
    route = [((i - distance) % len(devices), i) for i in devices]
    return lax.ppermute(block, axis, route)


def any_mesh_body(
    patches,
    doc_lengths,
    norm1_gain,
    norm1_bias,
    w_qkv,
    b_qv,
    w_out,
    b_out,
    norm2_gain,
    norm2_bias,
    w_up,
    b_up,
    w_down,
    b_down,
    cotangent,
):
    tok_rows = patches.shape[1]
    model_width = patches.shape[2]
    ctx_size = lax.axis_size("ctx")
    ctx_place = lax.axis_index("ctx")
    gathered = (
        lax.all_gather(norm1_gain, "wsh", axis=0, tiled=True),
        lax.all_gather(norm1_bias, "wsh", axis=0, tiled=True),
        lax.all_gather(w_qkv, "wsh", axis=0, tiled=True),
        lax.all_gather(b_qv, "wsh", axis=0, tiled=True),
        lax.all_gather(w_out, "wsh", axis=0, tiled=True),
        lax.all_gather(b_out, "wsh", axis=0, tiled=True),
        lax.all_gather(norm2_gain, "wsh", axis=0, tiled=True),
        lax.all_gather(norm2_bias, "wsh", axis=0, tiled=True),
        lax.all_gather(w_up, "wsh", axis=0, tiled=True),
        lax.all_gather(b_up, "wsh", axis=0, tiled=True),
        lax.all_gather(w_down, "wsh", axis=0, tiled=True),
        lax.all_gather(b_down, "wsh", axis=0, tiled=True),
    )
    (
        gain1,
        bias1,
        wqkv_full,
        bqv_full,
        wout_full,
        bout_full,
        gain2,
        bias2,
        wup_full,
        bup_full,
        wdown_full,
        bdown_full,
    ) = gathered
    inputs = patches[0].astype(jnp.float32)
    lengths = doc_lengths[0]
    doc_starts = jnp.cumsum(lengths) - lengths
    row_offsets = lax.iota(jnp.int32, tok_rows)
    query_docs = doc_index(ctx_place * tok_rows + row_offsets, doc_starts)
    gain1_float = gain1.astype(jnp.float32)
    bias1_float = bias1.astype(jnp.float32)
    normed1 = layer_norm(inputs, gain1_float, bias1_float).astype(jnp.bfloat16)
    projected = jnp.dot(normed1, wqkv_full, preferred_element_type=jnp.float32)
    bqv_float = bqv_full.astype(jnp.float32)
    query_low = (projected[:, :model_width] + bqv_float[:model_width]).astype(jnp.bfloat16)
    key_low = projected[:, model_width : 2 * model_width].astype(jnp.bfloat16)
    value_low = (projected[:, 2 * model_width :] + bqv_float[model_width:]).astype(jnp.bfloat16)
    query_heads = query_low.reshape(tok_rows, H, HD)

    def attend_block(state, key_block, value_block, key_start):
        run_max, run_total, run_acc = state
        key_docs = doc_index(key_start + row_offsets, doc_starts)
        same_doc = (query_docs[:, None] == key_docs[None, :])[None]
        scores = (
            jnp.einsum(
                "qhd,khd->hqk",
                query_heads,
                key_block.reshape(tok_rows, H, HD),
                preferred_element_type=jnp.float32,
            )
            * 0.125
        )
        scores = jnp.where(same_doc, scores, masked_score)
        new_max = jnp.maximum(run_max, jnp.max(scores, axis=2))
        weights = jnp.where(same_doc, jnp.exp(scores - new_max[:, :, None]), 0.0)
        factor = jnp.exp(run_max - new_max)
        new_total = run_total * factor + jnp.sum(weights, axis=2)
        new_acc = run_acc * factor[:, :, None] + jnp.einsum(
            "hqk,khd->hqd",
            weights.astype(jnp.bfloat16),
            value_block.reshape(tok_rows, H, HD),
            preferred_element_type=jnp.float32,
        )
        return (new_max, new_total, new_acc)

    initial = (
        jnp.full((H, tok_rows), masked_score, jnp.float32),
        jnp.zeros((H, tok_rows), jnp.float32),
        jnp.zeros((H, tok_rows, HD), jnp.float32),
    )
    state = initial
    key_piece = lax.all_gather(key_low, "ctx", axis=0, tiled=True)
    value_piece = lax.all_gather(value_low, "ctx", axis=0, tiled=True)
    blocks = key_piece.shape[0] // tok_rows
    key_blocks = key_piece.reshape(blocks, tok_rows, model_width)
    value_blocks = value_piece.reshape(blocks, tok_rows, model_width)
    block_starts = tok_rows * lax.iota(jnp.int32, blocks)

    def one_block(inner, item):
        key_block, value_block, key_start = item
        return (attend_block(inner, key_block, value_block, key_start), None)

    state, unused = lax.scan(one_block, state, (key_blocks, value_blocks, block_starts))
    run_max, run_total, run_acc = state
    log_total = run_max + jnp.log(run_total)
    attended = jnp.transpose(run_acc / run_total[:, :, None], (1, 0, 2)).reshape(
        tok_rows, model_width
    )
    attended_low = attended.astype(jnp.bfloat16)
    branch = jnp.dot(
        attended_low, wout_full, preferred_element_type=jnp.float32
    ) + bout_full.astype(jnp.float32)
    hidden_sum = inputs + branch
    gain2_float = gain2.astype(jnp.float32)
    bias2_float = bias2.astype(jnp.float32)
    normed2 = layer_norm(hidden_sum, gain2_float, bias2_float).astype(jnp.bfloat16)
    pre_act = jnp.dot(normed2, wup_full, preferred_element_type=jnp.float32) + bup_full.astype(
        jnp.float32
    )
    activated = exact_gelu(pre_act).astype(jnp.bfloat16)
    mixed = (
        hidden_sum
        + jnp.dot(activated, wdown_full, preferred_element_type=jnp.float32)
        + bdown_full.astype(jnp.float32)
    )
    back_gain1 = gathered[0].astype(jnp.float32)
    back_bias1 = gathered[1].astype(jnp.float32)
    back_wqkv = gathered[2]
    back_wout = gathered[4]
    back_gain2 = gathered[6].astype(jnp.float32)
    back_bias2 = gathered[7].astype(jnp.float32)
    back_wup = gathered[8]
    back_wdown = gathered[10]
    out_grad = cotangent[0]
    wdown_grad = jnp.einsum("tf,td->fd", activated, out_grad, preferred_element_type=jnp.float32)
    bdown_grad = jnp.sum(out_grad.astype(jnp.float32), axis=0)
    act_grad = jnp.einsum("td,fd->tf", out_grad, back_wdown, preferred_element_type=jnp.float32)
    unused_act, gelu_back = jax.vjp(exact_gelu, pre_act)
    pre_grad = gelu_back(act_grad)[0].astype(jnp.bfloat16)
    wup_grad = jnp.einsum("tc,tf->cf", normed2, pre_grad, preferred_element_type=jnp.float32)
    bup_grad = jnp.sum(pre_grad.astype(jnp.float32), axis=0)
    normed2_grad = jnp.einsum("tf,cf->tc", pre_grad, back_wup, preferred_element_type=jnp.float32)
    unused_norm2, norm2_back = jax.vjp(layer_norm, hidden_sum, back_gain2, back_bias2)
    hidden_part, gain2_grad, bias2_grad = norm2_back(normed2_grad)
    hidden_grad = out_grad.astype(jnp.float32) + hidden_part
    branch_grad = hidden_grad.astype(jnp.bfloat16)
    wout_grad = jnp.einsum(
        "tc,td->cd", attended_low, branch_grad, preferred_element_type=jnp.float32
    )
    bout_grad = jnp.sum(branch_grad.astype(jnp.float32), axis=0)
    attended_grad = jnp.einsum(
        "td,cd->tc", branch_grad, back_wout, preferred_element_type=jnp.float32
    ).astype(jnp.bfloat16)
    delta = jnp.sum(
        (attended_grad.astype(jnp.float32) * attended).reshape(tok_rows, H, HD), axis=2
    ).T
    grad_heads = attended_grad.reshape(tok_rows, H, HD)

    def back_block(state, anchor):
        key_start = anchor * tok_rows
        key_cur, value_cur, key_grad, value_grad, query_grad = state
        key_docs = doc_index(key_start + row_offsets, doc_starts)
        same_doc = (query_docs[:, None] == key_docs[None, :])[None]
        key_heads = key_cur.reshape(tok_rows, H, HD)
        scores = (
            jnp.einsum("qhd,khd->hqk", query_heads, key_heads, preferred_element_type=jnp.float32)
            * 0.125
        )
        probs = jnp.where(same_doc, jnp.exp(scores - log_total[:, :, None]), 0.0)
        value_grad = value_grad + jnp.einsum(
            "hqk,qhd->khd",
            probs.astype(jnp.bfloat16),
            grad_heads,
            preferred_element_type=jnp.float32,
        ).reshape(tok_rows, model_width)
        prob_grad = jnp.einsum(
            "qhd,khd->hqk",
            grad_heads,
            value_cur.reshape(tok_rows, H, HD),
            preferred_element_type=jnp.float32,
        )
        score_grad = (probs * (prob_grad - delta[:, :, None])).astype(jnp.bfloat16)
        query_grad = (
            query_grad
            + jnp.einsum(
                "hqk,khd->qhd", score_grad, key_heads, preferred_element_type=jnp.float32
            ).reshape(tok_rows, model_width)
            * 0.125
        )
        key_grad = (
            key_grad
            + jnp.einsum(
                "hqk,qhd->khd", score_grad, query_heads, preferred_element_type=jnp.float32
            ).reshape(tok_rows, model_width)
            * 0.125
        )
        return (key_cur, value_cur, key_grad, value_grad, query_grad)

    def pass_on(state):
        key_cur, value_cur, key_grad, value_grad, query_grad = state
        moved_keys = shifted_2((key_cur, value_cur), "ctx", 1)
        moved_sums = (
            shifted_2(key_grad.astype(jnp.bfloat16), "ctx", 1).astype(key_grad.dtype),
            shifted_2(value_grad.astype(jnp.bfloat16), "ctx", 1).astype(value_grad.dtype),
        )
        return (moved_keys[0], moved_keys[1], moved_sums[0], moved_sums[1], query_grad)

    def two_steps(turn, state):
        state = pass_on(back_block(state, (ctx_place - 2 * turn) % ctx_size))
        state = pass_on(back_block(state, (ctx_place - 2 * turn - 1) % ctx_size))
        return state

    zero_rows = jnp.zeros((tok_rows, model_width), jnp.float32)
    final_state = lax.fori_loop(
        0, ctx_size // 2, two_steps, (key_low, value_low, zero_rows, zero_rows, zero_rows)
    )
    key_grad_low = final_state[2].astype(jnp.bfloat16)
    value_grad_low = final_state[3].astype(jnp.bfloat16)
    query_grad_low = final_state[4].astype(jnp.bfloat16)
    projected_grad = jnp.concatenate([query_grad_low, key_grad_low, value_grad_low], axis=1)
    wqkv_grad = jnp.einsum("tc,te->ce", normed1, projected_grad, preferred_element_type=jnp.float32)
    bqv_grad = jnp.concatenate(
        [
            jnp.sum(query_grad_low.astype(jnp.float32), axis=0),
            jnp.sum(value_grad_low.astype(jnp.float32), axis=0),
        ]
    )
    normed1_grad = jnp.einsum(
        "te,ce->tc", projected_grad, back_wqkv, preferred_element_type=jnp.float32
    )
    unused_norm1, norm1_back = jax.vjp(layer_norm, inputs, back_gain1, back_bias1)
    input_part, gain1_grad, bias1_grad = norm1_back(normed1_grad)
    inputs_grad = hidden_grad + input_part
    shares = (
        lax.psum_scatter(
            gain1_grad.astype(jnp.bfloat16), "wsh", scatter_dimension=0, tiled=True
        ).astype(jnp.float32),
        lax.psum_scatter(
            bias1_grad.astype(jnp.bfloat16), "wsh", scatter_dimension=0, tiled=True
        ).astype(jnp.float32),
        lax.psum_scatter(
            wqkv_grad.astype(jnp.bfloat16), "wsh", scatter_dimension=0, tiled=True
        ).astype(jnp.float32),
        lax.psum_scatter(
            bqv_grad.astype(jnp.bfloat16), "wsh", scatter_dimension=0, tiled=True
        ).astype(jnp.float32),
        lax.psum_scatter(
            wout_grad.astype(jnp.bfloat16), "wsh", scatter_dimension=0, tiled=True
        ).astype(jnp.float32),
        lax.psum_scatter(
            bout_grad.astype(jnp.bfloat16), "wsh", scatter_dimension=0, tiled=True
        ).astype(jnp.float32),
        lax.psum_scatter(
            gain2_grad.astype(jnp.bfloat16), "wsh", scatter_dimension=0, tiled=True
        ).astype(jnp.float32),
        lax.psum_scatter(
            bias2_grad.astype(jnp.bfloat16), "wsh", scatter_dimension=0, tiled=True
        ).astype(jnp.float32),
        lax.psum_scatter(
            wup_grad.astype(jnp.bfloat16), "wsh", scatter_dimension=0, tiled=True
        ).astype(jnp.float32),
        lax.psum_scatter(
            bup_grad.astype(jnp.bfloat16), "wsh", scatter_dimension=0, tiled=True
        ).astype(jnp.float32),
        lax.psum_scatter(
            wdown_grad.astype(jnp.bfloat16), "wsh", scatter_dimension=0, tiled=True
        ).astype(jnp.float32),
        lax.psum_scatter(
            bdown_grad.astype(jnp.bfloat16), "wsh", scatter_dimension=0, tiled=True
        ).astype(jnp.float32),
    )
    totals = (
        lax.psum(shares[0].astype(jnp.bfloat16), "ctx").astype(jnp.float32),
        lax.psum(shares[1].astype(jnp.bfloat16), "ctx").astype(jnp.float32),
        lax.psum(shares[2].astype(jnp.bfloat16), "ctx").astype(jnp.float32),
        lax.psum(shares[3].astype(jnp.bfloat16), "ctx").astype(jnp.float32),
        lax.psum(shares[4].astype(jnp.bfloat16), "ctx").astype(jnp.float32),
        lax.psum(shares[5].astype(jnp.bfloat16), "ctx").astype(jnp.float32),
        lax.psum(shares[6].astype(jnp.bfloat16), "ctx").astype(jnp.float32),
        lax.psum(shares[7].astype(jnp.bfloat16), "ctx").astype(jnp.float32),
        lax.psum(shares[8].astype(jnp.bfloat16), "ctx").astype(jnp.float32),
        lax.psum(shares[9].astype(jnp.bfloat16), "ctx").astype(jnp.float32),
        lax.psum(shares[10].astype(jnp.bfloat16), "ctx").astype(jnp.float32),
        lax.psum(shares[11].astype(jnp.bfloat16), "ctx").astype(jnp.float32),
    )
    return (
        mixed.astype(jnp.bfloat16)[None],
        inputs_grad[None],
        totals[0],
        totals[1],
        totals[2],
        totals[3],
        totals[4],
        totals[5],
        totals[6],
        totals[7],
        totals[8],
        totals[9],
        totals[10],
        totals[11],
    )


def solution(mesh):
    as_planned = mesh.shape["ctx"] == GROUPS * PEERS and mesh.shape["wsh"] == 2
    return jax.shard_map(
        body if as_planned else any_mesh_body,
        mesh=mesh,
        in_specs=(
            P("wsh", "ctx", None),
            P("wsh", None),
            P("wsh"),
            P("wsh"),
            P("wsh", None),
            P("wsh"),
            P("wsh", None),
            P("wsh"),
            P("wsh"),
            P("wsh"),
            P("wsh", None),
            P("wsh"),
            P("wsh", None),
            P("wsh"),
            P("wsh", "ctx", None),
        ),
        out_specs=(
            P("wsh", "ctx", None),
            P("wsh", "ctx", None),
            P("wsh"),
            P("wsh"),
            P("wsh", None),
            P("wsh"),
            P("wsh", None),
            P("wsh"),
            P("wsh"),
            P("wsh"),
            P("wsh", None),
            P("wsh"),
            P("wsh", None),
            P("wsh"),
        ),
        check_vma=False,
    )
```

```python
import functools

import jax
import jax.numpy as jnp
from jax import lax
from jax.experimental import pallas as pl
from jax.experimental.pallas import tpu as pltpu
from jax.sharding import PartitionSpec as P

H = 12
HD = 64
GROUPS = 4
PER_GROUP = H // GROUPS
PEERS = 4
MESH = pl.DeviceIdType.MESH
MIB = 2**20

epsilon = 1e-05
masked_score = -1e30


def params(vmem_mib, collective_id=None):
    if collective_id is None:
        return pltpu.CompilerParams(vmem_limit_bytes=vmem_mib * MIB)
    return pltpu.CompilerParams(
        vmem_limit_bytes=vmem_mib * MIB, collective_id=collective_id, has_side_effects=True
    )


def here():
    ctx = lax.axis_index("ctx")
    return ctx // PEERS, (ctx // 2) % 2, ctx % 2, lax.axis_index("wsh")


def at(z, x, core, y):
    return (z * PEERS + x * 2 + core, y)


def remote(src, dst, send, recv, device):
    return pltpu.make_async_remote_copy(
        src_ref=src,
        dst_ref=dst,
        send_sem=send,
        recv_sem=recv,
        device_id=device,
        device_id_type=MESH,
    )


def greet(devices):
    barrier = pltpu.get_barrier_semaphore()
    for device in devices:
        pl.semaphore_signal(barrier, inc=1, device_id=device, device_id_type=MESH)
    pl.semaphore_wait(barrier, len(devices))


def dot(left, right):
    return jnp.dot(left, right, preferred_element_type=jnp.float32)


def dot_turned(left, right):
    return lax.dot_general(
        left, right, (((1,), (1,)), ((), ())), preferred_element_type=jnp.float32
    )


def normalise(values):
    centre = jnp.mean(values, axis=-1, keepdims=True)
    shifted = values - centre
    spread = jnp.mean(shifted * shifted, axis=-1, keepdims=True)
    scale = lax.rsqrt(spread + epsilon)
    return shifted * scale, scale


def normalise_back(grad, gain, normed, scale):
    inner = grad * gain
    centre = jnp.mean(inner, axis=-1, keepdims=True)
    along = jnp.mean(inner * normed, axis=-1, keepdims=True)
    gain_grad = jnp.sum(grad * normed, axis=0, keepdims=True)
    bias_grad = jnp.sum(grad, axis=0, keepdims=True)
    return scale * (inner - centre - normed * along), gain_grad, bias_grad


LANES = 128


class Packed:
    names = ("gain1", "bias1", "bqv", "bout", "gain2", "bias2", "bup", "bdown")

    def __init__(self, sizes):
        self.sizes = dict(zip(self.names, sizes))
        self.starts, row = {}, 0
        for name in self.names:
            self.starts[name] = row
            row += self.sizes[name] // LANES
        self.used = row
        self.rows = row + -row % 8

    def pack(self, halves):
        total, flat = self.rows * LANES, 0.0
        for name, half in zip(self.names, halves):
            start = self.starts[name] * LANES
            after = total - start - half.shape[0]
            flat += jnp.pad(half.astype(jnp.float32), (start, after))
        return flat.reshape(-1, LANES)

    def read(self, ref, name, first=0, count=None):
        count = 2 * self.sizes[name] if count is None else count
        parts = []
        for lane in range(first, first + count, LANES):
            y, inner = divmod(lane, self.sizes[name])
            row = self.starts[name] + inner // LANES
            parts.append(ref[y, row : row + 1])
        return jnp.concatenate(parts, axis=1)

    def write(self, ref, name, values, first=0):
        for lane in range(0, values.shape[1], LANES):
            y, inner = divmod(first + lane, self.sizes[name])
            row = self.starts[name] + inner // LANES
            ref[y, row : row + 1] = values[:, lane : lane + LANES]

    def unpack(self, rows):
        flat = rows[: self.used].reshape(-1)
        parts, start = [], 0
        for name in self.names:
            parts.append(flat[start : start + self.sizes[name]])
            start += self.sizes[name]
        return parts


class Sender:
    def __init__(self):
        self.copies = []

    def __call__(self, src, dst, send, recv, device):
        copy = remote(src, dst, send, recv, device)
        copy.start()
        self.copies.append(copy)

    def finish(self):
        for copy in self.copies:
            copy.wait_send()


def front_kernel(
    pack,
    patches,
    small_half,
    qkv_half,
    out_half,
    up_half,
    down_half,
    query,
    keys,
    normed_low,
    small,
    qkv_far,
    out_far,
    up_far,
    down_got,
    down_part,
    qkv_own,
    staged,
    local,
    small_sem,
    ysend,
    yrecv,
    xsend,
    xrecv,
    csend,
    crecv,
    fsend,
    frecv,
    psend,
    precv,
    nsend,
    nrecv,
    pxsend,
    pxrecv,
    pfsend,
    pfrecv,
    query_send,
    query_recv,
    zsend,
    zrecv,
    kxsend,
    kxrecv,
    kcsend,
    kcrecv,
    kfsend,
    kfrecv,
):
    bf16 = jnp.bfloat16
    z, x, core, y = here()
    over_x, over_core, over_y = (
        at(z, 1 - x, core, y),
        at(z, x, 1 - core, y),
        at(z, x, core, 1 - y),
    )
    around = [at((z + d) % GROUPS, x, core, y) for d in range(1, GROUPS)]
    rows, width = patches.shape
    part = query.shape[1]
    half = qkv_half.shape[0]
    quarter = half // PEERS
    down, later = down_half.shape[0] // 2, down_part.shape[0]
    sooner = down - later
    greet(around + [over_x, over_core, over_y])
    go = Sender()

    def landed(view, sem):
        remote(view, view, sem, sem, over_core).wait_recv()

    def columns(b):
        return pl.ds(b * width, width)

    def share(px, pcore, b):
        return qkv_far.at[pl.ds((px * 2 + pcore) * quarter, quarter), columns(b)]

    order = (1, 2, 0)
    go(small_half, small.at[y], small_sem.at[0], small_sem.at[1], over_y)
    for b in order:
        src = qkv_half.at[pl.ds((x * 2 + core) * quarter, quarter), columns(b)]
        go(src, share(x, core, b), ysend.at[b], yrecv.at[b], over_y)
    copies = [
        pltpu.make_async_copy(small_half, small.at[y], local.at[0]),
        pltpu.make_async_copy(qkv_half, qkv_own, local.at[1]),
        pltpu.make_async_copy(
            down_half.at[pl.ds(core * down + sooner, later)], down_part, local.at[2]
        ),
    ]
    for copy in copies:
        copy.start()

    step = quarter // 2
    pieces = [(up_half, up_far, quarter, quarter, step, i * step, half // 2) for i in range(2)]
    shared = len(pieces)
    pieces += [(out_half, out_far, half // 2, half // 2, half // 2, 0, 0)]
    step = sooner // 2
    pieces += [(down_half, down_got, down, sooner, step, i * step, 0) for i in range(2)]

    def piece_view(k, px, pcore):
        unused, full, unused, apart, count, first, across = pieces[k]
        return full.at[pl.ds(px * across + pcore * apart + first, count)]

    def piece_in(k):
        view = piece_view(k, x, core)
        landed(view, precv.at[k])
        if k < shared:
            go(view, view, pxsend.at[k], pxrecv.at[k], over_x)
        go(view, view, nsend.at[k], nrecv.at[k], over_core)

    def piece_over(k):
        view = piece_view(k, 1 - x, core)
        landed(view, pxrecv.at[k])
        go(view, view, pfsend.at[k], pfrecv.at[k], over_core)

    copies[0].wait()
    landed(small.at[1 - y], small_sem.at[1])
    normed, scale = normalise(patches[...].astype(jnp.float32))
    low = (normed * pack.read(small, "gain1") + pack.read(small, "bias1")).astype(bf16)
    normed_low[...] = low
    low_own = jnp.where(y == 0, low[:, :half], low[:, half:])
    low_far = jnp.where(y == 0, low[:, half:], low[:, :half])
    for i, b in enumerate(order):
        view = share(x, core, b)
        landed(view, yrecv.at[b])
        go(view, view, xsend.at[b], xrecv.at[b], over_x)
        go(view, view, csend.at[b], crecv.at[b], over_core)
    for k, (src, unused, apart, unused, count, first, across) in enumerate(pieces):
        span = pl.ds(x * across + core * apart + first, count)
        go(src.at[span], piece_view(k, x, core), psend.at[k], precv.at[k], over_y)

    copies[1].wait()

    def block(pz, px, pcore, b):
        return keys.at[pz * PEERS + px * 2 + pcore, pl.ds((b - 1) * part, part)]

    own = []
    for i, b in enumerate(order):
        view = share(1 - x, core, b)
        landed(view, xrecv.at[b])
        go(view, view, fsend.at[b], frecv.at[b], over_core)
        landed(share(x, 1 - core, b), crecv.at[b])
        landed(share(1 - x, 1 - core, b), frecv.at[b])
        made = dot(low_own, qkv_own[:, b * width : (b + 1) * width])
        made = made + dot(low_far, qkv_far[:, b * width : (b + 1) * width])
        if b != 1:
            made = made + pack.read(small, "bqv", (b // 2) * width, width)
        staged[b] = made.astype(bf16).T.reshape(GROUPS, part, rows)
        for d in (2, 1, 3):
            target = (z + d) % GROUPS
            if b == 0:
                dst, sems = query.at[z], (query_send.at[d], query_recv.at[d])
            else:
                sem = (b - 1) * GROUPS + d
                dst, sems = block(z, x, core, b), (zsend.at[sem], zrecv.at[sem])
            go(staged.at[b, target], dst, sems[0], sems[1], around[d - 1])
        dst = query.at[z] if b == 0 else block(z, x, core, b)
        own.append(pltpu.make_async_copy(staged.at[b, z], dst, local.at[3 + i]))
        own[-1].start()
        if b > 0:
            sem = (b - 1) * GROUPS
            go(staged.at[b, z], dst, kxsend.at[sem], kxrecv.at[sem], over_x)
            go(staged.at[b, z], dst, kcsend.at[sem], kcrecv.at[sem], over_core)

    sequence = [(1, 0), (2, 0)] + [(b, d) for b in (1, 2) for d in (1, 3, 2)]
    for i in range(len(sequence) + 1):
        if i < len(sequence):
            b, d = sequence[i]
            sem = (b - 1) * GROUPS + d
            if d > 0:
                view = block((z + GROUPS - d) % GROUPS, x, core, b)
                landed(view, zrecv.at[sem])
                go(view, view, kxsend.at[sem], kxrecv.at[sem], over_x)
                go(view, view, kcsend.at[sem], kcrecv.at[sem], over_core)
        if i >= 1:
            b, d = sequence[i - 1]
            sem = (b - 1) * GROUPS + d
            view = block((z + GROUPS - d) % GROUPS, 1 - x, core, b)
            landed(view, kxrecv.at[sem])
            go(view, view, kfsend.at[sem], kfrecv.at[sem], over_core)
        if 2 <= i < 2 + shared:
            piece_in(i - 2)
    for k in range(shared, len(pieces)):
        piece_in(k)
    for k in range(shared):
        piece_over(k)
    for b, d in sequence:
        sem = (b - 1) * GROUPS + d
        pz = (z + GROUPS - d) % GROUPS
        landed(block(pz, x, 1 - core, b), kcrecv.at[sem])
        landed(block(pz, 1 - x, 1 - core, b), kfrecv.at[sem])
    for d in range(1, GROUPS):
        landed(query.at[(z + GROUPS - d) % GROUPS], query_recv.at[d])
    for k in range(len(pieces)):
        landed(piece_view(k, x, 1 - core), nrecv.at[k])
    for k in range(shared):
        landed(piece_view(k, 1 - x, 1 - core), pfrecv.at[k])
    for copy in copies[2:] + own:
        copy.wait()
    go.finish()


def front(pack, patches, small_half, qkv_half, out_half, up_half, down_half):
    f32, bf16 = jnp.float32, jnp.bfloat16
    vmem = pl.BlockSpec(memory_space=pltpu.VMEM)
    hbm = pl.BlockSpec(memory_space=pltpu.HBM)
    rows, width = patches.shape
    part, half = width // GROUPS, qkv_half.shape[0]
    dma = pltpu.SemaphoreType.DMA

    def pair(n):
        return [dma((n,))] * 2

    return pl.pallas_call(
        functools.partial(front_kernel, pack),
        out_shape=[
            jax.ShapeDtypeStruct((GROUPS, part, rows), bf16),
            jax.ShapeDtypeStruct((GROUPS * PEERS, 2 * part, rows), bf16),
            jax.ShapeDtypeStruct((rows, width), bf16),
            jax.ShapeDtypeStruct((2,) + small_half.shape, f32),
            jax.ShapeDtypeStruct(qkv_half.shape, bf16),
            jax.ShapeDtypeStruct(out_half.shape, bf16),
            jax.ShapeDtypeStruct(up_half.shape, bf16),
            jax.ShapeDtypeStruct((down_half.shape[0] // 2, width), bf16),
            jax.ShapeDtypeStruct((down_half.shape[0] // 4, width), bf16),
        ],
        in_specs=[vmem, hbm, hbm, hbm, hbm, hbm],
        out_specs=[vmem] * 9,
        scratch_shapes=[
            pltpu.VMEM(qkv_half.shape, bf16),
            pltpu.VMEM((3, GROUPS, part, rows), bf16),
            dma((6,)),
        ]
        + [dma((2,))]
        + pair(3) * 4
        + pair(5) * 2
        + pair(2) * 2
        + pair(GROUPS)
        + pair(2 * GROUPS) * 4,
        compiler_params=params(60, 1),
        name="front",
    )(patches, small_half, qkv_half, out_half, up_half, down_half)


def split_rows(first, x, y, quarter):
    if first == "y":
        return [((1 - y) * 2 * quarter, 2 * quarter)], [(y * 2 * quarter, 2 * quarter)]
    other, mine = (1 - x) * quarter, x * quarter
    return (
        [(other, quarter), (2 * quarter + other, quarter)],
        [(mine, quarter), (2 * quarter + mine, quarter)],
    )


def core_sum(first, own, land, send_ref, keep_ref, x, y):
    quarter = land.shape[0] // 4
    gone, kept = split_rows(first, x, y, quarter)
    for ref, parts in ((send_ref, gone), (keep_ref, kept)):
        place = 0
        for start, count in parts:
            rows = pl.ds(start, count)
            total = own(rows).astype(jnp.float32) + land[rows].astype(jnp.float32)
            ref[pl.ds(place, count)] = total.astype(ref.dtype)
            place += count


def middle_kernel(
    pack,
    firsts,
    heads,
    patches,
    out_grad,
    small,
    w_out,
    w_out_far,
    w_up,
    w_up_far,
    w_down_half,
    w_down_got,
    w_down_far,
    mixed,
    hidden_grad,
    grad_heads,
    send_over_x,
    send_over_y,
    send_rest,
    keep,
    vector,
    o_land,
    o_grad,
    wout,
    wup,
    wdown,
    act_grad,
    act_turned,
    pre_grad,
    bup_rows,
    grads,
    c_land,
    local,
    osend,
    orecv,
    gsend,
    grecv,
    wsem,
    csend,
    crecv,
):
    f32, bf16 = jnp.float32, jnp.bfloat16
    z, x, core, y = here()
    over_core = at(z, x, 1 - core, y)
    around = [at((z + d) % GROUPS, x, core, y) for d in range(1, GROUPS)]
    rows, width = patches.shape
    tiles = wdown.shape[0] // width
    half = w_down_half.shape[0]
    far = w_down_far.shape[0]
    greet(around + [over_core])
    go = Sender()
    near = half // 2 - far
    far_rows = pl.ds((1 - y) * half + core * (half // 2) + near, far)
    other_rows = pl.ds((1 - y) * half + (1 - core) * (half // 2) + near, far)
    for d in (2, 1, 3):
        go(heads.at[(z + d) % GROUPS], o_land.at[z], osend.at[d], orecv.at[d], around[d - 1])
    go(w_down_far, wdown.at[far_rows], wsem.at[0], wsem.at[1], over_core)
    down_copies = [
        pltpu.make_async_copy(w_down_half, wdown.at[pl.ds(y * half, half)], local.at[0]),
        pltpu.make_async_copy(w_down_far, wdown.at[far_rows], local.at[1]),
    ]
    for c in range(2):
        src = w_down_got.at[pl.ds(c * near, near)]
        dst = wdown.at[pl.ds((1 - y) * half + c * (half // 2), near)]
        down_copies.append(pltpu.make_async_copy(src, dst, local.at[8 + c]))
    copies = [
        pltpu.make_async_copy(heads.at[z], o_land.at[z], local.at[2]),
    ]
    pairs = [(w_out, wout, y), (w_out_far, wout, 1 - y), (w_up, wup, y), (w_up_far, wup, 1 - y)]
    for i, (src, dst, side) in enumerate(pairs):
        count = src.shape[0]
        span = pl.ds(side * count, count)
        copies.append(pltpu.make_async_copy(src, dst.at[span], local.at[4 + i]))

    for copy in down_copies + copies:
        copy.start()
    dy = out_grad[...]
    vector[...] = jnp.zeros(vector.shape, f32)
    pack.write(vector, "bdown", jnp.sum(dy.astype(f32), axis=0, keepdims=True))
    for f in range(tiles):
        bup_rows[f, 0:1] = pack.read(small, "bup", f * width, width)
    for copy in down_copies:
        copy.wait()
    landed = wdown.at[other_rows]
    remote(landed, landed, wsem.at[0], wsem.at[1], over_core).wait_recv()

    def tile(f):
        return pl.ds(pl.multiple_of(f * width, width), width)

    def first_grad(f, carry):
        act_grad[f] = dot_turned(dy, wdown[tile(f)])
        return carry

    lax.fori_loop(0, tiles, first_grad, 0)
    for copy in copies:
        copy.wait()
    for d in range(1, GROUPS):
        landed = o_land.at[(z + GROUPS - d) % GROUPS]
        remote(landed, landed, osend.at[d], orecv.at[d], over_core).wait_recv()
    turned = o_land[...].reshape(width, rows)
    hidden = patches[...].astype(f32) + (dot(turned.T, wout[...]) + pack.read(small, "bout"))
    gain2 = pack.read(small, "gain2")
    normed, scale = normalise(hidden)
    c = (normed * gain2 + pack.read(small, "bias2")).astype(bf16)
    mixed_acc = hidden + pack.read(small, "bdown")
    c_grad = jnp.zeros((rows, width), f32)

    def forward_back(f, carry):
        mixed_acc, c_grad = carry
        up = wup[:, tile(f)]
        pre = dot(c, up) + bup_rows[f, 0:1]
        share = 0.5 + 0.5 * lax.erf(pre * (0.5**0.5))
        slope = share + pre * jnp.exp(-0.5 * pre * pre) * ((0.5 / jnp.pi) ** 0.5)
        act = (pre * share).astype(bf16)
        grad = (act_grad[f] * slope).astype(bf16)
        act_turned[tile(f)] = act.T
        pre_grad[f] = grad
        bup_rows[f, 0:1] = jnp.sum(grad.astype(f32), axis=0, keepdims=True)
        return (
            mixed_acc + dot(act, wdown[tile(f)]),
            c_grad + dot_turned(grad, up),
        )

    mixed_acc, c_grad = lax.fori_loop(0, tiles, forward_back, (mixed_acc, c_grad))
    mixed[...] = mixed_acc.astype(bf16)
    for f in range(tiles):
        pack.write(vector, "bup", bup_rows[f, 0:1], f * width)
    part, gain_grad, bias_grad = normalise_back(c_grad, gain2, normed, scale)
    pack.write(vector, "gain2", gain_grad)
    pack.write(vector, "bias2", bias_grad)
    whole = dy.astype(f32) + part
    hidden_grad[...] = whole
    dz = whole.astype(bf16)
    pack.write(vector, "bout", jnp.sum(dz.astype(f32), axis=0, keepdims=True))
    o_grad[...] = dot_turned(wout[...], dz).astype(bf16).reshape(o_grad.shape)
    for d in (2, 1, 3):
        go(o_grad.at[(z + d) % GROUPS], grad_heads.at[z], gsend.at[d], grecv.at[d], around[d - 1])
    own = pltpu.make_async_copy(o_grad.at[z], grad_heads.at[z], local.at[3])
    own.start()

    columns = c_land.shape[2]
    count = grads.shape[0]
    mine = pl.ds(pl.multiple_of(core * columns, columns), columns)
    others = pl.ds(pl.multiple_of((1 - core) * columns, columns), columns)

    def over(k):
        go(grads.at[k, :, others], c_land.at[k], csend.at[k], crecv.at[k], over_core)

    def settle(k):
        landed = c_land.at[k]
        remote(landed, landed, csend.at[k], crecv.at[k], over_core).wait_recv()
        place, sent = k, None
        for ref in (send_over_x, send_over_y, send_rest):
            if sent is None and place < ref.shape[0]:
                sent = ref.at[place]
            place -= ref.shape[0]
        core_sum(firsts[k], lambda r: grads[k, r, mine], c_land.at[k], sent, keep.at[k], x, y)

    c_turned = c.T
    piece = half // tiles
    for k in range(count):
        if k < tiles:
            for top in range(2):
                grads[k, top * piece : (top + 1) * piece] = dot(
                    act_turned[top * half + k * piece : top * half + (k + 1) * piece], dy
                ).astype(bf16)
        elif k < 2 * tiles:
            grads[k] = dot(c_turned, pre_grad[k - tiles]).astype(bf16)
        else:
            grads[k] = dot(turned, dz).astype(bf16)
        over(k)
        if k >= 2:
            settle(k - 2)
    settle(count - 2)
    settle(count - 1)
    for d in range(1, GROUPS):
        landed = grad_heads.at[(z + GROUPS - d) % GROUPS]
        remote(landed, landed, gsend.at[d], grecv.at[d], over_core).wait_recv()
    own.wait()
    go.finish()


def middle(pack, firsts, ahead, heads, patches, out_grad, small, *weights):
    rows, width = patches.shape
    hidden = weights[2].shape[1]
    tiles = hidden // width
    count = 2 * tiles + 1
    f32, bf16 = jnp.float32, jnp.bfloat16
    vmem = pl.BlockSpec(memory_space=pltpu.VMEM)
    hbm = pl.BlockSpec(memory_space=pltpu.HBM)
    dma = pltpu.SemaphoreType.DMA
    return pl.pallas_call(
        functools.partial(middle_kernel, pack, firsts),
        out_shape=[
            jax.ShapeDtypeStruct((rows, width), bf16),
            jax.ShapeDtypeStruct((rows, width), f32),
            jax.ShapeDtypeStruct(heads.shape, bf16),
            jax.ShapeDtypeStruct((ahead, width // 2, width // 2), bf16),
            jax.ShapeDtypeStruct((ahead, width // 2, width // 2), bf16),
            jax.ShapeDtypeStruct((count - 2 * ahead, width // 2, width // 2), bf16),
            jax.ShapeDtypeStruct((count, width // 2, width // 2), bf16),
            jax.ShapeDtypeStruct((2, pack.rows, LANES), f32),
        ],
        in_specs=[hbm, vmem, vmem, vmem] + [hbm] * 7,
        out_specs=[vmem] * 8,
        scratch_shapes=[
            pltpu.VMEM(heads.shape, bf16),
            pltpu.VMEM(heads.shape, bf16),
            pltpu.VMEM((width, width), bf16),
            pltpu.VMEM((width, hidden), bf16),
            pltpu.VMEM((hidden, width), bf16),
            pltpu.VMEM((tiles, rows, width), f32),
            pltpu.VMEM((hidden, rows), bf16),
            pltpu.VMEM((tiles, rows, width), bf16),
            pltpu.VMEM((tiles, 8, width), f32),
            pltpu.VMEM((count, width, width), bf16),
            pltpu.VMEM((count, width, width // 2), bf16),
            dma((10,)),
            dma((GROUPS,)),
            dma((GROUPS,)),
            dma((GROUPS,)),
            dma((GROUPS,)),
            dma((2,)),
            dma((count,)),
            dma((count,)),
        ],
        compiler_params=params(60, 3),
        name="middle",
    )(heads, patches, out_grad, small, *weights)


class Totals:
    def __init__(self, refs, tiles):
        self.refs, self.tiles = refs, tiles

    def place(self, k, row, count, column, columns):
        width = self.refs[2].shape[1]
        start = 0
        if k < self.tiles:
            which, row = 0, k * (width // 2) + row
        elif k < 2 * self.tiles:
            which, start = 1, (k - self.tiles) * width
        elif k == 2 * self.tiles:
            which = 2
        else:
            which, start = 3, (k - 2 * self.tiles - 1) * width
        return which, pl.ds(row, count), pl.ds(pl.multiple_of(start + column, LANES), columns)

    def view(self, *place):
        which, rows, columns = self.place(*place)
        return self.refs[which].at[rows, columns]

    def store(self, values, *place):
        which, rows, columns = self.place(*place)
        ref = self.refs[which]
        ref[rows, columns] = values.astype(ref.dtype)


def last_kernel(
    pack,
    firsts,
    tiles,
    query_grad,
    key_grad,
    normed_low,
    w_qkv,
    w_qkv_far,
    patches,
    hidden_grad,
    small,
    ahead_x,
    ahead_y,
    send_rest,
    keep,
    vector_in,
    inputs_grad,
    down_out,
    up_out,
    out_out,
    qkv_out,
    vector_out,
    down_total,
    up_total,
    out_total,
    qkv_total,
    got,
    near,
    both,
    far,
    own,
    wqkv,
    grads,
    c_land,
    late_send,
    first_land,
    half_sum,
    second_land,
    quarter_sum,
    z_land,
    eighth_sum,
    far_land,
    vectors,
    v_land,
    local,
    loads,
    n_send,
    n_recv,
    f_send,
    f_recv,
    q_send,
    q_recv,
    csend,
    crecv,
    asend,
    arecv,
    bsend,
    brecv,
    zsend,
    zrecv,
    wsend,
    wrecv,
    dsend,
    drecv,
    gsend,
    grecv,
    hsend,
    hrecv,
    isend,
    irecv,
    vsend,
    vrecv,
):
    f32, bf16 = jnp.float32, jnp.bfloat16
    z, x, core, y = here()
    pair, side = z // 2, z % 2
    over_x, over_core, over_y = (
        at(z, 1 - x, core, y),
        at(z, x, 1 - core, y),
        at(z, x, core, 1 - y),
    )
    around = [at((z + d) % GROUPS, x, core, y) for d in range(1, GROUPS)]
    over_near, over_far = at(z + 1 - 2 * side, x, core, y), around[1]
    peer = {"y": over_y, "x": over_x}
    greet(around + [over_x, over_core, over_y])
    go = Sender()
    totals = Totals((down_total, up_total, out_total, qkv_total), tiles)
    outs = Totals((down_out, up_out, out_out, qkv_out), tiles)
    part = query_grad.shape[1]
    rows, width = patches.shape
    chunks, early, late = len(firsts), keep.shape[0], c_land.shape[0]
    ahead = ahead_x.shape[0]
    hidden = ahead + ahead_y.shape[0]
    half = c_land.shape[2]
    quarter, shard = width // 4, width // 16

    def landed(view, sem):
        remote(view, view, sem, sem, over_core).wait_recv()

    order = (2, 1, 3, 0)
    held = []
    for d in order:
        pz = (z + d) % GROUPS
        for k in range(2):
            px = (x + 1 + k) % 2
            slot = 2 * d + k
            src = key_grad.at[pz * PEERS + px * 2 + 1 - core]
            go(src, near.at[slot], n_send.at[slot], n_recv.at[slot], over_core)
            src = key_grad.at[pz * PEERS + px * 2 + core]
            copy = pltpu.make_async_copy(src, both.at[slot], local.at[4 + slot])
            copy.start()
            held.append((slot, copy))
    held = dict(held)
    for d in (2, 1, 3):
        pz = (z + d) % GROUPS
        go(query_grad.at[pz], got.at[z, pl.ds(0, part)], q_send.at[d], q_recv.at[d], around[d - 1])
    own_query = pltpu.make_async_copy(query_grad.at[z], got.at[z, pl.ds(0, part)], local.at[0])
    own_query.start()
    arrivals = []
    for k in range(early):
        arrivals.append([pltpu.make_async_copy(keep.at[k], half_sum.at[k], loads.at[2 * k])])
        if k < hidden:
            src = ahead_x.at[k] if k < ahead else ahead_y.at[k - ahead]
            copy = pltpu.make_async_copy(src, first_land.at[k], loads.at[2 * k + 1])
            arrivals[k].append(copy)
        else:
            sem = late + k - hidden
            src = send_rest.at[k - hidden]
            go(src, first_land.at[k], asend.at[sem], arecv.at[sem], peer[firsts[k]])
        for copy in arrivals[k]:
            copy.start()
    count = w_qkv.shape[0]
    weights = [
        pltpu.make_async_copy(w_qkv, wqkv.at[pl.ds(y * count, count)], local.at[2]),
        pltpu.make_async_copy(w_qkv_far, wqkv.at[pl.ds((1 - y) * count, count)], local.at[3]),
    ]
    for copy in weights:
        copy.start()

    def collect_near(step):
        d = order[step]
        for k in range(2):
            slot = 2 * d + k
            landed(near.at[slot], n_recv.at[slot])
            held[slot].wait()
            both[slot] = (both[slot].astype(f32) + near[slot].astype(f32)).astype(bf16)
            if k == 0:
                go(both.at[slot], far.at[d], f_send.at[d], f_recv.at[d], over_x)

    def collect_far(step):
        d = order[step]
        landed(far.at[d], f_recv.at[d])
        own[d] = (both[2 * d + 1].astype(f32) + far[d].astype(f32)).astype(bf16)
        place = got.at[z, pl.ds(part, 2 * part)]
        if d == 0:
            copy = pltpu.make_async_copy(own.at[0], place, local.at[1])
            copy.start()
            return copy
        sem = GROUPS + d
        go(own.at[d], place, q_send.at[sem], q_recv.at[sem], around[d - 1])
        return None

    def stage_core(k):
        i = k - early
        landed(c_land.at[i], crecv.at[i])
        mine = pl.ds(pl.multiple_of(core * half, half), half)
        core_sum(
            firsts[k],
            lambda r: grads[i, r, mine],
            c_land.at[i],
            late_send.at[i],
            half_sum.at[k],
            x,
            y,
        )
        go(late_send.at[i], first_land.at[k], asend.at[i], arecv.at[i], peer[firsts[k]])

    def stage_first(k):
        if k < early:
            for copy in arrivals[k]:
                copy.wait()
        if k >= hidden:
            landed(first_land.at[k], arecv.at[k - early if k >= early else late + k - hidden])
        half_sum[k] = (half_sum[k].astype(f32) + first_land[k].astype(f32)).astype(bf16)
        place = x if firsts[k] == "y" else y
        other = half_sum.at[k, pl.ds((1 - place) * quarter, quarter)]
        second = over_x if firsts[k] == "y" else over_y
        go(other, second_land.at[k], bsend.at[k], brecv.at[k], second)

    def stage_second(k):
        landed(second_land.at[k], brecv.at[k])
        place = x if firsts[k] == "y" else y
        total = half_sum[k, pl.ds(place * quarter, quarter)].astype(f32)
        quarter_sum[k] = (total + second_land[k].astype(f32)).astype(bf16)
        other = quarter_sum.at[k, pl.ds((1 - side) * 2 * shard, 2 * shard)]
        go(other, z_land.at[k], zsend.at[k], zrecv.at[k], over_near)

    def stage_near(k):
        landed(z_land.at[k], zrecv.at[k])
        total = quarter_sum[k, pl.ds(side * 2 * shard, 2 * shard)].astype(f32)
        eighth_sum[k] = (total + z_land[k].astype(f32)).astype(bf16)
        other = eighth_sum.at[k, pl.ds((1 - pair) * shard, shard)]
        go(other, far_land.at[k], wsend.at[k], wrecv.at[k], over_far)

    def spot(k, px, pside, ppair, count):
        row = px * quarter + pside * 2 * shard + ppair * shard
        return totals.view(k, row, count, core * half, half)

    def stage_far(k):
        landed(far_land.at[k], wrecv.at[k])
        total = eighth_sum[k, pl.ds(pair * shard, shard)].astype(f32) + far_land[k].astype(f32)
        row = x * quarter + side * 2 * shard + pair * shard
        totals.store(total, k, row, shard, core * half, half)
        view = spot(k, x, side, pair, shard)
        go(view, view, dsend.at[k], drecv.at[k], over_far)

    def stage_back(k):
        landed(spot(k, x, side, 1 - pair, shard), drecv.at[k])
        view = spot(k, x, side, 0, 2 * shard)
        go(view, view, gsend.at[k], grecv.at[k], over_near)

    def stage_out(k):
        landed(spot(k, x, 1 - side, 0, 2 * shard), grecv.at[k])
        view = spot(k, x, 0, 0, quarter)
        go(view, view, hsend.at[k], hrecv.at[k], over_x)
        go(view, view, isend.at[2 * k], irecv.at[2 * k], over_core)

    def stage_last(k):
        view = spot(k, 1 - x, 0, 0, quarter)
        landed(view, hrecv.at[k])
        go(view, view, isend.at[2 * k + 1], irecv.at[2 * k + 1], over_core)

    written = []

    def stage_write(k):
        for px in range(2):
            place = (x + px) % 2
            view = totals.view(k, place * quarter, quarter, (1 - core) * half, half)
            landed(view, irecv.at[2 * k + px])
        place = (k, 0, 2 * quarter, 0, 2 * half)
        copy = pltpu.make_async_copy(totals.view(*place), outs.view(*place), loads.at[2 * early + k])
        copy.start()
        written.append(copy)

    stages = (
        stage_first,
        stage_second,
        stage_near,
        stage_far,
        stage_back,
        stage_out,
        stage_last,
        stage_write,
    )

    def vector_step(n):
        if n == 0:
            landed(v_land.at[0], vrecv.at[0])
            vectors[1] = vectors[0] + v_land[0]
            go(vectors.at[1], v_land.at[1], vsend.at[1], vrecv.at[1], over_x)
        elif n == 1:
            landed(v_land.at[1], vrecv.at[1])
            vectors[2] = vectors[1] + v_land[1]
            go(vectors.at[2], v_land.at[2], vsend.at[2], vrecv.at[2], over_y)
        elif n == 2:
            landed(v_land.at[2], vrecv.at[2])
            vectors[3] = vectors[2] + v_land[2]
            for d in range(1, GROUPS):
                sem = 2 + d
                go(vectors.at[3], v_land.at[sem], vsend.at[sem], vrecv.at[sem], around[d - 1])
        elif n == 3:
            total = vectors[3]
            for d in range(1, GROUPS):
                landed(v_land.at[2 + d], vrecv.at[2 + d])
                total += v_land[2 + d]
            v_land[0] = total
            vector_out[...] = v_land[0, y]

    mixed = [2 * k for k in range(ahead)] + [2 * k + 1 for k in range(hidden - ahead)]
    entry = mixed + list(range(hidden, early)) + [LATE_TURN + i for i in range(late)]
    turns = iter(range(entry[-1] + len(stages)))

    def turn():
        step = next(turns, None)
        if step is None:
            return False
        for depth, stage in enumerate(stages):
            for k in range(chunks):
                if step - depth == entry[k]:
                    stage(k)
        return True

    collect_near(0)
    turn()
    for step in range(1, GROUPS):
        collect_near(step)
        collect_far(step - 1)
        turn()
    own_keys = collect_far(GROUPS - 1)
    turn()
    normed_turned = normed_low[...].T
    normed, scale = normalise(patches[...].astype(f32))
    gain1 = pack.read(small, "gain1")
    turn()
    for d in range(1, GROUPS):
        landed(got.at[(z + GROUPS - d) % GROUPS, pl.ds(0, part)], q_recv.at[d])
    own_query.wait()
    turn()
    others = pl.ds(pl.multiple_of((1 - core) * half, half), half)

    def project(i):
        turned = got[:, i * part : (i + 1) * part].reshape(width, rows)
        grads[i] = dot_turned(normed_turned, turned).astype(bf16)
        go(grads.at[i, :, others], c_land.at[i], csend.at[i], crecv.at[i], over_core)

    project(0)
    for d in range(1, GROUPS):
        landed(got.at[(z + GROUPS - d) % GROUPS, pl.ds(part, 2 * part)], q_recv.at[GROUPS + d])
    own_keys.wait()
    for i in range(1, late):
        project(i)
    turn()
    for copy in weights:
        copy.wait()
    vectors[0] = vector_in[...]
    ones = jnp.ones((8, rows), bf16)
    normed_grad = jnp.zeros((width, rows), f32)
    for i in range(late):
        turned = got[:, i * part : (i + 1) * part].reshape(width, rows)
        if i != 1:
            sums = dot_turned(ones, turned)[0:1]
            pack.write(vectors.at[0], "bqv", sums, (i // 2) * width)
        normed_grad += dot(wqkv[:, i * width : (i + 1) * width], turned)
        stage_core(early + i)
    turn()
    change, gain_grad, bias_grad = normalise_back(normed_grad.T, gain1, normed, scale)
    inputs_grad[...] = hidden_grad[...] + change
    pack.write(vectors.at[0], "gain1", gain_grad)
    pack.write(vectors.at[0], "bias1", bias_grad)
    go(vectors.at[0], v_land.at[0], vsend.at[0], vrecv.at[0], over_core)
    step = 0
    while turn():
        vector_step(step)
        step += 1
    for copy in written:
        copy.wait()
    go.finish()


LATE_TURN = 8


def last(
    pack, firsts, query_grad, key_grad, normed_low, w_qkv, w_qkv_far, patches, hidden_grad, small,
    ahead_x, ahead_y, send_rest, keep, vector
):
    f32, bf16 = jnp.float32, jnp.bfloat16
    vmem = pl.BlockSpec(memory_space=pltpu.VMEM)
    hbm = pl.BlockSpec(memory_space=pltpu.HBM)
    groups, part, rows = query_grad.shape
    width = patches.shape[1]
    early, half = keep.shape[0], width // 2
    tiles, chunks, late = (early - 1) // 2, len(firsts), len(firsts) - early
    piece = (2 * part, rows)
    dma = pltpu.SemaphoreType.DMA
    totals = [
        (tiles * half, width),
        (half, tiles * width),
        (half, width),
        (half, late * width),
    ]

    def pair(n):
        return [dma((n,))] * 2

    return pl.pallas_call(
        functools.partial(last_kernel, pack, firsts, tiles),
        out_shape=[jax.ShapeDtypeStruct((rows, width), f32)]
        + [jax.ShapeDtypeStruct(shape, bf16) for shape in totals]
        + [jax.ShapeDtypeStruct(vector.shape[1:], f32)],
        in_specs=[hbm, hbm, vmem, hbm, hbm, vmem, vmem, vmem, hbm, hbm, hbm, hbm, vmem],
        out_specs=[vmem] + [hbm] * 4 + [vmem],
        scratch_shapes=[pltpu.VMEM(shape, bf16) for shape in totals]
        + [
            pltpu.VMEM((groups, 3 * part, rows), bf16),
            pltpu.VMEM((2 * groups,) + piece, bf16),
            pltpu.VMEM((2 * groups,) + piece, bf16),
            pltpu.VMEM((groups,) + piece, bf16),
            pltpu.VMEM((groups,) + piece, bf16),
            pltpu.VMEM((width, late * width), bf16),
            pltpu.VMEM((late, width, width), bf16),
            pltpu.VMEM((late, width, half), bf16),
            pltpu.VMEM((late, half, half), bf16),
            pltpu.VMEM((chunks, half, half), bf16),
            pltpu.VMEM((chunks, half, half), bf16),
            pltpu.VMEM((chunks, half // 2, half), bf16),
            pltpu.VMEM((chunks, half // 2, half), bf16),
            pltpu.VMEM((chunks, half // 4, half), bf16),
            pltpu.VMEM((chunks, half // 4, half), bf16),
            pltpu.VMEM((chunks, half // 8, half), bf16),
            pltpu.VMEM((4,) + vector.shape, f32),
            pltpu.VMEM((6,) + vector.shape, f32),
            dma((4 + 2 * groups,)),
            dma((2 * early + chunks,)),
        ]
        + pair(2 * groups)
        + pair(groups)
        + pair(2 * groups)
        + pair(late)
        + pair(chunks)
        + pair(chunks) * 6
        + pair(2 * chunks)
        + pair(6),
        compiler_params=params(60, 4),
        name="last",
    )(
        query_grad, key_grad, normed_low, w_qkv, w_qkv_far, patches, hidden_grad, small,
        ahead_x, ahead_y, send_rest, keep, vector,
    )


class Documents:
    def __init__(self, lengths, rows):
        self.rows, self.count = rows, lengths.shape[1]
        self.starts, self.ends, place = [], [], 0
        for d in range(self.count):
            self.starts.append(place)
            place = place + lengths[0, d]
            self.ends.append(place)

    def span(self, block):
        first, last = block * self.rows, (block + 1) * self.rows - 1
        low, high = 0, 0
        for d in range(self.count):
            low = jnp.where(self.starts[d] <= first, self.starts[d], low)
        for d in reversed(range(self.count)):
            high = jnp.where(self.ends[d] > last, self.ends[d], high)
        return low // self.rows, (high + self.rows - 1) // self.rows

    def inside(self, block, yes, no):
        shape = (8, self.rows)
        row = lax.broadcasted_iota(jnp.int32, shape, 0)
        place = block * self.rows + lax.broadcasted_iota(jnp.int32, shape, 1)
        found = jnp.where(row < self.count, no, 0.0)
        for d in range(self.count):
            hit = (row == d) & (place >= self.starts[d]) & (place < self.ends[d])
            found = jnp.where(hit, yes, found)
        return found

    def marks(self, block):
        ones, rest = jnp.ones((8, self.rows)), jnp.zeros((HD - 16, self.rows))
        return jnp.concatenate([self.inside(block, 1.0, 0.0), ones, rest]).astype(jnp.bfloat16)

    def veto(self, block):
        rest = jnp.zeros((HD - 8, self.rows))
        return jnp.concatenate([self.inside(block, 0.0, masked_score), rest])


def attend_kernel(
    lengths, place, query, keys, out, out_low, sums, key_rows, query_aug, acc, stat
):
    blocks, rows = keys.shape[0], keys.shape[2]
    width = query.shape[1]
    groups = query.shape[0]
    documents = Documents(lengths, rows)

    def turn(j, carry):
        mark = documents.marks(j)
        for h in range(PER_GROUP):
            both = jnp.concatenate([keys[j, h * HD : (h + 1) * HD], mark], axis=0)
            key_rows[h, j] = both.T
        return carry

    lax.fori_loop(0, blocks, turn, 0)
    for i in range(groups):
        block = i * PEERS + place[0]
        veto = documents.veto(block).astype(jnp.bfloat16)
        for h in range(PER_GROUP):
            query_aug[h, :HD] = query[i, h * HD : (h + 1) * HD] * jnp.bfloat16(0.125)
            query_aug[h, HD:] = veto
        stat[0] = jnp.full(stat.shape[1:], masked_score, jnp.float32)
        stat[1] = jnp.zeros(stat.shape[1:], jnp.float32)
        acc[...] = jnp.zeros(acc.shape, jnp.float32)

        low, high = documents.span(block)
        steps = (high - low + 1) // 2
        low = jnp.minimum(low, blocks - 2 * steps)

        def step(n, carry):
            j = low + 2 * n
            made = [
                [dot(key_rows[h, j + k], query_aug[h]) for k in range(2)] for h in range(PER_GROUP)
            ]
            for h in range(PER_GROUP):
                first, second = made[h]
                old = stat[0, h : h + 1]
                most = jnp.max(jnp.maximum(first, second), axis=0, keepdims=True)
                new = jnp.maximum(old, most)
                first, second = jnp.exp(first - new), jnp.exp(second - new)
                factor = jnp.exp(old - new)
                stat[0, h : h + 1] = new
                stat[1, h : h + 1] = stat[1, h : h + 1] * factor + jnp.sum(
                    first + second, axis=0, keepdims=True
                )
                span = slice(width + h * HD, width + (h + 1) * HD)
                shared = dot(keys[j, span], first.astype(jnp.bfloat16))
                shared += dot(keys[j + 1, span], second.astype(jnp.bfloat16))
                acc[h] = acc[h] * factor + shared
            return carry

        lax.fori_loop(0, steps, step, 0)
        for h in range(PER_GROUP):
            total = stat[1, h : h + 1]
            shared = acc[h] / total
            out[i, h * HD : (h + 1) * HD] = shared
            out_low[i, h * HD : (h + 1) * HD] = shared.astype(jnp.bfloat16)
            sums[i, h : h + 1] = stat[0, h : h + 1] + jnp.log(total)


def attend(lengths, place, query, keys):
    groups, width, rows = query.shape
    blocks = keys.shape[0]
    vmem = pl.BlockSpec(memory_space=pltpu.VMEM)
    return pl.pallas_call(
        attend_kernel,
        out_shape=[
            jax.ShapeDtypeStruct(query.shape, jnp.float32),
            jax.ShapeDtypeStruct(query.shape, jnp.bfloat16),
            jax.ShapeDtypeStruct((groups, 8, rows), jnp.float32),
        ],
        in_specs=[pl.BlockSpec(memory_space=pltpu.SMEM)] * 2 + [vmem] * 2,
        out_specs=[vmem] * 3,
        scratch_shapes=[
            pltpu.VMEM((PER_GROUP, blocks, rows, 2 * HD), jnp.bfloat16),
            pltpu.VMEM((PER_GROUP, 2 * HD, rows), jnp.bfloat16),
            pltpu.VMEM((PER_GROUP, HD, rows), jnp.float32),
            pltpu.VMEM((2, 8, rows), jnp.float32),
        ],
        compiler_params=params(60),
        name="attend",
    )(lengths, place, query, keys)


def three_parts(values):
    high = values.astype(jnp.bfloat16)
    rest = values - high.astype(jnp.float32)
    middle = rest.astype(jnp.bfloat16)
    low = (rest - middle.astype(jnp.float32)).astype(jnp.bfloat16)
    return high, middle, low


def attend_back_kernel(
    lengths,
    place,
    query,
    keys,
    out,
    sums,
    out_grad,
    query_grad,
    key_grad,
    key_rows,
    value_rows,
    query_aug,
    grad_aug,
    query_rows,
    grad_rows,
    query_acc,
    key_acc,
):
    blocks, rows = keys.shape[0], keys.shape[2]
    width = query.shape[1]
    groups = query.shape[0]
    bf16 = jnp.bfloat16
    documents = Documents(lengths, rows)

    def turn(j, carry):
        mark = documents.marks(j)
        for h in range(PER_GROUP):
            both = jnp.concatenate([keys[j, h * HD : (h + 1) * HD], mark], axis=0)
            key_rows[h, pl.ds(pl.multiple_of(j * rows, rows), rows)] = both.T
            values = keys[j, width + h * HD : width + (h + 1) * HD]
            place = pl.ds(pl.multiple_of(j * rows, rows), rows)
            value_rows[h, place] = jnp.concatenate([values, mark], axis=0).T
            key_acc[h, place] = jnp.zeros((rows, 2 * HD), jnp.float32)
        return carry

    lax.fori_loop(0, blocks, turn, 0)
    index = lax.broadcasted_iota(jnp.int32, (HD, rows), 0)
    none = jnp.zeros((HD, rows), bf16)

    def spread(values):
        high, middle, low = three_parts(-values)
        wide = jnp.where(index == 8, high.astype(jnp.float32), 0.0)
        wide = jnp.where(index == 9, middle.astype(jnp.float32), wide)
        return jnp.where(index == 10, low.astype(jnp.float32), wide)

    for i in range(groups):
        block = i * PEERS + place[0]
        veto = documents.veto(block)
        for h in range(PER_GROUP):
            span = slice(h * HD, (h + 1) * HD)
            part = query[i, span] * bf16(0.125)
            grad = out_grad[i, span]
            delta = jnp.sum(grad.astype(jnp.float32) * out[i, span], axis=0, keepdims=True)
            query_aug[h, :HD] = part
            query_aug[h, HD:] = (veto + spread(sums[i, h : h + 1])).astype(bf16)
            grad_aug[h, :HD] = grad
            grad_aug[h, HD:] = spread(delta).astype(bf16)
            query_rows[h] = jnp.concatenate([part, none], axis=0).T
            grad_rows[h] = jnp.concatenate([none, grad], axis=0).T
        query_acc[...] = jnp.zeros(query_acc.shape, jnp.float32)

        low, high = documents.span(block)
        steps = (high - low + 1) // 2
        low = jnp.minimum(low, blocks - 2 * steps)

        def step(n, carry):
            j = low + 2 * n
            span = pl.ds(pl.multiple_of(j * rows, rows), 2 * rows)
            for h in range(PER_GROUP):
                probs = jnp.exp(dot(key_rows[h, span], query_aug[h]))
                change = (probs * dot(value_rows[h, span], grad_aug[h])).astype(bf16)
                low_probs = probs.astype(bf16)
                key_acc[h, span] += dot(low_probs, grad_rows[h]) + dot(change, query_rows[h])
                turned = slice(h * HD, (h + 1) * HD)
                query_acc[h] += dot(keys[j, turned], change[:rows]) + dot(
                    keys[j + 1, turned], change[rows:]
                )
            return carry

        lax.fori_loop(0, steps, step, 0)
        for h in range(PER_GROUP):
            query_grad[i, h * HD : (h + 1) * HD] = (query_acc[h] * 0.125).astype(bf16)

    def finish(j, carry):
        for h in range(PER_GROUP):
            both = key_acc[h, pl.ds(pl.multiple_of(j * rows, rows), rows)].astype(bf16).T
            key_grad[j, h * HD : (h + 1) * HD] = both[:HD]
            key_grad[j, width + h * HD : width + (h + 1) * HD] = both[HD:]
        return carry

    lax.fori_loop(0, blocks, finish, 0)


def attend_back(lengths, place, query, keys, out, sums, out_grad):
    groups, width, rows = query.shape
    blocks = keys.shape[0]
    vmem = pl.BlockSpec(memory_space=pltpu.VMEM)
    bf16 = jnp.bfloat16
    return pl.pallas_call(
        attend_back_kernel,
        out_shape=[
            jax.ShapeDtypeStruct(query.shape, bf16),
            jax.ShapeDtypeStruct(keys.shape, bf16),
        ],
        in_specs=[pl.BlockSpec(memory_space=pltpu.SMEM)] * 2 + [vmem] * 5,
        out_specs=[vmem] * 2,
        scratch_shapes=[
            pltpu.VMEM((PER_GROUP, blocks * rows, 2 * HD), bf16),
            pltpu.VMEM((PER_GROUP, blocks * rows, 2 * HD), bf16),
            pltpu.VMEM((PER_GROUP, 2 * HD, rows), bf16),
            pltpu.VMEM((PER_GROUP, 2 * HD, rows), bf16),
            pltpu.VMEM((PER_GROUP, rows, 2 * HD), bf16),
            pltpu.VMEM((PER_GROUP, rows, 2 * HD), bf16),
            pltpu.VMEM((PER_GROUP, HD, rows), jnp.float32),
            pltpu.VMEM((PER_GROUP, blocks * rows, 2 * HD), jnp.float32),
        ],
        compiler_params=params(60),
        name="attend_back",
    )(lengths, place, query, keys, out, sums, out_grad)


def layer_norm(values, gain, offset):
    centre = jnp.mean(values, axis=-1, keepdims=True)
    shifted = values - centre
    spread = jnp.mean(shifted * shifted, axis=-1, keepdims=True)
    return shifted * lax.rsqrt(spread + epsilon) * gain + offset


def exact_gelu(values):
    return jax.nn.gelu(values, approximate=False)


def doc_index(positions, doc_starts):
    hits = (doc_starts[None, :] <= positions[:, None]).astype(jnp.int32)
    return jnp.sum(hits, axis=1) - 1


def body(
    patches,
    doc_lengths,
    norm1_gain,
    norm1_bias,
    w_qkv,
    b_qv,
    w_out,
    b_out,
    norm2_gain,
    norm2_bias,
    w_up,
    b_up,
    w_down,
    b_down,
    cotangent,
):
    f32, bf16 = jnp.float32, jnp.bfloat16
    rows, width = patches.shape[1:]
    ctx_place = lax.axis_index("ctx")
    blocks = lax.axis_size("ctx")
    place = (ctx_place % PEERS).astype(jnp.int32).reshape(1)
    vectors = [norm1_gain, norm1_bias, b_qv, b_out, norm2_gain, norm2_bias, b_up, b_down]
    pack = Packed([v.shape[0] for v in vectors])
    query, keys, normed1, small, qkv_far, out_far, up_far, down_got, down_part = front(
        pack, patches[0], pack.pack(vectors), w_qkv, w_out, w_up, w_down
    )
    down_far = lax.ppermute(down_part, "wsh", [(0, 1), (1, 0)])
    out_heads, heads_low, sums = attend(doc_lengths, place, query, keys)
    tiles = w_up.shape[1] // width
    chunks = 2 * tiles + 1 + w_qkv.shape[1] // width
    ahead = tiles
    firsts = ["x"] * ahead + ["y"] * (chunks - ahead)
    mixed, hidden_grad, grad_heads, send_over_x, send_over_y, send_rest, keep, vector = middle(
        pack, firsts, ahead, heads_low, patches[0], cotangent[0], small, w_out, out_far, w_up,
        up_far, w_down, down_got, down_far,
    )
    across = [(c, c + 2 - c // 2 % 2 * 4) for c in range(blocks)]
    ahead_x = lax.ppermute(send_over_x, "ctx", across)
    ahead_y = lax.ppermute(send_over_y, "wsh", [(0, 1), (1, 0)])
    query_grad, key_grad = attend_back(
        doc_lengths, place, query, keys, out_heads, sums, grad_heads
    )
    inputs_grad, down_total, up_total, out_total, qkv_total, vector_total = last(
        pack, firsts, query_grad, key_grad, normed1, w_qkv, qkv_far, patches[0], hidden_grad, small,
        ahead_x, ahead_y, send_rest, keep, vector,
    )
    shares = pack.unpack(vector_total)
    return (
        mixed[None],
        inputs_grad[None],
        shares[0],
        shares[1],
        qkv_total.astype(f32),
        shares[2],
        out_total.astype(f32),
        shares[3],
        shares[4],
        shares[5],
        up_total.astype(f32),
        shares[6],
        down_total.astype(f32),
        shares[7],
    )


def shifted_2(block, axis, distance):
    devices = range(lax.axis_size(axis))
    route = [((i - distance) % len(devices), i) for i in devices]
    return lax.ppermute(block, axis, route)


def any_mesh_body(
    patches,
    doc_lengths,
    norm1_gain,
    norm1_bias,
    w_qkv,
    b_qv,
    w_out,
    b_out,
    norm2_gain,
    norm2_bias,
    w_up,
    b_up,
    w_down,
    b_down,
    cotangent,
):
    tok_rows = patches.shape[1]
    model_width = patches.shape[2]
    ctx_size = lax.axis_size("ctx")
    ctx_place = lax.axis_index("ctx")
    gathered = (
        lax.all_gather(norm1_gain, "wsh", axis=0, tiled=True),
        lax.all_gather(norm1_bias, "wsh", axis=0, tiled=True),
        lax.all_gather(w_qkv, "wsh", axis=0, tiled=True),
        lax.all_gather(b_qv, "wsh", axis=0, tiled=True),
        lax.all_gather(w_out, "wsh", axis=0, tiled=True),
        lax.all_gather(b_out, "wsh", axis=0, tiled=True),
        lax.all_gather(norm2_gain, "wsh", axis=0, tiled=True),
        lax.all_gather(norm2_bias, "wsh", axis=0, tiled=True),
        lax.all_gather(w_up, "wsh", axis=0, tiled=True),
        lax.all_gather(b_up, "wsh", axis=0, tiled=True),
        lax.all_gather(w_down, "wsh", axis=0, tiled=True),
        lax.all_gather(b_down, "wsh", axis=0, tiled=True),
    )
    (
        gain1,
        bias1,
        wqkv_full,
        bqv_full,
        wout_full,
        bout_full,
        gain2,
        bias2,
        wup_full,
        bup_full,
        wdown_full,
        bdown_full,
    ) = gathered
    inputs = patches[0].astype(jnp.float32)
    lengths = doc_lengths[0]
    doc_starts = jnp.cumsum(lengths) - lengths
    row_offsets = lax.iota(jnp.int32, tok_rows)
    query_docs = doc_index(ctx_place * tok_rows + row_offsets, doc_starts)
    gain1_float = gain1.astype(jnp.float32)
    bias1_float = bias1.astype(jnp.float32)
    normed1 = layer_norm(inputs, gain1_float, bias1_float).astype(jnp.bfloat16)
    projected = jnp.dot(normed1, wqkv_full, preferred_element_type=jnp.float32)
    bqv_float = bqv_full.astype(jnp.float32)
    query_low = (projected[:, :model_width] + bqv_float[:model_width]).astype(jnp.bfloat16)
    key_low = projected[:, model_width : 2 * model_width].astype(jnp.bfloat16)
    value_low = (projected[:, 2 * model_width :] + bqv_float[model_width:]).astype(jnp.bfloat16)
    query_heads = query_low.reshape(tok_rows, H, HD)

    def attend_block(state, key_block, value_block, key_start):
        run_max, run_total, run_acc = state
        key_docs = doc_index(key_start + row_offsets, doc_starts)
        same_doc = (query_docs[:, None] == key_docs[None, :])[None]
        scores = (
            jnp.einsum(
                "qhd,khd->hqk",
                query_heads,
                key_block.reshape(tok_rows, H, HD),
                preferred_element_type=jnp.float32,
            )
            * 0.125
        )
        scores = jnp.where(same_doc, scores, masked_score)
        new_max = jnp.maximum(run_max, jnp.max(scores, axis=2))
        weights = jnp.where(same_doc, jnp.exp(scores - new_max[:, :, None]), 0.0)
        factor = jnp.exp(run_max - new_max)
        new_total = run_total * factor + jnp.sum(weights, axis=2)
        new_acc = run_acc * factor[:, :, None] + jnp.einsum(
            "hqk,khd->hqd",
            weights.astype(jnp.bfloat16),
            value_block.reshape(tok_rows, H, HD),
            preferred_element_type=jnp.float32,
        )
        return (new_max, new_total, new_acc)

    initial = (
        jnp.full((H, tok_rows), masked_score, jnp.float32),
        jnp.zeros((H, tok_rows), jnp.float32),
        jnp.zeros((H, tok_rows, HD), jnp.float32),
    )
    state = initial
    key_piece = lax.all_gather(key_low, "ctx", axis=0, tiled=True)
    value_piece = lax.all_gather(value_low, "ctx", axis=0, tiled=True)
    blocks = key_piece.shape[0] // tok_rows
    key_blocks = key_piece.reshape(blocks, tok_rows, model_width)
    value_blocks = value_piece.reshape(blocks, tok_rows, model_width)
    block_starts = tok_rows * lax.iota(jnp.int32, blocks)

    def one_block(inner, item):
        key_block, value_block, key_start = item
        return (attend_block(inner, key_block, value_block, key_start), None)

    state, unused = lax.scan(one_block, state, (key_blocks, value_blocks, block_starts))
    run_max, run_total, run_acc = state
    log_total = run_max + jnp.log(run_total)
    attended = jnp.transpose(run_acc / run_total[:, :, None], (1, 0, 2)).reshape(
        tok_rows, model_width
    )
    attended_low = attended.astype(jnp.bfloat16)
    branch = jnp.dot(
        attended_low, wout_full, preferred_element_type=jnp.float32
    ) + bout_full.astype(jnp.float32)
    hidden_sum = inputs + branch
    gain2_float = gain2.astype(jnp.float32)
    bias2_float = bias2.astype(jnp.float32)
    normed2 = layer_norm(hidden_sum, gain2_float, bias2_float).astype(jnp.bfloat16)
    pre_act = jnp.dot(normed2, wup_full, preferred_element_type=jnp.float32) + bup_full.astype(
        jnp.float32
    )
    activated = exact_gelu(pre_act).astype(jnp.bfloat16)
    mixed = (
        hidden_sum
        + jnp.dot(activated, wdown_full, preferred_element_type=jnp.float32)
        + bdown_full.astype(jnp.float32)
    )
    back_gain1 = gathered[0].astype(jnp.float32)
    back_bias1 = gathered[1].astype(jnp.float32)
    back_wqkv = gathered[2]
    back_wout = gathered[4]
    back_gain2 = gathered[6].astype(jnp.float32)
    back_bias2 = gathered[7].astype(jnp.float32)
    back_wup = gathered[8]
    back_wdown = gathered[10]
    out_grad = cotangent[0]
    wdown_grad = jnp.einsum("tf,td->fd", activated, out_grad, preferred_element_type=jnp.float32)
    bdown_grad = jnp.sum(out_grad.astype(jnp.float32), axis=0)
    act_grad = jnp.einsum("td,fd->tf", out_grad, back_wdown, preferred_element_type=jnp.float32)
    unused_act, gelu_back = jax.vjp(exact_gelu, pre_act)
    pre_grad = gelu_back(act_grad)[0].astype(jnp.bfloat16)
    wup_grad = jnp.einsum("tc,tf->cf", normed2, pre_grad, preferred_element_type=jnp.float32)
    bup_grad = jnp.sum(pre_grad.astype(jnp.float32), axis=0)
    normed2_grad = jnp.einsum("tf,cf->tc", pre_grad, back_wup, preferred_element_type=jnp.float32)
    unused_norm2, norm2_back = jax.vjp(layer_norm, hidden_sum, back_gain2, back_bias2)
    hidden_part, gain2_grad, bias2_grad = norm2_back(normed2_grad)
    hidden_grad = out_grad.astype(jnp.float32) + hidden_part
    branch_grad = hidden_grad.astype(jnp.bfloat16)
    wout_grad = jnp.einsum(
        "tc,td->cd", attended_low, branch_grad, preferred_element_type=jnp.float32
    )
    bout_grad = jnp.sum(branch_grad.astype(jnp.float32), axis=0)
    attended_grad = jnp.einsum(
        "td,cd->tc", branch_grad, back_wout, preferred_element_type=jnp.float32
    ).astype(jnp.bfloat16)
    delta = jnp.sum(
        (attended_grad.astype(jnp.float32) * attended).reshape(tok_rows, H, HD), axis=2
    ).T
    grad_heads = attended_grad.reshape(tok_rows, H, HD)

    def back_block(state, anchor):
        key_start = anchor * tok_rows
        key_cur, value_cur, key_grad, value_grad, query_grad = state
        key_docs = doc_index(key_start + row_offsets, doc_starts)
        same_doc = (query_docs[:, None] == key_docs[None, :])[None]
        key_heads = key_cur.reshape(tok_rows, H, HD)
        scores = (
            jnp.einsum("qhd,khd->hqk", query_heads, key_heads, preferred_element_type=jnp.float32)
            * 0.125
        )
        probs = jnp.where(same_doc, jnp.exp(scores - log_total[:, :, None]), 0.0)
        value_grad = value_grad + jnp.einsum(
            "hqk,qhd->khd",
            probs.astype(jnp.bfloat16),
            grad_heads,
            preferred_element_type=jnp.float32,
        ).reshape(tok_rows, model_width)
        prob_grad = jnp.einsum(
            "qhd,khd->hqk",
            grad_heads,
            value_cur.reshape(tok_rows, H, HD),
            preferred_element_type=jnp.float32,
        )
        score_grad = (probs * (prob_grad - delta[:, :, None])).astype(jnp.bfloat16)
        query_grad = (
            query_grad
            + jnp.einsum(
                "hqk,khd->qhd", score_grad, key_heads, preferred_element_type=jnp.float32
            ).reshape(tok_rows, model_width)
            * 0.125
        )
        key_grad = (
            key_grad
            + jnp.einsum(
                "hqk,qhd->khd", score_grad, query_heads, preferred_element_type=jnp.float32
            ).reshape(tok_rows, model_width)
            * 0.125
        )
        return (key_cur, value_cur, key_grad, value_grad, query_grad)

    def pass_on(state):
        key_cur, value_cur, key_grad, value_grad, query_grad = state
        moved_keys = shifted_2((key_cur, value_cur), "ctx", 1)
        moved_sums = (
            shifted_2(key_grad.astype(jnp.bfloat16), "ctx", 1).astype(key_grad.dtype),
            shifted_2(value_grad.astype(jnp.bfloat16), "ctx", 1).astype(value_grad.dtype),
        )
        return (moved_keys[0], moved_keys[1], moved_sums[0], moved_sums[1], query_grad)

    def two_steps(turn, state):
        state = pass_on(back_block(state, (ctx_place - 2 * turn) % ctx_size))
        state = pass_on(back_block(state, (ctx_place - 2 * turn - 1) % ctx_size))
        return state

    zero_rows = jnp.zeros((tok_rows, model_width), jnp.float32)
    final_state = lax.fori_loop(
        0, ctx_size // 2, two_steps, (key_low, value_low, zero_rows, zero_rows, zero_rows)
    )
    key_grad_low = final_state[2].astype(jnp.bfloat16)
    value_grad_low = final_state[3].astype(jnp.bfloat16)
    query_grad_low = final_state[4].astype(jnp.bfloat16)
    projected_grad = jnp.concatenate([query_grad_low, key_grad_low, value_grad_low], axis=1)
    wqkv_grad = jnp.einsum("tc,te->ce", normed1, projected_grad, preferred_element_type=jnp.float32)
    bqv_grad = jnp.concatenate(
        [
            jnp.sum(query_grad_low.astype(jnp.float32), axis=0),
            jnp.sum(value_grad_low.astype(jnp.float32), axis=0),
        ]
    )
    normed1_grad = jnp.einsum(
        "te,ce->tc", projected_grad, back_wqkv, preferred_element_type=jnp.float32
    )
    unused_norm1, norm1_back = jax.vjp(layer_norm, inputs, back_gain1, back_bias1)
    input_part, gain1_grad, bias1_grad = norm1_back(normed1_grad)
    inputs_grad = hidden_grad + input_part
    shares = (
        lax.psum_scatter(
            gain1_grad.astype(jnp.bfloat16), "wsh", scatter_dimension=0, tiled=True
        ).astype(jnp.float32),
        lax.psum_scatter(
            bias1_grad.astype(jnp.bfloat16), "wsh", scatter_dimension=0, tiled=True
        ).astype(jnp.float32),
        lax.psum_scatter(
            wqkv_grad.astype(jnp.bfloat16), "wsh", scatter_dimension=0, tiled=True
        ).astype(jnp.float32),
        lax.psum_scatter(
            bqv_grad.astype(jnp.bfloat16), "wsh", scatter_dimension=0, tiled=True
        ).astype(jnp.float32),
        lax.psum_scatter(
            wout_grad.astype(jnp.bfloat16), "wsh", scatter_dimension=0, tiled=True
        ).astype(jnp.float32),
        lax.psum_scatter(
            bout_grad.astype(jnp.bfloat16), "wsh", scatter_dimension=0, tiled=True
        ).astype(jnp.float32),
        lax.psum_scatter(
            gain2_grad.astype(jnp.bfloat16), "wsh", scatter_dimension=0, tiled=True
        ).astype(jnp.float32),
        lax.psum_scatter(
            bias2_grad.astype(jnp.bfloat16), "wsh", scatter_dimension=0, tiled=True
        ).astype(jnp.float32),
        lax.psum_scatter(
            wup_grad.astype(jnp.bfloat16), "wsh", scatter_dimension=0, tiled=True
        ).astype(jnp.float32),
        lax.psum_scatter(
            bup_grad.astype(jnp.bfloat16), "wsh", scatter_dimension=0, tiled=True
        ).astype(jnp.float32),
        lax.psum_scatter(
            wdown_grad.astype(jnp.bfloat16), "wsh", scatter_dimension=0, tiled=True
        ).astype(jnp.float32),
        lax.psum_scatter(
            bdown_grad.astype(jnp.bfloat16), "wsh", scatter_dimension=0, tiled=True
        ).astype(jnp.float32),
    )
    totals = (
        lax.psum(shares[0].astype(jnp.bfloat16), "ctx").astype(jnp.float32),
        lax.psum(shares[1].astype(jnp.bfloat16), "ctx").astype(jnp.float32),
        lax.psum(shares[2].astype(jnp.bfloat16), "ctx").astype(jnp.float32),
        lax.psum(shares[3].astype(jnp.bfloat16), "ctx").astype(jnp.float32),
        lax.psum(shares[4].astype(jnp.bfloat16), "ctx").astype(jnp.float32),
        lax.psum(shares[5].astype(jnp.bfloat16), "ctx").astype(jnp.float32),
        lax.psum(shares[6].astype(jnp.bfloat16), "ctx").astype(jnp.float32),
        lax.psum(shares[7].astype(jnp.bfloat16), "ctx").astype(jnp.float32),
        lax.psum(shares[8].astype(jnp.bfloat16), "ctx").astype(jnp.float32),
        lax.psum(shares[9].astype(jnp.bfloat16), "ctx").astype(jnp.float32),
        lax.psum(shares[10].astype(jnp.bfloat16), "ctx").astype(jnp.float32),
        lax.psum(shares[11].astype(jnp.bfloat16), "ctx").astype(jnp.float32),
    )
    return (
        mixed.astype(jnp.bfloat16)[None],
        inputs_grad[None],
        totals[0],
        totals[1],
        totals[2],
        totals[3],
        totals[4],
        totals[5],
        totals[6],
        totals[7],
        totals[8],
        totals[9],
        totals[10],
        totals[11],
    )


def solution(mesh):
    as_planned = mesh.shape["ctx"] == GROUPS * PEERS and mesh.shape["wsh"] == 2
    return jax.shard_map(
        body if as_planned else any_mesh_body,
        mesh=mesh,
        in_specs=(
            P("wsh", "ctx", None),
            P("wsh", None),
            P("wsh"),
            P("wsh"),
            P("wsh", None),
            P("wsh"),
            P("wsh", None),
            P("wsh"),
            P("wsh"),
            P("wsh"),
            P("wsh", None),
            P("wsh"),
            P("wsh", None),
            P("wsh"),
            P("wsh", "ctx", None),
        ),
        out_specs=(
            P("wsh", "ctx", None),
            P("wsh", "ctx", None),
            P("wsh"),
            P("wsh"),
            P("wsh", None),
            P("wsh"),
            P("wsh", None),
            P("wsh"),
            P("wsh"),
            P("wsh"),
            P("wsh", None),
            P("wsh"),
            P("wsh", None),
            P("wsh"),
        ),
        check_vma=False,
    )
```
